256 devices in a mesh: ctx: 8 (over x, core), dp: 32 (over y, z).
Axes of the slice: x: 4, y: 4, z: 8, core: 2. Of those that a mesh axis runs over, the one named last changes fastest.
Arguments:
- tokens: bfloat16 [32, 1024, 1536], P('dp', 'ctx')
- grad_heads: bfloat16 [32, 1024, 1536], P('dp', 'ctx'), may hold values from -6 to 6
- tile_mask: int32 [32, 8, 8], P('dp', 'ctx'), may hold values from 0 to 1
- segments: int32 [32, 1024], P('dp'), may hold values from 0 to 3, never falling along the last dimension, each value on 1 to 512 neighbouring positions
- w_query: bfloat16 [1536, 1536], replicated
- w_key: bfloat16 [1536, 256], replicated
- w_value: bfloat16 [1536, 256], replicated, may hold values from -0.15625 to 0.15625
Outputs:
- grad_tokens: bfloat16 [32, 1024, 1536], P('dp', 'ctx')
- grad_projection: float32 [1536, 2048], P('dp', 'ctx')
The draws below stay inside these ranges and needn't reach their ends.
Inputs may be any that keep to these rules, and one draw needn't show every extreme that they name: `segments`: segment numbers never fall along a sequence.
All inputs are finite; a program needn't handle non-finite values.
Results may differ from the reference program's by a relative error of at most 0.029.
Values may be sent and summed in bfloat16 or wider, within the bound.
No kernel may reach another device: no remote copies, remote signals or barrier semaphores. Data moves between devices by JAX's collectives and lax.ppermute only.
A program may use at most 128 MiB of HBM per device.

```python
import math
import jax
import jax.numpy as jnp
import numpy as np
from jax import lax

D = 1536
QH = 12
KVH = 2
HD = 128
TILE = 128
SEQ = 1024
SEQS = 32
NT = 8
QF = 1536
KVF = 256


def key_basis(key):
    return jnp.clip(jax.random.normal(key, (D, KVH * HD), jnp.float32), -5.0, 5.0)


def draw_w_key(key, part):
    basis = key_basis(key)
    key = jax.random.fold_in(key, 3)
    own = jnp.clip(jax.random.normal(key, (D, KVH * HD), jnp.float32), -5.0, 5.0)
    return ((0.9 * basis + 0.4 * own) * D ** (-0.5)).astype(jnp.bfloat16)


def draw_w_query(key, part):
    key = jax.random.fold_in(key, 5)
    own = jnp.clip(jax.random.normal(key, (D, QH * HD), jnp.float32), -5.0, 5.0)
    mixed = own
    return (mixed * D ** (-0.5)).astype(jnp.bfloat16)


def draw_tokens(key, part):
    key = jax.random.fold_in(key, 7)
    first = jax.random.fold_in(key, 0)
    base = jnp.clip(jax.random.normal(first, (SEQS, SEQ, D), jnp.float32), -6.0, 6.0)
    return base.astype(jnp.bfloat16)


def draw_tile_mask(key, part):
    key = jax.random.fold_in(key, 11)
    first, second = jax.random.split(key)
    levels = jax.random.randint(first, (SEQS, NT, 1), 15, 71)
    entries = jax.random.randint(second, (SEQS, NT, NT), 0, 100)
    return (entries < levels).astype(jnp.int32)


def steps_of(stream_key, shape, cuts, low, largest):
    level = 1.0
    for position, shards_of in cuts:
        steps = jax.random.uniform(jax.random.fold_in(jax.random.fold_in(stream_key, 6), position), (shards_of,), jnp.float32, low / len(cuts), largest / len(cuts))
        level = level * jnp.repeat(jnp.exp(steps), shape[position] // shards_of).reshape((-1,) + (1,) * (len(shape) - 1 - position))
    return level


def profile(amount, total, limit, slope):
    loads = [(1 << 20) // math.isqrt(rank ** slope) + 1 for rank in range(2, amount + 1)]
    rest, given = total - limit - (amount - 1), [1] * (amount - 1)
    while rest > 0:
        candidates = [i for i in range(amount - 1) if given[i] < limit]
        whole, budget = sum([loads[i] for i in candidates]), rest
        for i in candidates:
            extra = min(limit - given[i], max(1, budget * loads[i] // whole), rest)
            given[i] = given[i] + extra
            rest = rest - extra
    return np.array([limit] + given)


def uneven_parts(key, count, total, bound, skew):
    if count == 2:
        one = jax.random.randint(key, (), max(1, total - bound), min(bound, total - 1) + 1)
        return jnp.stack([one, total - one])
    lengths = jnp.asarray(profile(count, total, bound, skew), jnp.int32)
    couples = (count - 1) // 2
    source_of, sink = lengths[1:1 + 2 * couples:2], lengths[2:2 + 2 * couples:2]
    room = jnp.minimum(source_of - 1, bound - sink)
    shifted = jax.random.randint(jax.random.fold_in(key, 1), (couples,), 0, 1 << 20) % (room + 1)
    lengths = lengths.at[1:1 + 2 * couples:2].set(source_of - shifted).at[2:2 + 2 * couples:2].set(sink + shifted)
    return lengths[jax.random.permutation(jax.random.fold_in(key, 2), count)]


def gaussian(stream_key, dims, scale, limit, shards=(), held_as=jnp.bfloat16):
    drawn = jax.random.normal(stream_key, dims, jnp.float32) * scale
    if len(shards) > 0:
        drawn = steps_of(stream_key, dims, shards, -0.22, 0.18) * drawn
    return jnp.clip(drawn, min=-limit, max=limit).astype(held_as)


def setup_inputs(seed: int = 0) -> dict:
    key_list = jax.random.split(jax.random.key(seed), 8)
    tokens = draw_tokens(jax.random.fold_in(key_list[7], 71), 0)
    grad_heads = gaussian(key_list[1], (SEQS, SEQ, QF), 1.0, 6.0, ((0, 32), (1, 8)))
    tile_mask = draw_tile_mask(jax.random.fold_in(key_list[7], 71), 0)
    segments = jax.vmap(lambda own: jnp.searchsorted(jnp.cumsum(uneven_parts(own, max(SEQ // 256, 4), SEQ, min(1024, SEQ // 2), 1)), jnp.arange(SEQ), side="right"))(jax.random.split(key_list[3], SEQS)).reshape((SEQS, SEQ)).astype(jnp.int32)
    w_query = draw_w_query(jax.random.fold_in(key_list[7], 71), 0)
    w_key = draw_w_key(jax.random.fold_in(key_list[7], 71), 0)
    w_value = gaussian(key_list[6], (D, KVF), D ** -0.5, 0.15625)
    return {"tokens": tokens, "grad_heads": grad_heads, "tile_mask": tile_mask, "segments": segments, "w_query": w_query, "w_key": w_key, "w_value": w_value}


def allowed_pairs(tiles, row_segments, col_segments):
    spread = jnp.repeat(jnp.repeat(tiles, TILE, axis=0), TILE, axis=1)
    return (spread == 1) | (row_segments[:, None] == col_segments[None, :])

def one_sequence(tokens, grad_heads, tiles, segments, w_query, w_key, w_value):
    softmax_scale = 1.0 / math.sqrt(HD)
    queries = jnp.dot(tokens, w_query, preferred_element_type=jnp.float32).astype(jnp.bfloat16)
    keys = jnp.dot(tokens, w_key, preferred_element_type=jnp.float32).astype(jnp.bfloat16)
    values = jnp.dot(tokens, w_value, preferred_element_type=jnp.float32).astype(jnp.bfloat16)
    allowed = allowed_pairs(tiles, segments, segments)
    group = QH // KVH
    query_parts = []
    key_parts = []
    value_parts = []
    for kv_head in range(KVH):
        key_head = keys[:, kv_head * HD:(kv_head + 1) * HD]
        value_head = values[:, kv_head * HD:(kv_head + 1) * HD]
        key_total = jnp.zeros((keys.shape[0], HD), jnp.float32)
        value_total = jnp.zeros((keys.shape[0], HD), jnp.float32)
        for member in range(group):
            head = kv_head * group + member
            query_head = queries[:, head * HD:(head + 1) * HD]
            upstream = grad_heads[:, head * HD:(head + 1) * HD]
            scores = jnp.dot(query_head, key_head.T, preferred_element_type=jnp.float32) * softmax_scale
            scores = jnp.where(allowed, scores, -jnp.inf)
            probs = jax.nn.softmax(scores, axis=-1)
            probs_low = probs.astype(jnp.bfloat16)
            attended = jnp.dot(probs_low, value_head, preferred_element_type=jnp.float32)
            delta = lax.optimization_barrier(jnp.sum(upstream.astype(jnp.float32) * attended, axis=-1, keepdims=True))
            grad_probs = jnp.dot(upstream, value_head.T, preferred_element_type=jnp.float32)
            grad_scores = (probs * (grad_probs - delta)).astype(jnp.bfloat16)
            query_parts.append((jnp.dot(grad_scores, key_head, preferred_element_type=jnp.float32) * softmax_scale).astype(jnp.bfloat16))
            key_total = key_total + jnp.dot(grad_scores.T, query_head, preferred_element_type=jnp.float32) * softmax_scale
            value_total = value_total + jnp.dot(probs_low.T, upstream, preferred_element_type=jnp.float32)
        key_parts.append(key_total.astype(jnp.bfloat16))
        value_parts.append(value_total.astype(jnp.bfloat16))
    grad_query = jnp.concatenate(query_parts, axis=1)
    grad_key = jnp.concatenate(key_parts, axis=1)
    grad_value = jnp.concatenate(value_parts, axis=1)
    grad_tokens = jnp.dot(grad_query, w_query.T, preferred_element_type=jnp.float32)
    grad_tokens = grad_tokens + jnp.dot(grad_key, w_key.T, preferred_element_type=jnp.float32)
    grad_tokens = grad_tokens + jnp.dot(grad_value, w_value.T, preferred_element_type=jnp.float32)
    stacked = jnp.concatenate([grad_query, grad_key, grad_value], axis=1)
    return (grad_tokens.astype(jnp.bfloat16), jnp.dot(tokens.T, stacked, preferred_element_type=jnp.float32))

def reference(tokens, grad_heads, tile_mask, segments, w_query, w_key, w_value):

    def advance(total, items):
        grad_tokens, term = one_sequence(items[0], items[1], items[2], items[3], w_query, w_key, w_value)
        return (total + term, grad_tokens)
    start_total = jnp.zeros((D, (QH + 2 * KVH) * HD), jnp.float32)
    total, grad_tokens = lax.scan(advance, start_total, (tokens, grad_heads, tile_mask, segments))
    return (grad_tokens, total)
```

```python
import functools
import math

import jax
import jax.numpy as jnp
from jax import lax
from jax.experimental import pallas as pl
from jax.experimental.pallas import tpu as pltpu
from jax.sharding import PartitionSpec as P

QH = 12
KVH = 2
HD = 128
TILE = 128
D = 1536
KEYS = 1024
CHIPS = 4
GROUP = QH // KVH
GF = GROUP * HD
YS = 4
ZS = 8
SCALE = 1.0 / math.sqrt(HD)
LOG2_SCALE = SCALE * math.log2(math.e)
BF = jnp.bfloat16
F32 = jnp.float32
VMEM_LIMIT = 48 * 1024 * 1024

CORE = [(i, i ^ 1) for i in range(8)]
NT = (((1,), (1,)), ((), ()))


def chip_shift(d):
    return [(i, ((i // 2 + d) % CHIPS) * 2 + i % 2) for i in range(8)]


def y_shift(d):
    return [(i, ((i // ZS + d) % YS) * ZS + i % ZS) for i in range(32)]


Z_GROUPS = [[y * ZS + z for z in range(ZS)] for y in range(YS)]


def dot(a, b):
    return jnp.dot(a, b, preferred_element_type=F32)


def dot_nt(a, b):
    return lax.dot_general(a, b, NT, preferred_element_type=F32)


def cost(flops, bytes_accessed, transcendentals=0):
    return pl.CostEstimate(
        flops=flops, bytes_accessed=bytes_accessed, transcendentals=transcendentals
    )


PARAMS = pltpu.CompilerParams(vmem_limit_bytes=VMEM_LIMIT)
WHOLE = pl.BlockSpec(memory_space=pltpu.VMEM)


def kv_kernel(place, own, other, w_key, w_value, out):
    weights = jnp.concatenate([w_key[...], w_value[...]], axis=1)
    out[:TILE] = dot(own[...], weights).astype(BF)
    out[TILE:] = dot(other[...], weights).astype(BF)


def project_kv(place, own, other, w_key, w_value):
    return pl.pallas_call(
        kv_kernel,
        grid_spec=pltpu.PrefetchScalarGridSpec(
            num_scalar_prefetch=1,
            grid=(1,),
            in_specs=[
                pl.BlockSpec((TILE, D), lambda i, p: (0, 0)),
                pl.BlockSpec((TILE, D), lambda i, p: (0, 0)),
                pl.BlockSpec((D, HD), lambda i, p: (0, p[1])),
                pl.BlockSpec((D, HD), lambda i, p: (0, p[1])),
            ],
            out_specs=pl.BlockSpec((2 * TILE, 2 * HD), lambda i, p: (0, 0)),
        ),
        out_shape=jax.ShapeDtypeStruct((2 * TILE, 2 * HD), BF),
        compiler_params=PARAMS,
        cost_estimate=cost(2 * 256 * D * 256, 2 * (256 * D + D * 256)),
        name="project_kv",
    )(place, own, other, w_key, w_value)


def query_kernel(place, own, other, w_query, segments, mask_own, mask_other, out, bias):
    out[:TILE] = dot(own[...], w_query[...]).astype(BF)
    out[TILE:] = dot(other[...], w_query[...]).astype(BF)

    @pl.when(pl.program_id(0) == 0)
    def _():
        chip, core = place[0], place[1]
        passages = segments[...]
        ends = [jnp.sum((passages <= s).astype(jnp.int32)) for s in range(3)]
        for slot in range(2):
            masks = mask_own if slot == 0 else mask_other
            tile = 2 * chip + (core if slot == 0 else 1 - core)
            mine = segments[:, pl.ds(pl.multiple_of(tile * TILE, TILE), TILE)]
            low = jnp.where(
                mine == 0, 0, jnp.where(mine == 1, ends[0], jnp.where(mine == 2, ends[1], ends[2]))
            )
            high = jnp.where(
                mine == 0,
                ends[0],
                jnp.where(mine == 1, ends[1], jnp.where(mine == 2, ends[2], KEYS)),
            )
            for d in range(CHIPS):
                for key_slot in range(2):
                    key_tile = 2 * lax.rem(chip + CHIPS - d, CHIPS) + (
                        core if key_slot == 0 else 1 - core
                    )
                    seen = masks[0, key_tile] == 1
                    position = key_tile * TILE + lax.broadcasted_iota(
                        jnp.int32, (TILE, TILE), 0
                    )
                    first = jnp.where(seen, 0, low)
                    last = jnp.where(seen, KEYS, high)
                    allowed = (position >= first) & (position < last)
                    row = d * 2 * TILE + key_slot * TILE
                    bias[row : row + TILE, slot * TILE : (slot + 1) * TILE] = jnp.where(
                        allowed, 0.0, -jnp.inf
                    )


def project_query(place, own, other, w_query, segments, mask_own, mask_other):
    blocks = GF // 256
    return pl.pallas_call(
        query_kernel,
        grid_spec=pltpu.PrefetchScalarGridSpec(
            num_scalar_prefetch=1,
            grid=(blocks,),
            in_specs=[
                pl.BlockSpec((TILE, D), lambda i, p: (0, 0)),
                pl.BlockSpec((TILE, D), lambda i, p: (0, 0)),
                pl.BlockSpec((D, 256), lambda i, p: (0, p[1] * blocks + i)),
                pl.BlockSpec((1, KEYS), lambda i, p: (0, 0)),
                pl.BlockSpec(memory_space=pltpu.SMEM),
                pl.BlockSpec(memory_space=pltpu.SMEM),
            ],
            out_specs=[
                pl.BlockSpec((2 * TILE, 256), lambda i, p: (0, i)),
                pl.BlockSpec((KEYS, 2 * TILE), lambda i, p: (0, 0)),
            ],
        ),
        out_shape=[
            jax.ShapeDtypeStruct((2 * TILE, GF), BF),
            jax.ShapeDtypeStruct((KEYS, 2 * TILE), F32),
        ],
        compiler_params=PARAMS,
        cost_estimate=cost(2 * 256 * D * GF, 2 * (256 * D + D * GF + 256 * GF)),
        name="project_query",
    )(place, own, other, w_query, segments, mask_own, mask_other)


def attention_kernel(
    place, query, up_own, up_other, kv0, kv1, kv2, kv3, bias,
    grad_query, out0, out1, out2, out3,
    keys, values, keys_t, grad_key, grad_value,
):
    step = pl.program_id(0)

    @pl.when(step == 0)
    def _():
        for d, kv in enumerate((kv0, kv1, kv2, kv3)):
            keys[d * 256 : (d + 1) * 256] = kv[:, :HD]
            values[d * 256 : (d + 1) * 256] = kv[:, HD:]
            keys_t[:, d * 256 : (d + 1) * 256] = kv[:, :HD].T
        grad_key[...] = jnp.zeros_like(grad_key)
        grad_value[...] = jnp.zeros_like(grad_value)

    for member in range(2):
        columns = slice(member * HD, (member + 1) * HD)
        q = query[:, columns]
        up = jnp.concatenate([up_own[:, columns], up_other[:, columns]], axis=0)
        scores = dot_nt(keys[...], q) * LOG2_SCALE + bias[...]
        top = jnp.max(scores, axis=0, keepdims=True)
        powers = jnp.exp2(scores - top)
        probs = powers * (1.0 / jnp.sum(powers, axis=0, keepdims=True))
        probs_low = probs.astype(BF)
        grad_probs = dot_nt(values[...], up)
        delta = jnp.sum(probs_low.astype(F32) * grad_probs, axis=0, keepdims=True)
        grad_scores = (probs * (grad_probs - delta)).astype(BF)
        grad_value[...] += dot(probs_low, up)
        grad_key[...] += dot(grad_scores, q)
        grad_query[:, columns] = (dot(keys_t[...], grad_scores) * SCALE).T.astype(BF)

    @pl.when(step == pl.num_programs(0) - 1)
    def _():
        for d, out in enumerate((out0, out1, out2, out3)):
            rows = slice(d * 256, (d + 1) * 256)
            out[:, :HD] = (grad_key[rows] * SCALE).astype(out.dtype)
            out[:, HD:] = grad_value[rows].astype(out.dtype)


def attention(place, query, up_own, up_other, kvs, bias):
    blocks = GF // 256
    fixed = pl.BlockSpec((256, 256), lambda i, p: (0, 0))
    return pl.pallas_call(
        attention_kernel,
        grid_spec=pltpu.PrefetchScalarGridSpec(
            num_scalar_prefetch=1,
            grid=(blocks,),
            in_specs=[
                pl.BlockSpec((256, 256), lambda i, p: (0, i)),
                pl.BlockSpec((TILE, 256), lambda i, p: (0, p[1] * blocks + i)),
                pl.BlockSpec((TILE, 256), lambda i, p: (0, p[1] * blocks + i)),
                fixed, fixed, fixed, fixed,
                pl.BlockSpec((KEYS, 256), lambda i, p: (0, 0)),
            ],
            out_specs=[pl.BlockSpec((256, 256), lambda i, p: (0, i)), fixed, fixed, fixed, fixed],
            scratch_shapes=[
                pltpu.VMEM((KEYS, HD), BF),
                pltpu.VMEM((KEYS, HD), BF),
                pltpu.VMEM((HD, KEYS), BF),
                pltpu.VMEM((KEYS, HD), F32),
                pltpu.VMEM((KEYS, HD), F32),
            ],
        ),
        out_shape=[
            jax.ShapeDtypeStruct((256, GF), BF),
            jax.ShapeDtypeStruct((256, 256), F32),
            jax.ShapeDtypeStruct((256, 256), BF),
            jax.ShapeDtypeStruct((256, 256), BF),
            jax.ShapeDtypeStruct((256, 256), BF),
        ],
        compiler_params=PARAMS,
        cost_estimate=cost(10 * GROUP * 256 * KEYS * HD * 2, 4 << 20, GROUP * 256 * KEYS),
        name="attention",
    )(place, query, up_own, up_other, *kvs, bias)


def sum_kernel(a, b, c, d, out):
    total = (a[...] + b[...].astype(F32)) + (c[...].astype(F32) + d[...].astype(F32))
    out[...] = total.astype(out.dtype)


def sum_four(a, b, c, d):
    return pl.pallas_call(
        sum_kernel,
        in_specs=[WHOLE] * 4,
        out_specs=WHOLE,
        out_shape=jax.ShapeDtypeStruct(a.shape, BF),
        compiler_params=PARAMS,
        cost_estimate=cost(4 * a.size, 12 * a.size),
        name="sum_four",
    )(a, b, c, d)


def pack_kernel(place, dq, dq_other, dkv, dkv_other, out0, out1, out2, out3, blocks):
    core = place[1]

    def swapped(ref, columns):
        return jnp.concatenate([ref[TILE:, columns], ref[:TILE, columns]], axis=0)

    middle = slice(256, 512)

    @pl.when(core == 0)
    def _():
        blocks[0] = dq[:, 0:256]
        blocks[1] = dq[:, 512:768]
        blocks[2] = swapped(dq_other, middle)
        blocks[3, :, :HD] = dkv[:, :HD]
        blocks[3, :, HD:] = swapped(dkv_other, slice(0, HD))

    @pl.when(core == 1)
    def _():
        blocks[0] = swapped(dq_other, middle)
        blocks[1] = dq[:, 0:256]
        blocks[2] = dq[:, 512:768]
        blocks[3, :, :HD] = swapped(dkv_other, slice(HD, 2 * HD))
        blocks[3, :, HD:] = dkv[:, HD:]

    for d, out in enumerate((out0, out1, out2, out3)):
        out[...] = blocks[lax.rem(place[0] + d, CHIPS)]


def pack(place, dq, dq_other, dkv, dkv_other):
    return pl.pallas_call(
        pack_kernel,
        in_specs=[pl.BlockSpec(memory_space=pltpu.SMEM)] + [WHOLE] * 4,
        out_specs=[WHOLE] * 4,
        out_shape=[jax.ShapeDtypeStruct((256, 256), BF)] * 4,
        scratch_shapes=[pltpu.VMEM((4, 256, 256), BF)],
        compiler_params=PARAMS,
        cost_estimate=cost(0, 4 << 19),
        name="pack",
    )(place, dq, dq_other, dkv, dkv_other)


def transpose_kernel(*refs):
    out = refs[-1]
    for i, ref in enumerate(refs[:-1]):
        out[:, i * TILE : (i + 1) * TILE] = ref[...].T


def transpose(parts):
    return pl.pallas_call(
        transpose_kernel,
        in_specs=[WHOLE] * 8,
        out_specs=WHOLE,
        out_shape=jax.ShapeDtypeStruct((D, KEYS), BF),
        compiler_params=PARAMS,
        cost_estimate=cost(0, 4 * D * KEYS),
        name="transpose_tokens",
    )(*parts)


def weight_kernel(place, tokens_t, a, b, c, d, out0, out1, out2, out3):
    right = jnp.concatenate([a[...], b[...], c[...], d[...]], axis=0)
    for shift, out in enumerate((out0, out1, out2, out3)):
        row = pl.multiple_of(lax.rem(place[2] + shift, YS) * (D // YS), 128)
        out[...] = dot(tokens_t[pl.ds(row, D // YS)], right).astype(out.dtype)


def weight_grad(place, tokens_t, parts):
    shape = (D // YS, 256)
    return pl.pallas_call(
        weight_kernel,
        in_specs=[pl.BlockSpec(memory_space=pltpu.SMEM)] + [WHOLE] * 5,
        out_specs=[WHOLE] * 4,
        out_shape=[jax.ShapeDtypeStruct(shape, F32)] + [jax.ShapeDtypeStruct(shape, BF)] * 3,
        compiler_params=PARAMS,
        cost_estimate=cost(2 * D * KEYS * 256, 2 * D * KEYS + 3 * D * 256),
        name="weight_grad",
    )(place, tokens_t, *parts)


def input_kernel(place, dq, dq_other, dkv, dkv_other, w_query, w_key, w_value, out, left):
    core = place[1]

    @pl.when(pl.program_id(0) == 0)
    def _():
        mine = pl.ds(pl.multiple_of(core * GF, 128), GF)
        theirs = pl.ds(pl.multiple_of((1 - core) * GF, 128), GF)
        left[:, mine] = dq[:TILE]
        left[:, theirs] = dq_other[TILE:]
        for part in range(2):
            columns = slice(part * HD, (part + 1) * HD)
            base = D + part * KVH * HD
            left[:, pl.ds(pl.multiple_of(base + core * HD, 128), HD)] = dkv[:TILE, columns]
            left[:, pl.ds(pl.multiple_of(base + (1 - core) * HD, 128), HD)] = dkv_other[
                TILE:, columns
            ]

    total = dot_nt(left[:, :D], w_query[...])
    total += dot_nt(left[:, D : D + 256], w_key[...])
    total += dot_nt(left[:, D + 256 :], w_value[...])
    out[...] = total.astype(BF)


def input_grad(place, dq, dq_other, dkv, dkv_other, w_query, w_key, w_value):
    width = 256
    return pl.pallas_call(
        input_kernel,
        grid_spec=pltpu.PrefetchScalarGridSpec(
            num_scalar_prefetch=1,
            grid=(D // width,),
            in_specs=[
                pl.BlockSpec((256, GF), lambda i, p: (0, 0)),
                pl.BlockSpec((256, GF), lambda i, p: (0, 0)),
                pl.BlockSpec((256, 256), lambda i, p: (0, 0)),
                pl.BlockSpec((256, 256), lambda i, p: (0, 0)),
                pl.BlockSpec((width, D), lambda i, p: (i, 0)),
                pl.BlockSpec((width, 256), lambda i, p: (i, 0)),
                pl.BlockSpec((width, 256), lambda i, p: (i, 0)),
            ],
            out_specs=pl.BlockSpec((TILE, width), lambda i, p: (0, i)),
            scratch_shapes=[pltpu.VMEM((TILE, D + 512), BF)],
        ),
        out_shape=jax.ShapeDtypeStruct((TILE, D), BF),
        compiler_params=PARAMS,
        cost_estimate=cost(2 * TILE * D * 2048, 2 * D * 2048),
        name="input_grad",
    )(place, dq, dq_other, dkv, dkv_other, w_query, w_key, w_value)


def final_kernel(parts, out):
    total = parts[0:48].astype(F32)
    for z in range(1, ZS):
        total += parts[z * 48 : (z + 1) * 48].astype(F32)
    out[...] = total


def final_sum(parts):
    return pl.pallas_call(
        final_kernel,
        in_specs=[WHOLE],
        out_specs=WHOLE,
        out_shape=jax.ShapeDtypeStruct((48, 256), F32),
        compiler_params=PARAMS,
        cost_estimate=cost(parts.size, 2 * parts.size),
        name="final_sum",
    )(parts)


def shards(tokens, grad_heads, tile_mask, segments, w_query, w_key, w_value):
    ctx = lax.axis_index("ctx")
    dp = lax.axis_index("dp")
    place = jnp.stack([ctx // 2, ctx % 2, dp // ZS, dp % ZS]).astype(jnp.int32)
    own, up = tokens[0], grad_heads[0]
    other = lax.ppermute(own, "ctx", CORE)
    up_other = lax.ppermute(up, "ctx", CORE)
    mask_other = lax.ppermute(tile_mask[0], "ctx", CORE)

    kv = project_kv(place, own, other, w_key, w_value)
    kvs = [kv] + [lax.ppermute(kv, "ctx", chip_shift(d)) for d in (1, 2, 3)]
    query, bias = project_query(
        place, own, other, w_query, segments, tile_mask[0], mask_other
    )
    kvs, late_own = lax.optimization_barrier((kvs, own))
    far = [lax.ppermute(late_own, "ctx", chip_shift(d)) for d in (1, 2, 3)]

    dq, g0, g1, g2, g3 = attention(place, query, up, up_other, kvs, bias)
    dq_other = lax.ppermute(dq, "ctx", CORE)
    back = [
        lax.ppermute(g, "ctx", chip_shift(CHIPS - d)) for d, g in ((1, g1), (2, g2), (3, g3))
    ]
    dkv = sum_four(g0, *back)
    dkv_other = lax.ppermute(dkv, "ctx", CORE)

    far_other = [lax.ppermute(part, "ctx", CORE) for part in far]
    tokens_t = transpose(
        [own, other] + [part for pair in zip(far, far_other) for part in pair]
    )

    packed = pack(place, dq, dq_other, dkv, dkv_other)
    columns = [packed[0]] + [
        lax.ppermute(packed[d], "ctx", chip_shift(d)) for d in (1, 2, 3)
    ]
    terms = weight_grad(place, tokens_t, columns)
    y_parts = [terms[0]] + [lax.ppermute(terms[d], "dp", y_shift(d)) for d in (1, 2, 3)]
    y_sum = sum_four(*y_parts)
    z_parts = lax.all_to_all(y_sum, "dp", 0, 0, tiled=True, axis_index_groups=Z_GROUPS)
    grad_projection = final_sum(z_parts)

    grad_tokens = input_grad(
        place, dq, dq_other, dkv, dkv_other, w_query, w_key, w_value
    )
    return grad_tokens[None], grad_projection


def solution(mesh):
    return jax.shard_map(
        shards,
        mesh=mesh,
        in_specs=(
            P("dp", "ctx", None),
            P("dp", "ctx", None),
            P("dp", "ctx", None),
            P("dp", None),
            P(),
            P(),
            P(),
        ),
        out_specs=(P("dp", "ctx", None), P("dp", "ctx")),
        check_vma=False,
    )
```

```python
import functools
import math

import jax
import jax.numpy as jnp
from jax import lax
from jax.experimental import pallas as pl
from jax.experimental.pallas import tpu as pltpu
from jax.sharding import PartitionSpec as P

QH = 12
KVH = 2
HD = 128
TILE = 128
D = 1536
KEYS = 1024
CHIPS = 4
GROUP = QH // KVH
GF = GROUP * HD
YS = 4
ZS = 8
SCALE = 1.0 / math.sqrt(HD)
LOG2_SCALE = SCALE * math.log2(math.e)
BF = jnp.bfloat16
F32 = jnp.float32
VMEM_LIMIT = 24 * 1024 * 1024
W_CHUNKS = 4
Q_CHUNKS = 6
IN_CHUNKS = 6

CORE = [(i, i ^ 1) for i in range(8)]
NT = (((1,), (1,)), ((), ()))


def chip_shift(d):
    return [(i, ((i // 2 + d) % CHIPS) * 2 + i % 2) for i in range(8)]


def y_shift(d):
    return [(i, ((i // ZS + d) % YS) * ZS + i % ZS) for i in range(32)]


Z_GROUPS = [[y * ZS + z for z in range(ZS)] for y in range(YS)]


def dot(a, b):
    return jnp.dot(a, b, preferred_element_type=F32)


def dot_nt(a, b):
    return lax.dot_general(a, b, NT, preferred_element_type=F32)


def in_hbm(array):
    return pltpu.with_memory_space_constraint(array, pltpu.HBM)


def cost(flops, bytes_accessed, transcendentals=0):
    return pl.CostEstimate(
        flops=flops, bytes_accessed=bytes_accessed, transcendentals=transcendentals
    )


PARAMS = pltpu.CompilerParams(vmem_limit_bytes=VMEM_LIMIT)
WHOLE = pl.BlockSpec(memory_space=pltpu.VMEM)
SCALARS = pl.BlockSpec(memory_space=pltpu.SMEM)
STAY = pl.BlockSpec(memory_space=pltpu.HBM)


def kv_own_kernel(place, own, w_key, w_value, weights, out, rows, sems):
    columns = pl.ds(pl.multiple_of(place[1] * HD, HD), HD)
    copies = []
    for chunk in range(W_CHUNKS):
        part = pl.ds(chunk * (TILE // W_CHUNKS), TILE // W_CHUNKS)
        copies.append(pltpu.make_async_copy(own.at[part], rows.at[part], sems.at[chunk, 2]))
        part = pl.ds(chunk * (D // W_CHUNKS), D // W_CHUNKS)
        for side, source in enumerate((w_key, w_value)):
            copies.append(
                pltpu.make_async_copy(
                    source.at[part, columns],
                    weights.at[part, pl.ds(side * HD, HD)],
                    sems.at[chunk, side],
                )
            )
    for copy in copies:
        copy.start()
    for copy in copies:
        copy.wait()
    out[...] = dot(rows[...], weights[...]).astype(BF)


def project_kv_own(place, own, w_key, w_value):
    return pl.pallas_call(
        kv_own_kernel,
        in_specs=[SCALARS, STAY, STAY, STAY],
        out_specs=[WHOLE, WHOLE],
        out_shape=[
            jax.ShapeDtypeStruct((D, 2 * HD), BF),
            jax.ShapeDtypeStruct((TILE, 2 * HD), BF),
        ],
        scratch_shapes=[pltpu.VMEM((TILE, D), BF), pltpu.SemaphoreType.DMA((W_CHUNKS, 3))],
        compiler_params=PARAMS,
        cost_estimate=cost(2 * TILE * D * 256, 2 * (TILE * D + D * 256)),
        name="project_kv_own",
    )(place, own, w_key, w_value)


def kv_kernel(other, weights, kv_own, out):
    out[:TILE] = kv_own[...]
    out[TILE:] = dot(other[...], weights[...]).astype(BF)


def project_kv(other, weights, kv_own):
    return pl.pallas_call(
        kv_kernel,
        in_specs=[WHOLE] * 3,
        out_specs=WHOLE,
        out_shape=jax.ShapeDtypeStruct((2 * TILE, 2 * HD), BF),
        compiler_params=PARAMS,
        cost_estimate=cost(2 * TILE * D * 256, 2 * (TILE * D + D * 256)),
        name="project_kv",
    )(other, weights, kv_own)


def query_kernel(
    place, own, other, w_query, segments, mask_own, mask_other, out, bias, weights, sems
):
    columns = pl.ds(pl.multiple_of(place[1] * GF, HD), GF)
    copies = []
    for chunk in range(Q_CHUNKS):
        part = pl.ds(chunk * (D // Q_CHUNKS), D // Q_CHUNKS)
        copies.append(
            pltpu.make_async_copy(w_query.at[part, columns], weights.at[part], sems.at[chunk])
        )
    for copy in copies:
        copy.start()

    chip, core = place[0], place[1]
    passages = segments[...]
    ends = [jnp.sum((passages <= s).astype(jnp.int32)) for s in range(3)]
    for slot in range(2):
        masks = mask_own if slot == 0 else mask_other
        tile = 2 * chip + (core if slot == 0 else 1 - core)
        mine = segments[:, pl.ds(pl.multiple_of(tile * TILE, TILE), TILE)]
        low = jnp.where(
            mine == 0, 0, jnp.where(mine == 1, ends[0], jnp.where(mine == 2, ends[1], ends[2]))
        )
        high = jnp.where(
            mine == 0,
            ends[0],
            jnp.where(mine == 1, ends[1], jnp.where(mine == 2, ends[2], KEYS)),
        )
        for d in range(CHIPS):
            for key_slot in range(2):
                key_tile = 2 * lax.rem(chip + CHIPS - d, CHIPS) + (
                    core if key_slot == 0 else 1 - core
                )
                seen = masks[0, key_tile] == 1
                position = key_tile * TILE + lax.broadcasted_iota(
                    jnp.int32, (TILE, TILE), 0
                )
                first = jnp.where(seen, 0, low)
                last = jnp.where(seen, KEYS, high)
                allowed = (position >= first) & (position < last)
                row = d * 2 * TILE + key_slot * TILE
                bias[row : row + TILE, slot * TILE : (slot + 1) * TILE] = jnp.where(
                    allowed, 0.0, -jnp.inf
                )

    for copy in copies:
        copy.wait()
    out[:TILE] = dot(own[...], weights[...]).astype(BF)
    out[TILE:] = dot(other[...], weights[...]).astype(BF)


def project_query(place, own, other, w_query, segments, mask_own, mask_other):
    return pl.pallas_call(
        query_kernel,
        in_specs=[SCALARS, WHOLE, WHOLE, STAY, WHOLE, SCALARS, SCALARS],
        out_specs=[WHOLE, WHOLE],
        out_shape=[
            jax.ShapeDtypeStruct((2 * TILE, GF), BF),
            jax.ShapeDtypeStruct((KEYS, 2 * TILE), F32),
        ],
        scratch_shapes=[pltpu.VMEM((D, GF), BF), pltpu.SemaphoreType.DMA((Q_CHUNKS,))],
        compiler_params=PARAMS,
        cost_estimate=cost(2 * 256 * D * GF, 2 * (256 * D + D * GF + 256 * GF)),
        name="project_query",
    )(place, own, other, w_query, segments, mask_own, mask_other)


def attention_kernel(
    place, query, up_own, up_other, kv0, kv1, kv2, kv3, bias,
    grad_query, out0, out1, out2, out3,
    keys, values, keys_t, grad_key, grad_value,
):
    step = pl.program_id(0)

    @pl.when(step == 0)
    def _():
        for d, kv in enumerate((kv0, kv1, kv2, kv3)):
            keys[d * 256 : (d + 1) * 256] = kv[:, :HD]
            values[d * 256 : (d + 1) * 256] = kv[:, HD:]
            keys_t[:, d * 256 : (d + 1) * 256] = kv[:, :HD].T
        grad_key[...] = jnp.zeros_like(grad_key)
        grad_value[...] = jnp.zeros_like(grad_value)

    for member in range(2):
        columns = slice(member * HD, (member + 1) * HD)
        q = query[:, columns]
        up = jnp.concatenate([up_own[:, columns], up_other[:, columns]], axis=0)
        scores = dot_nt(keys[...], q) * LOG2_SCALE + bias[...]
        top = jnp.max(scores, axis=0, keepdims=True)
        powers = jnp.exp2(scores - top)
        probs = powers * (1.0 / jnp.sum(powers, axis=0, keepdims=True))
        probs_low = probs.astype(BF)
        grad_probs = dot_nt(values[...], up)
        delta = jnp.sum(probs_low.astype(F32) * grad_probs, axis=0, keepdims=True)
        grad_scores = (probs * (grad_probs - delta)).astype(BF)
        grad_value[...] += dot(probs_low, up)
        grad_key[...] += dot(grad_scores, q)
        grad_query[:, columns] = (dot(keys_t[...], grad_scores) * SCALE).T.astype(BF)

    @pl.when(step == pl.num_programs(0) - 1)
    def _():
        for d, out in enumerate((out0, out1, out2, out3)):
            rows = slice(d * 256, (d + 1) * 256)
            out[:, :HD] = (grad_key[rows] * SCALE).astype(out.dtype)
            out[:, HD:] = grad_value[rows].astype(out.dtype)


def attention(place, query, up_own, up_other, kvs, bias):
    blocks = GF // 256
    fixed = pl.BlockSpec((256, 256), lambda i, p: (0, 0))
    return pl.pallas_call(
        attention_kernel,
        grid_spec=pltpu.PrefetchScalarGridSpec(
            num_scalar_prefetch=1,
            grid=(blocks,),
            in_specs=[
                pl.BlockSpec((256, 256), lambda i, p: (0, i)),
                pl.BlockSpec((TILE, 256), lambda i, p: (0, p[1] * blocks + i)),
                pl.BlockSpec((TILE, 256), lambda i, p: (0, p[1] * blocks + i)),
                fixed, fixed, fixed, fixed,
                pl.BlockSpec((KEYS, 256), lambda i, p: (0, 0)),
            ],
            out_specs=[pl.BlockSpec((256, 256), lambda i, p: (0, i)), fixed, fixed, fixed, fixed],
            scratch_shapes=[
                pltpu.VMEM((KEYS, HD), BF),
                pltpu.VMEM((KEYS, HD), BF),
                pltpu.VMEM((HD, KEYS), BF),
                pltpu.VMEM((KEYS, HD), F32),
                pltpu.VMEM((KEYS, HD), F32),
            ],
        ),
        out_shape=[
            jax.ShapeDtypeStruct((256, GF), BF),
            jax.ShapeDtypeStruct((256, 256), F32),
            jax.ShapeDtypeStruct((256, 256), BF),
            jax.ShapeDtypeStruct((256, 256), BF),
            jax.ShapeDtypeStruct((256, 256), BF),
        ],
        compiler_params=PARAMS,
        cost_estimate=cost(10 * GROUP * 256 * KEYS * HD * 2, 4 << 20, GROUP * 256 * KEYS),
        name="attention",
    )(place, query, up_own, up_other, *kvs, bias)


def sum_kernel(a, b, c, d, out):
    total = (a[...] + b[...].astype(F32)) + (c[...].astype(F32) + d[...].astype(F32))
    out[...] = total.astype(out.dtype)


def sum_four(a, b, c, d):
    return pl.pallas_call(
        sum_kernel,
        in_specs=[WHOLE] * 4,
        out_specs=WHOLE,
        out_shape=jax.ShapeDtypeStruct(a.shape, BF),
        compiler_params=PARAMS,
        cost_estimate=cost(4 * a.size, 12 * a.size),
        name="sum_four",
    )(a, b, c, d)


def pack_kernel(place, dq, dq_other, dkv, dkv_other, out0, out1, out2, out3, blocks):
    core = place[1]

    def swapped(ref, columns):
        return jnp.concatenate([ref[TILE:, columns], ref[:TILE, columns]], axis=0)

    middle = slice(256, 512)

    @pl.when(core == 0)
    def _():
        blocks[0] = dq[:, 0:256]
        blocks[1] = dq[:, 512:768]
        blocks[2] = swapped(dq_other, middle)
        blocks[3, :, :HD] = dkv[:, :HD]
        blocks[3, :, HD:] = swapped(dkv_other, slice(0, HD))

    @pl.when(core == 1)
    def _():
        blocks[0] = swapped(dq_other, middle)
        blocks[1] = dq[:, 0:256]
        blocks[2] = dq[:, 512:768]
        blocks[3, :, :HD] = swapped(dkv_other, slice(HD, 2 * HD))
        blocks[3, :, HD:] = dkv[:, HD:]

    for d, out in enumerate((out0, out1, out2, out3)):
        out[...] = blocks[lax.rem(place[0] + d, CHIPS)]


def pack(place, dq, dq_other, dkv, dkv_other):
    return pl.pallas_call(
        pack_kernel,
        in_specs=[SCALARS] + [WHOLE] * 4,
        out_specs=[WHOLE] * 4,
        out_shape=[jax.ShapeDtypeStruct((256, 256), BF)] * 4,
        scratch_shapes=[pltpu.VMEM((4, 256, 256), BF)],
        compiler_params=PARAMS,
        cost_estimate=cost(0, 4 << 19),
        name="pack",
    )(place, dq, dq_other, dkv, dkv_other)


def transpose_kernel(tokens, out, rows, sems):
    copies = []
    for chunk in range(KEYS // TILE):
        part = pl.ds(chunk * TILE, TILE)
        copies.append(pltpu.make_async_copy(tokens.at[part], rows.at[part], sems.at[chunk]))
    for copy in copies:
        copy.start()
    for chunk, copy in enumerate(copies):
        copy.wait()
        part = slice(chunk * TILE, (chunk + 1) * TILE)
        out[:, part] = rows[part].T


def transpose(tokens):
    return pl.pallas_call(
        transpose_kernel,
        in_specs=[STAY],
        out_specs=WHOLE,
        out_shape=jax.ShapeDtypeStruct((D, KEYS), BF),
        scratch_shapes=[
            pltpu.VMEM((KEYS, D), BF),
            pltpu.SemaphoreType.DMA((KEYS // TILE,)),
        ],
        compiler_params=PARAMS,
        cost_estimate=cost(0, 4 * D * KEYS),
        name="transpose_tokens",
    )(tokens)


def weight_kernel(place, tokens_t, a, b, c, d, out0, out1, out2, out3, right):
    for shift, part in enumerate((a, b, c, d)):
        chip = lax.rem(place[0] + CHIPS - shift, CHIPS)
        for slot in range(2):
            tile = 2 * chip + (place[1] if slot == 0 else 1 - place[1])
            right[pl.ds(pl.multiple_of(tile * TILE, TILE), TILE)] = part[
                slot * TILE : (slot + 1) * TILE
            ]
    for shift, out in enumerate((out0, out1, out2, out3)):
        row = pl.multiple_of(lax.rem(place[2] + shift, YS) * (D // YS), 128)
        out[...] = dot(tokens_t[pl.ds(row, D // YS)], right[...]).astype(out.dtype)


def weight_grad(place, tokens_t, parts):
    shape = (D // YS, 256)
    return pl.pallas_call(
        weight_kernel,
        in_specs=[SCALARS] + [WHOLE] * 5,
        out_specs=[WHOLE] * 4,
        out_shape=[jax.ShapeDtypeStruct(shape, F32)] + [jax.ShapeDtypeStruct(shape, BF)] * 3,
        scratch_shapes=[pltpu.VMEM((KEYS, 256), BF)],
        compiler_params=PARAMS,
        cost_estimate=cost(2 * D * KEYS * 256, 2 * D * KEYS + 3 * D * 256),
        name="weight_grad",
    )(place, tokens_t, *parts)


def input_kernel(
    place, dq, dq_other, dkv, dkv_other, w_query, w_key, w_value, out, left, right, sems
):
    core = place[1]
    width = D // IN_CHUNKS
    copies = []
    for chunk in range(IN_CHUNKS):
        part = pl.ds(chunk * width, width)
        copies.append(
            [
                pltpu.make_async_copy(
                    source.at[part],
                    right.at[part, pl.ds(start, size)],
                    sems.at[chunk, side],
                )
                for side, (source, start, size) in enumerate(
                    ((w_query, 0, D), (w_key, D, 256), (w_value, D + 256, 256))
                )
            ]
        )
    for group in copies:
        for copy in group:
            copy.start()
    mine = pl.ds(pl.multiple_of(core * GF, 128), GF)
    theirs = pl.ds(pl.multiple_of((1 - core) * GF, 128), GF)
    left[:, mine] = dq[:TILE]
    left[:, theirs] = dq_other[TILE:]
    for part in range(2):
        columns = slice(part * HD, (part + 1) * HD)
        base = D + part * KVH * HD
        left[:, pl.ds(pl.multiple_of(base + core * HD, 128), HD)] = dkv[:TILE, columns]
        left[:, pl.ds(pl.multiple_of(base + (1 - core) * HD, 128), HD)] = dkv_other[
            TILE:, columns
        ]
    for chunk, group in enumerate(copies):
        for copy in group:
            copy.wait()
        part = slice(chunk * width, (chunk + 1) * width)
        out[:, part] = dot_nt(left[...], right[part]).astype(BF)


def input_grad(place, dq, dq_other, dkv, dkv_other, w_query, w_key, w_value):
    return pl.pallas_call(
        input_kernel,
        in_specs=[SCALARS] + [WHOLE] * 4 + [STAY] * 3,
        out_specs=WHOLE,
        out_shape=jax.ShapeDtypeStruct((TILE, D), BF),
        scratch_shapes=[
            pltpu.VMEM((TILE, D + 512), BF),
            pltpu.VMEM((D, D + 512), BF),
            pltpu.SemaphoreType.DMA((IN_CHUNKS, 3)),
        ],
        compiler_params=PARAMS,
        cost_estimate=cost(2 * TILE * D * 2048, 2 * D * 2048),
        name="input_grad",
    )(place, dq, dq_other, dkv, dkv_other, w_query, w_key, w_value)


def final_kernel(parts, out):
    total = parts[0:48].astype(F32)
    for z in range(1, ZS):
        total += parts[z * 48 : (z + 1) * 48].astype(F32)
    out[...] = total


def final_sum(parts):
    return pl.pallas_call(
        final_kernel,
        in_specs=[WHOLE],
        out_specs=WHOLE,
        out_shape=jax.ShapeDtypeStruct((48, 256), F32),
        compiler_params=PARAMS,
        cost_estimate=cost(parts.size, 2 * parts.size),
        name="final_sum",
    )(parts)


def shards(tokens, grad_heads, tile_mask, segments, w_query, w_key, w_value):
    ctx = lax.axis_index("ctx")
    dp = lax.axis_index("dp")
    place = jnp.stack([ctx // 2, ctx % 2, dp // ZS, dp % ZS]).astype(jnp.int32)
    own, up = tokens[0], grad_heads[0]
    other = lax.ppermute(own, "ctx", CORE)
    up_other = lax.ppermute(up, "ctx", CORE)
    mask_other = lax.ppermute(tile_mask[0], "ctx", CORE)
    gathered = lax.all_gather(own, "ctx", axis=0, tiled=True)

    w_query, w_key, w_value = (in_hbm(w) for w in (w_query, w_key, w_value))
    weights, kv_own = project_kv_own(place, in_hbm(own), w_key, w_value)
    kv = project_kv(other, weights, kv_own)
    kvs = [kv] + [lax.ppermute(kv, "ctx", chip_shift(d)) for d in (1, 2, 3)]
    query, bias = project_query(
        place, own, other, w_query, segments, tile_mask[0], mask_other
    )

    dq, g0, g1, g2, g3 = attention(place, query, up, up_other, kvs, bias)
    dq_other = lax.ppermute(dq, "ctx", CORE)
    back = [
        lax.ppermute(g, "ctx", chip_shift(CHIPS - d)) for d, g in ((1, g1), (2, g2), (3, g3))
    ]
    dkv = sum_four(g0, *back)
    dkv_other = lax.ppermute(dkv, "ctx", CORE)

    gathered, dkv_late = lax.optimization_barrier((gathered, dkv_other))
    tokens_t = transpose(in_hbm(gathered))

    packed = pack(place, dq, dq_other, dkv, dkv_late)
    columns = [packed[0]] + [
        lax.ppermute(packed[d], "ctx", chip_shift(d)) for d in (1, 2, 3)
    ]
    terms = weight_grad(place, tokens_t, columns)
    y_parts = [terms[0]] + [lax.ppermute(terms[d], "dp", y_shift(d)) for d in (1, 2, 3)]
    grad_tokens = input_grad(
        place, dq, dq_other, dkv, dkv_late, w_query, w_key, w_value
    )
    y_parts, grad_tokens = lax.optimization_barrier((y_parts, grad_tokens))
    y_sum = sum_four(*y_parts)
    z_parts = lax.all_to_all(y_sum, "dp", 0, 0, tiled=True, axis_index_groups=Z_GROUPS)
    grad_projection = final_sum(z_parts)
    return grad_tokens[None], grad_projection


def solution(mesh):
    return jax.shard_map(
        shards,
        mesh=mesh,
        in_specs=(
            P("dp", "ctx", None),
            P("dp", "ctx", None),
            P("dp", "ctx", None),
            P("dp", None),
            P(),
            P(),
            P(),
        ),
        out_specs=(P("dp", "ctx", None), P("dp", "ctx")),
        check_vma=False,
    )
```

```python
import functools
import math

import jax
import jax.numpy as jnp
from jax import lax
from jax.experimental import pallas as pl
from jax.experimental.pallas import tpu as pltpu
from jax.sharding import PartitionSpec as P

QH = 12
KVH = 2
HD = 128
TILE = 128
D = 1536
KEYS = 1024
CHIPS = 4
GROUP = QH // KVH
GF = GROUP * HD
YS = 4
ZS = 8
SCALE = 1.0 / math.sqrt(HD)
LOG2_SCALE = SCALE * math.log2(math.e)
BF = jnp.bfloat16
F32 = jnp.float32
VMEM_LIMIT = 24 * 1024 * 1024
W_CHUNKS = 4
Q_CHUNKS = 6
IN_CHUNKS = 6

CORE = [(i, i ^ 1) for i in range(8)]
NT = (((1,), (1,)), ((), ()))


def chip_shift(d):
    return [(i, ((i // 2 + d) % CHIPS) * 2 + i % 2) for i in range(8)]


def y_shift(d):
    return [(i, ((i // ZS + d) % YS) * ZS + i % ZS) for i in range(32)]


Z_GROUPS = [[y * ZS + z for z in range(ZS)] for y in range(YS)]


def dot(a, b):
    return jnp.dot(a, b, preferred_element_type=F32)


def dot_nt(a, b):
    return lax.dot_general(a, b, NT, preferred_element_type=F32)


def in_hbm(array):
    return pltpu.with_memory_space_constraint(array, pltpu.HBM)


def cost(flops, bytes_accessed, transcendentals=0):
    return pl.CostEstimate(
        flops=flops, bytes_accessed=bytes_accessed, transcendentals=transcendentals
    )


PARAMS = pltpu.CompilerParams(vmem_limit_bytes=VMEM_LIMIT)
WHOLE = pl.BlockSpec(memory_space=pltpu.VMEM)
SCALARS = pl.BlockSpec(memory_space=pltpu.SMEM)
STAY = pl.BlockSpec(memory_space=pltpu.HBM)


def kv_own_kernel(place, own, w_key, w_value, weights, out, rows, sems):
    columns = pl.ds(pl.multiple_of(place[1] * HD, HD), HD)
    copies = []
    for chunk in range(W_CHUNKS):
        part = pl.ds(chunk * (TILE // W_CHUNKS), TILE // W_CHUNKS)
        copies.append(pltpu.make_async_copy(own.at[part], rows.at[part], sems.at[chunk, 2]))
        part = pl.ds(chunk * (D // W_CHUNKS), D // W_CHUNKS)
        for side, source in enumerate((w_key, w_value)):
            copies.append(
                pltpu.make_async_copy(
                    source.at[part, columns],
                    weights.at[part, pl.ds(side * HD, HD)],
                    sems.at[chunk, side],
                )
            )
    for copy in copies:
        copy.start()
    for copy in copies:
        copy.wait()
    out[...] = dot(rows[...], weights[...]).astype(BF)


def project_kv_own(place, own, w_key, w_value):
    return pl.pallas_call(
        kv_own_kernel,
        in_specs=[SCALARS, STAY, STAY, STAY],
        out_specs=[WHOLE, WHOLE],
        out_shape=[
            jax.ShapeDtypeStruct((D, 2 * HD), BF),
            jax.ShapeDtypeStruct((TILE, 2 * HD), BF),
        ],
        scratch_shapes=[pltpu.VMEM((TILE, D), BF), pltpu.SemaphoreType.DMA((W_CHUNKS, 3))],
        compiler_params=PARAMS,
        cost_estimate=cost(2 * TILE * D * 256, 2 * (TILE * D + D * 256)),
        name="project_kv_own",
    )(place, own, w_key, w_value)


def kv_pair_kernel(own, other, weights, out):
    out[:TILE] = dot(own[...], weights[...]).astype(BF)
    out[TILE:] = dot(other[...], weights[...]).astype(BF)


def project_kv_pair(own, other, weights):
    return pl.pallas_call(
        kv_pair_kernel,
        in_specs=[WHOLE] * 3,
        out_specs=WHOLE,
        out_shape=jax.ShapeDtypeStruct((2 * TILE, 2 * HD), BF),
        compiler_params=PARAMS,
        cost_estimate=cost(4 * TILE * D * 256, 2 * (2 * TILE * D + D * 256)),
        name="project_kv_pair",
    )(own, other, weights)


def kv_kernel(other, weights, kv_own, out):
    out[:TILE] = kv_own[...]
    out[TILE:] = dot(other[...], weights[...]).astype(BF)


def project_kv(other, weights, kv_own):
    return pl.pallas_call(
        kv_kernel,
        in_specs=[WHOLE] * 3,
        out_specs=WHOLE,
        out_shape=jax.ShapeDtypeStruct((2 * TILE, 2 * HD), BF),
        compiler_params=PARAMS,
        cost_estimate=cost(2 * TILE * D * 256, 2 * (TILE * D + D * 256)),
        name="project_kv",
    )(other, weights, kv_own)


def query_kernel(
    place, own, other, w_query, segments, mask_own, mask_other, out, bias, weights, sems
):
    columns = pl.ds(pl.multiple_of(place[1] * GF, HD), GF)
    copies = []
    for chunk in range(Q_CHUNKS):
        part = pl.ds(chunk * (D // Q_CHUNKS), D // Q_CHUNKS)
        copies.append(
            pltpu.make_async_copy(w_query.at[part, columns], weights.at[part], sems.at[chunk])
        )
    for copy in copies:
        copy.start()

    chip, core = place[0], place[1]
    passages = segments[...]
    ends = [jnp.sum((passages <= s).astype(jnp.int32)) for s in range(3)]
    for slot in range(2):
        masks = mask_own if slot == 0 else mask_other
        tile = 2 * chip + (core if slot == 0 else 1 - core)
        mine = segments[:, pl.ds(pl.multiple_of(tile * TILE, TILE), TILE)]
        low = jnp.where(
            mine == 0, 0, jnp.where(mine == 1, ends[0], jnp.where(mine == 2, ends[1], ends[2]))
        )
        high = jnp.where(
            mine == 0,
            ends[0],
            jnp.where(mine == 1, ends[1], jnp.where(mine == 2, ends[2], KEYS)),
        )
        for d in range(CHIPS):
            for key_slot in range(2):
                key_tile = 2 * lax.rem(chip + CHIPS - d, CHIPS) + (
                    core if key_slot == 0 else 1 - core
                )
                seen = masks[0, key_tile] == 1
                position = key_tile * TILE + lax.broadcasted_iota(
                    jnp.int32, (TILE, TILE), 0
                )
                first = jnp.where(seen, 0, low)
                last = jnp.where(seen, KEYS, high)
                allowed = (position >= first) & (position < last)
                row = d * 2 * TILE + key_slot * TILE
                bias[row : row + TILE, slot * TILE : (slot + 1) * TILE] = jnp.where(
                    allowed, 0.0, -jnp.inf
                )

    for copy in copies:
        copy.wait()
    out[:TILE] = dot(own[...], weights[...]).astype(BF)
    out[TILE:] = dot(other[...], weights[...]).astype(BF)


def project_query(place, own, other, w_query, segments, mask_own, mask_other):
    return pl.pallas_call(
        query_kernel,
        in_specs=[SCALARS, WHOLE, WHOLE, STAY, WHOLE, SCALARS, SCALARS],
        out_specs=[WHOLE, WHOLE],
        out_shape=[
            jax.ShapeDtypeStruct((2 * TILE, GF), BF),
            jax.ShapeDtypeStruct((KEYS, 2 * TILE), F32),
        ],
        scratch_shapes=[pltpu.VMEM((D, GF), BF), pltpu.SemaphoreType.DMA((Q_CHUNKS,))],
        compiler_params=PARAMS,
        cost_estimate=cost(2 * 256 * D * GF, 2 * (256 * D + D * GF + 256 * GF)),
        name="project_query",
    )(place, own, other, w_query, segments, mask_own, mask_other)


def attention_kernel(
    place, query, up_own, up_other, kv0, kv1, kv2, kv3, bias,
    grad_query, out0, out1, out2, out3,
    keys, values, keys_t, grad_key, grad_value,
):
    step = pl.program_id(0)

    @pl.when(step == 0)
    def _():
        for d, kv in enumerate((kv0, kv1, kv2, kv3)):
            keys[d * 256 : (d + 1) * 256] = kv[:, :HD]
            values[d * 256 : (d + 1) * 256] = kv[:, HD:]
            keys_t[:, d * 256 : (d + 1) * 256] = kv[:, :HD].T
        grad_key[...] = jnp.zeros_like(grad_key)
        grad_value[...] = jnp.zeros_like(grad_value)

    for member in range(2):
        columns = slice(member * HD, (member + 1) * HD)
        q = query[:, columns]
        up = jnp.concatenate([up_own[:, columns], up_other[:, columns]], axis=0)
        scores = dot_nt(keys[...], q) * LOG2_SCALE + bias[...]
        top = jnp.max(scores, axis=0, keepdims=True)
        powers = jnp.exp2(scores - top)
        probs = powers * (1.0 / jnp.sum(powers, axis=0, keepdims=True))
        probs_low = probs.astype(BF)
        grad_probs = dot_nt(values[...], up)
        delta = jnp.sum(probs_low.astype(F32) * grad_probs, axis=0, keepdims=True)
        grad_scores = (probs * (grad_probs - delta)).astype(BF)
        grad_value[...] += dot(probs_low, up)
        grad_key[...] += dot(grad_scores, q)
        grad_query[:, columns] = (dot(keys_t[...], grad_scores) * SCALE).T.astype(BF)

    @pl.when(step == pl.num_programs(0) - 1)
    def _():
        for d, out in enumerate((out0, out1, out2, out3)):
            rows = slice(d * 256, (d + 1) * 256)
            out[:, :HD] = (grad_key[rows] * SCALE).astype(out.dtype)
            out[:, HD:] = grad_value[rows].astype(out.dtype)


def attention(place, query, up_own, up_other, kvs, bias):
    blocks = GF // 256
    fixed = pl.BlockSpec((256, 256), lambda i, p: (0, 0))
    return pl.pallas_call(
        attention_kernel,
        grid_spec=pltpu.PrefetchScalarGridSpec(
            num_scalar_prefetch=1,
            grid=(blocks,),
            in_specs=[
                pl.BlockSpec((256, 256), lambda i, p: (0, i)),
                pl.BlockSpec((TILE, 256), lambda i, p: (0, p[1] * blocks + i)),
                pl.BlockSpec((TILE, 256), lambda i, p: (0, p[1] * blocks + i)),
                fixed, fixed, fixed, fixed,
                pl.BlockSpec((KEYS, 256), lambda i, p: (0, 0)),
            ],
            out_specs=[pl.BlockSpec((256, 256), lambda i, p: (0, i)), fixed, fixed, fixed, fixed],
            scratch_shapes=[
                pltpu.VMEM((KEYS, HD), BF),
                pltpu.VMEM((KEYS, HD), BF),
                pltpu.VMEM((HD, KEYS), BF),
                pltpu.VMEM((KEYS, HD), F32),
                pltpu.VMEM((KEYS, HD), F32),
            ],
        ),
        out_shape=[
            jax.ShapeDtypeStruct((256, GF), BF),
            jax.ShapeDtypeStruct((256, 256), F32),
            jax.ShapeDtypeStruct((256, 256), BF),
            jax.ShapeDtypeStruct((256, 256), BF),
            jax.ShapeDtypeStruct((256, 256), BF),
        ],
        compiler_params=PARAMS,
        cost_estimate=cost(10 * GROUP * 256 * KEYS * HD * 2, 4 << 20, GROUP * 256 * KEYS),
        name="attention",
    )(place, query, up_own, up_other, *kvs, bias)


def sum_kernel(a, b, c, d, out):
    total = (a[...] + b[...].astype(F32)) + (c[...].astype(F32) + d[...].astype(F32))
    out[...] = total.astype(out.dtype)


def sum_four(a, b, c, d):
    return pl.pallas_call(
        sum_kernel,
        in_specs=[WHOLE] * 4,
        out_specs=WHOLE,
        out_shape=jax.ShapeDtypeStruct(a.shape, BF),
        compiler_params=PARAMS,
        cost_estimate=cost(4 * a.size, 12 * a.size),
        name="sum_four",
    )(a, b, c, d)


def pack_kernel(place, dq, dq_other, dkv, dkv_other, out0, out1, out2, out3, blocks):
    core = place[1]

    def swapped(ref, columns):
        return jnp.concatenate([ref[TILE:, columns], ref[:TILE, columns]], axis=0)

    middle = slice(256, 512)

    @pl.when(core == 0)
    def _():
        blocks[0] = dq[:, 0:256]
        blocks[1] = dq[:, 512:768]
        blocks[2] = swapped(dq_other, middle)
        blocks[3, :, :HD] = dkv[:, :HD]
        blocks[3, :, HD:] = swapped(dkv_other, slice(0, HD))

    @pl.when(core == 1)
    def _():
        blocks[0] = swapped(dq_other, middle)
        blocks[1] = dq[:, 0:256]
        blocks[2] = dq[:, 512:768]
        blocks[3, :, :HD] = swapped(dkv_other, slice(HD, 2 * HD))
        blocks[3, :, HD:] = dkv[:, HD:]

    for d, out in enumerate((out0, out1, out2, out3)):
        out[...] = blocks[lax.rem(place[0] + d, CHIPS)]


def pack(place, dq, dq_other, dkv, dkv_other):
    return pl.pallas_call(
        pack_kernel,
        in_specs=[SCALARS] + [WHOLE] * 4,
        out_specs=[WHOLE] * 4,
        out_shape=[jax.ShapeDtypeStruct((256, 256), BF)] * 4,
        scratch_shapes=[pltpu.VMEM((4, 256, 256), BF)],
        compiler_params=PARAMS,
        cost_estimate=cost(0, 4 << 19),
        name="pack",
    )(place, dq, dq_other, dkv, dkv_other)


def transpose_kernel(*refs):
    out = refs[-1]
    for i, ref in enumerate(refs[:-1]):
        out[:, i * TILE : (i + 1) * TILE] = ref[...].T


def transpose(parts):
    return pl.pallas_call(
        transpose_kernel,
        in_specs=[WHOLE] * 8,
        out_specs=WHOLE,
        out_shape=jax.ShapeDtypeStruct((D, KEYS), BF),
        compiler_params=PARAMS,
        cost_estimate=cost(0, 4 * D * KEYS),
        name="transpose_tokens",
    )(*parts)


def weight_kernel(place, tokens_t, a, b, c, d, out0, out1, out2, out3):
    right = jnp.concatenate([a[...], b[...], c[...], d[...]], axis=0)
    for shift, out in enumerate((out0, out1, out2, out3)):
        row = pl.multiple_of(lax.rem(place[2] + shift, YS) * (D // YS), 128)
        out[...] = dot(tokens_t[pl.ds(row, D // YS)], right).astype(out.dtype)


def weight_grad(place, tokens_t, parts):
    shape = (D // YS, 256)
    return pl.pallas_call(
        weight_kernel,
        in_specs=[SCALARS] + [WHOLE] * 5,
        out_specs=[WHOLE] * 4,
        out_shape=[jax.ShapeDtypeStruct(shape, F32)] + [jax.ShapeDtypeStruct(shape, BF)] * 3,
        compiler_params=PARAMS,
        cost_estimate=cost(2 * D * KEYS * 256, 2 * D * KEYS + 3 * D * 256),
        name="weight_grad",
    )(place, tokens_t, *parts)


def input_kernel(
    place, dq, dq_other, dkv, dkv_other, w_query, w_key, w_value, out, left, right, sems
):
    core = place[1]
    width = D // IN_CHUNKS
    copies = []
    for chunk in range(IN_CHUNKS):
        part = pl.ds(chunk * width, width)
        copies.append(
            [
                pltpu.make_async_copy(
                    source.at[part],
                    right.at[part, pl.ds(start, size)],
                    sems.at[chunk, side],
                )
                for side, (source, start, size) in enumerate(
                    ((w_query, 0, D), (w_key, D, 256), (w_value, D + 256, 256))
                )
            ]
        )
    for group in copies:
        for copy in group:
            copy.start()
    mine = pl.ds(pl.multiple_of(core * GF, 128), GF)
    theirs = pl.ds(pl.multiple_of((1 - core) * GF, 128), GF)
    left[:, mine] = dq[:TILE]
    left[:, theirs] = dq_other[TILE:]
    for part in range(2):
        columns = slice(part * HD, (part + 1) * HD)
        base = D + part * KVH * HD
        left[:, pl.ds(pl.multiple_of(base + core * HD, 128), HD)] = dkv[:TILE, columns]
        left[:, pl.ds(pl.multiple_of(base + (1 - core) * HD, 128), HD)] = dkv_other[
            TILE:, columns
        ]
    for chunk, group in enumerate(copies):
        for copy in group:
            copy.wait()
        part = slice(chunk * width, (chunk + 1) * width)
        out[:, part] = dot_nt(left[...], right[part]).astype(BF)


def input_grad(place, dq, dq_other, dkv, dkv_other, w_query, w_key, w_value):
    return pl.pallas_call(
        input_kernel,
        in_specs=[SCALARS] + [WHOLE] * 4 + [STAY] * 3,
        out_specs=WHOLE,
        out_shape=jax.ShapeDtypeStruct((TILE, D), BF),
        scratch_shapes=[
            pltpu.VMEM((TILE, D + 512), BF),
            pltpu.VMEM((D, D + 512), BF),
            pltpu.SemaphoreType.DMA((IN_CHUNKS, 3)),
        ],
        compiler_params=PARAMS,
        cost_estimate=cost(2 * TILE * D * 2048, 2 * D * 2048),
        name="input_grad",
    )(place, dq, dq_other, dkv, dkv_other, w_query, w_key, w_value)


def final_kernel(parts, out):
    total = parts[0:48].astype(F32)
    for z in range(1, ZS):
        total += parts[z * 48 : (z + 1) * 48].astype(F32)
    out[...] = total


def final_sum(parts):
    return pl.pallas_call(
        final_kernel,
        in_specs=[WHOLE],
        out_specs=WHOLE,
        out_shape=jax.ShapeDtypeStruct((48, 256), F32),
        compiler_params=PARAMS,
        cost_estimate=cost(parts.size, 2 * parts.size),
        name="final_sum",
    )(parts)


def shards(tokens, grad_heads, tile_mask, segments, w_query, w_key, w_value):
    ctx = lax.axis_index("ctx")
    dp = lax.axis_index("dp")
    place = jnp.stack([ctx // 2, ctx % 2, dp // ZS, dp % ZS]).astype(jnp.int32)
    own, up = tokens[0], grad_heads[0]
    far = {d: lax.ppermute(own, "ctx", chip_shift(d)) for d in (1, 3, 2)}
    other = lax.ppermute(own, "ctx", CORE)
    up_other = lax.ppermute(up, "ctx", CORE)
    mask_other = lax.ppermute(tile_mask[0], "ctx", CORE)

    w_query, w_key, w_value = (in_hbm(w) for w in (w_query, w_key, w_value))
    weights, kv_own = project_kv_own(place, in_hbm(own), w_key, w_value)
    kv = project_kv(other, weights, kv_own)
    query, bias = project_query(
        place, own, other, w_query, segments, tile_mask[0], mask_other
    )
    far, query, kv = lax.optimization_barrier((far, query, kv))
    far_other = {d: lax.ppermute(far[d], "ctx", CORE) for d in (1, 3, 2)}
    kvs = [kv] + [project_kv_pair(far[d], far_other[d], weights) for d in (1, 2, 3)]

    dq, g0, g1, g2, g3 = attention(place, query, up, up_other, kvs, bias)
    dq_other = lax.ppermute(dq, "ctx", CORE)
    back = [
        lax.ppermute(g, "ctx", chip_shift(CHIPS - d)) for d, g in ((1, g1), (2, g2), (3, g3))
    ]
    dkv = sum_four(g0, *back)
    dkv_other = lax.ppermute(dkv, "ctx", CORE)

    tokens_t = transpose(
        [own, other] + [part for d in (1, 2, 3) for part in (far[d], far_other[d])]
    )
    packed = pack(place, dq, dq_other, dkv, dkv_other)
    columns = [packed[0]] + [
        lax.ppermute(packed[d], "ctx", chip_shift(d)) for d in (1, 2, 3)
    ]
    terms = weight_grad(place, tokens_t, columns)
    y_parts = [terms[0]] + [lax.ppermute(terms[d], "dp", y_shift(d)) for d in (1, 2, 3)]
    grad_tokens = input_grad(
        place, dq, dq_other, dkv, dkv_other, w_query, w_key, w_value
    )
    y_parts, grad_tokens = lax.optimization_barrier((y_parts, grad_tokens))
    y_sum = sum_four(*y_parts)
    z_parts = lax.all_to_all(y_sum, "dp", 0, 0, tiled=True, axis_index_groups=Z_GROUPS)
    grad_projection = final_sum(z_parts)
    return grad_tokens[None], grad_projection


def solution(mesh):
    return jax.shard_map(
        shards,
        mesh=mesh,
        in_specs=(
            P("dp", "ctx", None),
            P("dp", "ctx", None),
            P("dp", "ctx", None),
            P("dp", None),
            P(),
            P(),
            P(),
        ),
        out_specs=(P("dp", "ctx", None), P("dp", "ctx")),
        check_vma=False,
    )
```

```python
import functools
import math

import jax
import jax.numpy as jnp
from jax import lax
from jax.experimental import pallas as pl
from jax.experimental.pallas import tpu as pltpu
from jax.sharding import PartitionSpec as P

QH = 12
KVH = 2
HD = 128
TILE = 128
D = 1536
KEYS = 1024
CHIPS = 4
GROUP = QH // KVH
GF = GROUP * HD
YS = 4
ZS = 8
SCALE = 1.0 / math.sqrt(HD)
LOG2_SCALE = SCALE * math.log2(math.e)
BF = jnp.bfloat16
F32 = jnp.float32
VMEM_LIMIT = 24 * 1024 * 1024
W_CHUNKS = 4
Q_CHUNKS = 6
IN_CHUNKS = 6

CORE = [(i, i ^ 1) for i in range(8)]
NT = (((1,), (1,)), ((), ()))


def chip_shift(d):
    return [(i, ((i // 2 + d) % CHIPS) * 2 + i % 2) for i in range(8)]


def y_shift(d):
    return [(i, ((i // ZS + d) % YS) * ZS + i % ZS) for i in range(32)]


Z_GROUPS = [[y * ZS + z for z in range(ZS)] for y in range(YS)]


def dot(a, b):
    return jnp.dot(a, b, preferred_element_type=F32)


def dot_nt(a, b):
    return lax.dot_general(a, b, NT, preferred_element_type=F32)


def in_hbm(array):
    return pltpu.with_memory_space_constraint(array, pltpu.HBM)


def cost(flops, bytes_accessed, transcendentals=0):
    return pl.CostEstimate(
        flops=flops, bytes_accessed=bytes_accessed, transcendentals=transcendentals
    )


PARAMS = pltpu.CompilerParams(vmem_limit_bytes=VMEM_LIMIT)
WHOLE = pl.BlockSpec(memory_space=pltpu.VMEM)
SCALARS = pl.BlockSpec(memory_space=pltpu.SMEM)
STAY = pl.BlockSpec(memory_space=pltpu.HBM)


def kv_own_kernel(place, own, w_key, w_value, weights, out, rows, sems):
    columns = pl.ds(pl.multiple_of(place[1] * HD, HD), HD)
    copies = []
    for chunk in range(W_CHUNKS):
        part = pl.ds(chunk * (TILE // W_CHUNKS), TILE // W_CHUNKS)
        copies.append(pltpu.make_async_copy(own.at[part], rows.at[part], sems.at[chunk, 2]))
        part = pl.ds(chunk * (D // W_CHUNKS), D // W_CHUNKS)
        for side, source in enumerate((w_key, w_value)):
            copies.append(
                pltpu.make_async_copy(
                    source.at[part, columns],
                    weights.at[part, pl.ds(side * HD, HD)],
                    sems.at[chunk, side],
                )
            )
    for copy in copies:
        copy.start()
    for copy in copies:
        copy.wait()
    out[...] = dot(rows[...], weights[...]).astype(BF)


def project_kv_own(place, own, w_key, w_value):
    return pl.pallas_call(
        kv_own_kernel,
        in_specs=[SCALARS, STAY, STAY, STAY],
        out_specs=[WHOLE, WHOLE],
        out_shape=[
            jax.ShapeDtypeStruct((D, 2 * HD), BF),
            jax.ShapeDtypeStruct((TILE, 2 * HD), BF),
        ],
        scratch_shapes=[pltpu.VMEM((TILE, D), BF), pltpu.SemaphoreType.DMA((W_CHUNKS, 3))],
        compiler_params=PARAMS,
        cost_estimate=cost(2 * TILE * D * 256, 2 * (TILE * D + D * 256)),
        name="project_kv_own",
    )(place, own, w_key, w_value)


def kv_kernel(other, weights, kv_own, out):
    out[:TILE] = kv_own[...]
    out[TILE:] = dot(other[...], weights[...]).astype(BF)


def project_kv(other, weights, kv_own):
    return pl.pallas_call(
        kv_kernel,
        in_specs=[WHOLE] * 3,
        out_specs=WHOLE,
        out_shape=jax.ShapeDtypeStruct((2 * TILE, 2 * HD), BF),
        compiler_params=PARAMS,
        cost_estimate=cost(2 * TILE * D * 256, 2 * (TILE * D + D * 256)),
        name="project_kv",
    )(other, weights, kv_own)


def query_kernel(
    place, own, other, w_query, segments_far, mask_far, mask_other, out, bias,
    weights, segments, mask_own, sems, small_sems,
):
    small = [
        pltpu.make_async_copy(segments_far, segments, small_sems.at[0]),
        pltpu.make_async_copy(mask_far, mask_own, small_sems.at[1]),
    ]
    for copy in small:
        copy.start()
    columns = pl.ds(pl.multiple_of(place[1] * GF, HD), GF)
    copies = []
    for chunk in range(Q_CHUNKS):
        part = pl.ds(chunk * (D // Q_CHUNKS), D // Q_CHUNKS)
        copies.append(
            pltpu.make_async_copy(w_query.at[part, columns], weights.at[part], sems.at[chunk])
        )
    for copy in copies:
        copy.start()
    for copy in small:
        copy.wait()

    chip, core = place[0], place[1]
    passages = segments[...]
    ends = [jnp.sum((passages <= s).astype(jnp.int32)) for s in range(3)]
    for slot in range(2):
        masks = mask_own if slot == 0 else mask_other
        tile = 2 * chip + (core if slot == 0 else 1 - core)
        mine = segments[:, pl.ds(pl.multiple_of(tile * TILE, TILE), TILE)]
        low = jnp.where(
            mine == 0, 0, jnp.where(mine == 1, ends[0], jnp.where(mine == 2, ends[1], ends[2]))
        )
        high = jnp.where(
            mine == 0,
            ends[0],
            jnp.where(mine == 1, ends[1], jnp.where(mine == 2, ends[2], KEYS)),
        )
        for d in range(CHIPS):
            for key_slot in range(2):
                key_tile = 2 * lax.rem(chip + CHIPS - d, CHIPS) + (
                    core if key_slot == 0 else 1 - core
                )
                seen = masks[0, key_tile] == 1
                position = key_tile * TILE + lax.broadcasted_iota(
                    jnp.int32, (TILE, TILE), 0
                )
                first = jnp.where(seen, 0, low)
                last = jnp.where(seen, KEYS, high)
                allowed = (position >= first) & (position < last)
                row = d * 2 * TILE + key_slot * TILE
                bias[row : row + TILE, slot * TILE : (slot + 1) * TILE] = jnp.where(
                    allowed, 0.0, -jnp.inf
                )

    for copy in copies:
        copy.wait()
    out[:TILE] = dot(own[...], weights[...]).astype(BF)
    out[TILE:] = dot(other[...], weights[...]).astype(BF)


def project_query(place, own, other, w_query, segments, mask_own, mask_other):
    return pl.pallas_call(
        query_kernel,
        in_specs=[SCALARS, WHOLE, WHOLE, STAY, STAY, STAY, SCALARS],
        out_specs=[WHOLE, WHOLE],
        out_shape=[
            jax.ShapeDtypeStruct((2 * TILE, GF), BF),
            jax.ShapeDtypeStruct((KEYS, 2 * TILE), F32),
        ],
        scratch_shapes=[
            pltpu.VMEM((D, GF), BF),
            pltpu.VMEM((1, KEYS), jnp.int32),
            pltpu.SMEM((1, KEYS // TILE), jnp.int32),
            pltpu.SemaphoreType.DMA((Q_CHUNKS,)),
            pltpu.SemaphoreType.DMA((2,)),
        ],
        compiler_params=PARAMS,
        cost_estimate=cost(2 * 256 * D * GF, 2 * (256 * D + D * GF + 256 * GF)),
        name="project_query",
    )(place, own, other, w_query, segments, mask_own, mask_other)


def attention_kernel(
    place, query, up_own, up_other, kv0, kv1, kv2, kv3, bias,
    grad_query, out0, out1, out2, out3,
    keys, values, keys_t, grad_key, grad_value,
):
    step = pl.program_id(0)

    @pl.when(step == 0)
    def _():
        for d, kv in enumerate((kv0, kv1, kv2, kv3)):
            keys[d * 256 : (d + 1) * 256] = kv[:, :HD]
            values[d * 256 : (d + 1) * 256] = kv[:, HD:]
            keys_t[:, d * 256 : (d + 1) * 256] = kv[:, :HD].T
        grad_key[...] = jnp.zeros_like(grad_key)
        grad_value[...] = jnp.zeros_like(grad_value)

    for member in range(2):
        columns = slice(member * HD, (member + 1) * HD)
        q = query[:, columns]
        up = jnp.concatenate([up_own[:, columns], up_other[:, columns]], axis=0)
        scores = dot_nt(keys[...], q) * LOG2_SCALE + bias[...]
        top = jnp.max(scores, axis=0, keepdims=True)
        powers = jnp.exp2(scores - top)
        probs = powers * (1.0 / jnp.sum(powers, axis=0, keepdims=True))
        probs_low = probs.astype(BF)
        grad_probs = dot_nt(values[...], up)
        delta = jnp.sum(probs_low.astype(F32) * grad_probs, axis=0, keepdims=True)
        grad_scores = (probs * (grad_probs - delta)).astype(BF)
        grad_value[...] += dot(probs_low, up)
        grad_key[...] += dot(grad_scores, q)
        grad_query[:, columns] = (dot(keys_t[...], grad_scores) * SCALE).T.astype(BF)

    @pl.when(step == pl.num_programs(0) - 1)
    def _():
        for d, out in enumerate((out0, out1, out2, out3)):
            rows = slice(d * 256, (d + 1) * 256)
            out[:, :HD] = (grad_key[rows] * SCALE).astype(out.dtype)
            out[:, HD:] = grad_value[rows].astype(out.dtype)


def attention(place, query, up_own, up_other, kvs, bias):
    blocks = GF // 256
    fixed = pl.BlockSpec((256, 256), lambda i, p: (0, 0))
    return pl.pallas_call(
        attention_kernel,
        grid_spec=pltpu.PrefetchScalarGridSpec(
            num_scalar_prefetch=1,
            grid=(blocks,),
            in_specs=[
                pl.BlockSpec((256, 256), lambda i, p: (0, i)),
                pl.BlockSpec((TILE, 256), lambda i, p: (0, p[1] * blocks + i)),
                pl.BlockSpec((TILE, 256), lambda i, p: (0, p[1] * blocks + i)),
                fixed, fixed, fixed, fixed,
                pl.BlockSpec((KEYS, 256), lambda i, p: (0, 0)),
            ],
            out_specs=[pl.BlockSpec((256, 256), lambda i, p: (0, i)), fixed, fixed, fixed, fixed],
            scratch_shapes=[
                pltpu.VMEM((KEYS, HD), BF),
                pltpu.VMEM((KEYS, HD), BF),
                pltpu.VMEM((HD, KEYS), BF),
                pltpu.VMEM((KEYS, HD), F32),
                pltpu.VMEM((KEYS, HD), F32),
            ],
        ),
        out_shape=[
            jax.ShapeDtypeStruct((256, GF), BF),
            jax.ShapeDtypeStruct((256, 256), F32),
            jax.ShapeDtypeStruct((256, 256), BF),
            jax.ShapeDtypeStruct((256, 256), BF),
            jax.ShapeDtypeStruct((256, 256), BF),
        ],
        compiler_params=PARAMS,
        cost_estimate=cost(10 * GROUP * 256 * KEYS * HD * 2, 4 << 20, GROUP * 256 * KEYS),
        name="attention",
    )(place, query, up_own, up_other, *kvs, bias)


def sum_kernel(a, b, c, d, out):
    total = (a[...] + b[...].astype(F32)) + (c[...].astype(F32) + d[...].astype(F32))
    out[...] = total.astype(out.dtype)


def sum_four(a, b, c, d):
    return pl.pallas_call(
        sum_kernel,
        in_specs=[WHOLE] * 4,
        out_specs=WHOLE,
        out_shape=jax.ShapeDtypeStruct(a.shape, BF),
        compiler_params=PARAMS,
        cost_estimate=cost(4 * a.size, 12 * a.size),
        name="sum_four",
    )(a, b, c, d)


def pack_kernel(place, dq, dq_other, dkv, dkv_other, out0, out1, out2, out3, blocks):
    core = place[1]

    def swapped(ref, columns):
        return jnp.concatenate([ref[TILE:, columns], ref[:TILE, columns]], axis=0)

    middle = slice(256, 512)

    @pl.when(core == 0)
    def _():
        blocks[0] = dq[:, 0:256]
        blocks[1] = dq[:, 512:768]
        blocks[2] = swapped(dq_other, middle)
        blocks[3, :, :HD] = dkv[:, :HD]
        blocks[3, :, HD:] = swapped(dkv_other, slice(0, HD))

    @pl.when(core == 1)
    def _():
        blocks[0] = swapped(dq_other, middle)
        blocks[1] = dq[:, 0:256]
        blocks[2] = dq[:, 512:768]
        blocks[3, :, :HD] = swapped(dkv_other, slice(HD, 2 * HD))
        blocks[3, :, HD:] = dkv[:, HD:]

    for d, out in enumerate((out0, out1, out2, out3)):
        out[...] = blocks[lax.rem(place[0] + d, CHIPS)]


def pack(place, dq, dq_other, dkv, dkv_other):
    return pl.pallas_call(
        pack_kernel,
        in_specs=[SCALARS] + [WHOLE] * 4,
        out_specs=[WHOLE] * 4,
        out_shape=[jax.ShapeDtypeStruct((256, 256), BF)] * 4,
        scratch_shapes=[pltpu.VMEM((4, 256, 256), BF)],
        compiler_params=PARAMS,
        cost_estimate=cost(0, 4 << 19),
        name="pack",
    )(place, dq, dq_other, dkv, dkv_other)


def transpose_kernel(*refs):
    out = refs[-1]
    for i, ref in enumerate(refs[:-1]):
        out[:, i * TILE : (i + 1) * TILE] = ref[...].T


def transpose(parts):
    return pl.pallas_call(
        transpose_kernel,
        in_specs=[WHOLE] * 8,
        out_specs=WHOLE,
        out_shape=jax.ShapeDtypeStruct((D, KEYS), BF),
        compiler_params=PARAMS,
        cost_estimate=cost(0, 4 * D * KEYS),
        name="transpose_tokens",
    )(*parts)


def weight_kernel(place, tokens_t, a, b, c, d, out0, out1, out2, out3):
    right = jnp.concatenate([a[...], b[...], c[...], d[...]], axis=0)
    for shift, out in enumerate((out0, out1, out2, out3)):
        row = pl.multiple_of(lax.rem(place[2] + shift, YS) * (D // YS), 128)
        out[...] = dot(tokens_t[pl.ds(row, D // YS)], right).astype(out.dtype)


def weight_grad(place, tokens_t, parts):
    shape = (D // YS, 256)
    return pl.pallas_call(
        weight_kernel,
        in_specs=[SCALARS] + [WHOLE] * 5,
        out_specs=[WHOLE] * 4,
        out_shape=[jax.ShapeDtypeStruct(shape, F32)] + [jax.ShapeDtypeStruct(shape, BF)] * 3,
        compiler_params=PARAMS,
        cost_estimate=cost(2 * D * KEYS * 256, 2 * D * KEYS + 3 * D * 256),
        name="weight_grad",
    )(place, tokens_t, *parts)


def input_kernel(
    place, dq, dq_other, dkv, dkv_other, w_query, w_key, w_value, out, left, right, sems
):
    core = place[1]
    width = D // IN_CHUNKS
    copies = []
    for chunk in range(IN_CHUNKS):
        part = pl.ds(chunk * width, width)
        copies.append(
            [
                pltpu.make_async_copy(
                    source.at[part],
                    right.at[part, pl.ds(start, size)],
                    sems.at[chunk, side],
                )
                for side, (source, start, size) in enumerate(
                    ((w_query, 0, D), (w_key, D, 256), (w_value, D + 256, 256))
                )
            ]
        )
    for group in copies:
        for copy in group:
            copy.start()
    mine = pl.ds(pl.multiple_of(core * GF, 128), GF)
    theirs = pl.ds(pl.multiple_of((1 - core) * GF, 128), GF)
    left[:, mine] = dq[:TILE]
    left[:, theirs] = dq_other[TILE:]
    for part in range(2):
        columns = slice(part * HD, (part + 1) * HD)
        base = D + part * KVH * HD
        left[:, pl.ds(pl.multiple_of(base + core * HD, 128), HD)] = dkv[:TILE, columns]
        left[:, pl.ds(pl.multiple_of(base + (1 - core) * HD, 128), HD)] = dkv_other[
            TILE:, columns
        ]
    for chunk, group in enumerate(copies):
        for copy in group:
            copy.wait()
        part = slice(chunk * width, (chunk + 1) * width)
        out[:, part] = dot_nt(left[...], right[part]).astype(BF)


def input_grad(place, dq, dq_other, dkv, dkv_other, w_query, w_key, w_value):
    return pl.pallas_call(
        input_kernel,
        in_specs=[SCALARS] + [WHOLE] * 4 + [STAY] * 3,
        out_specs=WHOLE,
        out_shape=jax.ShapeDtypeStruct((TILE, D), BF),
        scratch_shapes=[
            pltpu.VMEM((TILE, D + 512), BF),
            pltpu.VMEM((D, D + 512), BF),
            pltpu.SemaphoreType.DMA((IN_CHUNKS, 3)),
        ],
        compiler_params=PARAMS,
        cost_estimate=cost(2 * TILE * D * 2048, 2 * D * 2048),
        name="input_grad",
    )(place, dq, dq_other, dkv, dkv_other, w_query, w_key, w_value)


def final_kernel(parts, out):
    total = parts[0:48].astype(F32)
    for z in range(1, ZS):
        total += parts[z * 48 : (z + 1) * 48].astype(F32)
    out[...] = total


def final_sum(parts):
    return pl.pallas_call(
        final_kernel,
        in_specs=[WHOLE],
        out_specs=WHOLE,
        out_shape=jax.ShapeDtypeStruct((48, 256), F32),
        compiler_params=PARAMS,
        cost_estimate=cost(parts.size, 2 * parts.size),
        name="final_sum",
    )(parts)


def shards(tokens, grad_heads, tile_mask, segments, w_query, w_key, w_value):
    ctx = lax.axis_index("ctx")
    dp = lax.axis_index("dp")
    place = jnp.stack([ctx // 2, ctx % 2, dp // ZS, dp % ZS]).astype(jnp.int32)
    own, up = tokens[0], grad_heads[0]
    other = lax.ppermute(own, "ctx", CORE)
    up_other = lax.ppermute(up, "ctx", CORE)
    mask_other = lax.ppermute(tile_mask[0], "ctx", CORE)

    w_query, w_key, w_value = (in_hbm(w) for w in (w_query, w_key, w_value))
    weights, kv_own = project_kv_own(place, in_hbm(own), w_key, w_value)
    kv = project_kv(other, weights, kv_own)
    kvs = [kv] + [lax.ppermute(kv, "ctx", chip_shift(d)) for d in (1, 2, 3)]
    query, bias = project_query(
        place, own, other, w_query, in_hbm(segments), in_hbm(tile_mask[0]), mask_other
    )
    far = {2: lax.ppermute(own, "ctx", chip_shift(2))}
    kvs, query, far, late_own = lax.optimization_barrier((kvs, query, far, own))
    near = {d: lax.ppermute(late_own, "ctx", chip_shift(d)) for d in (1, 3)}

    far_other = {2: lax.ppermute(far[2], "ctx", CORE)}
    grads = attention(place, query, up, up_other, kvs, bias)
    near, far_other, (dq, g0, g1, g2, g3) = lax.optimization_barrier((near, far_other, grads))
    dq_other = lax.ppermute(dq, "ctx", CORE)
    back = [
        lax.ppermute(g, "ctx", chip_shift(CHIPS - d)) for d, g in ((1, g1), (2, g2), (3, g3))
    ]
    back, dq_other = lax.optimization_barrier((back, dq_other))
    dkv = sum_four(g0, *back)
    dkv_other = lax.ppermute(dkv, "ctx", CORE)

    near, dkv_other = lax.optimization_barrier((near, dkv_other))
    for d in (1, 3):
        far[d] = near[d]
        far_other[d] = lax.ppermute(near[d], "ctx", CORE)
    tokens_t = transpose(
        [own, other] + [part for d in (1, 2, 3) for part in (far[d], far_other[d])]
    )
    packed = pack(place, dq, dq_other, dkv, dkv_other)
    columns = [packed[0]] + [
        lax.ppermute(packed[d], "ctx", chip_shift(d)) for d in (1, 2, 3)
    ]
    terms = weight_grad(place, tokens_t, columns)
    y_parts = [terms[0]] + [lax.ppermute(terms[d], "dp", y_shift(d)) for d in (1, 2, 3)]
    grad_tokens = input_grad(
        place, dq, dq_other, dkv, dkv_other, w_query, w_key, w_value
    )
    y_parts, grad_tokens = lax.optimization_barrier((y_parts, grad_tokens))
    y_sum = sum_four(*y_parts)
    z_parts = lax.all_to_all(y_sum, "dp", 0, 0, tiled=True, axis_index_groups=Z_GROUPS)
    grad_projection = final_sum(z_parts)
    return grad_tokens[None], grad_projection


def solution(mesh):
    return jax.shard_map(
        shards,
        mesh=mesh,
        in_specs=(
            P("dp", "ctx", None),
            P("dp", "ctx", None),
            P("dp", "ctx", None),
            P("dp", None),
            P(),
            P(),
            P(),
        ),
        out_specs=(P("dp", "ctx", None), P("dp", "ctx")),
        check_vma=False,
    )
```

```python
import functools
import math

import jax
import jax.numpy as jnp
from jax import lax
from jax.experimental import pallas as pl
from jax.experimental.pallas import tpu as pltpu
from jax.sharding import PartitionSpec as P

QH = 12
KVH = 2
HD = 128
TILE = 128
D = 1536
KEYS = 1024
CHIPS = 4
GROUP = QH // KVH
GF = GROUP * HD
YS = 4
ZS = 8
SCALE = 1.0 / math.sqrt(HD)
LOG2_SCALE = SCALE * math.log2(math.e)
BF = jnp.bfloat16
F32 = jnp.float32
VMEM_LIMIT = 24 * 1024 * 1024
W_CHUNKS = 4
Q_CHUNKS = 6
IN_CHUNKS = 6

CORE = [(i, i ^ 1) for i in range(8)]
NT = (((1,), (1,)), ((), ()))


def chip_shift(d):
    return [(i, ((i // 2 + d) % CHIPS) * 2 + i % 2) for i in range(8)]


def y_shift(d):
    return [(i, ((i // ZS + d) % YS) * ZS + i % ZS) for i in range(32)]


Z_GROUPS = [[y * ZS + z for z in range(ZS)] for y in range(YS)]


def dot(a, b):
    return jnp.dot(a, b, preferred_element_type=F32)


def dot_nt(a, b):
    return lax.dot_general(a, b, NT, preferred_element_type=F32)


def in_hbm(array):
    return pltpu.with_memory_space_constraint(array, pltpu.HBM)


def cost(flops, bytes_accessed, transcendentals=0):
    return pl.CostEstimate(
        flops=flops, bytes_accessed=bytes_accessed, transcendentals=transcendentals
    )


PARAMS = pltpu.CompilerParams(vmem_limit_bytes=VMEM_LIMIT)
WHOLE = pl.BlockSpec(memory_space=pltpu.VMEM)
SCALARS = pl.BlockSpec(memory_space=pltpu.SMEM)
STAY = pl.BlockSpec(memory_space=pltpu.HBM)


def kv_own_kernel(place, own, w_key, w_value, weights, out, rows, sems):
    columns = pl.ds(pl.multiple_of(place[1] * HD, HD), HD)
    copies = []
    for chunk in range(W_CHUNKS):
        part = pl.ds(chunk * (TILE // W_CHUNKS), TILE // W_CHUNKS)
        copies.append(pltpu.make_async_copy(own.at[part], rows.at[part], sems.at[chunk, 2]))
        part = pl.ds(chunk * (D // W_CHUNKS), D // W_CHUNKS)
        for side, source in enumerate((w_key, w_value)):
            copies.append(
                pltpu.make_async_copy(
                    source.at[part, columns],
                    weights.at[part, pl.ds(side * HD, HD)],
                    sems.at[chunk, side],
                )
            )
    for copy in copies:
        copy.start()
    for copy in copies:
        copy.wait()
    out[...] = dot(rows[...], weights[...]).astype(BF)


def project_kv_own(place, own, w_key, w_value):
    return pl.pallas_call(
        kv_own_kernel,
        in_specs=[SCALARS, STAY, STAY, STAY],
        out_specs=[WHOLE, WHOLE],
        out_shape=[
            jax.ShapeDtypeStruct((D, 2 * HD), BF),
            jax.ShapeDtypeStruct((TILE, 2 * HD), BF),
        ],
        scratch_shapes=[pltpu.VMEM((TILE, D), BF), pltpu.SemaphoreType.DMA((W_CHUNKS, 3))],
        compiler_params=PARAMS,
        cost_estimate=cost(2 * TILE * D * 256, 2 * (TILE * D + D * 256)),
        name="project_kv_own",
    )(place, own, w_key, w_value)


def kv_pair_kernel(own, other, weights, out):
    out[:TILE] = dot(own[...], weights[...]).astype(BF)
    out[TILE:] = dot(other[...], weights[...]).astype(BF)


def project_kv_pair(own, other, weights):
    return pl.pallas_call(
        kv_pair_kernel,
        in_specs=[WHOLE] * 3,
        out_specs=WHOLE,
        out_shape=jax.ShapeDtypeStruct((2 * TILE, 2 * HD), BF),
        compiler_params=PARAMS,
        cost_estimate=cost(4 * TILE * D * 256, 2 * (2 * TILE * D + D * 256)),
        name="project_kv_pair",
    )(own, other, weights)


def kv_kernel(other, weights, kv_own, out):
    out[:TILE] = kv_own[...]
    out[TILE:] = dot(other[...], weights[...]).astype(BF)


def project_kv(other, weights, kv_own):
    return pl.pallas_call(
        kv_kernel,
        in_specs=[WHOLE] * 3,
        out_specs=WHOLE,
        out_shape=jax.ShapeDtypeStruct((2 * TILE, 2 * HD), BF),
        compiler_params=PARAMS,
        cost_estimate=cost(2 * TILE * D * 256, 2 * (TILE * D + D * 256)),
        name="project_kv",
    )(other, weights, kv_own)


def query_kernel(
    place, own, other, w_query, segments_far, mask_far, mask_other, out, bias,
    weights, segments, mask_own, sems, small_sems,
):
    small = [
        pltpu.make_async_copy(segments_far, segments, small_sems.at[0]),
        pltpu.make_async_copy(mask_far, mask_own, small_sems.at[1]),
    ]
    for copy in small:
        copy.start()
    columns = pl.ds(pl.multiple_of(place[1] * GF, HD), GF)
    copies = []
    for chunk in range(Q_CHUNKS):
        part = pl.ds(chunk * (D // Q_CHUNKS), D // Q_CHUNKS)
        copies.append(
            pltpu.make_async_copy(w_query.at[part, columns], weights.at[part], sems.at[chunk])
        )
    for copy in copies:
        copy.start()
    for copy in small:
        copy.wait()

    chip, core = place[0], place[1]
    passages = segments[...]
    ends = [jnp.sum((passages <= s).astype(jnp.int32)) for s in range(3)]
    for slot in range(2):
        masks = mask_own if slot == 0 else mask_other
        tile = 2 * chip + (core if slot == 0 else 1 - core)
        mine = segments[:, pl.ds(pl.multiple_of(tile * TILE, TILE), TILE)]
        low = jnp.where(
            mine == 0, 0, jnp.where(mine == 1, ends[0], jnp.where(mine == 2, ends[1], ends[2]))
        )
        high = jnp.where(
            mine == 0,
            ends[0],
            jnp.where(mine == 1, ends[1], jnp.where(mine == 2, ends[2], KEYS)),
        )
        for d in range(CHIPS):
            for key_slot in range(2):
                key_tile = 2 * lax.rem(chip + CHIPS - d, CHIPS) + (
                    core if key_slot == 0 else 1 - core
                )
                seen = masks[0, key_tile] == 1
                position = key_tile * TILE + lax.broadcasted_iota(
                    jnp.int32, (TILE, TILE), 0
                )
                first = jnp.where(seen, 0, low)
                last = jnp.where(seen, KEYS, high)
                allowed = (position >= first) & (position < last)
                row = d * 2 * TILE + key_slot * TILE
                bias[row : row + TILE, slot * TILE : (slot + 1) * TILE] = jnp.where(
                    allowed, 0.0, -jnp.inf
                )

    for copy in copies:
        copy.wait()
    out[:TILE] = dot(own[...], weights[...]).astype(BF)
    out[TILE:] = dot(other[...], weights[...]).astype(BF)


def project_query(place, own, other, w_query, segments, mask_own, mask_other):
    return pl.pallas_call(
        query_kernel,
        in_specs=[SCALARS, WHOLE, WHOLE, STAY, STAY, STAY, SCALARS],
        out_specs=[WHOLE, WHOLE],
        out_shape=[
            jax.ShapeDtypeStruct((2 * TILE, GF), BF),
            jax.ShapeDtypeStruct((KEYS, 2 * TILE), F32),
        ],
        scratch_shapes=[
            pltpu.VMEM((D, GF), BF),
            pltpu.VMEM((1, KEYS), jnp.int32),
            pltpu.SMEM((1, KEYS // TILE), jnp.int32),
            pltpu.SemaphoreType.DMA((Q_CHUNKS,)),
            pltpu.SemaphoreType.DMA((2,)),
        ],
        compiler_params=PARAMS,
        cost_estimate=cost(2 * 256 * D * GF, 2 * (256 * D + D * GF + 256 * GF)),
        name="project_query",
    )(place, own, other, w_query, segments, mask_own, mask_other)


def attention_kernel(
    place, query, up_own, up_other, kv0, kv1, kv2, kv3, bias,
    grad_query, out0, out1, out2, out3,
    keys, values, keys_t, grad_key, grad_value,
):
    step = pl.program_id(0)

    @pl.when(step == 0)
    def _():
        for d, kv in enumerate((kv0, kv1, kv2, kv3)):
            keys[d * 256 : (d + 1) * 256] = kv[:, :HD]
            values[d * 256 : (d + 1) * 256] = kv[:, HD:]
            keys_t[:, d * 256 : (d + 1) * 256] = kv[:, :HD].T
        grad_key[...] = jnp.zeros_like(grad_key)
        grad_value[...] = jnp.zeros_like(grad_value)

    for member in range(2):
        columns = slice(member * HD, (member + 1) * HD)
        q = query[:, columns]
        up = jnp.concatenate([up_own[:, columns], up_other[:, columns]], axis=0)
        scores = dot_nt(keys[...], q) * LOG2_SCALE + bias[...]
        top = jnp.max(scores, axis=0, keepdims=True)
        powers = jnp.exp2(scores - top)
        probs = powers * (1.0 / jnp.sum(powers, axis=0, keepdims=True))
        probs_low = probs.astype(BF)
        grad_probs = dot_nt(values[...], up)
        delta = jnp.sum(probs_low.astype(F32) * grad_probs, axis=0, keepdims=True)
        grad_scores = (probs * (grad_probs - delta)).astype(BF)
        grad_value[...] += dot(probs_low, up)
        grad_key[...] += dot(grad_scores, q)
        grad_query[:, columns] = (dot(keys_t[...], grad_scores) * SCALE).T.astype(BF)

    @pl.when(step == pl.num_programs(0) - 1)
    def _():
        for d, out in enumerate((out0, out1, out2, out3)):
            rows = slice(d * 256, (d + 1) * 256)
            out[:, :HD] = (grad_key[rows] * SCALE).astype(out.dtype)
            out[:, HD:] = grad_value[rows].astype(out.dtype)


def attention(place, query, up_own, up_other, kvs, bias):
    blocks = GF // 256
    fixed = pl.BlockSpec((256, 256), lambda i, p: (0, 0))
    return pl.pallas_call(
        attention_kernel,
        grid_spec=pltpu.PrefetchScalarGridSpec(
            num_scalar_prefetch=1,
            grid=(blocks,),
            in_specs=[
                pl.BlockSpec((256, 256), lambda i, p: (0, i)),
                pl.BlockSpec((TILE, 256), lambda i, p: (0, p[1] * blocks + i)),
                pl.BlockSpec((TILE, 256), lambda i, p: (0, p[1] * blocks + i)),
                fixed, fixed, fixed, fixed,
                pl.BlockSpec((KEYS, 256), lambda i, p: (0, 0)),
            ],
            out_specs=[pl.BlockSpec((256, 256), lambda i, p: (0, i)), fixed, fixed, fixed, fixed],
            scratch_shapes=[
                pltpu.VMEM((KEYS, HD), BF),
                pltpu.VMEM((KEYS, HD), BF),
                pltpu.VMEM((HD, KEYS), BF),
                pltpu.VMEM((KEYS, HD), F32),
                pltpu.VMEM((KEYS, HD), F32),
            ],
        ),
        out_shape=[
            jax.ShapeDtypeStruct((256, GF), BF),
            jax.ShapeDtypeStruct((256, 256), F32),
            jax.ShapeDtypeStruct((256, 256), BF),
            jax.ShapeDtypeStruct((256, 256), BF),
            jax.ShapeDtypeStruct((256, 256), BF),
        ],
        compiler_params=PARAMS,
        cost_estimate=cost(10 * GROUP * 256 * KEYS * HD * 2, 4 << 20, GROUP * 256 * KEYS),
        name="attention",
    )(place, query, up_own, up_other, *kvs, bias)


def sum_kernel(a, b, c, d, out):
    total = (a[...] + b[...].astype(F32)) + (c[...].astype(F32) + d[...].astype(F32))
    out[...] = total.astype(out.dtype)


def sum_four(a, b, c, d):
    return pl.pallas_call(
        sum_kernel,
        in_specs=[WHOLE] * 4,
        out_specs=WHOLE,
        out_shape=jax.ShapeDtypeStruct(a.shape, BF),
        compiler_params=PARAMS,
        cost_estimate=cost(4 * a.size, 12 * a.size),
        name="sum_four",
    )(a, b, c, d)


def pack_kernel(place, dq, dq_other, dkv, dkv_other, out0, out1, out2, out3, blocks):
    core = place[1]

    def swapped(ref, columns):
        return jnp.concatenate([ref[TILE:, columns], ref[:TILE, columns]], axis=0)

    middle = slice(256, 512)

    @pl.when(core == 0)
    def _():
        blocks[0] = dq[:, 0:256]
        blocks[1] = dq[:, 512:768]
        blocks[2] = swapped(dq_other, middle)
        blocks[3, :, :HD] = dkv[:, :HD]
        blocks[3, :, HD:] = swapped(dkv_other, slice(0, HD))

    @pl.when(core == 1)
    def _():
        blocks[0] = swapped(dq_other, middle)
        blocks[1] = dq[:, 0:256]
        blocks[2] = dq[:, 512:768]
        blocks[3, :, :HD] = swapped(dkv_other, slice(HD, 2 * HD))
        blocks[3, :, HD:] = dkv[:, HD:]

    for d, out in enumerate((out0, out1, out2, out3)):
        out[...] = blocks[lax.rem(place[0] + d, CHIPS)]


def pack(place, dq, dq_other, dkv, dkv_other):
    return pl.pallas_call(
        pack_kernel,
        in_specs=[SCALARS] + [WHOLE] * 4,
        out_specs=[WHOLE] * 4,
        out_shape=[jax.ShapeDtypeStruct((256, 256), BF)] * 4,
        scratch_shapes=[pltpu.VMEM((4, 256, 256), BF)],
        compiler_params=PARAMS,
        cost_estimate=cost(0, 4 << 19),
        name="pack",
    )(place, dq, dq_other, dkv, dkv_other)


def transpose_kernel(*refs):
    out = refs[-1]
    for i, ref in enumerate(refs[:-1]):
        out[:, i * TILE : (i + 1) * TILE] = ref[...].T


def transpose(parts):
    return pl.pallas_call(
        transpose_kernel,
        in_specs=[WHOLE] * 8,
        out_specs=WHOLE,
        out_shape=jax.ShapeDtypeStruct((D, KEYS), BF),
        compiler_params=PARAMS,
        cost_estimate=cost(0, 4 * D * KEYS),
        name="transpose_tokens",
    )(*parts)


def weight_kernel(place, tokens_t, a, b, c, d, out0, out1, out2, out3):
    right = jnp.concatenate([a[...], b[...], c[...], d[...]], axis=0)
    for shift, out in enumerate((out0, out1, out2, out3)):
        row = pl.multiple_of(lax.rem(place[2] + shift, YS) * (D // YS), 128)
        out[...] = dot(tokens_t[pl.ds(row, D // YS)], right).astype(out.dtype)


def weight_grad(place, tokens_t, parts):
    shape = (D // YS, 256)
    return pl.pallas_call(
        weight_kernel,
        in_specs=[SCALARS] + [WHOLE] * 5,
        out_specs=[WHOLE] * 4,
        out_shape=[jax.ShapeDtypeStruct(shape, F32)] + [jax.ShapeDtypeStruct(shape, BF)] * 3,
        compiler_params=PARAMS,
        cost_estimate=cost(2 * D * KEYS * 256, 2 * D * KEYS + 3 * D * 256),
        name="weight_grad",
    )(place, tokens_t, *parts)


def input_kernel(
    place, dq, dq_other, dkv, dkv_other, w_query, w_key, w_value, out, left, right, sems
):
    core = place[1]
    width = D // IN_CHUNKS
    copies = []
    for chunk in range(IN_CHUNKS):
        part = pl.ds(chunk * width, width)
        copies.append(
            [
                pltpu.make_async_copy(
                    source.at[part],
                    right.at[part, pl.ds(start, size)],
                    sems.at[chunk, side],
                )
                for side, (source, start, size) in enumerate(
                    ((w_query, 0, D), (w_key, D, 256), (w_value, D + 256, 256))
                )
            ]
        )
    for group in copies:
        for copy in group:
            copy.start()
    mine = pl.ds(pl.multiple_of(core * GF, 128), GF)
    theirs = pl.ds(pl.multiple_of((1 - core) * GF, 128), GF)
    left[:, mine] = dq[:TILE]
    left[:, theirs] = dq_other[TILE:]
    for part in range(2):
        columns = slice(part * HD, (part + 1) * HD)
        base = D + part * KVH * HD
        left[:, pl.ds(pl.multiple_of(base + core * HD, 128), HD)] = dkv[:TILE, columns]
        left[:, pl.ds(pl.multiple_of(base + (1 - core) * HD, 128), HD)] = dkv_other[
            TILE:, columns
        ]
    for chunk, group in enumerate(copies):
        for copy in group:
            copy.wait()
        part = slice(chunk * width, (chunk + 1) * width)
        out[:, part] = dot_nt(left[...], right[part]).astype(BF)


def input_grad(place, dq, dq_other, dkv, dkv_other, w_query, w_key, w_value):
    return pl.pallas_call(
        input_kernel,
        in_specs=[SCALARS] + [WHOLE] * 4 + [STAY] * 3,
        out_specs=WHOLE,
        out_shape=jax.ShapeDtypeStruct((TILE, D), BF),
        scratch_shapes=[
            pltpu.VMEM((TILE, D + 512), BF),
            pltpu.VMEM((D, D + 512), BF),
            pltpu.SemaphoreType.DMA((IN_CHUNKS, 3)),
        ],
        compiler_params=PARAMS,
        cost_estimate=cost(2 * TILE * D * 2048, 2 * D * 2048),
        name="input_grad",
    )(place, dq, dq_other, dkv, dkv_other, w_query, w_key, w_value)


def final_kernel(parts, out):
    total = parts[0:48].astype(F32)
    for z in range(1, ZS):
        total += parts[z * 48 : (z + 1) * 48].astype(F32)
    out[...] = total


def final_sum(parts):
    return pl.pallas_call(
        final_kernel,
        in_specs=[WHOLE],
        out_specs=WHOLE,
        out_shape=jax.ShapeDtypeStruct((48, 256), F32),
        compiler_params=PARAMS,
        cost_estimate=cost(parts.size, 2 * parts.size),
        name="final_sum",
    )(parts)


def shards(tokens, grad_heads, tile_mask, segments, w_query, w_key, w_value):
    ctx = lax.axis_index("ctx")
    dp = lax.axis_index("dp")
    place = jnp.stack([ctx // 2, ctx % 2, dp // ZS, dp % ZS]).astype(jnp.int32)
    own, up = tokens[0], grad_heads[0]
    far = {d: lax.ppermute(own, "ctx", chip_shift(d)) for d in (1, 3)}
    other = lax.ppermute(own, "ctx", CORE)
    up_other = lax.ppermute(up, "ctx", CORE)
    mask_other = lax.ppermute(tile_mask[0], "ctx", CORE)

    w_query, w_key, w_value = (in_hbm(w) for w in (w_query, w_key, w_value))
    weights, kv_own = project_kv_own(place, in_hbm(own), w_key, w_value)
    kv = project_kv(other, weights, kv_own)
    kv2 = lax.ppermute(kv, "ctx", chip_shift(2))
    query, bias = project_query(
        place, own, other, w_query, in_hbm(segments), in_hbm(tile_mask[0]), mask_other
    )
    far, kv2, query, late_own = lax.optimization_barrier((far, kv2, query, own))
    far_other = {d: lax.ppermute(far[d], "ctx", CORE) for d in (1, 3)}
    late = lax.ppermute(late_own, "ctx", chip_shift(2))
    kv1, kv3 = (project_kv_pair(far[d], far_other[d], weights) for d in (1, 3))

    grads = attention(place, query, up, up_other, [kv, kv1, kv2, kv3], bias)
    late, (dq, g0, g1, g2, g3) = lax.optimization_barrier((late, grads))
    dq_other = lax.ppermute(dq, "ctx", CORE)
    back = [
        lax.ppermute(g, "ctx", chip_shift(CHIPS - d)) for d, g in ((1, g1), (2, g2), (3, g3))
    ]
    back, dq_other = lax.optimization_barrier((back, dq_other))
    dkv = sum_four(g0, *back)
    dkv_other = lax.ppermute(dkv, "ctx", CORE)

    far[2], dkv_other = lax.optimization_barrier((late, dkv_other))
    far_other[2] = lax.ppermute(far[2], "ctx", CORE)
    tokens_t = transpose(
        [own, other] + [part for d in (1, 2, 3) for part in (far[d], far_other[d])]
    )
    packed = pack(place, dq, dq_other, dkv, dkv_other)
    columns = [packed[0]] + [
        lax.ppermute(packed[d], "ctx", chip_shift(d)) for d in (1, 2, 3)
    ]
    terms = weight_grad(place, tokens_t, columns)
    y_parts = [terms[0]] + [lax.ppermute(terms[d], "dp", y_shift(d)) for d in (1, 2, 3)]
    grad_tokens = input_grad(
        place, dq, dq_other, dkv, dkv_other, w_query, w_key, w_value
    )
    y_parts, grad_tokens = lax.optimization_barrier((y_parts, grad_tokens))
    y_sum = sum_four(*y_parts)
    z_parts = lax.all_to_all(y_sum, "dp", 0, 0, tiled=True, axis_index_groups=Z_GROUPS)
    grad_projection = final_sum(z_parts)
    return grad_tokens[None], grad_projection


def solution(mesh):
    return jax.shard_map(
        shards,
        mesh=mesh,
        in_specs=(
            P("dp", "ctx", None),
            P("dp", "ctx", None),
            P("dp", "ctx", None),
            P("dp", None),
            P(),
            P(),
            P(),
        ),
        out_specs=(P("dp", "ctx", None), P("dp", "ctx")),
        check_vma=False,
    )
```

```python
import functools
import math

import jax
import jax.numpy as jnp
from jax import lax
from jax.experimental import pallas as pl
from jax.experimental.pallas import tpu as pltpu
from jax.sharding import PartitionSpec as P

QH = 12
KVH = 2
HD = 128
TILE = 128
D = 1536
KEYS = 1024
CHIPS = 4
GROUP = QH // KVH
GF = GROUP * HD
STACK = GROUP * 256
YS = 4
ZS = 8
SCALE = 1.0 / math.sqrt(HD)
LOG2_SCALE = SCALE * math.log2(math.e)
BF = jnp.bfloat16
F32 = jnp.float32
VMEM_LIMIT = 24 * 1024 * 1024
W_CHUNKS = 1
Q_CHUNKS = 3
IN_CHUNKS = 3

CORE = [(i, i ^ 1) for i in range(8)]
NT = (((1,), (1,)), ((), ()))


def chip_shift(d):
    return [(i, ((i // 2 + d) % CHIPS) * 2 + i % 2) for i in range(8)]


def y_shift(d):
    return [(i, ((i // ZS + d) % YS) * ZS + i % ZS) for i in range(32)]


Z_GROUPS = [[y * ZS + z for z in range(ZS)] for y in range(YS)]


def dot(a, b):
    return jnp.dot(a, b, preferred_element_type=F32)


def dot_nt(a, b):
    return lax.dot_general(a, b, NT, preferred_element_type=F32)


def in_hbm(array):
    return pltpu.with_memory_space_constraint(array, pltpu.HBM)


def cost(flops, bytes_accessed, transcendentals=0):
    return pl.CostEstimate(
        flops=1, bytes_accessed=1, transcendentals=0
    )


PARAMS = pltpu.CompilerParams(vmem_limit_bytes=VMEM_LIMIT)
WHOLE = pl.BlockSpec(memory_space=pltpu.VMEM)
SCALARS = pl.BlockSpec(memory_space=pltpu.SMEM)
STAY = pl.BlockSpec(memory_space=pltpu.HBM)


def kv_own_kernel(place, own, w_key, w_value, weights, out, rows, sems):
    columns = pl.ds(pl.multiple_of(place[1] * HD, HD), HD)
    copies = []
    for chunk in range(W_CHUNKS):
        part = pl.ds(chunk * (TILE // W_CHUNKS), TILE // W_CHUNKS)
        copies.append(pltpu.make_async_copy(own.at[part], rows.at[part], sems.at[chunk, 2]))
        part = pl.ds(chunk * (D // W_CHUNKS), D // W_CHUNKS)
        for side, source in enumerate((w_key, w_value)):
            copies.append(
                pltpu.make_async_copy(
                    source.at[part, columns],
                    weights.at[part, pl.ds(side * HD, HD)],
                    sems.at[chunk, side],
                )
            )
    for copy in copies:
        copy.start()
    for copy in copies:
        copy.wait()
    out[...] = dot(rows[...], weights[...]).astype(BF)


def project_kv_own(place, own, w_key, w_value):
    return pl.pallas_call(
        kv_own_kernel,
        in_specs=[SCALARS, STAY, STAY, STAY],
        out_specs=[WHOLE, WHOLE],
        out_shape=[
            jax.ShapeDtypeStruct((D, 2 * HD), BF),
            jax.ShapeDtypeStruct((TILE, 2 * HD), BF),
        ],
        scratch_shapes=[pltpu.VMEM((TILE, D), BF), pltpu.SemaphoreType.DMA((W_CHUNKS, 3))],
        compiler_params=PARAMS,
        cost_estimate=cost(2 * TILE * D * 256, 2 * (TILE * D + D * 256)),
        name="project_kv_own",
    )(place, own, w_key, w_value)


def kv_pair_kernel(own, other, weights, out):
    out[:TILE] = dot(own[...], weights[...]).astype(BF)
    out[TILE:] = dot(other[...], weights[...]).astype(BF)


def project_kv_pair(own, other, weights):
    return pl.pallas_call(
        kv_pair_kernel,
        in_specs=[WHOLE] * 3,
        out_specs=WHOLE,
        out_shape=jax.ShapeDtypeStruct((2 * TILE, 2 * HD), BF),
        compiler_params=PARAMS,
        cost_estimate=cost(4 * TILE * D * 256, 2 * (2 * TILE * D + D * 256)),
        name="project_kv_pair",
    )(own, other, weights)


def kv_kernel(other, weights, kv_own, out):
    out[:TILE] = kv_own[...]
    out[TILE:] = dot(other[...], weights[...]).astype(BF)


def project_kv(other, weights, kv_own):
    return pl.pallas_call(
        kv_kernel,
        in_specs=[WHOLE] * 3,
        out_specs=WHOLE,
        out_shape=jax.ShapeDtypeStruct((2 * TILE, 2 * HD), BF),
        compiler_params=PARAMS,
        cost_estimate=cost(2 * TILE * D * 256, 2 * (TILE * D + D * 256)),
        name="project_kv",
    )(other, weights, kv_own)


def query_kernel(
    place, own, other, w_query, segments_far, mask_far, mask_other, out, limits,
    weights, segments, mask_own, sems, small_sems,
):
    small = [
        pltpu.make_async_copy(segments_far, segments, small_sems.at[0]),
        pltpu.make_async_copy(mask_far, mask_own, small_sems.at[1]),
    ]
    for copy in small:
        copy.start()
    columns = pl.ds(pl.multiple_of(place[1] * GF, HD), GF)
    copies = []
    for chunk in range(Q_CHUNKS):
        part = pl.ds(chunk * (D // Q_CHUNKS), D // Q_CHUNKS)
        copies.append(
            pltpu.make_async_copy(w_query.at[part, columns], weights.at[part], sems.at[chunk])
        )
    for copy in copies:
        copy.start()
    for copy in small:
        copy.wait()

    chip, core = place[0], place[1]
    passages = segments[...]
    ends = [jnp.sum((passages <= s).astype(jnp.int32)) for s in range(3)]
    for slot in range(2):
        masks = mask_own if slot == 0 else mask_other
        tile = 2 * chip + (core if slot == 0 else 1 - core)
        mine = segments[:, pl.ds(pl.multiple_of(tile * TILE, TILE), TILE)]
        low = jnp.where(
            mine == 0, 0, jnp.where(mine == 1, ends[0], jnp.where(mine == 2, ends[1], ends[2]))
        )
        high = jnp.where(
            mine == 0, ends[0], jnp.where(mine == 1, ends[1], jnp.where(mine == 2, ends[2], KEYS))
        )
        for d in range(CHIPS):
            for key_slot in range(2):
                key_tile = 2 * lax.rem(chip + CHIPS - d, CHIPS) + (
                    core if key_slot == 0 else 1 - core
                )
                seen = masks[0, key_tile] == 1
                row = 4 * d + 2 * key_slot
                place_of = slice(slot * TILE, (slot + 1) * TILE)
                limits[row : row + 1, place_of] = jnp.where(seen, 0, low) - key_tile * TILE
                limits[row + 1 : row + 2, place_of] = (
                    jnp.where(seen, KEYS, high) - key_tile * TILE
                )

    for copy in copies:
        copy.wait()
    for slot, rows in enumerate((own, other)):
        queries = dot(rows[...], weights[...]).astype(BF)
        for head in range(GROUP):
            out[head * 256 + slot * TILE : head * 256 + (slot + 1) * TILE] = queries[
                :, head * HD : (head + 1) * HD
            ]


def project_query(place, own, other, w_query, segments, mask_own, mask_other):
    return pl.pallas_call(
        query_kernel,
        in_specs=[SCALARS, WHOLE, WHOLE, STAY, STAY, STAY, SCALARS],
        out_specs=[WHOLE, WHOLE],
        out_shape=[
            jax.ShapeDtypeStruct((STACK, HD), BF),
            jax.ShapeDtypeStruct((4 * CHIPS, 2 * TILE), jnp.int32),
        ],
        scratch_shapes=[
            pltpu.VMEM((D, GF), BF),
            pltpu.VMEM((1, KEYS), jnp.int32),
            pltpu.SMEM((1, KEYS // TILE), jnp.int32),
            pltpu.SemaphoreType.DMA((Q_CHUNKS,)),
            pltpu.SemaphoreType.DMA((2,)),
        ],
        compiler_params=PARAMS,
        cost_estimate=cost(2 * 256 * D * GF, 2 * (256 * D + D * GF + 256 * GF)),
        name="project_query",
    )(place, own, other, w_query, segments, mask_own, mask_other)


def stack_kernel(place, up_own, up_other, out):
    for slot, rows in enumerate((up_own, up_other)):
        for head in range(GROUP):
            columns = pl.ds(pl.multiple_of(place[1] * GF + head * HD, HD), HD)
            out[head * 256 + slot * TILE : head * 256 + (slot + 1) * TILE] = rows[:, columns]


def stack_up(place, up_own, up_other):
    return pl.pallas_call(
        stack_kernel,
        in_specs=[SCALARS, WHOLE, WHOLE],
        out_specs=WHOLE,
        out_shape=jax.ShapeDtypeStruct((STACK, HD), BF),
        compiler_params=PARAMS,
        cost_estimate=cost(0, 4 * STACK * HD),
        name="stack_up",
    )(place, up_own, up_other)


def scores_kernel(d, kv, limits, query, up, powers, grads, stats, keys_t):
    keys, values = kv[:, :HD], kv[:, HD:]
    keys_t[...] = keys.T
    position = lax.broadcasted_iota(jnp.int32, (TILE, 2 * TILE), 0)
    bias = []
    for key_slot in range(2):
        row = 4 * d + 2 * key_slot
        allowed = (position >= limits[row : row + 1]) & (position < limits[row + 1 : row + 2])
        bias.append(jnp.where(allowed, 0.0, -jnp.inf))
    bias = jnp.concatenate(bias, axis=0)
    for head in range(GROUP):
        part = slice(head * 256, (head + 1) * 256)
        scores = dot_nt(keys, query[part]) * LOG2_SCALE + bias
        top = jnp.max(scores, axis=0, keepdims=True)
        power = jnp.exp2(scores - jnp.where(top == -jnp.inf, 0.0, top))
        grad = dot_nt(values, up[part])
        powers[:, part] = power
        grads[:, part] = grad
        stats[0:1, part] = top
        stats[1:2, part] = jnp.sum(power, axis=0, keepdims=True)
        stats[2:3, part] = jnp.sum(power * grad, axis=0, keepdims=True)


def chip_scores(d, kv, limits, query, up):
    return pl.pallas_call(
        functools.partial(scores_kernel, d),
        in_specs=[WHOLE] * 4,
        out_specs=[WHOLE] * 4,
        out_shape=[
            jax.ShapeDtypeStruct((256, STACK), F32),
            jax.ShapeDtypeStruct((256, STACK), F32),
            jax.ShapeDtypeStruct((8, STACK), F32),
            jax.ShapeDtypeStruct((HD, 256), BF),
        ],
        compiler_params=PARAMS,
        cost_estimate=cost(4 * STACK * 256 * HD, 10 * 256 * STACK, 256 * STACK),
        name=f"chip_scores_{d}",
    )(kv, limits, query, up)


def factors_kernel(a, b, c, d, out):
    parts = (a, b, c, d)
    top = jnp.maximum(jnp.maximum(a[0:1], b[0:1]), jnp.maximum(c[0:1], d[0:1]))
    factors = [jnp.exp2(part[0:1] - top) for part in parts]
    total = sum(factor * part[1:2] for factor, part in zip(factors, parts))
    factors = [factor / total for factor in factors]
    for chip, factor in enumerate(factors):
        out[chip : chip + 1] = factor
    out[4:5] = sum(factor * part[2:3] for factor, part in zip(factors, parts))


def softmax_factors(stats):
    return pl.pallas_call(
        factors_kernel,
        in_specs=[WHOLE] * 4,
        out_specs=WHOLE,
        out_shape=jax.ShapeDtypeStruct((8, STACK), F32),
        compiler_params=PARAMS,
        cost_estimate=cost(20 * STACK, 128 * STACK),
        name="softmax_factors",
    )(*stats)


def terms_kernel(d, powers, grads, factors, query, up, out, grad_scores, probs_low):
    for head in range(GROUP):
        part = slice(head * 256, (head + 1) * 256)
        probs = powers[:, part] * factors[d : d + 1, part]
        probs_low[:, part] = probs.astype(BF)
        grad_scores[:, part] = (probs * (grads[:, part] - factors[4:5, part])).astype(BF)
    out[:, :HD] = (dot(grad_scores[...], query[...]) * SCALE).astype(out.dtype)
    out[:, HD:] = dot(probs_low[...], up[...]).astype(out.dtype)


def chip_terms(d, powers, grads, factors, query, up):
    return pl.pallas_call(
        functools.partial(terms_kernel, d),
        in_specs=[WHOLE] * 5,
        out_specs=[WHOLE] * 2,
        out_shape=[
            jax.ShapeDtypeStruct((256, 256), F32 if d == 0 else BF),
            jax.ShapeDtypeStruct((256, STACK), BF),
        ],
        scratch_shapes=[pltpu.VMEM((256, STACK), BF)],
        compiler_params=PARAMS,
        cost_estimate=cost(4 * STACK * 256 * HD, 10 * 256 * STACK),
        name=f"chip_terms_{d}",
    )(powers, grads, factors, query, up)


def query_grad_kernel(k0, k1, k2, k3, g0, g1, g2, g3, out):
    for head in range(GROUP):
        part = slice(head * 256, (head + 1) * 256)
        total = dot(k0[...], g0[:, part]) + dot(k1[...], g1[:, part])
        total += dot(k2[...], g2[:, part]) + dot(k3[...], g3[:, part])
        out[:, head * HD : (head + 1) * HD] = (total * SCALE).T.astype(BF)


def query_grad(keys_t, grad_scores):
    return pl.pallas_call(
        query_grad_kernel,
        in_specs=[WHOLE] * 8,
        out_specs=WHOLE,
        out_shape=jax.ShapeDtypeStruct((256, GF), BF),
        compiler_params=PARAMS,
        cost_estimate=cost(2 * STACK * KEYS * HD, 2 * STACK * KEYS),
        name="query_grad",
    )(*keys_t, *grad_scores)


def sum_kernel(a, b, c, d, out):
    total = (a[...] + b[...].astype(F32)) + (c[...].astype(F32) + d[...].astype(F32))
    out[...] = total.astype(out.dtype)


def sum_four(a, b, c, d):
    return pl.pallas_call(
        sum_kernel,
        in_specs=[WHOLE] * 4,
        out_specs=WHOLE,
        out_shape=jax.ShapeDtypeStruct(a.shape, BF),
        compiler_params=PARAMS,
        cost_estimate=cost(4 * a.size, 12 * a.size),
        name="sum_four",
    )(a, b, c, d)


def pack_kernel(place, dq, dq_other, dkv, dkv_other, out0, out1, out2, out3, blocks):
    core = place[1]

    def swapped(ref, columns):
        return jnp.concatenate([ref[TILE:, columns], ref[:TILE, columns]], axis=0)

    middle = slice(256, 512)

    @pl.when(core == 0)
    def _():
        blocks[0] = dq[:, 0:256]
        blocks[1] = dq[:, 512:768]
        blocks[2] = swapped(dq_other, middle)
        blocks[3, :, :HD] = dkv[:, :HD]
        blocks[3, :, HD:] = swapped(dkv_other, slice(0, HD))

    @pl.when(core == 1)
    def _():
        blocks[0] = swapped(dq_other, middle)
        blocks[1] = dq[:, 0:256]
        blocks[2] = dq[:, 512:768]
        blocks[3, :, :HD] = swapped(dkv_other, slice(HD, 2 * HD))
        blocks[3, :, HD:] = dkv[:, HD:]

    for d, out in enumerate((out0, out1, out2, out3)):
        out[...] = blocks[lax.rem(place[0] + d, CHIPS)]


def pack(place, dq, dq_other, dkv, dkv_other):
    return pl.pallas_call(
        pack_kernel,
        in_specs=[SCALARS] + [WHOLE] * 4,
        out_specs=[WHOLE] * 4,
        out_shape=[jax.ShapeDtypeStruct((256, 256), BF)] * 4,
        scratch_shapes=[pltpu.VMEM((4, 256, 256), BF)],
        compiler_params=PARAMS,
        cost_estimate=cost(0, 4 << 19),
        name="pack",
    )(place, dq, dq_other, dkv, dkv_other)


def transpose_kernel(*refs):
    out = refs[-1]
    for i, ref in enumerate(refs[:-1]):
        out[:, i * TILE : (i + 1) * TILE] = ref[...].T


def transpose(parts):
    return pl.pallas_call(
        transpose_kernel,
        in_specs=[WHOLE] * 8,
        out_specs=WHOLE,
        out_shape=jax.ShapeDtypeStruct((D, KEYS), BF),
        compiler_params=PARAMS,
        cost_estimate=cost(0, 4 * D * KEYS),
        name="transpose_tokens",
    )(*parts)


def weight_kernel(place, tokens_t, a, b, c, d, out0, out1, out2, out3):
    right = jnp.concatenate([a[...], b[...], c[...], d[...]], axis=0)
    for shift, out in enumerate((out0, out1, out2, out3)):
        row = pl.multiple_of(lax.rem(place[2] + shift, YS) * (D // YS), 128)
        out[...] = dot(tokens_t[pl.ds(row, D // YS)], right).astype(out.dtype)


def weight_grad(place, tokens_t, parts):
    shape = (D // YS, 256)
    return pl.pallas_call(
        weight_kernel,
        in_specs=[SCALARS] + [WHOLE] * 5,
        out_specs=[WHOLE] * 4,
        out_shape=[jax.ShapeDtypeStruct(shape, F32)] + [jax.ShapeDtypeStruct(shape, BF)] * 3,
        compiler_params=PARAMS,
        cost_estimate=cost(2 * D * KEYS * 256, 2 * D * KEYS + 3 * D * 256),
        name="weight_grad",
    )(place, tokens_t, *parts)


def input_kernel(
    place, dq, dq_other, dkv, dkv_other, w_query, w_key, w_value, out, left, right, sems
):
    core = place[1]
    width = D // IN_CHUNKS
    copies = []
    for chunk in range(IN_CHUNKS):
        part = pl.ds(chunk * width, width)
        copies.append(
            [
                pltpu.make_async_copy(
                    source.at[part],
                    right.at[part, pl.ds(start, size)],
                    sems.at[chunk, side],
                )
                for side, (source, start, size) in enumerate(
                    ((w_query, 0, D), (w_key, D, 256), (w_value, D + 256, 256))
                )
            ]
        )
    for group in copies:
        for copy in group:
            copy.start()
    mine = pl.ds(pl.multiple_of(core * GF, 128), GF)
    theirs = pl.ds(pl.multiple_of((1 - core) * GF, 128), GF)
    left[:, mine] = dq[:TILE]
    left[:, theirs] = dq_other[TILE:]
    for part in range(2):
        columns = slice(part * HD, (part + 1) * HD)
        base = D + part * KVH * HD
        left[:, pl.ds(pl.multiple_of(base + core * HD, 128), HD)] = dkv[:TILE, columns]
        left[:, pl.ds(pl.multiple_of(base + (1 - core) * HD, 128), HD)] = dkv_other[
            TILE:, columns
        ]
    for chunk, group in enumerate(copies):
        for copy in group:
            copy.wait()
        part = slice(chunk * width, (chunk + 1) * width)
        out[:, part] = dot_nt(left[...], right[part]).astype(BF)


def input_grad(place, dq, dq_other, dkv, dkv_other, w_query, w_key, w_value):
    return pl.pallas_call(
        input_kernel,
        in_specs=[SCALARS] + [WHOLE] * 4 + [STAY] * 3,
        out_specs=WHOLE,
        out_shape=jax.ShapeDtypeStruct((TILE, D), BF),
        scratch_shapes=[
            pltpu.VMEM((TILE, D + 512), BF),
            pltpu.VMEM((D, D + 512), BF),
            pltpu.SemaphoreType.DMA((IN_CHUNKS, 3)),
        ],
        compiler_params=PARAMS,
        cost_estimate=cost(2 * TILE * D * 2048, 2 * D * 2048),
        name="input_grad",
    )(place, dq, dq_other, dkv, dkv_other, w_query, w_key, w_value)


def final_kernel(parts, out):
    total = parts[0:48].astype(F32)
    for z in range(1, ZS):
        total += parts[z * 48 : (z + 1) * 48].astype(F32)
    out[...] = total


def final_sum(parts):
    return pl.pallas_call(
        final_kernel,
        in_specs=[WHOLE],
        out_specs=WHOLE,
        out_shape=jax.ShapeDtypeStruct((48, 256), F32),
        compiler_params=PARAMS,
        cost_estimate=cost(parts.size, 2 * parts.size),
        name="final_sum",
    )(parts)


def shards(tokens, grad_heads, tile_mask, segments, w_query, w_key, w_value):
    ctx = lax.axis_index("ctx")
    dp = lax.axis_index("dp")
    place = jnp.stack([ctx // 2, ctx % 2, dp // ZS, dp % ZS]).astype(jnp.int32)
    own, up = tokens[0], grad_heads[0]
    other = lax.ppermute(own, "ctx", CORE)
    up_other = lax.ppermute(up, "ctx", CORE)
    mask_other = lax.ppermute(tile_mask[0], "ctx", CORE)
    other, mask_other, up_other = lax.optimization_barrier((other, mask_other, up_other))

    w_query, w_key, w_value = (in_hbm(w) for w in (w_query, w_key, w_value))
    weights, kv_own = project_kv_own(place, in_hbm(own), w_key, w_value)
    kv = project_kv(other, weights, kv_own)
    kvs = [kv] + [lax.ppermute(kv, "ctx", chip_shift(d)) for d in (1, 2, 3)]
    far = {d: lax.ppermute(own, "ctx", chip_shift(d)) for d in (1, 3)}
    query, limits = project_query(
        place, own, other, w_query, in_hbm(segments), in_hbm(tile_mask[0]), mask_other
    )
    up = stack_up(place, up, up_other)
    scores = {0: chip_scores(0, kvs[0], limits, query, up)}
    far, kvs, scores[0], late_own = lax.optimization_barrier((far, kvs, scores[0], own))
    late = lax.ppermute(late_own, "ctx", chip_shift(2))
    far_other = {d: lax.ppermute(far[d], "ctx", CORE) for d in (1, 3)}
    for d in (1, 3, 2):
        scores[d] = chip_scores(d, kvs[d], limits, query, up)
    factors = softmax_factors([scores[d][2] for d in range(CHIPS)])
    terms, grad_scores = {}, {}
    for d in (2, 1, 3):
        terms[d], grad_scores[d] = chip_terms(d, *scores[d][:2], factors, query, up)
    late, far_other, terms, scores[0] = lax.optimization_barrier(
        (late, far_other, terms, scores[0])
    )
    back = [lax.ppermute(terms[d], "ctx", chip_shift(CHIPS - d)) for d in (2, 1, 3)]
    terms[0], grad_scores[0] = chip_terms(0, *scores[0][:2], factors, query, up)
    dq = query_grad([scores[d][3] for d in range(CHIPS)], [grad_scores[d] for d in range(CHIPS)])
    back, dq = lax.optimization_barrier((back, dq))
    dq_other = lax.ppermute(dq, "ctx", CORE)
    dkv = sum_four(terms[0], *back)
    dkv_other = lax.ppermute(dkv, "ctx", CORE)
    far[2], dkv = lax.optimization_barrier((late, dkv))
    far_other[2] = lax.ppermute(far[2], "ctx", CORE)
    tokens_t = transpose(
        [own, other] + [part for d in (1, 2, 3) for part in (far[d], far_other[d])]
    )
    packed = pack(place, dq, dq_other, dkv, dkv_other)
    columns = [packed[0]] + [
        lax.ppermute(packed[d], "ctx", chip_shift(d)) for d in (1, 2, 3)
    ]
    terms = weight_grad(place, tokens_t, columns)
    y_parts = [terms[0]] + [lax.ppermute(terms[d], "dp", y_shift(d)) for d in (1, 2, 3)]
    grad_tokens = input_grad(
        place, dq, dq_other, dkv, dkv_other, w_query, w_key, w_value
    )
    y_parts, grad_tokens = lax.optimization_barrier((y_parts, grad_tokens))
    y_sum = sum_four(*y_parts)
    z_parts = lax.all_to_all(y_sum, "dp", 0, 0, tiled=True, axis_index_groups=Z_GROUPS)
    grad_projection = final_sum(z_parts)
    return grad_tokens[None], grad_projection


def solution(mesh):
    return jax.shard_map(
        shards,
        mesh=mesh,
        in_specs=(
            P("dp", "ctx", None),
            P("dp", "ctx", None),
            P("dp", "ctx", None),
            P("dp", None),
            P(),
            P(),
            P(),
        ),
        out_specs=(P("dp", "ctx", None), P("dp", "ctx")),
        check_vma=False,
    )
```

```python
import functools
import math

import jax
import jax.numpy as jnp
from jax import lax
from jax.experimental import pallas as pl
from jax.experimental.pallas import tpu as pltpu
from jax.sharding import PartitionSpec as P

QH = 12
KVH = 2
HD = 128
TILE = 128
D = 1536
KEYS = 1024
CHIPS = 4
GROUP = QH // KVH
GF = GROUP * HD
STACK = GROUP * 256
YS = 4
ZS = 8
SCALE = 1.0 / math.sqrt(HD)
LOG2_SCALE = SCALE * math.log2(math.e)
BF = jnp.bfloat16
F32 = jnp.float32
VMEM_LIMIT = 24 * 1024 * 1024
W_CHUNKS = 1
Q_CHUNKS = 3
IN_CHUNKS = 3

CORE = [(i, i ^ 1) for i in range(8)]
NT = (((1,), (1,)), ((), ()))


def chip_shift(d):
    return [(i, ((i // 2 + d) % CHIPS) * 2 + i % 2) for i in range(8)]


def y_shift(d):
    return [(i, ((i // ZS + d) % YS) * ZS + i % ZS) for i in range(32)]


Z_GROUPS = [[y * ZS + z for z in range(ZS)] for y in range(YS)]


def dot(a, b):
    return jnp.dot(a, b, preferred_element_type=F32)


def dot_nt(a, b):
    return lax.dot_general(a, b, NT, preferred_element_type=F32)


def in_hbm(array):
    return pltpu.with_memory_space_constraint(array, pltpu.HBM)


def cost(flops, bytes_accessed, transcendentals=0):
    return pl.CostEstimate(
        flops=1, bytes_accessed=1, transcendentals=0
    )


PARAMS = pltpu.CompilerParams(vmem_limit_bytes=VMEM_LIMIT)
WHOLE = pl.BlockSpec(memory_space=pltpu.VMEM)
SCALARS = pl.BlockSpec(memory_space=pltpu.SMEM)
STAY = pl.BlockSpec(memory_space=pltpu.HBM)


def kv_own_kernel(place, own, w_key, w_value, weights, out, rows, sems):
    columns = pl.ds(pl.multiple_of(place[1] * HD, HD), HD)
    copies = []
    for chunk in range(W_CHUNKS):
        part = pl.ds(chunk * (TILE // W_CHUNKS), TILE // W_CHUNKS)
        copies.append(pltpu.make_async_copy(own.at[part], rows.at[part], sems.at[chunk, 2]))
        part = pl.ds(chunk * (D // W_CHUNKS), D // W_CHUNKS)
        for side, source in enumerate((w_key, w_value)):
            copies.append(
                pltpu.make_async_copy(
                    source.at[part, columns],
                    weights.at[part, pl.ds(side * HD, HD)],
                    sems.at[chunk, side],
                )
            )
    for copy in copies:
        copy.start()
    for copy in copies:
        copy.wait()
    out[...] = dot(rows[...], weights[...]).astype(BF)


def project_kv_own(place, own, w_key, w_value):
    return pl.pallas_call(
        kv_own_kernel,
        in_specs=[SCALARS, STAY, STAY, STAY],
        out_specs=[WHOLE, WHOLE],
        out_shape=[
            jax.ShapeDtypeStruct((D, 2 * HD), BF),
            jax.ShapeDtypeStruct((TILE, 2 * HD), BF),
        ],
        scratch_shapes=[pltpu.VMEM((TILE, D), BF), pltpu.SemaphoreType.DMA((W_CHUNKS, 3))],
        compiler_params=PARAMS,
        cost_estimate=cost(2 * TILE * D * 256, 2 * (TILE * D + D * 256)),
        name="project_kv_own",
    )(place, own, w_key, w_value)


def kv_pair_kernel(own, other, weights, out):
    out[:TILE] = dot(own[...], weights[...]).astype(BF)
    out[TILE:] = dot(other[...], weights[...]).astype(BF)


def project_kv_pair(own, other, weights):
    return pl.pallas_call(
        kv_pair_kernel,
        in_specs=[WHOLE] * 3,
        out_specs=WHOLE,
        out_shape=jax.ShapeDtypeStruct((2 * TILE, 2 * HD), BF),
        compiler_params=PARAMS,
        cost_estimate=cost(4 * TILE * D * 256, 2 * (2 * TILE * D + D * 256)),
        name="project_kv_pair",
    )(own, other, weights)


def kv_kernel(other, weights, kv_own, out):
    out[:TILE] = kv_own[...]
    out[TILE:] = dot(other[...], weights[...]).astype(BF)


def project_kv(other, weights, kv_own):
    return pl.pallas_call(
        kv_kernel,
        in_specs=[WHOLE] * 3,
        out_specs=WHOLE,
        out_shape=jax.ShapeDtypeStruct((2 * TILE, 2 * HD), BF),
        compiler_params=PARAMS,
        cost_estimate=cost(2 * TILE * D * 256, 2 * (TILE * D + D * 256)),
        name="project_kv",
    )(other, weights, kv_own)


def query_kernel(
    place, own, other, w_query, segments_far, mask_far, mask_other, out, limits,
    weights, segments, mask_own, sems, small_sems,
):
    small = [
        pltpu.make_async_copy(segments_far, segments, small_sems.at[0]),
        pltpu.make_async_copy(mask_far, mask_own, small_sems.at[1]),
    ]
    for copy in small:
        copy.start()
    columns = pl.ds(pl.multiple_of(place[1] * GF, HD), GF)
    copies = []
    for chunk in range(Q_CHUNKS):
        part = pl.ds(chunk * (D // Q_CHUNKS), D // Q_CHUNKS)
        copies.append(
            pltpu.make_async_copy(w_query.at[part, columns], weights.at[part], sems.at[chunk])
        )
    for copy in copies:
        copy.start()
    for copy in small:
        copy.wait()

    chip, core = place[0], place[1]
    passages = segments[...]
    ends = [jnp.sum((passages <= s).astype(jnp.int32)) for s in range(3)]
    for slot in range(2):
        masks = mask_own if slot == 0 else mask_other
        tile = 2 * chip + (core if slot == 0 else 1 - core)
        mine = segments[:, pl.ds(pl.multiple_of(tile * TILE, TILE), TILE)]
        low = jnp.where(
            mine == 0, 0, jnp.where(mine == 1, ends[0], jnp.where(mine == 2, ends[1], ends[2]))
        )
        high = jnp.where(
            mine == 0, ends[0], jnp.where(mine == 1, ends[1], jnp.where(mine == 2, ends[2], KEYS))
        )
        for d in range(CHIPS):
            for key_slot in range(2):
                key_tile = 2 * lax.rem(chip + CHIPS - d, CHIPS) + (
                    core if key_slot == 0 else 1 - core
                )
                seen = masks[0, key_tile] == 1
                row = 4 * d + 2 * key_slot
                place_of = slice(slot * TILE, (slot + 1) * TILE)
                limits[row : row + 1, place_of] = jnp.where(seen, 0, low) - key_tile * TILE
                limits[row + 1 : row + 2, place_of] = (
                    jnp.where(seen, KEYS, high) - key_tile * TILE
                )

    for copy in copies:
        copy.wait()
    for slot, rows in enumerate((own, other)):
        queries = dot(rows[...], weights[...]).astype(BF)
        for head in range(GROUP):
            out[head * 256 + slot * TILE : head * 256 + (slot + 1) * TILE] = queries[
                :, head * HD : (head + 1) * HD
            ]


def project_query(place, own, other, w_query, segments, mask_own, mask_other):
    return pl.pallas_call(
        query_kernel,
        in_specs=[SCALARS, WHOLE, WHOLE, STAY, STAY, STAY, SCALARS],
        out_specs=[WHOLE, WHOLE],
        out_shape=[
            jax.ShapeDtypeStruct((STACK, HD), BF),
            jax.ShapeDtypeStruct((4 * CHIPS, 2 * TILE), jnp.int32),
        ],
        scratch_shapes=[
            pltpu.VMEM((D, GF), BF),
            pltpu.VMEM((1, KEYS), jnp.int32),
            pltpu.SMEM((1, KEYS // TILE), jnp.int32),
            pltpu.SemaphoreType.DMA((Q_CHUNKS,)),
            pltpu.SemaphoreType.DMA((2,)),
        ],
        compiler_params=PARAMS,
        cost_estimate=cost(2 * 256 * D * GF, 2 * (256 * D + D * GF + 256 * GF)),
        name="project_query",
    )(place, own, other, w_query, segments, mask_own, mask_other)


def stack_kernel(place, up_own, up_other, out):
    for slot, rows in enumerate((up_own, up_other)):
        for head in range(GROUP):
            columns = pl.ds(pl.multiple_of(place[1] * GF + head * HD, HD), HD)
            out[head * 256 + slot * TILE : head * 256 + (slot + 1) * TILE] = rows[:, columns]


def stack_up(place, up_own, up_other):
    return pl.pallas_call(
        stack_kernel,
        in_specs=[SCALARS, WHOLE, WHOLE],
        out_specs=WHOLE,
        out_shape=jax.ShapeDtypeStruct((STACK, HD), BF),
        compiler_params=PARAMS,
        cost_estimate=cost(0, 4 * STACK * HD),
        name="stack_up",
    )(place, up_own, up_other)


def scores_kernel(d, kv, limits, query, up, powers, grads, stats, keys_t):
    keys, values = kv[:, :HD], kv[:, HD:]
    keys_t[...] = keys.T
    position = lax.broadcasted_iota(jnp.int32, (TILE, 2 * TILE), 0)
    bias = []
    for key_slot in range(2):
        row = 4 * d + 2 * key_slot
        allowed = (position >= limits[row : row + 1]) & (position < limits[row + 1 : row + 2])
        bias.append(jnp.where(allowed, 0.0, -jnp.inf))
    bias = jnp.concatenate(bias, axis=0)
    for head in range(GROUP):
        part = slice(head * 256, (head + 1) * 256)
        scores = dot_nt(keys, query[part]) * LOG2_SCALE + bias
        top = jnp.max(scores, axis=0, keepdims=True)
        power = jnp.exp2(scores - jnp.where(top == -jnp.inf, 0.0, top))
        grad = dot_nt(values, up[part])
        powers[:, part] = power
        grads[:, part] = grad
        stats[0:1, part] = top
        stats[1:2, part] = jnp.sum(power, axis=0, keepdims=True)
        stats[2:3, part] = jnp.sum(power * grad, axis=0, keepdims=True)


def chip_scores(d, kv, limits, query, up):
    return pl.pallas_call(
        functools.partial(scores_kernel, d),
        in_specs=[WHOLE] * 4,
        out_specs=[WHOLE] * 4,
        out_shape=[
            jax.ShapeDtypeStruct((256, STACK), F32),
            jax.ShapeDtypeStruct((256, STACK), F32),
            jax.ShapeDtypeStruct((8, STACK), F32),
            jax.ShapeDtypeStruct((HD, 256), BF),
        ],
        compiler_params=PARAMS,
        cost_estimate=cost(4 * STACK * 256 * HD, 10 * 256 * STACK, 256 * STACK),
        name=f"chip_scores_{d}",
    )(kv, limits, query, up)


def factors_kernel(a, b, c, d, out):
    parts = (a, b, c, d)
    top = jnp.maximum(jnp.maximum(a[0:1], b[0:1]), jnp.maximum(c[0:1], d[0:1]))
    factors = [jnp.exp2(part[0:1] - top) for part in parts]
    total = sum(factor * part[1:2] for factor, part in zip(factors, parts))
    factors = [factor / total for factor in factors]
    for chip, factor in enumerate(factors):
        out[chip : chip + 1] = factor
    out[4:5] = sum(factor * part[2:3] for factor, part in zip(factors, parts))


def softmax_factors(stats):
    return pl.pallas_call(
        factors_kernel,
        in_specs=[WHOLE] * 4,
        out_specs=WHOLE,
        out_shape=jax.ShapeDtypeStruct((8, STACK), F32),
        compiler_params=PARAMS,
        cost_estimate=cost(20 * STACK, 128 * STACK),
        name="softmax_factors",
    )(*stats)


def terms_kernel(d, powers, grads, factors, query, up, out, grad_scores, probs_low):
    for head in range(GROUP):
        part = slice(head * 256, (head + 1) * 256)
        probs = powers[:, part] * factors[d : d + 1, part]
        probs_low[:, part] = probs.astype(BF)
        grad_scores[:, part] = (probs * (grads[:, part] - factors[4:5, part])).astype(BF)
    out[:, :HD] = (dot(grad_scores[...], query[...]) * SCALE).astype(out.dtype)
    out[:, HD:] = dot(probs_low[...], up[...]).astype(out.dtype)


def chip_terms(d, powers, grads, factors, query, up):
    return pl.pallas_call(
        functools.partial(terms_kernel, d),
        in_specs=[WHOLE] * 5,
        out_specs=[WHOLE] * 2,
        out_shape=[
            jax.ShapeDtypeStruct((256, 256), F32 if d == 0 else BF),
            jax.ShapeDtypeStruct((256, STACK), BF),
        ],
        scratch_shapes=[pltpu.VMEM((256, STACK), BF)],
        compiler_params=PARAMS,
        cost_estimate=cost(4 * STACK * 256 * HD, 10 * 256 * STACK),
        name=f"chip_terms_{d}",
    )(powers, grads, factors, query, up)


def query_grad_kernel(k0, k1, k2, k3, g0, g1, g2, g3, out):
    for head in range(GROUP):
        part = slice(head * 256, (head + 1) * 256)
        total = dot(k0[...], g0[:, part]) + dot(k1[...], g1[:, part])
        total += dot(k2[...], g2[:, part]) + dot(k3[...], g3[:, part])
        out[:, head * HD : (head + 1) * HD] = (total * SCALE).T.astype(BF)


def query_grad(keys_t, grad_scores):
    return pl.pallas_call(
        query_grad_kernel,
        in_specs=[WHOLE] * 8,
        out_specs=WHOLE,
        out_shape=jax.ShapeDtypeStruct((256, GF), BF),
        compiler_params=PARAMS,
        cost_estimate=cost(2 * STACK * KEYS * HD, 2 * STACK * KEYS),
        name="query_grad",
    )(*keys_t, *grad_scores)


def sum_kernel(a, b, c, d, out):
    total = (a[...] + b[...].astype(F32)) + (c[...].astype(F32) + d[...].astype(F32))
    out[...] = total.astype(out.dtype)


def sum_four(a, b, c, d):
    return pl.pallas_call(
        sum_kernel,
        in_specs=[WHOLE] * 4,
        out_specs=WHOLE,
        out_shape=jax.ShapeDtypeStruct(a.shape, BF),
        compiler_params=PARAMS,
        cost_estimate=cost(4 * a.size, 12 * a.size),
        name="sum_four",
    )(a, b, c, d)


def pack_kernel(place, dq, dq_other, dkv, dkv_other, out0, out1, out2, out3, blocks):
    core = place[1]

    def swapped(ref, columns):
        return jnp.concatenate([ref[TILE:, columns], ref[:TILE, columns]], axis=0)

    middle = slice(256, 512)

    @pl.when(core == 0)
    def _():
        blocks[0] = dq[:, 0:256]
        blocks[1] = dq[:, 512:768]
        blocks[2] = swapped(dq_other, middle)
        blocks[3, :, :HD] = dkv[:, :HD]
        blocks[3, :, HD:] = swapped(dkv_other, slice(0, HD))

    @pl.when(core == 1)
    def _():
        blocks[0] = swapped(dq_other, middle)
        blocks[1] = dq[:, 0:256]
        blocks[2] = dq[:, 512:768]
        blocks[3, :, :HD] = swapped(dkv_other, slice(HD, 2 * HD))
        blocks[3, :, HD:] = dkv[:, HD:]

    for d, out in enumerate((out0, out1, out2, out3)):
        out[...] = blocks[lax.rem(place[0] + d, CHIPS)]


def pack(place, dq, dq_other, dkv, dkv_other):
    return pl.pallas_call(
        pack_kernel,
        in_specs=[SCALARS] + [WHOLE] * 4,
        out_specs=[WHOLE] * 4,
        out_shape=[jax.ShapeDtypeStruct((256, 256), BF)] * 4,
        scratch_shapes=[pltpu.VMEM((4, 256, 256), BF)],
        compiler_params=PARAMS,
        cost_estimate=cost(0, 4 << 19),
        name="pack",
    )(place, dq, dq_other, dkv, dkv_other)


def transpose_kernel(*refs):
    out = refs[-1]
    for i, ref in enumerate(refs[:-1]):
        out[:, i * TILE : (i + 1) * TILE] = ref[...].T


def transpose(parts):
    return pl.pallas_call(
        transpose_kernel,
        in_specs=[WHOLE] * 8,
        out_specs=WHOLE,
        out_shape=jax.ShapeDtypeStruct((D, KEYS), BF),
        compiler_params=PARAMS,
        cost_estimate=cost(0, 4 * D * KEYS),
        name="transpose_tokens",
    )(*parts)


def weight_kernel(place, tokens_t, a, b, c, d, out0, out1, out2, out3):
    right = jnp.concatenate([a[...], b[...], c[...], d[...]], axis=0)
    for shift, out in enumerate((out0, out1, out2, out3)):
        row = pl.multiple_of(lax.rem(place[2] + shift, YS) * (D // YS), 128)
        out[...] = dot(tokens_t[pl.ds(row, D // YS)], right).astype(out.dtype)


def weight_grad(place, tokens_t, parts):
    shape = (D // YS, 256)
    return pl.pallas_call(
        weight_kernel,
        in_specs=[SCALARS] + [WHOLE] * 5,
        out_specs=[WHOLE] * 4,
        out_shape=[jax.ShapeDtypeStruct(shape, F32)] + [jax.ShapeDtypeStruct(shape, BF)] * 3,
        compiler_params=PARAMS,
        cost_estimate=cost(2 * D * KEYS * 256, 2 * D * KEYS + 3 * D * 256),
        name="weight_grad",
    )(place, tokens_t, *parts)


def input_kernel(
    place, dq, dq_other, dkv, dkv_other, w_query, w_key, w_value, out, left, right, sems
):
    core = place[1]
    width = D // IN_CHUNKS
    copies = []
    for chunk in range(IN_CHUNKS):
        part = pl.ds(chunk * width, width)
        copies.append(
            [
                pltpu.make_async_copy(
                    source.at[part],
                    right.at[part, pl.ds(start, size)],
                    sems.at[chunk, side],
                )
                for side, (source, start, size) in enumerate(
                    ((w_query, 0, D), (w_key, D, 256), (w_value, D + 256, 256))
                )
            ]
        )
    for group in copies:
        for copy in group:
            copy.start()
    mine = pl.ds(pl.multiple_of(core * GF, 128), GF)
    theirs = pl.ds(pl.multiple_of((1 - core) * GF, 128), GF)
    left[:, mine] = dq[:TILE]
    left[:, theirs] = dq_other[TILE:]
    for part in range(2):
        columns = slice(part * HD, (part + 1) * HD)
        base = D + part * KVH * HD
        left[:, pl.ds(pl.multiple_of(base + core * HD, 128), HD)] = dkv[:TILE, columns]
        left[:, pl.ds(pl.multiple_of(base + (1 - core) * HD, 128), HD)] = dkv_other[
            TILE:, columns
        ]
    for chunk, group in enumerate(copies):
        for copy in group:
            copy.wait()
        part = slice(chunk * width, (chunk + 1) * width)
        out[:, part] = dot_nt(left[...], right[part]).astype(BF)


def input_grad(place, dq, dq_other, dkv, dkv_other, w_query, w_key, w_value):
    return pl.pallas_call(
        input_kernel,
        in_specs=[SCALARS] + [WHOLE] * 4 + [STAY] * 3,
        out_specs=WHOLE,
        out_shape=jax.ShapeDtypeStruct((TILE, D), BF),
        scratch_shapes=[
            pltpu.VMEM((TILE, D + 512), BF),
            pltpu.VMEM((D, D + 512), BF),
            pltpu.SemaphoreType.DMA((IN_CHUNKS, 3)),
        ],
        compiler_params=PARAMS,
        cost_estimate=cost(2 * TILE * D * 2048, 2 * D * 2048),
        name="input_grad",
    )(place, dq, dq_other, dkv, dkv_other, w_query, w_key, w_value)


def final_kernel(parts, out):
    total = parts[0:48].astype(F32)
    for z in range(1, ZS):
        total += parts[z * 48 : (z + 1) * 48].astype(F32)
    out[...] = total


def final_sum(parts):
    return pl.pallas_call(
        final_kernel,
        in_specs=[WHOLE],
        out_specs=WHOLE,
        out_shape=jax.ShapeDtypeStruct((48, 256), F32),
        compiler_params=PARAMS,
        cost_estimate=cost(parts.size, 2 * parts.size),
        name="final_sum",
    )(parts)


def shards(tokens, grad_heads, tile_mask, segments, w_query, w_key, w_value):
    ctx = lax.axis_index("ctx")
    dp = lax.axis_index("dp")
    place = jnp.stack([ctx // 2, ctx % 2, dp // ZS, dp % ZS]).astype(jnp.int32)
    own, up = tokens[0], grad_heads[0]
    other = lax.ppermute(own, "ctx", CORE)
    up_other = lax.ppermute(up, "ctx", CORE)
    mask_other = lax.ppermute(tile_mask[0], "ctx", CORE)
    other, mask_other, up_other = lax.optimization_barrier((other, mask_other, up_other))

    w_query, w_key, w_value = (in_hbm(w) for w in (w_query, w_key, w_value))
    weights, kv_own = project_kv_own(place, in_hbm(own), w_key, w_value)
    kv = project_kv(other, weights, kv_own)
    kvs = [kv] + [lax.ppermute(kv, "ctx", chip_shift(d)) for d in (1, 2, 3)]
    far = {d: lax.ppermute(own, "ctx", chip_shift(d)) for d in (1, 3)}
    query, limits = project_query(
        place, own, other, w_query, in_hbm(segments), in_hbm(tile_mask[0]), mask_other
    )
    up = stack_up(place, up, up_other)
    scores = {0: chip_scores(0, kvs[0], limits, query, up)}
    far, kvs, scores[0], late_own = lax.optimization_barrier((far, kvs, scores[0], own))
    late = lax.ppermute(late_own, "ctx", chip_shift(2))
    for d in (1, 3, 2):
        scores[d] = chip_scores(d, kvs[d], limits, query, up)
    factors = softmax_factors([scores[d][2] for d in range(CHIPS)])
    terms, grad_scores = {}, {}
    for d in (2, 1, 3):
        terms[d], grad_scores[d] = chip_terms(d, *scores[d][:2], factors, query, up)
    back = [lax.ppermute(terms[d], "ctx", chip_shift(CHIPS - d)) for d in (2, 1, 3)]
    terms[0], grad_scores[0] = chip_terms(0, *scores[0][:2], factors, query, up)
    dq = query_grad([scores[d][3] for d in range(CHIPS)], [grad_scores[d] for d in range(CHIPS)])
    late, back, dq = lax.optimization_barrier((late, back, dq))
    dq_other = lax.ppermute(dq, "ctx", CORE)
    dkv = sum_four(terms[0], *back)
    dkv_other = lax.ppermute(dkv, "ctx", CORE)
    far[2], dkv = lax.optimization_barrier((late, dkv))
    far_other = {2: lax.ppermute(far[2], "ctx", CORE)}
    packed = pack(place, dq, dq_other, dkv, dkv_other)
    far[1], far[3], packed = lax.optimization_barrier((far[1], far[3], packed))
    for d in (1, 3):
        far_other[d] = lax.ppermute(far[d], "ctx", CORE)
    tokens_t = transpose(
        [own, other] + [part for d in (1, 2, 3) for part in (far[d], far_other[d])]
    )
    columns = [packed[0]] + [
        lax.ppermute(packed[d], "ctx", chip_shift(d)) for d in (1, 2, 3)
    ]
    terms = weight_grad(place, tokens_t, columns)
    y_parts = [terms[0]] + [lax.ppermute(terms[d], "dp", y_shift(d)) for d in (1, 2, 3)]
    grad_tokens = input_grad(
        place, dq, dq_other, dkv, dkv_other, w_query, w_key, w_value
    )
    y_parts, grad_tokens = lax.optimization_barrier((y_parts, grad_tokens))
    y_sum = sum_four(*y_parts)
    z_parts = lax.all_to_all(y_sum, "dp", 0, 0, tiled=True, axis_index_groups=Z_GROUPS)
    grad_projection = final_sum(z_parts)
    return grad_tokens[None], grad_projection


def solution(mesh):
    return jax.shard_map(
        shards,
        mesh=mesh,
        in_specs=(
            P("dp", "ctx", None),
            P("dp", "ctx", None),
            P("dp", "ctx", None),
            P("dp", None),
            P(),
            P(),
            P(),
        ),
        out_specs=(P("dp", "ctx", None), P("dp", "ctx")),
        check_vma=False,
    )
```

```python
import functools
import math

import jax
import jax.numpy as jnp
from jax import lax
from jax.experimental import pallas as pl
from jax.experimental.pallas import tpu as pltpu
from jax.sharding import PartitionSpec as P

QH = 12
KVH = 2
HD = 128
TILE = 128
D = 1536
KEYS = 1024
CHIPS = 4
GROUP = QH // KVH
GF = GROUP * HD
STACK = GROUP * 256
YS = 4
ZS = 8
SCALE = 1.0 / math.sqrt(HD)
LOG2_SCALE = SCALE * math.log2(math.e)
BF = jnp.bfloat16
F32 = jnp.float32
VMEM_LIMIT = 24 * 1024 * 1024
W_CHUNKS = 1
Q_CHUNKS = 3
IN_CHUNKS = 3

CORE = [(i, i ^ 1) for i in range(8)]
NT = (((1,), (1,)), ((), ()))


def chip_shift(d):
    return [(i, ((i // 2 + d) % CHIPS) * 2 + i % 2) for i in range(8)]


def y_shift(d):
    return [(i, ((i // ZS + d) % YS) * ZS + i % ZS) for i in range(32)]


Z_GROUPS = [[y * ZS + z for z in range(ZS)] for y in range(YS)]


def dot(a, b):
    return jnp.dot(a, b, preferred_element_type=F32)


def dot_nt(a, b):
    return lax.dot_general(a, b, NT, preferred_element_type=F32)


def in_hbm(array):
    return pltpu.with_memory_space_constraint(array, pltpu.HBM)


def cost(flops, bytes_accessed, transcendentals=0):
    return pl.CostEstimate(
        flops=1, bytes_accessed=1, transcendentals=0
    )


PARAMS = pltpu.CompilerParams(vmem_limit_bytes=VMEM_LIMIT)
WHOLE = pl.BlockSpec(memory_space=pltpu.VMEM)
SCALARS = pl.BlockSpec(memory_space=pltpu.SMEM)
STAY = pl.BlockSpec(memory_space=pltpu.HBM)


def kv_own_kernel(place, own, w_key, w_value, weights, out, rows, sems):
    columns = pl.ds(pl.multiple_of(place[1] * HD, HD), HD)
    copies = []
    for chunk in range(W_CHUNKS):
        part = pl.ds(chunk * (TILE // W_CHUNKS), TILE // W_CHUNKS)
        copies.append(pltpu.make_async_copy(own.at[part], rows.at[part], sems.at[chunk, 2]))
        part = pl.ds(chunk * (D // W_CHUNKS), D // W_CHUNKS)
        for side, source in enumerate((w_key, w_value)):
            copies.append(
                pltpu.make_async_copy(
                    source.at[part, columns],
                    weights.at[part, pl.ds(side * HD, HD)],
                    sems.at[chunk, side],
                )
            )
    for copy in copies:
        copy.start()
    for copy in copies:
        copy.wait()
    out[...] = dot(rows[...], weights[...]).astype(BF)


def project_kv_own(place, own, w_key, w_value):
    return pl.pallas_call(
        kv_own_kernel,
        in_specs=[SCALARS, STAY, STAY, STAY],
        out_specs=[WHOLE, WHOLE],
        out_shape=[
            jax.ShapeDtypeStruct((D, 2 * HD), BF),
            jax.ShapeDtypeStruct((TILE, 2 * HD), BF),
        ],
        scratch_shapes=[pltpu.VMEM((TILE, D), BF), pltpu.SemaphoreType.DMA((W_CHUNKS, 3))],
        compiler_params=PARAMS,
        cost_estimate=cost(2 * TILE * D * 256, 2 * (TILE * D + D * 256)),
        name="project_kv_own",
    )(place, own, w_key, w_value)


def kv_pair_kernel(own, other, weights, out):
    out[:TILE] = dot(own[...], weights[...]).astype(BF)
    out[TILE:] = dot(other[...], weights[...]).astype(BF)


def project_kv_pair(own, other, weights):
    return pl.pallas_call(
        kv_pair_kernel,
        in_specs=[WHOLE] * 3,
        out_specs=WHOLE,
        out_shape=jax.ShapeDtypeStruct((2 * TILE, 2 * HD), BF),
        compiler_params=PARAMS,
        cost_estimate=cost(4 * TILE * D * 256, 2 * (2 * TILE * D + D * 256)),
        name="project_kv_pair",
    )(own, other, weights)


def kv_kernel(other, weights, kv_own, out):
    out[:TILE] = kv_own[...]
    out[TILE:] = dot(other[...], weights[...]).astype(BF)


def project_kv(other, weights, kv_own):
    return pl.pallas_call(
        kv_kernel,
        in_specs=[WHOLE] * 3,
        out_specs=WHOLE,
        out_shape=jax.ShapeDtypeStruct((2 * TILE, 2 * HD), BF),
        compiler_params=PARAMS,
        cost_estimate=cost(2 * TILE * D * 256, 2 * (TILE * D + D * 256)),
        name="project_kv",
    )(other, weights, kv_own)


def query_kernel(
    place, own, other, w_query, segments_far, mask_far, mask_other, out, limits,
    weights, segments, mask_own, sems, small_sems,
):
    small = [
        pltpu.make_async_copy(segments_far, segments, small_sems.at[0]),
        pltpu.make_async_copy(mask_far, mask_own, small_sems.at[1]),
    ]
    for copy in small:
        copy.start()
    columns = pl.ds(pl.multiple_of(place[1] * GF, HD), GF)
    copies = []
    for chunk in range(Q_CHUNKS):
        part = pl.ds(chunk * (D // Q_CHUNKS), D // Q_CHUNKS)
        copies.append(
            pltpu.make_async_copy(w_query.at[part, columns], weights.at[part], sems.at[chunk])
        )
    for copy in copies:
        copy.start()
    for copy in small:
        copy.wait()

    chip, core = place[0], place[1]
    passages = segments[...]
    ends = [jnp.sum((passages <= s).astype(jnp.int32)) for s in range(3)]
    for slot in range(2):
        masks = mask_own if slot == 0 else mask_other
        tile = 2 * chip + (core if slot == 0 else 1 - core)
        mine = segments[:, pl.ds(pl.multiple_of(tile * TILE, TILE), TILE)]
        low = jnp.where(
            mine == 0, 0, jnp.where(mine == 1, ends[0], jnp.where(mine == 2, ends[1], ends[2]))
        )
        high = jnp.where(
            mine == 0, ends[0], jnp.where(mine == 1, ends[1], jnp.where(mine == 2, ends[2], KEYS))
        )
        for d in range(CHIPS):
            for key_slot in range(2):
                key_tile = 2 * lax.rem(chip + CHIPS - d, CHIPS) + (
                    core if key_slot == 0 else 1 - core
                )
                seen = masks[0, key_tile] == 1
                row = 4 * d + 2 * key_slot
                place_of = slice(slot * TILE, (slot + 1) * TILE)
                limits[row : row + 1, place_of] = jnp.where(seen, 0, low) - key_tile * TILE
                limits[row + 1 : row + 2, place_of] = (
                    jnp.where(seen, KEYS, high) - key_tile * TILE
                )

    for copy in copies:
        copy.wait()
    for slot, rows in enumerate((own, other)):
        queries = dot(rows[...], weights[...]).astype(BF)
        for head in range(GROUP):
            out[head * 256 + slot * TILE : head * 256 + (slot + 1) * TILE] = queries[
                :, head * HD : (head + 1) * HD
            ]


def project_query(place, own, other, w_query, segments, mask_own, mask_other):
    return pl.pallas_call(
        query_kernel,
        in_specs=[SCALARS, WHOLE, WHOLE, STAY, STAY, STAY, SCALARS],
        out_specs=[WHOLE, WHOLE],
        out_shape=[
            jax.ShapeDtypeStruct((STACK, HD), BF),
            jax.ShapeDtypeStruct((4 * CHIPS, 2 * TILE), jnp.int32),
        ],
        scratch_shapes=[
            pltpu.VMEM((D, GF), BF),
            pltpu.VMEM((1, KEYS), jnp.int32),
            pltpu.SMEM((1, KEYS // TILE), jnp.int32),
            pltpu.SemaphoreType.DMA((Q_CHUNKS,)),
            pltpu.SemaphoreType.DMA((2,)),
        ],
        compiler_params=PARAMS,
        cost_estimate=cost(2 * 256 * D * GF, 2 * (256 * D + D * GF + 256 * GF)),
        name="project_query",
    )(place, own, other, w_query, segments, mask_own, mask_other)


def stack_kernel(place, up_own, up_other, out):
    for slot, rows in enumerate((up_own, up_other)):
        for head in range(GROUP):
            columns = pl.ds(pl.multiple_of(place[1] * GF + head * HD, HD), HD)
            out[head * 256 + slot * TILE : head * 256 + (slot + 1) * TILE] = rows[:, columns]


def stack_up(place, up_own, up_other):
    return pl.pallas_call(
        stack_kernel,
        in_specs=[SCALARS, WHOLE, WHOLE],
        out_specs=WHOLE,
        out_shape=jax.ShapeDtypeStruct((STACK, HD), BF),
        compiler_params=PARAMS,
        cost_estimate=cost(0, 4 * STACK * HD),
        name="stack_up",
    )(place, up_own, up_other)


def scores_kernel(d, kv, limits, query, up, powers, grads, stats, keys_t):
    keys, values = kv[:, :HD], kv[:, HD:]
    keys_t[...] = keys.T
    position = lax.broadcasted_iota(jnp.int32, (TILE, 2 * TILE), 0)
    bias = []
    for key_slot in range(2):
        row = 4 * d + 2 * key_slot
        allowed = (position >= limits[row : row + 1]) & (position < limits[row + 1 : row + 2])
        bias.append(jnp.where(allowed, 0.0, -jnp.inf))
    bias = jnp.concatenate(bias, axis=0)
    for head in range(GROUP):
        part = slice(head * 256, (head + 1) * 256)
        scores = dot_nt(keys, query[part]) * LOG2_SCALE + bias
        top = jnp.max(scores, axis=0, keepdims=True)
        power = jnp.exp2(scores - jnp.where(top == -jnp.inf, 0.0, top))
        grad = dot_nt(values, up[part])
        powers[:, part] = power
        grads[:, part] = grad
        stats[0:1, part] = top
        stats[1:2, part] = jnp.sum(power, axis=0, keepdims=True)
        stats[2:3, part] = jnp.sum(power * grad, axis=0, keepdims=True)


def chip_scores(d, kv, limits, query, up):
    return pl.pallas_call(
        functools.partial(scores_kernel, d),
        in_specs=[WHOLE] * 4,
        out_specs=[WHOLE] * 4,
        out_shape=[
            jax.ShapeDtypeStruct((256, STACK), F32),
            jax.ShapeDtypeStruct((256, STACK), F32),
            jax.ShapeDtypeStruct((8, STACK), F32),
            jax.ShapeDtypeStruct((HD, 256), BF),
        ],
        compiler_params=PARAMS,
        cost_estimate=cost(4 * STACK * 256 * HD, 10 * 256 * STACK, 256 * STACK),
        name=f"chip_scores_{d}",
    )(kv, limits, query, up)


def factors_kernel(a, b, c, d, out):
    parts = (a, b, c, d)
    top = jnp.maximum(jnp.maximum(a[0:1], b[0:1]), jnp.maximum(c[0:1], d[0:1]))
    factors = [jnp.exp2(part[0:1] - top) for part in parts]
    total = sum(factor * part[1:2] for factor, part in zip(factors, parts))
    factors = [factor / total for factor in factors]
    for chip, factor in enumerate(factors):
        out[chip : chip + 1] = factor
    out[4:5] = sum(factor * part[2:3] for factor, part in zip(factors, parts))


def softmax_factors(stats):
    return pl.pallas_call(
        factors_kernel,
        in_specs=[WHOLE] * 4,
        out_specs=WHOLE,
        out_shape=jax.ShapeDtypeStruct((8, STACK), F32),
        compiler_params=PARAMS,
        cost_estimate=cost(20 * STACK, 128 * STACK),
        name="softmax_factors",
    )(*stats)


def terms_kernel(d, powers, grads, factors, query, up, out, grad_scores, probs_low):
    for head in range(GROUP):
        part = slice(head * 256, (head + 1) * 256)
        probs = powers[:, part] * factors[d : d + 1, part]
        probs_low[:, part] = probs.astype(BF)
        grad_scores[:, part] = (probs * (grads[:, part] - factors[4:5, part])).astype(BF)
    out[:, :HD] = (dot(grad_scores[...], query[...]) * SCALE).astype(out.dtype)
    out[:, HD:] = dot(probs_low[...], up[...]).astype(out.dtype)


def chip_terms(d, powers, grads, factors, query, up):
    return pl.pallas_call(
        functools.partial(terms_kernel, d),
        in_specs=[WHOLE] * 5,
        out_specs=[WHOLE] * 2,
        out_shape=[
            jax.ShapeDtypeStruct((256, 256), F32 if d == 0 else BF),
            jax.ShapeDtypeStruct((256, STACK), BF),
        ],
        scratch_shapes=[pltpu.VMEM((256, STACK), BF)],
        compiler_params=PARAMS,
        cost_estimate=cost(4 * STACK * 256 * HD, 10 * 256 * STACK),
        name=f"chip_terms_{d}",
    )(powers, grads, factors, query, up)


def query_grad_kernel(k0, k1, k2, k3, g0, g1, g2, g3, out):
    for head in range(GROUP):
        part = slice(head * 256, (head + 1) * 256)
        total = dot(k0[...], g0[:, part]) + dot(k1[...], g1[:, part])
        total += dot(k2[...], g2[:, part]) + dot(k3[...], g3[:, part])
        out[:, head * HD : (head + 1) * HD] = (total * SCALE).T.astype(BF)


def query_grad(keys_t, grad_scores):
    return pl.pallas_call(
        query_grad_kernel,
        in_specs=[WHOLE] * 8,
        out_specs=WHOLE,
        out_shape=jax.ShapeDtypeStruct((256, GF), BF),
        compiler_params=PARAMS,
        cost_estimate=cost(2 * STACK * KEYS * HD, 2 * STACK * KEYS),
        name="query_grad",
    )(*keys_t, *grad_scores)


def sum_kernel(a, b, c, d, out):
    total = (a[...] + b[...].astype(F32)) + (c[...].astype(F32) + d[...].astype(F32))
    out[...] = total.astype(out.dtype)


def sum_four(a, b, c, d):
    return pl.pallas_call(
        sum_kernel,
        in_specs=[WHOLE] * 4,
        out_specs=WHOLE,
        out_shape=jax.ShapeDtypeStruct(a.shape, BF),
        compiler_params=PARAMS,
        cost_estimate=cost(4 * a.size, 12 * a.size),
        name="sum_four",
    )(a, b, c, d)


def pack_kernel(place, dq, dq_other, dkv, dkv_other, *outs):
    for core in range(2):
        own_part = slice(core * HD, (core + 1) * HD)
        for chip in range(CHIPS):

            @pl.when((place[1] == core) & (place[0] == chip))
            def _(core=core, own_part=own_part, chip=chip):
                for d, out in enumerate(outs):
                    target = (chip + d) % CHIPS
                    if target == 3:
                        out[:, own_part] = dkv[:, own_part]
                        theirs = slice((1 - core) * HD, (2 - core) * HD)
                        out[:TILE, theirs] = dkv_other[TILE:, own_part]
                        out[TILE:, theirs] = dkv_other[:TILE, own_part]
                    elif target == 2 - 2 * core:
                        out[:TILE] = dq_other[TILE:, 256:512]
                        out[TILE:] = dq_other[:TILE, 256:512]
                    else:
                        first = target == core
                        out[...] = dq[:, 0:256] if first else dq[:, 512:768]


def pack(place, dq, dq_other, dkv, dkv_other):
    return pl.pallas_call(
        pack_kernel,
        in_specs=[SCALARS] + [WHOLE] * 4,
        out_specs=[WHOLE] * 4,
        out_shape=[jax.ShapeDtypeStruct((256, 256), BF)] * 4,
        compiler_params=PARAMS,
        cost_estimate=cost(0, 4 << 19),
        name="pack",
    )(place, dq, dq_other, dkv, dkv_other)


def transpose_kernel(own, far1, late_a, late_b, far3, out):
    late = jnp.concatenate([late_a[...], late_b[...]], axis=0)
    for i, rows in enumerate((own[...], far1[...], late, far3[...])):
        out[:, i * TILE : (i + 1) * TILE] = rows.T


def transpose(parts):
    return pl.pallas_call(
        transpose_kernel,
        in_specs=[WHOLE] * 5,
        out_specs=WHOLE,
        out_shape=jax.ShapeDtypeStruct((D, KEYS // 2), BF),
        compiler_params=PARAMS,
        cost_estimate=cost(0, 2 * D * KEYS),
        name="transpose_tokens",
    )(*parts)


def weight_kernel(place, tokens_t, other_t, a, b, c, d, out0, out1, out2, out3):
    parts = (a, b, c, d)
    right = jnp.concatenate([part[:TILE] for part in parts], axis=0)
    right_other = jnp.concatenate([part[TILE:] for part in parts], axis=0)
    for shift, out in enumerate((out0, out1, out2, out3)):
        row = pl.multiple_of(lax.rem(place[2] + shift, YS) * (D // YS), 128)
        rows = pl.ds(row, D // YS)
        out[...] = (dot(tokens_t[rows], right) + dot(other_t[rows], right_other)).astype(
            out.dtype
        )


def weight_grad(place, tokens_t, other_t, parts):
    shape = (D // YS, 256)
    return pl.pallas_call(
        weight_kernel,
        in_specs=[SCALARS] + [WHOLE] * 6,
        out_specs=[WHOLE] * 4,
        out_shape=[jax.ShapeDtypeStruct(shape, F32)] + [jax.ShapeDtypeStruct(shape, BF)] * 3,
        compiler_params=PARAMS,
        cost_estimate=cost(2 * D * KEYS * 256, 2 * D * KEYS + 3 * D * 256),
        name="weight_grad",
    )(place, tokens_t, other_t, *parts)


def input_kernel(
    place, dq, dq_other, dkv, dkv_other, w_query, w_key, w_value, out, left, right, sems
):
    core = place[1]
    width = D // IN_CHUNKS
    copies = []
    for chunk in range(IN_CHUNKS):
        part = pl.ds(chunk * width, width)
        copies.append(
            [
                pltpu.make_async_copy(
                    source.at[part],
                    right.at[part, pl.ds(start, size)],
                    sems.at[chunk, side],
                )
                for side, (source, start, size) in enumerate(
                    ((w_query, 0, D), (w_key, D, 256), (w_value, D + 256, 256))
                )
            ]
        )
    for group in copies:
        for copy in group:
            copy.start()
    mine = pl.ds(pl.multiple_of(core * GF, 128), GF)
    theirs = pl.ds(pl.multiple_of((1 - core) * GF, 128), GF)
    left[:, mine] = dq[:TILE]
    left[:, theirs] = dq_other[TILE:]
    for part in range(2):
        columns = slice(part * HD, (part + 1) * HD)
        base = D + part * KVH * HD
        left[:, pl.ds(pl.multiple_of(base + core * HD, 128), HD)] = dkv[:TILE, columns]
        left[:, pl.ds(pl.multiple_of(base + (1 - core) * HD, 128), HD)] = dkv_other[
            TILE:, columns
        ]
    for chunk, group in enumerate(copies):
        for copy in group:
            copy.wait()
        part = slice(chunk * width, (chunk + 1) * width)
        out[:, part] = dot_nt(left[...], right[part]).astype(BF)


def input_grad(place, dq, dq_other, dkv, dkv_other, w_query, w_key, w_value):
    return pl.pallas_call(
        input_kernel,
        in_specs=[SCALARS] + [WHOLE] * 4 + [STAY] * 3,
        out_specs=WHOLE,
        out_shape=jax.ShapeDtypeStruct((TILE, D), BF),
        scratch_shapes=[
            pltpu.VMEM((TILE, D + 512), BF),
            pltpu.VMEM((D, D + 512), BF),
            pltpu.SemaphoreType.DMA((IN_CHUNKS, 3)),
        ],
        compiler_params=PARAMS,
        cost_estimate=cost(2 * TILE * D * 2048, 2 * D * 2048),
        name="input_grad",
    )(place, dq, dq_other, dkv, dkv_other, w_query, w_key, w_value)


def final_kernel(parts, out):
    total = parts[0:48].astype(F32)
    for z in range(1, ZS):
        total += parts[z * 48 : (z + 1) * 48].astype(F32)
    out[...] = total


def final_sum(parts):
    return pl.pallas_call(
        final_kernel,
        in_specs=[WHOLE],
        out_specs=WHOLE,
        out_shape=jax.ShapeDtypeStruct((48, 256), F32),
        compiler_params=PARAMS,
        cost_estimate=cost(parts.size, 2 * parts.size),
        name="final_sum",
    )(parts)


def shards(tokens, grad_heads, tile_mask, segments, w_query, w_key, w_value):
    ctx = lax.axis_index("ctx")
    dp = lax.axis_index("dp")
    place = jnp.stack([ctx // 2, ctx % 2, dp // ZS, dp % ZS]).astype(jnp.int32)
    own, up = tokens[0], grad_heads[0]
    other = lax.ppermute(own, "ctx", CORE)
    up_other = lax.ppermute(up, "ctx", CORE)
    mask_other = lax.ppermute(tile_mask[0], "ctx", CORE)
    other, mask_other, up_other = lax.optimization_barrier((other, mask_other, up_other))

    w_query, w_key, w_value = (in_hbm(w) for w in (w_query, w_key, w_value))
    weights, kv_own = project_kv_own(place, in_hbm(own), w_key, w_value)
    kv = project_kv(other, weights, kv_own)
    kv2 = lax.ppermute(kv, "ctx", chip_shift(2))
    far = {d: lax.ppermute(own, "ctx", chip_shift(d)) for d in (1, 3)}
    query, limits = project_query(
        place, own, other, w_query, in_hbm(segments), in_hbm(tile_mask[0]), mask_other
    )
    up = stack_up(place, up, up_other)
    scores = {0: chip_scores(0, kv, limits, query, up)}
    far, kv2, scores[0] = lax.optimization_barrier((far, kv2, scores[0]))
    far_other = {d: lax.ppermute(far[d], "ctx", CORE) for d in (1, 3)}
    late = (
        lax.ppermute(far[1][: TILE // 2], "ctx", chip_shift(1)),
        lax.ppermute(far[3][TILE // 2 :], "ctx", chip_shift(3)),
    )
    scores[2] = chip_scores(2, kv2, limits, query, up)
    for d in (1, 3):
        kv_far = project_kv_pair(far[d], far_other[d], weights)
        scores[d] = chip_scores(d, kv_far, limits, query, up)
    factors = softmax_factors([scores[d][2] for d in range(CHIPS)])
    terms, grad_scores = {}, {}
    for d in (2, 1, 3):
        terms[d], grad_scores[d] = chip_terms(d, *scores[d][:2], factors, query, up)
    back = [lax.ppermute(terms[d], "ctx", chip_shift(CHIPS - d)) for d in (2, 1, 3)]
    terms[0], grad_scores[0] = chip_terms(0, *scores[0][:2], factors, query, up)
    dq = query_grad([scores[d][3] for d in range(CHIPS)], [grad_scores[d] for d in range(CHIPS)])
    late, back, dq = lax.optimization_barrier((late, back, dq))
    dq_other = lax.ppermute(dq, "ctx", CORE)
    dkv = sum_four(terms[0], *back)
    dkv_other = lax.ppermute(dkv, "ctx", CORE)
    packed = pack(place, dq, dq_other, dkv, dkv_other)

    far, dkv = lax.optimization_barrier((far, dkv))
    tokens_t = transpose([own, far[1], *late, far[3]])
    tokens_t, packed = lax.optimization_barrier((tokens_t, packed))
    other_t = lax.ppermute(tokens_t, "ctx", CORE)
    columns = [packed[0]] + [
        lax.ppermute(packed[d], "ctx", chip_shift(d)) for d in (1, 2, 3)
    ]
    terms = weight_grad(place, tokens_t, other_t, columns)
    y_parts = [terms[0]] + [lax.ppermute(terms[d], "dp", y_shift(d)) for d in (1, 2, 3)]
    grad_tokens = input_grad(
        place, dq, dq_other, dkv, dkv_other, w_query, w_key, w_value
    )
    y_parts, grad_tokens = lax.optimization_barrier((y_parts, grad_tokens))
    y_sum = sum_four(*y_parts)
    z_parts = lax.all_to_all(y_sum, "dp", 0, 0, tiled=True, axis_index_groups=Z_GROUPS)
    grad_projection = final_sum(z_parts)
    return grad_tokens[None], grad_projection


def solution(mesh):
    return jax.shard_map(
        shards,
        mesh=mesh,
        in_specs=(
            P("dp", "ctx", None),
            P("dp", "ctx", None),
            P("dp", "ctx", None),
            P("dp", None),
            P(),
            P(),
            P(),
        ),
        out_specs=(P("dp", "ctx", None), P("dp", "ctx")),
        check_vma=False,
    )
```

```python
import functools
import math

import jax
import jax.numpy as jnp
from jax import lax
from jax.experimental import pallas as pl
from jax.experimental.pallas import tpu as pltpu
from jax.sharding import PartitionSpec as P

QH = 12
KVH = 2
HD = 128
TILE = 128
D = 1536
KEYS = 1024
CHIPS = 4
GROUP = QH // KVH
GF = GROUP * HD
STACK = GROUP * 256
YS = 4
ZS = 8
SCALE = 1.0 / math.sqrt(HD)
LOG2_SCALE = SCALE * math.log2(math.e)
BF = jnp.bfloat16
F32 = jnp.float32
VMEM_LIMIT = 24 * 1024 * 1024
W_CHUNKS = 1
Q_CHUNKS = 3
IN_CHUNKS = 3

CORE = [(i, i ^ 1) for i in range(8)]
NT = (((1,), (1,)), ((), ()))


def chip_shift(d):
    return [(i, ((i // 2 + d) % CHIPS) * 2 + i % 2) for i in range(8)]


def y_shift(d):
    return [(i, ((i // ZS + d) % YS) * ZS + i % ZS) for i in range(32)]


Z_GROUPS = [[y * ZS + z for z in range(ZS)] for y in range(YS)]


def dot(a, b):
    return jnp.dot(a, b, preferred_element_type=F32)


def dot_nt(a, b):
    return lax.dot_general(a, b, NT, preferred_element_type=F32)


def in_hbm(array):
    return pltpu.with_memory_space_constraint(array, pltpu.HBM)


def cost(flops, bytes_accessed, transcendentals=0):
    return pl.CostEstimate(
        flops=1, bytes_accessed=1, transcendentals=0
    )


PARAMS = pltpu.CompilerParams(vmem_limit_bytes=VMEM_LIMIT)
WHOLE = pl.BlockSpec(memory_space=pltpu.VMEM)
SCALARS = pl.BlockSpec(memory_space=pltpu.SMEM)
STAY = pl.BlockSpec(memory_space=pltpu.HBM)


def kv_own_kernel(place, own, w_key, w_value, weights, out, rows, sems):
    columns = pl.ds(pl.multiple_of(place[1] * HD, HD), HD)
    copies = []
    for chunk in range(W_CHUNKS):
        part = pl.ds(chunk * (TILE // W_CHUNKS), TILE // W_CHUNKS)
        copies.append(pltpu.make_async_copy(own.at[part], rows.at[part], sems.at[chunk, 2]))
        part = pl.ds(chunk * (D // W_CHUNKS), D // W_CHUNKS)
        for side, source in enumerate((w_key, w_value)):
            copies.append(
                pltpu.make_async_copy(
                    source.at[part, columns],
                    weights.at[part, pl.ds(side * HD, HD)],
                    sems.at[chunk, side],
                )
            )
    for copy in copies:
        copy.start()
    for copy in copies:
        copy.wait()
    out[...] = dot(rows[...], weights[...]).astype(BF)


def project_kv_own(place, own, w_key, w_value):
    return pl.pallas_call(
        kv_own_kernel,
        in_specs=[SCALARS, STAY, STAY, STAY],
        out_specs=[WHOLE, WHOLE],
        out_shape=[
            jax.ShapeDtypeStruct((D, 2 * HD), BF),
            jax.ShapeDtypeStruct((TILE, 2 * HD), BF),
        ],
        scratch_shapes=[pltpu.VMEM((TILE, D), BF), pltpu.SemaphoreType.DMA((W_CHUNKS, 3))],
        compiler_params=PARAMS,
        cost_estimate=cost(2 * TILE * D * 256, 2 * (TILE * D + D * 256)),
        name="project_kv_own",
    )(place, own, w_key, w_value)


def kv_far_kernel(rows, weights, weights_other, mine, theirs):
    mine[...] = dot(rows[...], weights[...]).astype(BF)
    theirs[...] = dot(rows[...], weights_other[...]).astype(BF)


def project_kv_far(rows, weights, weights_other):
    return pl.pallas_call(
        kv_far_kernel,
        in_specs=[WHOLE] * 3,
        out_specs=[WHOLE] * 2,
        out_shape=[jax.ShapeDtypeStruct((TILE, 2 * HD), BF)] * 2,
        compiler_params=PARAMS,
        cost_estimate=cost(4 * TILE * D * 256, 2 * (TILE * D + 2 * D * 256)),
        name="project_kv_far",
    )(rows, weights, weights_other)


def kv_kernel(other, weights, kv_own, out):
    out[:TILE] = kv_own[...]
    out[TILE:] = dot(other[...], weights[...]).astype(BF)


def project_kv(other, weights, kv_own):
    return pl.pallas_call(
        kv_kernel,
        in_specs=[WHOLE] * 3,
        out_specs=WHOLE,
        out_shape=jax.ShapeDtypeStruct((2 * TILE, 2 * HD), BF),
        compiler_params=PARAMS,
        cost_estimate=cost(2 * TILE * D * 256, 2 * (TILE * D + D * 256)),
        name="project_kv",
    )(other, weights, kv_own)


def query_kernel(
    place, own, other, w_query, w_key, w_value, segments_far, mask_far, mask_other,
    out, limits, weights_other, weights, segments, mask_own, sems, small_sems,
):
    theirs = pl.ds(pl.multiple_of((1 - place[1]) * HD, HD), HD)
    small = [
        pltpu.make_async_copy(segments_far, segments, small_sems.at[0]),
        pltpu.make_async_copy(mask_far, mask_own, small_sems.at[1]),
    ]
    for copy in small:
        copy.start()
    columns = pl.ds(pl.multiple_of(place[1] * GF, HD), GF)
    copies = []
    for chunk in range(Q_CHUNKS):
        part = pl.ds(chunk * (D // Q_CHUNKS), D // Q_CHUNKS)
        copies.append(
            pltpu.make_async_copy(w_query.at[part, columns], weights.at[part], sems.at[chunk])
        )
    for side, source in enumerate((w_key, w_value)):
        copies.append(
            pltpu.make_async_copy(
                source.at[:, theirs],
                weights_other.at[:, pl.ds(side * HD, HD)],
                small_sems.at[2 + side],
            )
        )
    for copy in copies:
        copy.start()
    for copy in small:
        copy.wait()

    chip, core = place[0], place[1]
    passages = segments[...]
    ends = [jnp.sum((passages <= s).astype(jnp.int32)) for s in range(3)]
    for slot in range(2):
        masks = mask_own if slot == 0 else mask_other
        tile = 2 * chip + (core if slot == 0 else 1 - core)
        mine = segments[:, pl.ds(pl.multiple_of(tile * TILE, TILE), TILE)]
        low = jnp.where(
            mine == 0, 0, jnp.where(mine == 1, ends[0], jnp.where(mine == 2, ends[1], ends[2]))
        )
        high = jnp.where(
            mine == 0, ends[0], jnp.where(mine == 1, ends[1], jnp.where(mine == 2, ends[2], KEYS))
        )
        for d in range(CHIPS):
            for key_slot in range(2):
                key_tile = 2 * lax.rem(chip + CHIPS - d, CHIPS) + (
                    core if key_slot == 0 else 1 - core
                )
                seen = masks[0, key_tile] == 1
                row = 4 * d + 2 * key_slot
                place_of = slice(slot * TILE, (slot + 1) * TILE)
                limits[row : row + 1, place_of] = jnp.where(seen, 0, low) - key_tile * TILE
                limits[row + 1 : row + 2, place_of] = (
                    jnp.where(seen, KEYS, high) - key_tile * TILE
                )

    for copy in copies:
        copy.wait()
    for slot, rows in enumerate((own, other)):
        queries = dot(rows[...], weights[...]).astype(BF)
        for head in range(GROUP):
            out[head * 256 + slot * TILE : head * 256 + (slot + 1) * TILE] = queries[
                :, head * HD : (head + 1) * HD
            ]


def project_query(
    place, own, other, w_query, w_key, w_value, segments, mask_own, mask_other
):
    return pl.pallas_call(
        query_kernel,
        in_specs=[SCALARS, WHOLE, WHOLE] + [STAY] * 5 + [SCALARS],
        out_specs=[WHOLE] * 3,
        out_shape=[
            jax.ShapeDtypeStruct((STACK, HD), BF),
            jax.ShapeDtypeStruct((4 * CHIPS, 2 * TILE), jnp.int32),
            jax.ShapeDtypeStruct((D, 2 * HD), BF),
        ],
        scratch_shapes=[
            pltpu.VMEM((D, GF), BF),
            pltpu.VMEM((1, KEYS), jnp.int32),
            pltpu.SMEM((1, KEYS // TILE), jnp.int32),
            pltpu.SemaphoreType.DMA((Q_CHUNKS,)),
            pltpu.SemaphoreType.DMA((4,)),
        ],
        compiler_params=PARAMS,
        cost_estimate=cost(2 * 256 * D * GF, 2 * (256 * D + D * GF + 256 * GF)),
        name="project_query",
    )(place, own, other, w_query, w_key, w_value, segments, mask_own, mask_other)


def stack_kernel(place, up_own, up_other, out):
    for slot, rows in enumerate((up_own, up_other)):
        for head in range(GROUP):
            columns = pl.ds(pl.multiple_of(place[1] * GF + head * HD, HD), HD)
            out[head * 256 + slot * TILE : head * 256 + (slot + 1) * TILE] = rows[:, columns]


def stack_up(place, up_own, up_other):
    return pl.pallas_call(
        stack_kernel,
        in_specs=[SCALARS, WHOLE, WHOLE],
        out_specs=WHOLE,
        out_shape=jax.ShapeDtypeStruct((STACK, HD), BF),
        compiler_params=PARAMS,
        cost_estimate=cost(0, 4 * STACK * HD),
        name="stack_up",
    )(place, up_own, up_other)


def scores_kernel(d, limits, query, up, *refs):
    powers, grads, stats, keys_t = refs[-4:]
    kv = jnp.concatenate([ref[...] for ref in refs[:-4]], axis=0)
    keys, values = kv[:, :HD], kv[:, HD:]
    keys_t[...] = keys.T
    position = lax.broadcasted_iota(jnp.int32, (TILE, 2 * TILE), 0)
    bias = []
    for key_slot in range(2):
        row = 4 * d + 2 * key_slot
        allowed = (position >= limits[row : row + 1]) & (position < limits[row + 1 : row + 2])
        bias.append(jnp.where(allowed, 0.0, -jnp.inf))
    bias = jnp.concatenate(bias, axis=0)
    for head in range(GROUP):
        part = slice(head * 256, (head + 1) * 256)
        scores = dot_nt(keys, query[part]) * LOG2_SCALE + bias
        top = jnp.max(scores, axis=0, keepdims=True)
        power = jnp.exp2(scores - jnp.where(top == -jnp.inf, 0.0, top))
        grad = dot_nt(values, up[part])
        powers[:, part] = power
        grads[:, part] = grad
        stats[0:1, part] = top
        stats[1:2, part] = jnp.sum(power, axis=0, keepdims=True)
        stats[2:3, part] = jnp.sum(power * grad, axis=0, keepdims=True)


def chip_scores(d, limits, query, up, *kv):
    return pl.pallas_call(
        functools.partial(scores_kernel, d),
        in_specs=[WHOLE] * (3 + len(kv)),
        out_specs=[WHOLE] * 4,
        out_shape=[
            jax.ShapeDtypeStruct((256, STACK), F32),
            jax.ShapeDtypeStruct((256, STACK), F32),
            jax.ShapeDtypeStruct((8, STACK), F32),
            jax.ShapeDtypeStruct((HD, 256), BF),
        ],
        compiler_params=PARAMS,
        cost_estimate=cost(4 * STACK * 256 * HD, 10 * 256 * STACK, 256 * STACK),
        name=f"chip_scores_{d}",
    )(limits, query, up, *kv)


def factors_kernel(a, b, c, d, out):
    parts = (a, b, c, d)
    top = jnp.maximum(jnp.maximum(a[0:1], b[0:1]), jnp.maximum(c[0:1], d[0:1]))
    factors = [jnp.exp2(part[0:1] - top) for part in parts]
    total = sum(factor * part[1:2] for factor, part in zip(factors, parts))
    factors = [factor / total for factor in factors]
    for chip, factor in enumerate(factors):
        out[chip : chip + 1] = factor
    out[4:5] = sum(factor * part[2:3] for factor, part in zip(factors, parts))


def softmax_factors(stats):
    return pl.pallas_call(
        factors_kernel,
        in_specs=[WHOLE] * 4,
        out_specs=WHOLE,
        out_shape=jax.ShapeDtypeStruct((8, STACK), F32),
        compiler_params=PARAMS,
        cost_estimate=cost(20 * STACK, 128 * STACK),
        name="softmax_factors",
    )(*stats)


def terms_kernel(d, powers, grads, factors, query, up, out, grad_scores, probs_low):
    for head in range(GROUP):
        part = slice(head * 256, (head + 1) * 256)
        probs = powers[:, part] * factors[d : d + 1, part]
        probs_low[:, part] = probs.astype(BF)
        grad_scores[:, part] = (probs * (grads[:, part] - factors[4:5, part])).astype(BF)
    out[:, :HD] = (dot(grad_scores[...], query[...]) * SCALE).astype(out.dtype)
    out[:, HD:] = dot(probs_low[...], up[...]).astype(out.dtype)


def chip_terms(d, powers, grads, factors, query, up):
    return pl.pallas_call(
        functools.partial(terms_kernel, d),
        in_specs=[WHOLE] * 5,
        out_specs=[WHOLE] * 2,
        out_shape=[
            jax.ShapeDtypeStruct((256, 256), F32 if d == 0 else BF),
            jax.ShapeDtypeStruct((256, STACK), BF),
        ],
        scratch_shapes=[pltpu.VMEM((256, STACK), BF)],
        compiler_params=PARAMS,
        cost_estimate=cost(4 * STACK * 256 * HD, 10 * 256 * STACK),
        name=f"chip_terms_{d}",
    )(powers, grads, factors, query, up)


def query_grad_kernel(k0, k1, k2, k3, g0, g1, g2, g3, out):
    for head in range(GROUP):
        part = slice(head * 256, (head + 1) * 256)
        total = dot(k0[...], g0[:, part]) + dot(k1[...], g1[:, part])
        total += dot(k2[...], g2[:, part]) + dot(k3[...], g3[:, part])
        out[:, head * HD : (head + 1) * HD] = (total * SCALE).T.astype(BF)


def query_grad(keys_t, grad_scores):
    return pl.pallas_call(
        query_grad_kernel,
        in_specs=[WHOLE] * 8,
        out_specs=WHOLE,
        out_shape=jax.ShapeDtypeStruct((256, GF), BF),
        compiler_params=PARAMS,
        cost_estimate=cost(2 * STACK * KEYS * HD, 2 * STACK * KEYS),
        name="query_grad",
    )(*keys_t, *grad_scores)


def sum_kernel(a, b, c, d, out):
    total = (a[...] + b[...].astype(F32)) + (c[...].astype(F32) + d[...].astype(F32))
    out[...] = total.astype(out.dtype)


def sum_four(a, b, c, d):
    return pl.pallas_call(
        sum_kernel,
        in_specs=[WHOLE] * 4,
        out_specs=WHOLE,
        out_shape=jax.ShapeDtypeStruct(a.shape, BF),
        compiler_params=PARAMS,
        cost_estimate=cost(4 * a.size, 12 * a.size),
        name="sum_four",
    )(a, b, c, d)


def pack_kernel(place, dq, dq_other, dkv, dkv_other, *outs):
    for core in range(2):
        own_part = slice(core * HD, (core + 1) * HD)
        for chip in range(CHIPS):

            @pl.when((place[1] == core) & (place[0] == chip))
            def _(core=core, own_part=own_part, chip=chip):
                for d, out in enumerate(outs):
                    target = (chip + d) % CHIPS
                    if target == 3:
                        out[:, own_part] = dkv[:, own_part]
                        theirs = slice((1 - core) * HD, (2 - core) * HD)
                        out[:TILE, theirs] = dkv_other[TILE:, own_part]
                        out[TILE:, theirs] = dkv_other[:TILE, own_part]
                    elif target == 2 - 2 * core:
                        out[:TILE] = dq_other[TILE:, 256:512]
                        out[TILE:] = dq_other[:TILE, 256:512]
                    else:
                        first = target == core
                        out[...] = dq[:, 0:256] if first else dq[:, 512:768]


def pack(place, dq, dq_other, dkv, dkv_other):
    return pl.pallas_call(
        pack_kernel,
        in_specs=[SCALARS] + [WHOLE] * 4,
        out_specs=[WHOLE] * 4,
        out_shape=[jax.ShapeDtypeStruct((256, 256), BF)] * 4,
        compiler_params=PARAMS,
        cost_estimate=cost(0, 4 << 19),
        name="pack",
    )(place, dq, dq_other, dkv, dkv_other)


def transpose_kernel(own, far1, late_a, late_b, far3, out):
    late = jnp.concatenate([late_a[...], late_b[...]], axis=0)
    for i, rows in enumerate((own[...], far1[...], late, far3[...])):
        out[:, i * TILE : (i + 1) * TILE] = rows.T


def transpose(parts):
    return pl.pallas_call(
        transpose_kernel,
        in_specs=[WHOLE] * 5,
        out_specs=WHOLE,
        out_shape=jax.ShapeDtypeStruct((D, KEYS // 2), BF),
        compiler_params=PARAMS,
        cost_estimate=cost(0, 2 * D * KEYS),
        name="transpose_tokens",
    )(*parts)


def weight_kernel(place, tokens_t, other_t, a, b, c, d, out0, out1, out2, out3):
    parts = (a, b, c, d)
    right = jnp.concatenate([part[:TILE] for part in parts], axis=0)
    right_other = jnp.concatenate([part[TILE:] for part in parts], axis=0)
    for shift, out in enumerate((out0, out1, out2, out3)):
        row = pl.multiple_of(lax.rem(place[2] + shift, YS) * (D // YS), 128)
        rows = pl.ds(row, D // YS)
        out[...] = (dot(tokens_t[rows], right) + dot(other_t[rows], right_other)).astype(
            out.dtype
        )


def weight_grad(place, tokens_t, other_t, parts):
    shape = (D // YS, 256)
    return pl.pallas_call(
        weight_kernel,
        in_specs=[SCALARS] + [WHOLE] * 6,
        out_specs=[WHOLE] * 4,
        out_shape=[jax.ShapeDtypeStruct(shape, F32)] + [jax.ShapeDtypeStruct(shape, BF)] * 3,
        compiler_params=PARAMS,
        cost_estimate=cost(2 * D * KEYS * 256, 2 * D * KEYS + 3 * D * 256),
        name="weight_grad",
    )(place, tokens_t, other_t, *parts)


def input_kernel(
    place, dq, dq_other, dkv, dkv_other, w_query, w_key, w_value, out, left, right, sems
):
    core = place[1]
    width = D // IN_CHUNKS
    copies = []
    for chunk in range(IN_CHUNKS):
        part = pl.ds(chunk * width, width)
        copies.append(
            [
                pltpu.make_async_copy(
                    source.at[part],
                    right.at[part, pl.ds(start, size)],
                    sems.at[chunk, side],
                )
                for side, (source, start, size) in enumerate(
                    ((w_query, 0, D), (w_key, D, 256), (w_value, D + 256, 256))
                )
            ]
        )
    for group in copies:
        for copy in group:
            copy.start()
    mine = pl.ds(pl.multiple_of(core * GF, 128), GF)
    theirs = pl.ds(pl.multiple_of((1 - core) * GF, 128), GF)
    left[:, mine] = dq[:TILE]
    left[:, theirs] = dq_other[TILE:]
    for part in range(2):
        columns = slice(part * HD, (part + 1) * HD)
        base = D + part * KVH * HD
        left[:, pl.ds(pl.multiple_of(base + core * HD, 128), HD)] = dkv[:TILE, columns]
        left[:, pl.ds(pl.multiple_of(base + (1 - core) * HD, 128), HD)] = dkv_other[
            TILE:, columns
        ]
    for chunk, group in enumerate(copies):
        for copy in group:
            copy.wait()
        part = slice(chunk * width, (chunk + 1) * width)
        out[:, part] = dot_nt(left[...], right[part]).astype(BF)


def input_grad(place, dq, dq_other, dkv, dkv_other, w_query, w_key, w_value):
    return pl.pallas_call(
        input_kernel,
        in_specs=[SCALARS] + [WHOLE] * 4 + [STAY] * 3,
        out_specs=WHOLE,
        out_shape=jax.ShapeDtypeStruct((TILE, D), BF),
        scratch_shapes=[
            pltpu.VMEM((TILE, D + 512), BF),
            pltpu.VMEM((D, D + 512), BF),
            pltpu.SemaphoreType.DMA((IN_CHUNKS, 3)),
        ],
        compiler_params=PARAMS,
        cost_estimate=cost(2 * TILE * D * 2048, 2 * D * 2048),
        name="input_grad",
    )(place, dq, dq_other, dkv, dkv_other, w_query, w_key, w_value)


def final_kernel(parts, out):
    total = parts[0:48].astype(F32)
    for z in range(1, ZS):
        total += parts[z * 48 : (z + 1) * 48].astype(F32)
    out[...] = total


def final_sum(parts):
    return pl.pallas_call(
        final_kernel,
        in_specs=[WHOLE],
        out_specs=WHOLE,
        out_shape=jax.ShapeDtypeStruct((48, 256), F32),
        compiler_params=PARAMS,
        cost_estimate=cost(parts.size, 2 * parts.size),
        name="final_sum",
    )(parts)


def shards(tokens, grad_heads, tile_mask, segments, w_query, w_key, w_value):
    ctx = lax.axis_index("ctx")
    dp = lax.axis_index("dp")
    place = jnp.stack([ctx // 2, ctx % 2, dp // ZS, dp % ZS]).astype(jnp.int32)
    own, up = tokens[0], grad_heads[0]
    other = lax.ppermute(own, "ctx", CORE)
    up_other = lax.ppermute(up, "ctx", CORE)
    mask_other = lax.ppermute(tile_mask[0], "ctx", CORE)
    other, mask_other, up_other = lax.optimization_barrier((other, mask_other, up_other))

    w_query, w_key, w_value = (in_hbm(w) for w in (w_query, w_key, w_value))
    weights, kv_own = project_kv_own(place, in_hbm(own), w_key, w_value)
    kv = project_kv(other, weights, kv_own)
    kv2 = lax.ppermute(kv, "ctx", chip_shift(2))
    far = {d: lax.ppermute(own, "ctx", chip_shift(d)) for d in (1, 3)}
    query, limits, weights_other = project_query(
        place, own, other, w_query, w_key, w_value,
        in_hbm(segments), in_hbm(tile_mask[0]), mask_other,
    )
    up = stack_up(place, up, up_other)
    scores = {0: chip_scores(0, limits, query, up, kv)}
    far, scores[0] = lax.optimization_barrier((far, scores[0]))
    kv_far = {d: project_kv_far(far[d], weights, weights_other) for d in (1, 3)}
    for d in (1, 3):
        mine, theirs = kv_far[d]
        kv_far[d] = (mine, lax.ppermute(theirs, "ctx", CORE))
    late = (
        lax.ppermute(far[1][: TILE // 2], "ctx", chip_shift(1)),
        lax.ppermute(far[3][TILE // 2 :], "ctx", chip_shift(3)),
    )
    for d in (1, 3):
        scores[d] = chip_scores(d, limits, query, up, *kv_far[d])
    scores[2] = chip_scores(2, limits, query, up, kv2)
    factors = softmax_factors([scores[d][2] for d in range(CHIPS)])
    terms, grad_scores = {}, {}
    for d in (2, 1, 3):
        terms[d], grad_scores[d] = chip_terms(d, *scores[d][:2], factors, query, up)
    back = [lax.ppermute(terms[d], "ctx", chip_shift(CHIPS - d)) for d in (2, 1, 3)]
    terms[0], grad_scores[0] = chip_terms(0, *scores[0][:2], factors, query, up)
    dq = query_grad([scores[d][3] for d in range(CHIPS)], [grad_scores[d] for d in range(CHIPS)])
    late, back, dq = lax.optimization_barrier((late, back, dq))
    dq_other = lax.ppermute(dq, "ctx", CORE)
    dkv = sum_four(terms[0], *back)
    dkv_other = lax.ppermute(dkv, "ctx", CORE)
    packed = pack(place, dq, dq_other, dkv, dkv_other)

    far, dkv = lax.optimization_barrier((far, dkv))
    tokens_t = transpose([own, far[1], *late, far[3]])
    tokens_t, packed = lax.optimization_barrier((tokens_t, packed))
    other_t = lax.ppermute(tokens_t, "ctx", CORE)
    columns = [packed[0]] + [
        lax.ppermute(packed[d], "ctx", chip_shift(d)) for d in (1, 2, 3)
    ]
    terms = weight_grad(place, tokens_t, other_t, columns)
    y_parts = [terms[0]] + [lax.ppermute(terms[d], "dp", y_shift(d)) for d in (1, 2, 3)]
    grad_tokens = input_grad(
        place, dq, dq_other, dkv, dkv_other, w_query, w_key, w_value
    )
    y_parts, grad_tokens = lax.optimization_barrier((y_parts, grad_tokens))
    y_sum = sum_four(*y_parts)
    z_parts = lax.all_to_all(y_sum, "dp", 0, 0, tiled=True, axis_index_groups=Z_GROUPS)
    grad_projection = final_sum(z_parts)
    return grad_tokens[None], grad_projection


def solution(mesh):
    return jax.shard_map(
        shards,
        mesh=mesh,
        in_specs=(
            P("dp", "ctx", None),
            P("dp", "ctx", None),
            P("dp", "ctx", None),
            P("dp", None),
            P(),
            P(),
            P(),
        ),
        out_specs=(P("dp", "ctx", None), P("dp", "ctx")),
        check_vma=False,
    )
```

```python
import functools
import math

import jax
import jax.numpy as jnp
from jax import lax
from jax.experimental import pallas as pl
from jax.experimental.pallas import tpu as pltpu
from jax.sharding import PartitionSpec as P

QH = 12
KVH = 2
HD = 128
TILE = 128
D = 1536
KEYS = 1024
CHIPS = 4
GROUP = QH // KVH
GF = GROUP * HD
STACK = GROUP * 256
YS = 4
ZS = 8
SCALE = 1.0 / math.sqrt(HD)
LOG2_SCALE = SCALE * math.log2(math.e)
BF = jnp.bfloat16
F32 = jnp.float32
VMEM_LIMIT = 24 * 1024 * 1024
W_CHUNKS = 1
Q_CHUNKS = 3
IN_CHUNKS = 3

CORE = [(i, i ^ 1) for i in range(8)]
NT = (((1,), (1,)), ((), ()))


def chip_shift(d):
    return [(i, ((i // 2 + d) % CHIPS) * 2 + i % 2) for i in range(8)]


def y_shift(d):
    return [(i, ((i // ZS + d) % YS) * ZS + i % ZS) for i in range(32)]


Z_GROUPS = [[y * ZS + z for z in range(ZS)] for y in range(YS)]


def dot(a, b):
    return jnp.dot(a, b, preferred_element_type=F32)


def dot_nt(a, b):
    return lax.dot_general(a, b, NT, preferred_element_type=F32)


def in_hbm(array):
    return pltpu.with_memory_space_constraint(array, pltpu.HBM)


def cost(flops, bytes_accessed, transcendentals=0):
    return pl.CostEstimate(
        flops=1, bytes_accessed=1, transcendentals=0
    )


PARAMS = pltpu.CompilerParams(vmem_limit_bytes=VMEM_LIMIT)
WHOLE = pl.BlockSpec(memory_space=pltpu.VMEM)
SCALARS = pl.BlockSpec(memory_space=pltpu.SMEM)
STAY = pl.BlockSpec(memory_space=pltpu.HBM)


def kv_own_kernel(place, own, w_key, w_value, weights, out, rows, sems):
    columns = pl.ds(pl.multiple_of(place[1] * HD, HD), HD)
    copies = []
    for chunk in range(W_CHUNKS):
        part = pl.ds(chunk * (TILE // W_CHUNKS), TILE // W_CHUNKS)
        copies.append(pltpu.make_async_copy(own.at[part], rows.at[part], sems.at[chunk, 2]))
        part = pl.ds(chunk * (D // W_CHUNKS), D // W_CHUNKS)
        for side, source in enumerate((w_key, w_value)):
            copies.append(
                pltpu.make_async_copy(
                    source.at[part, columns],
                    weights.at[part, pl.ds(side * HD, HD)],
                    sems.at[chunk, side],
                )
            )
    for copy in copies:
        copy.start()
    for copy in copies:
        copy.wait()
    out[...] = dot(rows[...], weights[...]).astype(BF)


def project_kv_own(place, own, w_key, w_value):
    return pl.pallas_call(
        kv_own_kernel,
        in_specs=[SCALARS, STAY, STAY, STAY],
        out_specs=[WHOLE, WHOLE],
        out_shape=[
            jax.ShapeDtypeStruct((D, 2 * HD), BF),
            jax.ShapeDtypeStruct((TILE, 2 * HD), BF),
        ],
        scratch_shapes=[pltpu.VMEM((TILE, D), BF), pltpu.SemaphoreType.DMA((W_CHUNKS, 3))],
        compiler_params=PARAMS,
        cost_estimate=cost(2 * TILE * D * 256, 2 * (TILE * D + D * 256)),
        name="project_kv_own",
    )(place, own, w_key, w_value)


def kv_far_kernel(rows, weights, weights_other, mine, theirs):
    mine[...] = dot(rows[...], weights[...]).astype(BF)
    theirs[...] = dot(rows[...], weights_other[...]).astype(BF)


def project_kv_far(rows, weights, weights_other):
    return pl.pallas_call(
        kv_far_kernel,
        in_specs=[WHOLE] * 3,
        out_specs=[WHOLE] * 2,
        out_shape=[jax.ShapeDtypeStruct((TILE, 2 * HD), BF)] * 2,
        compiler_params=PARAMS,
        cost_estimate=cost(4 * TILE * D * 256, 2 * (TILE * D + 2 * D * 256)),
        name="project_kv_far",
    )(rows, weights, weights_other)


def kv_kernel(other, weights, kv_own, out):
    out[:TILE] = kv_own[...]
    out[TILE:] = dot(other[...], weights[...]).astype(BF)


def project_kv(other, weights, kv_own):
    return pl.pallas_call(
        kv_kernel,
        in_specs=[WHOLE] * 3,
        out_specs=WHOLE,
        out_shape=jax.ShapeDtypeStruct((2 * TILE, 2 * HD), BF),
        compiler_params=PARAMS,
        cost_estimate=cost(2 * TILE * D * 256, 2 * (TILE * D + D * 256)),
        name="project_kv",
    )(other, weights, kv_own)


def query_kernel(
    place, own, other, w_query, w_key, w_value, segments_far, mask_far, mask_other,
    out, limits, weights_other, weights, segments, mask_own, sems, small_sems,
):
    theirs = pl.ds(pl.multiple_of((1 - place[1]) * HD, HD), HD)
    small = [
        pltpu.make_async_copy(segments_far, segments, small_sems.at[0]),
        pltpu.make_async_copy(mask_far, mask_own, small_sems.at[1]),
    ]
    for copy in small:
        copy.start()
    columns = pl.ds(pl.multiple_of(place[1] * GF, HD), GF)
    copies = []
    for chunk in range(Q_CHUNKS):
        part = pl.ds(chunk * (D // Q_CHUNKS), D // Q_CHUNKS)
        copies.append(
            pltpu.make_async_copy(w_query.at[part, columns], weights.at[part], sems.at[chunk])
        )
    for side, source in enumerate((w_key, w_value)):
        copies.append(
            pltpu.make_async_copy(
                source.at[:, theirs],
                weights_other.at[:, pl.ds(side * HD, HD)],
                small_sems.at[2 + side],
            )
        )
    for copy in copies:
        copy.start()
    for copy in small:
        copy.wait()

    chip, core = place[0], place[1]
    passages = segments[...]
    ends = [jnp.sum((passages <= s).astype(jnp.int32)) for s in range(3)]
    for slot in range(2):
        masks = mask_own if slot == 0 else mask_other
        tile = 2 * chip + (core if slot == 0 else 1 - core)
        mine = segments[:, pl.ds(pl.multiple_of(tile * TILE, TILE), TILE)]
        low = jnp.where(
            mine == 0, 0, jnp.where(mine == 1, ends[0], jnp.where(mine == 2, ends[1], ends[2]))
        )
        high = jnp.where(
            mine == 0, ends[0], jnp.where(mine == 1, ends[1], jnp.where(mine == 2, ends[2], KEYS))
        )
        for d in range(CHIPS):
            for key_slot in range(2):
                key_tile = 2 * lax.rem(chip + CHIPS - d, CHIPS) + (
                    core if key_slot == 0 else 1 - core
                )
                seen = masks[0, key_tile] == 1
                row = 4 * d + 2 * key_slot
                place_of = slice(slot * TILE, (slot + 1) * TILE)
                limits[row : row + 1, place_of] = jnp.where(seen, 0, low) - key_tile * TILE
                limits[row + 1 : row + 2, place_of] = (
                    jnp.where(seen, KEYS, high) - key_tile * TILE
                )

    for copy in copies:
        copy.wait()
    for slot, rows in enumerate((own, other)):
        queries = dot(rows[...], weights[...]).astype(BF)
        for head in range(GROUP):
            out[head * 256 + slot * TILE : head * 256 + (slot + 1) * TILE] = queries[
                :, head * HD : (head + 1) * HD
            ]


def project_query(
    place, own, other, w_query, w_key, w_value, segments, mask_own, mask_other
):
    return pl.pallas_call(
        query_kernel,
        in_specs=[SCALARS, WHOLE, WHOLE] + [STAY] * 5 + [SCALARS],
        out_specs=[WHOLE] * 3,
        out_shape=[
            jax.ShapeDtypeStruct((STACK, HD), BF),
            jax.ShapeDtypeStruct((4 * CHIPS, 2 * TILE), jnp.int32),
            jax.ShapeDtypeStruct((D, 2 * HD), BF),
        ],
        scratch_shapes=[
            pltpu.VMEM((D, GF), BF),
            pltpu.VMEM((1, KEYS), jnp.int32),
            pltpu.SMEM((1, KEYS // TILE), jnp.int32),
            pltpu.SemaphoreType.DMA((Q_CHUNKS,)),
            pltpu.SemaphoreType.DMA((4,)),
        ],
        compiler_params=PARAMS,
        cost_estimate=cost(2 * 256 * D * GF, 2 * (256 * D + D * GF + 256 * GF)),
        name="project_query",
    )(place, own, other, w_query, w_key, w_value, segments, mask_own, mask_other)


def stack_kernel(place, up_own, up_other, out):
    for slot, rows in enumerate((up_own, up_other)):
        for head in range(GROUP):
            columns = pl.ds(pl.multiple_of(place[1] * GF + head * HD, HD), HD)
            out[head * 256 + slot * TILE : head * 256 + (slot + 1) * TILE] = rows[:, columns]


def stack_up(place, up_own, up_other):
    return pl.pallas_call(
        stack_kernel,
        in_specs=[SCALARS, WHOLE, WHOLE],
        out_specs=WHOLE,
        out_shape=jax.ShapeDtypeStruct((STACK, HD), BF),
        compiler_params=PARAMS,
        cost_estimate=cost(0, 4 * STACK * HD),
        name="stack_up",
    )(place, up_own, up_other)


def scores_kernel(d, limits, query, up, *refs):
    powers, grads, stats, keys_t = refs[-4:]
    kv = jnp.concatenate([ref[...] for ref in refs[:-4]], axis=0)
    keys, values = kv[:, :HD], kv[:, HD:]
    keys_t[...] = keys.T
    position = lax.broadcasted_iota(jnp.int32, (TILE, 2 * TILE), 0)
    bias = []
    for key_slot in range(2):
        row = 4 * d + 2 * key_slot
        allowed = (position >= limits[row : row + 1]) & (position < limits[row + 1 : row + 2])
        bias.append(jnp.where(allowed, 0.0, -jnp.inf))
    bias = jnp.concatenate(bias, axis=0)
    for head in range(GROUP):
        part = slice(head * 256, (head + 1) * 256)
        scores = dot_nt(keys, query[part]) * LOG2_SCALE + bias
        top = jnp.max(scores, axis=0, keepdims=True)
        power = jnp.exp2(scores - jnp.where(top == -jnp.inf, 0.0, top))
        grad = dot_nt(values, up[part])
        powers[:, part] = power
        grads[:, part] = grad
        stats[0:1, part] = top
        stats[1:2, part] = jnp.sum(power, axis=0, keepdims=True)
        stats[2:3, part] = jnp.sum(power * grad, axis=0, keepdims=True)


def chip_scores(d, limits, query, up, *kv):
    return pl.pallas_call(
        functools.partial(scores_kernel, d),
        in_specs=[WHOLE] * (3 + len(kv)),
        out_specs=[WHOLE] * 4,
        out_shape=[
            jax.ShapeDtypeStruct((256, STACK), F32),
            jax.ShapeDtypeStruct((256, STACK), F32),
            jax.ShapeDtypeStruct((8, STACK), F32),
            jax.ShapeDtypeStruct((HD, 256), BF),
        ],
        compiler_params=PARAMS,
        cost_estimate=cost(4 * STACK * 256 * HD, 10 * 256 * STACK, 256 * STACK),
        name=f"chip_scores_{d}",
    )(limits, query, up, *kv)


def factors_kernel(a, b, c, d, out):
    parts = (a, b, c, d)
    top = jnp.maximum(jnp.maximum(a[0:1], b[0:1]), jnp.maximum(c[0:1], d[0:1]))
    factors = [jnp.exp2(part[0:1] - top) for part in parts]
    total = sum(factor * part[1:2] for factor, part in zip(factors, parts))
    factors = [factor / total for factor in factors]
    for chip, factor in enumerate(factors):
        out[chip : chip + 1] = factor
    out[4:5] = sum(factor * part[2:3] for factor, part in zip(factors, parts))


def softmax_factors(stats):
    return pl.pallas_call(
        factors_kernel,
        in_specs=[WHOLE] * 4,
        out_specs=WHOLE,
        out_shape=jax.ShapeDtypeStruct((8, STACK), F32),
        compiler_params=PARAMS,
        cost_estimate=cost(20 * STACK, 128 * STACK),
        name="softmax_factors",
    )(*stats)


def terms_kernel(d, powers, grads, factors, query, up, out, grad_scores, probs_low):
    for head in range(GROUP):
        part = slice(head * 256, (head + 1) * 256)
        probs = powers[:, part] * factors[d : d + 1, part]
        probs_low[:, part] = probs.astype(BF)
        grad_scores[:, part] = (probs * (grads[:, part] - factors[4:5, part])).astype(BF)
    out[:, :HD] = (dot(grad_scores[...], query[...]) * SCALE).astype(out.dtype)
    out[:, HD:] = dot(probs_low[...], up[...]).astype(out.dtype)


def chip_terms(d, powers, grads, factors, query, up):
    return pl.pallas_call(
        functools.partial(terms_kernel, d),
        in_specs=[WHOLE] * 5,
        out_specs=[WHOLE] * 2,
        out_shape=[
            jax.ShapeDtypeStruct((256, 256), F32 if d == 0 else BF),
            jax.ShapeDtypeStruct((256, STACK), BF),
        ],
        scratch_shapes=[pltpu.VMEM((256, STACK), BF)],
        compiler_params=PARAMS,
        cost_estimate=cost(4 * STACK * 256 * HD, 10 * 256 * STACK),
        name=f"chip_terms_{d}",
    )(powers, grads, factors, query, up)


def query_grad_kernel(k0, k1, k2, k3, g0, g1, g2, g3, out, middle, theirs):
    for head in range(GROUP):
        part = slice(head * 256, (head + 1) * 256)
        total = dot(k0[...], g0[:, part]) + dot(k1[...], g1[:, part])
        total += dot(k2[...], g2[:, part]) + dot(k3[...], g3[:, part])
        columns = slice(head * HD, (head + 1) * HD)
        result = (total * SCALE).T.astype(BF)
        out[:, columns] = result
        theirs[:, columns] = result[TILE:]
        if 2 <= head < 4:
            middle[:, (head - 2) * HD : (head - 1) * HD] = result


def query_grad(keys_t, grad_scores):
    return pl.pallas_call(
        query_grad_kernel,
        in_specs=[WHOLE] * 8,
        out_specs=[WHOLE] * 3,
        out_shape=[
            jax.ShapeDtypeStruct((256, GF), BF),
            jax.ShapeDtypeStruct((256, 256), BF),
            jax.ShapeDtypeStruct((TILE, GF), BF),
        ],
        compiler_params=PARAMS,
        cost_estimate=cost(2 * STACK * KEYS * HD, 2 * STACK * KEYS),
        name="query_grad",
    )(*keys_t, *grad_scores)


def sum_kernel(a, b, c, d, out):
    total = (a[...] + b[...].astype(F32)) + (c[...].astype(F32) + d[...].astype(F32))
    out[...] = total.astype(out.dtype)


def sum_four(a, b, c, d):
    return pl.pallas_call(
        sum_kernel,
        in_specs=[WHOLE] * 4,
        out_specs=WHOLE,
        out_shape=jax.ShapeDtypeStruct(a.shape, BF),
        compiler_params=PARAMS,
        cost_estimate=cost(4 * a.size, 12 * a.size),
        name="sum_four",
    )(a, b, c, d)


def pack_kernel(place, dq, middle_other, dkv, dkv_other, *outs):
    for core in range(2):
        own_part = slice(core * HD, (core + 1) * HD)
        for chip in range(CHIPS):

            @pl.when((place[1] == core) & (place[0] == chip))
            def _(core=core, own_part=own_part, chip=chip):
                for d, out in enumerate(outs):
                    target = (chip + d) % CHIPS
                    if target == 3:
                        out[:, own_part] = dkv[:, own_part]
                        theirs = slice((1 - core) * HD, (2 - core) * HD)
                        out[:TILE, theirs] = dkv_other[TILE:, own_part]
                        out[TILE:, theirs] = dkv_other[:TILE, own_part]
                    elif target == 2 - 2 * core:
                        out[:TILE] = middle_other[TILE:]
                        out[TILE:] = middle_other[:TILE]
                    else:
                        first = target == core
                        out[...] = dq[:, 0:256] if first else dq[:, 512:768]


def pack(place, dq, middle_other, dkv, dkv_other):
    return pl.pallas_call(
        pack_kernel,
        in_specs=[SCALARS] + [WHOLE] * 4,
        out_specs=[WHOLE] * 4,
        out_shape=[jax.ShapeDtypeStruct((256, 256), BF)] * 4,
        compiler_params=PARAMS,
        cost_estimate=cost(0, 4 << 19),
        name="pack",
    )(place, dq, middle_other, dkv, dkv_other)


def transpose_kernel(own, far2, far1, far3, out):
    for i, rows in enumerate((own, far2, far1, far3)):
        out[:, i * TILE : (i + 1) * TILE] = rows[...].T


def transpose(parts):
    return pl.pallas_call(
        transpose_kernel,
        in_specs=[WHOLE] * 4,
        out_specs=WHOLE,
        out_shape=jax.ShapeDtypeStruct((D, KEYS // 2), BF),
        compiler_params=PARAMS,
        cost_estimate=cost(0, 2 * D * KEYS),
        name="transpose_tokens",
    )(*parts)


def weight_kernel(shift, place, tokens_t, other_t, a, b, c, d, out):
    parts = (a, b, c, d)
    right = jnp.concatenate([part[:TILE] for part in parts], axis=0)
    right_other = jnp.concatenate([part[TILE:] for part in parts], axis=0)
    row = pl.multiple_of(lax.rem(place[2] + shift, YS) * (D // YS), 128)
    rows = pl.ds(row, D // YS)
    total = dot(tokens_t[rows], right) + dot(other_t[rows], right_other)
    out[...] = total.astype(out.dtype)


def weight_grad(shift, place, tokens_t, other_t, parts):
    return pl.pallas_call(
        functools.partial(weight_kernel, shift),
        in_specs=[SCALARS] + [WHOLE] * 6,
        out_specs=WHOLE,
        out_shape=jax.ShapeDtypeStruct((D // YS, 256), F32 if shift == 0 else BF),
        compiler_params=PARAMS,
        cost_estimate=cost(2 * D * KEYS * 256 // YS, 2 * D * KEYS // YS),
        name=f"weight_grad_{shift}",
    )(place, tokens_t, other_t, *parts)


def input_kernel(
    place, dq, dq_other, dkv, dkv_other, w_query, w_key, w_value, out, left, right, sems
):
    core = place[1]
    width = D // IN_CHUNKS
    copies = []
    for chunk in range(IN_CHUNKS):
        part = pl.ds(chunk * width, width)
        copies.append(
            [
                pltpu.make_async_copy(
                    source.at[part],
                    right.at[part, pl.ds(start, size)],
                    sems.at[chunk, side],
                )
                for side, (source, start, size) in enumerate(
                    ((w_query, 0, D), (w_key, D, 256), (w_value, D + 256, 256))
                )
            ]
        )
    for group in copies:
        for copy in group:
            copy.start()
    mine = pl.ds(pl.multiple_of(core * GF, 128), GF)
    theirs = pl.ds(pl.multiple_of((1 - core) * GF, 128), GF)
    left[:, mine] = dq[:TILE]
    left[:, theirs] = dq_other[...]
    for part in range(2):
        columns = slice(part * HD, (part + 1) * HD)
        base = D + part * KVH * HD
        left[:, pl.ds(pl.multiple_of(base + core * HD, 128), HD)] = dkv[:TILE, columns]
        left[:, pl.ds(pl.multiple_of(base + (1 - core) * HD, 128), HD)] = dkv_other[
            TILE:, columns
        ]
    for chunk, group in enumerate(copies):
        for copy in group:
            copy.wait()
        part = slice(chunk * width, (chunk + 1) * width)
        out[:, part] = dot_nt(left[...], right[part]).astype(BF)


def input_grad(place, dq, dq_other, dkv, dkv_other, w_query, w_key, w_value):
    return pl.pallas_call(
        input_kernel,
        in_specs=[SCALARS] + [WHOLE] * 4 + [STAY] * 3,
        out_specs=WHOLE,
        out_shape=jax.ShapeDtypeStruct((TILE, D), BF),
        scratch_shapes=[
            pltpu.VMEM((TILE, D + 512), BF),
            pltpu.VMEM((D, D + 512), BF),
            pltpu.SemaphoreType.DMA((IN_CHUNKS, 3)),
        ],
        compiler_params=PARAMS,
        cost_estimate=cost(2 * TILE * D * 2048, 2 * D * 2048),
        name="input_grad",
    )(place, dq, dq_other, dkv, dkv_other, w_query, w_key, w_value)


def final_kernel(parts, out):
    total = parts[0:48].astype(F32)
    for z in range(1, ZS):
        total += parts[z * 48 : (z + 1) * 48].astype(F32)
    out[...] = total


def final_sum(parts):
    return pl.pallas_call(
        final_kernel,
        in_specs=[WHOLE],
        out_specs=WHOLE,
        out_shape=jax.ShapeDtypeStruct((48, 256), F32),
        compiler_params=PARAMS,
        cost_estimate=cost(parts.size, 2 * parts.size),
        name="final_sum",
    )(parts)


def shards(tokens, grad_heads, tile_mask, segments, w_query, w_key, w_value):
    ctx = lax.axis_index("ctx")
    dp = lax.axis_index("dp")
    place = jnp.stack([ctx // 2, ctx % 2, dp // ZS, dp % ZS]).astype(jnp.int32)
    own, up = tokens[0], grad_heads[0]
    other = lax.ppermute(own, "ctx", CORE)
    up_other = lax.ppermute(up, "ctx", CORE)
    mask_other = lax.ppermute(tile_mask[0], "ctx", CORE)
    other, mask_other, up_other = lax.optimization_barrier((other, mask_other, up_other))

    w_query, w_key, w_value = (in_hbm(w) for w in (w_query, w_key, w_value))
    weights, kv_own = project_kv_own(place, in_hbm(own), w_key, w_value)
    kv = project_kv(other, weights, kv_own)
    kv2 = lax.ppermute(kv, "ctx", chip_shift(2))
    far = {d: lax.ppermute(own, "ctx", chip_shift(d)) for d in (1, 3)}
    query, limits, weights_other = project_query(
        place, own, other, w_query, w_key, w_value,
        in_hbm(segments), in_hbm(tile_mask[0]), mask_other,
    )
    up = stack_up(place, up, up_other)
    scores = {0: chip_scores(0, limits, query, up, kv)}
    far, kv2, scores[0] = lax.optimization_barrier((far, kv2, scores[0]))
    late = lax.ppermute(far[1], "ctx", chip_shift(1))
    kv_far = {d: project_kv_far(far[d], weights, weights_other) for d in (1, 3)}
    for d in (1, 3):
        mine, theirs = kv_far[d]
        kv_far[d] = (mine, lax.ppermute(theirs, "ctx", CORE))
    for d in (1, 3):
        scores[d] = chip_scores(d, limits, query, up, *kv_far[d])
    scores[2] = chip_scores(2, limits, query, up, kv2)
    factors = softmax_factors([scores[d][2] for d in range(CHIPS)])
    terms, grad_scores = {}, {}
    for d in (3, 1, 2):
        terms[d], grad_scores[d] = chip_terms(d, *scores[d][:2], factors, query, up)
    back = [lax.ppermute(terms[d], "ctx", chip_shift(CHIPS - d)) for d in (1, 3, 2)]
    terms[0], grad_scores[0] = chip_terms(0, *scores[0][:2], factors, query, up)
    dq, middle, theirs = query_grad(
        [scores[d][3] for d in range(CHIPS)], [grad_scores[d] for d in range(CHIPS)]
    )
    late, back, middle = lax.optimization_barrier((late, back, middle))
    middle_other = lax.ppermute(middle, "ctx", CORE)
    dkv = sum_four(terms[0], *back)
    dkv_other = lax.ppermute(dkv, "ctx", CORE)
    packed = pack(place, dq, middle_other, dkv, dkv_other)

    far, dkv = lax.optimization_barrier((far, dkv))
    tokens_t = transpose([own, late, far[1], far[3]])
    tokens_t, packed, theirs = lax.optimization_barrier((tokens_t, packed, theirs))
    dq_other = lax.ppermute(theirs, "ctx", CORE)
    other_t = lax.ppermute(tokens_t, "ctx", CORE)
    columns = {d: lax.ppermute(packed[d], "ctx", chip_shift(d)) for d in (2, 1, 3)}
    columns = [packed[0]] + [columns[d] for d in (2, 1, 3)]
    terms = [weight_grad(d, place, tokens_t, other_t, columns) for d in range(YS)]
    y_parts = [terms[0]] + [lax.ppermute(terms[d], "dp", y_shift(d)) for d in (1, 3, 2)]
    grad_tokens = input_grad(
        place, dq, dq_other, dkv, dkv_other, w_query, w_key, w_value
    )
    y_parts, grad_tokens = lax.optimization_barrier((y_parts, grad_tokens))
    y_sum = sum_four(*y_parts)
    z_parts = lax.all_to_all(y_sum, "dp", 0, 0, tiled=True, axis_index_groups=Z_GROUPS)
    grad_projection = final_sum(z_parts)
    return grad_tokens[None], grad_projection


def solution(mesh):
    return jax.shard_map(
        shards,
        mesh=mesh,
        in_specs=(
            P("dp", "ctx", None),
            P("dp", "ctx", None),
            P("dp", "ctx", None),
            P("dp", None),
            P(),
            P(),
            P(),
        ),
        out_specs=(P("dp", "ctx", None), P("dp", "ctx")),
        check_vma=False,
    )
```

```python
import functools
import math

import jax
import jax.numpy as jnp
from jax import lax
from jax.experimental import pallas as pl
from jax.experimental.pallas import tpu as pltpu
from jax.sharding import PartitionSpec as P

QH = 12
KVH = 2
HD = 128
TILE = 128
D = 1536
KEYS = 1024
CHIPS = 4
GROUP = QH // KVH
GF = GROUP * HD
STACK = GROUP * 256
YS = 4
ZS = 8
SCALE = 1.0 / math.sqrt(HD)
LOG2_SCALE = SCALE * math.log2(math.e)
BF = jnp.bfloat16
F32 = jnp.float32
VMEM_LIMIT = 24 * 1024 * 1024
W_CHUNKS = 1
Q_CHUNKS = 3
IN_CHUNKS = 3

CORE = [(i, i ^ 1) for i in range(8)]
NT = (((1,), (1,)), ((), ()))


def chip_shift(d):
    return [(i, ((i // 2 + d) % CHIPS) * 2 + i % 2) for i in range(8)]


def y_shift(d):
    return [(i, ((i // ZS + d) % YS) * ZS + i % ZS) for i in range(32)]


Z_GROUPS = [[y * ZS + z for z in range(ZS)] for y in range(YS)]


def dot(a, b):
    return jnp.dot(a, b, preferred_element_type=F32)


def dot_nt(a, b):
    return lax.dot_general(a, b, NT, preferred_element_type=F32)


def in_hbm(array):
    return pltpu.with_memory_space_constraint(array, pltpu.HBM)


def position():
    ctx, dp = lax.axis_index("ctx"), lax.axis_index("dp")
    return lax.div(ctx, 2), lax.rem(ctx, 2), lax.div(dp, ZS)


def cost(flops, bytes_accessed, transcendentals=0):
    return pl.CostEstimate(
        flops=1, bytes_accessed=1, transcendentals=0
    )


PARAMS = pltpu.CompilerParams(vmem_limit_bytes=VMEM_LIMIT)
WHOLE = pl.BlockSpec(memory_space=pltpu.VMEM)
SCALARS = pl.BlockSpec(memory_space=pltpu.SMEM)
STAY = pl.BlockSpec(memory_space=pltpu.HBM)


def kv_own_kernel(own, w_key, w_value, weights, out, rows, sems):
    _, core, _ = position()
    columns = pl.ds(pl.multiple_of(core * HD, HD), HD)
    copies = []
    for chunk in range(W_CHUNKS):
        part = pl.ds(chunk * (TILE // W_CHUNKS), TILE // W_CHUNKS)
        copies.append(pltpu.make_async_copy(own.at[part], rows.at[part], sems.at[chunk, 2]))
        part = pl.ds(chunk * (D // W_CHUNKS), D // W_CHUNKS)
        for side, source in enumerate((w_key, w_value)):
            copies.append(
                pltpu.make_async_copy(
                    source.at[part, columns],
                    weights.at[part, pl.ds(side * HD, HD)],
                    sems.at[chunk, side],
                )
            )
    for copy in copies:
        copy.start()
    for copy in copies:
        copy.wait()
    out[...] = dot(rows[...], weights[...]).astype(BF)


def project_kv_own(own, w_key, w_value):
    return pl.pallas_call(
        kv_own_kernel,
        in_specs=[STAY, STAY, STAY],
        out_specs=[WHOLE, WHOLE],
        out_shape=[
            jax.ShapeDtypeStruct((D, 2 * HD), BF),
            jax.ShapeDtypeStruct((TILE, 2 * HD), BF),
        ],
        scratch_shapes=[pltpu.VMEM((TILE, D), BF), pltpu.SemaphoreType.DMA((W_CHUNKS, 3))],
        compiler_params=PARAMS,
        cost_estimate=cost(2 * TILE * D * 256, 2 * (TILE * D + D * 256)),
        name="project_kv_own",
    )(own, w_key, w_value)


def kv_far_kernel(rows, weights, weights_other, mine, theirs):
    mine[...] = dot(rows[...], weights[...]).astype(BF)
    theirs[...] = dot(rows[...], weights_other[...]).astype(BF)


def project_kv_far(rows, weights, weights_other):
    return pl.pallas_call(
        kv_far_kernel,
        in_specs=[WHOLE] * 3,
        out_specs=[WHOLE] * 2,
        out_shape=[jax.ShapeDtypeStruct((TILE, 2 * HD), BF)] * 2,
        compiler_params=PARAMS,
        cost_estimate=cost(4 * TILE * D * 256, 2 * (TILE * D + 2 * D * 256)),
        name="project_kv_far",
    )(rows, weights, weights_other)


def kv_kernel(other, weights, kv_own, out):
    out[:TILE] = kv_own[...]
    out[TILE:] = dot(other[...], weights[...]).astype(BF)


def project_kv(other, weights, kv_own):
    return pl.pallas_call(
        kv_kernel,
        in_specs=[WHOLE] * 3,
        out_specs=WHOLE,
        out_shape=jax.ShapeDtypeStruct((2 * TILE, 2 * HD), BF),
        compiler_params=PARAMS,
        cost_estimate=cost(2 * TILE * D * 256, 2 * (TILE * D + D * 256)),
        name="project_kv",
    )(other, weights, kv_own)


def query_kernel(
    own, other, w_query, w_key, w_value, segments_far, mask_far, mask_other,
    out, limits, weights_other, weights, segments, mask_own, sems, small_sems,
):
    chip, core, _ = position()
    theirs = pl.ds(pl.multiple_of((1 - core) * HD, HD), HD)
    small = [
        pltpu.make_async_copy(segments_far, segments, small_sems.at[0]),
        pltpu.make_async_copy(mask_far, mask_own, small_sems.at[1]),
    ]
    for copy in small:
        copy.start()
    columns = pl.ds(pl.multiple_of(core * GF, HD), GF)
    copies = []
    for chunk in range(Q_CHUNKS):
        part = pl.ds(chunk * (D // Q_CHUNKS), D // Q_CHUNKS)
        copies.append(
            pltpu.make_async_copy(w_query.at[part, columns], weights.at[part], sems.at[chunk])
        )
    for side, source in enumerate((w_key, w_value)):
        copies.append(
            pltpu.make_async_copy(
                source.at[:, theirs],
                weights_other.at[:, pl.ds(side * HD, HD)],
                small_sems.at[2 + side],
            )
        )
    for copy in copies:
        copy.start()
    for copy in small:
        copy.wait()

    passages = segments[...]
    ends = [jnp.sum((passages <= s).astype(jnp.int32)) for s in range(3)]
    for slot in range(2):
        masks = mask_own if slot == 0 else mask_other
        tile = 2 * chip + (core if slot == 0 else 1 - core)
        mine = segments[:, pl.ds(pl.multiple_of(tile * TILE, TILE), TILE)]
        low = jnp.where(
            mine == 0, 0, jnp.where(mine == 1, ends[0], jnp.where(mine == 2, ends[1], ends[2]))
        )
        high = jnp.where(
            mine == 0, ends[0], jnp.where(mine == 1, ends[1], jnp.where(mine == 2, ends[2], KEYS))
        )
        for d in range(CHIPS):
            for key_slot in range(2):
                key_tile = 2 * lax.rem(chip + CHIPS - d, CHIPS) + (
                    core if key_slot == 0 else 1 - core
                )
                seen = masks[0, key_tile] == 1
                row = 4 * d + 2 * key_slot
                place_of = slice(slot * TILE, (slot + 1) * TILE)
                limits[row : row + 1, place_of] = jnp.where(seen, 0, low) - key_tile * TILE
                limits[row + 1 : row + 2, place_of] = (
                    jnp.where(seen, KEYS, high) - key_tile * TILE
                )

    for copy in copies:
        copy.wait()
    for slot, rows in enumerate((own, other)):
        queries = dot(rows[...], weights[...]).astype(BF)
        for head in range(GROUP):
            out[head * 256 + slot * TILE : head * 256 + (slot + 1) * TILE] = queries[
                :, head * HD : (head + 1) * HD
            ]


def project_query(
    own, other, w_query, w_key, w_value, segments, mask_own, mask_other
):
    return pl.pallas_call(
        query_kernel,
        in_specs=[WHOLE, WHOLE] + [STAY] * 5 + [SCALARS],
        out_specs=[WHOLE] * 3,
        out_shape=[
            jax.ShapeDtypeStruct((STACK, HD), BF),
            jax.ShapeDtypeStruct((4 * CHIPS, 2 * TILE), jnp.int32),
            jax.ShapeDtypeStruct((D, 2 * HD), BF),
        ],
        scratch_shapes=[
            pltpu.VMEM((D, GF), BF),
            pltpu.VMEM((1, KEYS), jnp.int32),
            pltpu.SMEM((1, KEYS // TILE), jnp.int32),
            pltpu.SemaphoreType.DMA((Q_CHUNKS,)),
            pltpu.SemaphoreType.DMA((4,)),
        ],
        compiler_params=PARAMS,
        cost_estimate=cost(2 * 256 * D * GF, 2 * (256 * D + D * GF + 256 * GF)),
        name="project_query",
    )(own, other, w_query, w_key, w_value, segments, mask_own, mask_other)


def stack_kernel(up_own, up_other, out):
    _, core, _ = position()
    for slot, rows in enumerate((up_own, up_other)):
        for head in range(GROUP):
            columns = pl.ds(pl.multiple_of(core * GF + head * HD, HD), HD)
            out[head * 256 + slot * TILE : head * 256 + (slot + 1) * TILE] = rows[:, columns]


def stack_up(up_own, up_other):
    return pl.pallas_call(
        stack_kernel,
        in_specs=[WHOLE, WHOLE],
        out_specs=WHOLE,
        out_shape=jax.ShapeDtypeStruct((STACK, HD), BF),
        compiler_params=PARAMS,
        cost_estimate=cost(0, 4 * STACK * HD),
        name="stack_up",
    )(up_own, up_other)


def scores_kernel(d, limits, query, up, *refs):
    powers, grads, stats, keys_t = refs[-4:]
    kv = jnp.concatenate([ref[...] for ref in refs[:-4]], axis=0)
    keys, values = kv[:, :HD], kv[:, HD:]
    keys_t[...] = keys.T
    position = lax.broadcasted_iota(jnp.int32, (TILE, 2 * TILE), 0)
    bias = []
    for key_slot in range(2):
        row = 4 * d + 2 * key_slot
        allowed = (position >= limits[row : row + 1]) & (position < limits[row + 1 : row + 2])
        bias.append(jnp.where(allowed, 0.0, -jnp.inf))
    bias = jnp.concatenate(bias, axis=0)
    for head in range(GROUP):
        part = slice(head * 256, (head + 1) * 256)
        scores = dot_nt(keys, query[part]) * LOG2_SCALE + bias
        top = jnp.max(scores, axis=0, keepdims=True)
        power = jnp.exp2(scores - jnp.where(top == -jnp.inf, 0.0, top))
        grad = dot_nt(values, up[part])
        powers[:, part] = power
        grads[:, part] = grad
        stats[0:1, part] = top
        stats[1:2, part] = jnp.sum(power, axis=0, keepdims=True)
        stats[2:3, part] = jnp.sum(power * grad, axis=0, keepdims=True)


def chip_scores(d, limits, query, up, *kv):
    return pl.pallas_call(
        functools.partial(scores_kernel, d),
        in_specs=[WHOLE] * (3 + len(kv)),
        out_specs=[WHOLE] * 4,
        out_shape=[
            jax.ShapeDtypeStruct((256, STACK), F32),
            jax.ShapeDtypeStruct((256, STACK), F32),
            jax.ShapeDtypeStruct((8, STACK), F32),
            jax.ShapeDtypeStruct((HD, 256), BF),
        ],
        compiler_params=PARAMS,
        cost_estimate=cost(4 * STACK * 256 * HD, 10 * 256 * STACK, 256 * STACK),
        name=f"chip_scores_{d}",
    )(limits, query, up, *kv)


def factors_kernel(a, b, c, d, out):
    parts = (a, b, c, d)
    top = jnp.maximum(jnp.maximum(a[0:1], b[0:1]), jnp.maximum(c[0:1], d[0:1]))
    factors = [jnp.exp2(part[0:1] - top) for part in parts]
    total = sum(factor * part[1:2] for factor, part in zip(factors, parts))
    factors = [factor / total for factor in factors]
    for chip, factor in enumerate(factors):
        out[chip : chip + 1] = factor
    out[4:5] = sum(factor * part[2:3] for factor, part in zip(factors, parts))


def softmax_factors(stats):
    return pl.pallas_call(
        factors_kernel,
        in_specs=[WHOLE] * 4,
        out_specs=WHOLE,
        out_shape=jax.ShapeDtypeStruct((8, STACK), F32),
        compiler_params=PARAMS,
        cost_estimate=cost(20 * STACK, 128 * STACK),
        name="softmax_factors",
    )(*stats)


def terms_kernel(d, powers, grads, factors, query, up, out, grad_scores, probs_low):
    for head in range(GROUP):
        part = slice(head * 256, (head + 1) * 256)
        probs = powers[:, part] * factors[d : d + 1, part]
        probs_low[:, part] = probs.astype(BF)
        grad_scores[:, part] = (probs * (grads[:, part] - factors[4:5, part])).astype(BF)
    out[:, :HD] = (dot(grad_scores[...], query[...]) * SCALE).astype(out.dtype)
    out[:, HD:] = dot(probs_low[...], up[...]).astype(out.dtype)


def chip_terms(d, powers, grads, factors, query, up):
    return pl.pallas_call(
        functools.partial(terms_kernel, d),
        in_specs=[WHOLE] * 5,
        out_specs=[WHOLE] * 2,
        out_shape=[
            jax.ShapeDtypeStruct((256, 256), F32 if d == 0 else BF),
            jax.ShapeDtypeStruct((256, STACK), BF),
        ],
        scratch_shapes=[pltpu.VMEM((256, STACK), BF)],
        compiler_params=PARAMS,
        cost_estimate=cost(4 * STACK * 256 * HD, 10 * 256 * STACK),
        name=f"chip_terms_{d}",
    )(powers, grads, factors, query, up)


def query_grad_kernel(k0, k1, k2, k3, g0, g1, g2, g3, out, middle, theirs):
    for head in range(GROUP):
        part = slice(head * 256, (head + 1) * 256)
        total = dot(k0[...], g0[:, part]) + dot(k1[...], g1[:, part])
        total += dot(k2[...], g2[:, part]) + dot(k3[...], g3[:, part])
        columns = slice(head * HD, (head + 1) * HD)
        result = (total * SCALE).T.astype(BF)
        out[:, columns] = result
        theirs[:, columns] = result[TILE:]
        if 2 <= head < 4:
            middle[:, (head - 2) * HD : (head - 1) * HD] = result


def query_grad(keys_t, grad_scores):
    return pl.pallas_call(
        query_grad_kernel,
        in_specs=[WHOLE] * 8,
        out_specs=[WHOLE] * 3,
        out_shape=[
            jax.ShapeDtypeStruct((256, GF), BF),
            jax.ShapeDtypeStruct((256, 256), BF),
            jax.ShapeDtypeStruct((TILE, GF), BF),
        ],
        compiler_params=PARAMS,
        cost_estimate=cost(2 * STACK * KEYS * HD, 2 * STACK * KEYS),
        name="query_grad",
    )(*keys_t, *grad_scores)


def sum_kernel(a, b, c, d, out):
    total = (a[...] + b[...].astype(F32)) + (c[...].astype(F32) + d[...].astype(F32))
    out[...] = total.astype(out.dtype)


def sum_four(a, b, c, d):
    return pl.pallas_call(
        sum_kernel,
        in_specs=[WHOLE] * 4,
        out_specs=WHOLE,
        out_shape=jax.ShapeDtypeStruct(a.shape, BF),
        compiler_params=PARAMS,
        cost_estimate=cost(4 * a.size, 12 * a.size),
        name="sum_four",
    )(a, b, c, d)


def pack_kernel(dq, middle_other, dkv, dkv_other, *outs):
    my_chip, my_core, _ = position()
    for core in range(2):
        own_part = slice(core * HD, (core + 1) * HD)
        for chip in range(CHIPS):

            @pl.when((my_core == core) & (my_chip == chip))
            def _(core=core, own_part=own_part, chip=chip):
                for d, out in enumerate(outs):
                    target = (chip + d) % CHIPS
                    if target == 3:
                        out[:, own_part] = dkv[:, own_part]
                        theirs = slice((1 - core) * HD, (2 - core) * HD)
                        out[:TILE, theirs] = dkv_other[TILE:, own_part]
                        out[TILE:, theirs] = dkv_other[:TILE, own_part]
                    elif target == 2 - 2 * core:
                        out[:TILE] = middle_other[TILE:]
                        out[TILE:] = middle_other[:TILE]
                    else:
                        first = target == core
                        out[...] = dq[:, 0:256] if first else dq[:, 512:768]


def pack(dq, middle_other, dkv, dkv_other):
    return pl.pallas_call(
        pack_kernel,
        in_specs=[WHOLE] * 4,
        out_specs=[WHOLE] * 4,
        out_shape=[jax.ShapeDtypeStruct((256, 256), BF)] * 4,
        compiler_params=PARAMS,
        cost_estimate=cost(0, 4 << 19),
        name="pack",
    )(dq, middle_other, dkv, dkv_other)


def transpose_kernel(own, far2, far1, far3, out):
    for i, rows in enumerate((own, far2, far1, far3)):
        out[:, i * TILE : (i + 1) * TILE] = rows[...].T


def transpose(parts):
    return pl.pallas_call(
        transpose_kernel,
        in_specs=[WHOLE] * 4,
        out_specs=WHOLE,
        out_shape=jax.ShapeDtypeStruct((D, KEYS // 2), BF),
        compiler_params=PARAMS,
        cost_estimate=cost(0, 2 * D * KEYS),
        name="transpose_tokens",
    )(*parts)


def weight_kernel(shift, tokens_t, other_t, a, b, c, d, out):
    parts = (a, b, c, d)
    right = jnp.concatenate([part[:TILE] for part in parts], axis=0)
    right_other = jnp.concatenate([part[TILE:] for part in parts], axis=0)
    _, _, chip = position()
    row = pl.multiple_of(lax.rem(chip + shift, YS) * (D // YS), 128)
    rows = pl.ds(row, D // YS)
    total = dot(tokens_t[rows], right) + dot(other_t[rows], right_other)
    out[...] = total.astype(out.dtype)


def weight_grad(shift, tokens_t, other_t, parts):
    return pl.pallas_call(
        functools.partial(weight_kernel, shift),
        in_specs=[WHOLE] * 6,
        out_specs=WHOLE,
        out_shape=jax.ShapeDtypeStruct((D // YS, 256), F32 if shift == 0 else BF),
        compiler_params=PARAMS,
        cost_estimate=cost(2 * D * KEYS * 256 // YS, 2 * D * KEYS // YS),
        name=f"weight_grad_{shift}",
    )(tokens_t, other_t, *parts)


def input_kernel(
    dq, dq_other, dkv, dkv_other, w_query, w_key, w_value, out, left, right, sems
):
    _, core, _ = position()
    width = D // IN_CHUNKS
    copies = []
    for chunk in range(IN_CHUNKS):
        part = pl.ds(chunk * width, width)
        copies.append(
            [
                pltpu.make_async_copy(
                    source.at[part],
                    right.at[part, pl.ds(start, size)],
                    sems.at[chunk, side],
                )
                for side, (source, start, size) in enumerate(
                    ((w_query, 0, D), (w_key, D, 256), (w_value, D + 256, 256))
                )
            ]
        )
    for group in copies:
        for copy in group:
            copy.start()
    mine = pl.ds(pl.multiple_of(core * GF, 128), GF)
    theirs = pl.ds(pl.multiple_of((1 - core) * GF, 128), GF)
    left[:, mine] = dq[:TILE]
    left[:, theirs] = dq_other[...]
    for part in range(2):
        columns = slice(part * HD, (part + 1) * HD)
        base = D + part * KVH * HD
        left[:, pl.ds(pl.multiple_of(base + core * HD, 128), HD)] = dkv[:TILE, columns]
        left[:, pl.ds(pl.multiple_of(base + (1 - core) * HD, 128), HD)] = dkv_other[
            TILE:, columns
        ]
    for chunk, group in enumerate(copies):
        for copy in group:
            copy.wait()
        part = slice(chunk * width, (chunk + 1) * width)
        out[:, part] = dot_nt(left[...], right[part]).astype(BF)


def input_grad(dq, dq_other, dkv, dkv_other, w_query, w_key, w_value):
    return pl.pallas_call(
        input_kernel,
        in_specs=[WHOLE] * 4 + [STAY] * 3,
        out_specs=WHOLE,
        out_shape=jax.ShapeDtypeStruct((TILE, D), BF),
        scratch_shapes=[
            pltpu.VMEM((TILE, D + 512), BF),
            pltpu.VMEM((D, D + 512), BF),
            pltpu.SemaphoreType.DMA((IN_CHUNKS, 3)),
        ],
        compiler_params=PARAMS,
        cost_estimate=cost(2 * TILE * D * 2048, 2 * D * 2048),
        name="input_grad",
    )(dq, dq_other, dkv, dkv_other, w_query, w_key, w_value)


def final_kernel(parts, out):
    total = parts[0:48].astype(F32)
    for z in range(1, ZS):
        total += parts[z * 48 : (z + 1) * 48].astype(F32)
    out[...] = total


def final_sum(parts):
    return pl.pallas_call(
        final_kernel,
        in_specs=[WHOLE],
        out_specs=WHOLE,
        out_shape=jax.ShapeDtypeStruct((48, 256), F32),
        compiler_params=PARAMS,
        cost_estimate=cost(parts.size, 2 * parts.size),
        name="final_sum",
    )(parts)


def shards(tokens, grad_heads, tile_mask, segments, w_query, w_key, w_value):
    own, up = tokens[0], grad_heads[0]
    other = lax.ppermute(own, "ctx", CORE)
    up_other = lax.ppermute(up, "ctx", CORE)
    mask_other = lax.ppermute(tile_mask[0], "ctx", CORE)
    other, mask_other, up_other = lax.optimization_barrier((other, mask_other, up_other))

    w_query, w_key, w_value = (in_hbm(w) for w in (w_query, w_key, w_value))
    weights, kv_own = project_kv_own(in_hbm(own), w_key, w_value)
    kv = project_kv(other, weights, kv_own)
    kv2 = lax.ppermute(kv, "ctx", chip_shift(2))
    far = {d: lax.ppermute(own, "ctx", chip_shift(d)) for d in (1, 3)}
    kv, other = lax.optimization_barrier((kv, other))
    query, limits, weights_other = project_query(
        own, other, w_query, w_key, w_value,
        in_hbm(segments), in_hbm(tile_mask[0]), mask_other,
    )
    query, late_own = lax.optimization_barrier((query, own))
    late = lax.ppermute(late_own, "ctx", chip_shift(2))
    up = stack_up(up, up_other)
    scores = {0: chip_scores(0, limits, query, up, kv)}
    far, scores[0] = lax.optimization_barrier((far, scores[0]))
    kv_far = {d: project_kv_far(far[d], weights, weights_other) for d in (1, 3)}
    for d in (1, 3):
        mine, theirs = kv_far[d]
        kv_far[d] = (mine, lax.ppermute(theirs, "ctx", CORE))
    for d in (1, 3):
        scores[d] = chip_scores(d, limits, query, up, *kv_far[d])
    scores[2] = chip_scores(2, limits, query, up, kv2)
    factors = softmax_factors([scores[d][2] for d in range(CHIPS)])
    terms, grad_scores = {}, {}
    for d in (3, 1, 2):
        terms[d], grad_scores[d] = chip_terms(d, *scores[d][:2], factors, query, up)
    back = [lax.ppermute(terms[d], "ctx", chip_shift(CHIPS - d)) for d in (1, 3, 2)]
    terms[0], grad_scores[0] = chip_terms(0, *scores[0][:2], factors, query, up)
    dq, middle, theirs = query_grad(
        [scores[d][3] for d in range(CHIPS)], [grad_scores[d] for d in range(CHIPS)]
    )
    late, back, middle = lax.optimization_barrier((late, back, middle))
    middle_other = lax.ppermute(middle, "ctx", CORE)
    dkv = sum_four(terms[0], *back)
    dkv_other = lax.ppermute(dkv, "ctx", CORE)
    packed = pack(dq, middle_other, dkv, dkv_other)

    far, dkv = lax.optimization_barrier((far, dkv))
    tokens_t = transpose([own, late, far[1], far[3]])
    tokens_t, packed, theirs = lax.optimization_barrier((tokens_t, packed, theirs))
    dq_other = lax.ppermute(theirs, "ctx", CORE)
    other_t = lax.ppermute(tokens_t, "ctx", CORE)
    columns = {d: lax.ppermute(packed[d], "ctx", chip_shift(d)) for d in (2, 1, 3)}
    columns = [packed[0]] + [columns[d] for d in (2, 1, 3)]
    terms = [weight_grad(d, tokens_t, other_t, columns) for d in range(YS)]
    y_parts = [terms[0]] + [lax.ppermute(terms[d], "dp", y_shift(d)) for d in (1, 3, 2)]
    grad_tokens = input_grad(
        dq, dq_other, dkv, dkv_other, w_query, w_key, w_value
    )
    y_parts, grad_tokens = lax.optimization_barrier((y_parts, grad_tokens))
    y_sum = sum_four(*y_parts)
    z_parts = lax.all_to_all(y_sum, "dp", 0, 0, tiled=True, axis_index_groups=Z_GROUPS)
    grad_projection = final_sum(z_parts)
    return grad_tokens[None], grad_projection


def solution(mesh):
    return jax.shard_map(
        shards,
        mesh=mesh,
        in_specs=(
            P("dp", "ctx", None),
            P("dp", "ctx", None),
            P("dp", "ctx", None),
            P("dp", None),
            P(),
            P(),
            P(),
        ),
        out_specs=(P("dp", "ctx", None), P("dp", "ctx")),
        check_vma=False,
    )
```

```python
import functools
import math

import jax
import jax.numpy as jnp
from jax import lax
from jax.experimental import pallas as pl
from jax.experimental.pallas import tpu as pltpu
from jax.sharding import PartitionSpec as P

QH = 12
KVH = 2
HD = 128
TILE = 128
D = 1536
KEYS = 1024
CHIPS = 4
GROUP = QH // KVH
GF = GROUP * HD
STACK = GROUP * 256
YS = 4
ZS = 8
SCALE = 1.0 / math.sqrt(HD)
LOG2_SCALE = SCALE * math.log2(math.e)
BF = jnp.bfloat16
F32 = jnp.float32
VMEM_LIMIT = 24 * 1024 * 1024
W_CHUNKS = 1
Q_CHUNKS = 3
IN_CHUNKS = 3

CORE = [(i, i ^ 1) for i in range(8)]
NT = (((1,), (1,)), ((), ()))


def chip_shift(d):
    return [(i, ((i // 2 + d) % CHIPS) * 2 + i % 2) for i in range(8)]


def y_shift(d):
    return [(i, ((i // ZS + d) % YS) * ZS + i % ZS) for i in range(32)]


Z_GROUPS = [[y * ZS + z for z in range(ZS)] for y in range(YS)]


def dot(a, b):
    return jnp.dot(a, b, preferred_element_type=F32)


def dot_nt(a, b):
    return lax.dot_general(a, b, NT, preferred_element_type=F32)


def in_hbm(array):
    return pltpu.with_memory_space_constraint(array, pltpu.HBM)


def position():
    ctx, dp = lax.axis_index("ctx"), lax.axis_index("dp")
    return lax.div(ctx, 2), lax.rem(ctx, 2), lax.div(dp, ZS)


def cost(flops, bytes_accessed, transcendentals=0):
    return pl.CostEstimate(
        flops=1, bytes_accessed=1, transcendentals=0
    )


PARAMS = pltpu.CompilerParams(vmem_limit_bytes=VMEM_LIMIT)
WHOLE = pl.BlockSpec(memory_space=pltpu.VMEM)
SCALARS = pl.BlockSpec(memory_space=pltpu.SMEM)
STAY = pl.BlockSpec(memory_space=pltpu.HBM)


def kv_own_kernel(own, w_key, w_value, weights, out, rows, sems):
    _, core, _ = position()
    columns = pl.ds(pl.multiple_of(core * HD, HD), HD)
    copies = []
    for chunk in range(W_CHUNKS):
        part = pl.ds(chunk * (TILE // W_CHUNKS), TILE // W_CHUNKS)
        copies.append(pltpu.make_async_copy(own.at[part], rows.at[part], sems.at[chunk, 2]))
        part = pl.ds(chunk * (D // W_CHUNKS), D // W_CHUNKS)
        for side, source in enumerate((w_key, w_value)):
            copies.append(
                pltpu.make_async_copy(
                    source.at[part, columns],
                    weights.at[part, pl.ds(side * HD, HD)],
                    sems.at[chunk, side],
                )
            )
    for copy in copies:
        copy.start()
    for copy in copies:
        copy.wait()
    out[...] = dot(rows[...], weights[...]).astype(BF)


def project_kv_own(own, w_key, w_value):
    return pl.pallas_call(
        kv_own_kernel,
        in_specs=[STAY, STAY, STAY],
        out_specs=[WHOLE, WHOLE],
        out_shape=[
            jax.ShapeDtypeStruct((D, 2 * HD), BF),
            jax.ShapeDtypeStruct((TILE, 2 * HD), BF),
        ],
        scratch_shapes=[pltpu.VMEM((TILE, D), BF), pltpu.SemaphoreType.DMA((W_CHUNKS, 3))],
        compiler_params=PARAMS,
        cost_estimate=cost(2 * TILE * D * 256, 2 * (TILE * D + D * 256)),
        name="project_kv_own",
    )(own, w_key, w_value)


def kv_far_kernel(far1, far3, weights, weights_other, mine, theirs):
    for i, rows in enumerate((far1, far3)):
        part = slice(i * TILE, (i + 1) * TILE)
        theirs[part] = dot(rows[...], weights_other[...]).astype(BF)
        mine[part] = dot(rows[...], weights[...]).astype(BF)


def project_kv_far(far1, far3, weights, weights_other):
    return pl.pallas_call(
        kv_far_kernel,
        in_specs=[WHOLE] * 4,
        out_specs=[WHOLE] * 2,
        out_shape=[jax.ShapeDtypeStruct((2 * TILE, 2 * HD), BF)] * 2,
        compiler_params=PARAMS,
        cost_estimate=cost(8 * TILE * D * 256, 4 * (TILE * D + D * 256)),
        name="project_kv_far",
    )(far1, far3, weights, weights_other)


def kv_kernel(other, weights, kv_own, out):
    out[:TILE] = kv_own[...]
    out[TILE:] = dot(other[...], weights[...]).astype(BF)


def project_kv(other, weights, kv_own):
    return pl.pallas_call(
        kv_kernel,
        in_specs=[WHOLE] * 3,
        out_specs=WHOLE,
        out_shape=jax.ShapeDtypeStruct((2 * TILE, 2 * HD), BF),
        compiler_params=PARAMS,
        cost_estimate=cost(2 * TILE * D * 256, 2 * (TILE * D + D * 256)),
        name="project_kv",
    )(other, weights, kv_own)


def query_kernel(
    own, other, w_query, w_key, w_value, segments_far, mask_far, mask_other,
    out, limits, weights_other, weights, segments, mask_own, sems, small_sems,
):
    chip, core, _ = position()
    theirs = pl.ds(pl.multiple_of((1 - core) * HD, HD), HD)
    small = [
        pltpu.make_async_copy(segments_far, segments, small_sems.at[0]),
        pltpu.make_async_copy(mask_far, mask_own, small_sems.at[1]),
    ]
    for copy in small:
        copy.start()
    columns = pl.ds(pl.multiple_of(core * GF, HD), GF)
    copies = []
    for chunk in range(Q_CHUNKS):
        part = pl.ds(chunk * (D // Q_CHUNKS), D // Q_CHUNKS)
        copies.append(
            pltpu.make_async_copy(w_query.at[part, columns], weights.at[part], sems.at[chunk])
        )
    for side, source in enumerate((w_key, w_value)):
        copies.append(
            pltpu.make_async_copy(
                source.at[:, theirs],
                weights_other.at[:, pl.ds(side * HD, HD)],
                small_sems.at[2 + side],
            )
        )
    for copy in copies:
        copy.start()
    for copy in small:
        copy.wait()

    passages = segments[...]
    ends = [jnp.sum((passages <= s).astype(jnp.int32)) for s in range(3)]
    for slot in range(2):
        masks = mask_own if slot == 0 else mask_other
        tile = 2 * chip + (core if slot == 0 else 1 - core)
        mine = segments[:, pl.ds(pl.multiple_of(tile * TILE, TILE), TILE)]
        low = jnp.where(
            mine == 0, 0, jnp.where(mine == 1, ends[0], jnp.where(mine == 2, ends[1], ends[2]))
        )
        high = jnp.where(
            mine == 0, ends[0], jnp.where(mine == 1, ends[1], jnp.where(mine == 2, ends[2], KEYS))
        )
        for d in range(CHIPS):
            for key_slot in range(2):
                key_tile = 2 * lax.rem(chip + CHIPS - d, CHIPS) + (
                    core if key_slot == 0 else 1 - core
                )
                seen = masks[0, key_tile] == 1
                row = 4 * d + 2 * key_slot
                place_of = slice(slot * TILE, (slot + 1) * TILE)
                limits[row : row + 1, place_of] = jnp.where(seen, 0, low) - key_tile * TILE
                limits[row + 1 : row + 2, place_of] = (
                    jnp.where(seen, KEYS, high) - key_tile * TILE
                )

    for copy in copies:
        copy.wait()
    for slot, rows in enumerate((own, other)):
        queries = dot(rows[...], weights[...]).astype(BF)
        for head in range(GROUP):
            out[head * 256 + slot * TILE : head * 256 + (slot + 1) * TILE] = queries[
                :, head * HD : (head + 1) * HD
            ]


def project_query(
    own, other, w_query, w_key, w_value, segments, mask_own, mask_other
):
    return pl.pallas_call(
        query_kernel,
        in_specs=[WHOLE, WHOLE] + [STAY] * 5 + [SCALARS],
        out_specs=[WHOLE] * 3,
        out_shape=[
            jax.ShapeDtypeStruct((STACK, HD), BF),
            jax.ShapeDtypeStruct((4 * CHIPS, 2 * TILE), jnp.int32),
            jax.ShapeDtypeStruct((D, 2 * HD), BF),
        ],
        scratch_shapes=[
            pltpu.VMEM((D, GF), BF),
            pltpu.VMEM((1, KEYS), jnp.int32),
            pltpu.SMEM((1, KEYS // TILE), jnp.int32),
            pltpu.SemaphoreType.DMA((Q_CHUNKS,)),
            pltpu.SemaphoreType.DMA((4,)),
        ],
        compiler_params=PARAMS,
        cost_estimate=cost(2 * 256 * D * GF, 2 * (256 * D + D * GF + 256 * GF)),
        name="project_query",
    )(own, other, w_query, w_key, w_value, segments, mask_own, mask_other)


def stack_kernel(up_own, up_other, out):
    _, core, _ = position()
    for slot, rows in enumerate((up_own, up_other)):
        for head in range(GROUP):
            columns = pl.ds(pl.multiple_of(core * GF + head * HD, HD), HD)
            out[head * 256 + slot * TILE : head * 256 + (slot + 1) * TILE] = rows[:, columns]


def stack_up(up_own, up_other):
    return pl.pallas_call(
        stack_kernel,
        in_specs=[WHOLE, WHOLE],
        out_specs=WHOLE,
        out_shape=jax.ShapeDtypeStruct((STACK, HD), BF),
        compiler_params=PARAMS,
        cost_estimate=cost(0, 4 * STACK * HD),
        name="stack_up",
    )(up_own, up_other)


def scores_kernel(d, part, limits, query, up, *refs):
    powers, grads, stats, keys_t = refs[-4:]
    rows = slice(None) if part is None else slice(part * TILE, (part + 1) * TILE)
    kv = jnp.concatenate([ref[rows] for ref in refs[:-4]], axis=0)
    keys, values = kv[:, :HD], kv[:, HD:]
    keys_t[...] = keys.T
    position = lax.broadcasted_iota(jnp.int32, (TILE, 2 * TILE), 0)
    bias = []
    for key_slot in range(2):
        row = 4 * d + 2 * key_slot
        allowed = (position >= limits[row : row + 1]) & (position < limits[row + 1 : row + 2])
        bias.append(jnp.where(allowed, 0.0, -jnp.inf))
    bias = jnp.concatenate(bias, axis=0)
    for head in range(GROUP):
        part = slice(head * 256, (head + 1) * 256)
        scores = dot_nt(keys, query[part]) * LOG2_SCALE + bias
        top = jnp.max(scores, axis=0, keepdims=True)
        power = jnp.exp2(scores - jnp.where(top == -jnp.inf, 0.0, top))
        grad = dot_nt(values, up[part])
        powers[:, part] = power
        grads[:, part] = grad
        stats[0:1, part] = top
        stats[1:2, part] = jnp.sum(power, axis=0, keepdims=True)
        stats[2:3, part] = jnp.sum(power * grad, axis=0, keepdims=True)


def chip_scores(d, limits, query, up, *kv, part=None):
    return pl.pallas_call(
        functools.partial(scores_kernel, d, part),
        in_specs=[WHOLE] * (3 + len(kv)),
        out_specs=[WHOLE] * 4,
        out_shape=[
            jax.ShapeDtypeStruct((256, STACK), F32),
            jax.ShapeDtypeStruct((256, STACK), F32),
            jax.ShapeDtypeStruct((8, STACK), F32),
            jax.ShapeDtypeStruct((HD, 256), BF),
        ],
        compiler_params=PARAMS,
        cost_estimate=cost(4 * STACK * 256 * HD, 10 * 256 * STACK, 256 * STACK),
        name=f"chip_scores_{d}",
    )(limits, query, up, *kv)


def factors_kernel(a, b, c, d, out):
    parts = (a, b, c, d)
    top = jnp.maximum(jnp.maximum(a[0:1], b[0:1]), jnp.maximum(c[0:1], d[0:1]))
    factors = [jnp.exp2(part[0:1] - top) for part in parts]
    total = sum(factor * part[1:2] for factor, part in zip(factors, parts))
    factors = [factor / total for factor in factors]
    for chip, factor in enumerate(factors):
        out[chip : chip + 1] = factor
    out[4:5] = sum(factor * part[2:3] for factor, part in zip(factors, parts))


def softmax_factors(stats):
    return pl.pallas_call(
        factors_kernel,
        in_specs=[WHOLE] * 4,
        out_specs=WHOLE,
        out_shape=jax.ShapeDtypeStruct((8, STACK), F32),
        compiler_params=PARAMS,
        cost_estimate=cost(20 * STACK, 128 * STACK),
        name="softmax_factors",
    )(*stats)


def terms_kernel(d, powers, grads, factors, query, up, out, grad_scores, probs_low):
    for head in range(GROUP):
        part = slice(head * 256, (head + 1) * 256)
        probs = powers[:, part] * factors[d : d + 1, part]
        probs_low[:, part] = probs.astype(BF)
        grad_scores[:, part] = (probs * (grads[:, part] - factors[4:5, part])).astype(BF)
    out[:, :HD] = (dot(grad_scores[...], query[...]) * SCALE).astype(out.dtype)
    out[:, HD:] = dot(probs_low[...], up[...]).astype(out.dtype)


def chip_terms(d, powers, grads, factors, query, up):
    return pl.pallas_call(
        functools.partial(terms_kernel, d),
        in_specs=[WHOLE] * 5,
        out_specs=[WHOLE] * 2,
        out_shape=[
            jax.ShapeDtypeStruct((256, 256), F32 if d == 0 else BF),
            jax.ShapeDtypeStruct((256, STACK), BF),
        ],
        scratch_shapes=[pltpu.VMEM((256, STACK), BF)],
        compiler_params=PARAMS,
        cost_estimate=cost(4 * STACK * 256 * HD, 10 * 256 * STACK),
        name=f"chip_terms_{d}",
    )(powers, grads, factors, query, up)


def query_grad_kernel(k0, k1, k2, k3, g0, g1, g2, g3, out, middle, theirs):
    for head in range(GROUP):
        part = slice(head * 256, (head + 1) * 256)
        total = dot(k0[...], g0[:, part]) + dot(k1[...], g1[:, part])
        total += dot(k2[...], g2[:, part]) + dot(k3[...], g3[:, part])
        columns = slice(head * HD, (head + 1) * HD)
        result = (total * SCALE).T.astype(BF)
        out[:, columns] = result
        theirs[:, columns] = result[TILE:]
        if 2 <= head < 4:
            middle[:, (head - 2) * HD : (head - 1) * HD] = result


def query_grad(keys_t, grad_scores):
    return pl.pallas_call(
        query_grad_kernel,
        in_specs=[WHOLE] * 8,
        out_specs=[WHOLE] * 3,
        out_shape=[
            jax.ShapeDtypeStruct((256, GF), BF),
            jax.ShapeDtypeStruct((256, 256), BF),
            jax.ShapeDtypeStruct((TILE, GF), BF),
        ],
        compiler_params=PARAMS,
        cost_estimate=cost(2 * STACK * KEYS * HD, 2 * STACK * KEYS),
        name="query_grad",
    )(*keys_t, *grad_scores)


def sum_kernel(a, b, c, d, out):
    total = (a[...] + b[...].astype(F32)) + (c[...].astype(F32) + d[...].astype(F32))
    out[...] = total.astype(out.dtype)


def sum_four(a, b, c, d):
    return pl.pallas_call(
        sum_kernel,
        in_specs=[WHOLE] * 4,
        out_specs=WHOLE,
        out_shape=jax.ShapeDtypeStruct(a.shape, BF),
        compiler_params=PARAMS,
        cost_estimate=cost(4 * a.size, 12 * a.size),
        name="sum_four",
    )(a, b, c, d)


def pack_kernel(dq, middle_other, dkv, dkv_other, *outs):
    my_chip, my_core, _ = position()
    for core in range(2):
        own_part = slice(core * HD, (core + 1) * HD)
        for chip in range(CHIPS):

            @pl.when((my_core == core) & (my_chip == chip))
            def _(core=core, own_part=own_part, chip=chip):
                for d, out in enumerate(outs):
                    target = (chip + d) % CHIPS
                    if target == 3:
                        out[:, own_part] = dkv[:, own_part]
                        theirs = slice((1 - core) * HD, (2 - core) * HD)
                        out[:TILE, theirs] = dkv_other[TILE:, own_part]
                        out[TILE:, theirs] = dkv_other[:TILE, own_part]
                    elif target == 2 - 2 * core:
                        out[:TILE] = middle_other[TILE:]
                        out[TILE:] = middle_other[:TILE]
                    else:
                        first = target == core
                        out[...] = dq[:, 0:256] if first else dq[:, 512:768]


def pack(dq, middle_other, dkv, dkv_other):
    return pl.pallas_call(
        pack_kernel,
        in_specs=[WHOLE] * 4,
        out_specs=[WHOLE] * 4,
        out_shape=[jax.ShapeDtypeStruct((256, 256), BF)] * 4,
        compiler_params=PARAMS,
        cost_estimate=cost(0, 4 << 19),
        name="pack",
    )(dq, middle_other, dkv, dkv_other)


def transpose_kernel(own, far2, far1, far3, out):
    for i, rows in enumerate((own, far2, far1, far3)):
        out[:, i * TILE : (i + 1) * TILE] = rows[...].T


def transpose(parts):
    return pl.pallas_call(
        transpose_kernel,
        in_specs=[WHOLE] * 4,
        out_specs=WHOLE,
        out_shape=jax.ShapeDtypeStruct((D, KEYS // 2), BF),
        compiler_params=PARAMS,
        cost_estimate=cost(0, 2 * D * KEYS),
        name="transpose_tokens",
    )(*parts)


def weight_kernel(shift, tokens_t, other_t, a, b, c, d, out):
    parts = (a, b, c, d)
    right = jnp.concatenate([part[:TILE] for part in parts], axis=0)
    right_other = jnp.concatenate([part[TILE:] for part in parts], axis=0)
    _, _, chip = position()
    row = pl.multiple_of(lax.rem(chip + shift, YS) * (D // YS), 128)
    rows = pl.ds(row, D // YS)
    total = dot(tokens_t[rows], right) + dot(other_t[rows], right_other)
    out[...] = total.astype(out.dtype)


def weight_grad(shift, tokens_t, other_t, parts):
    return pl.pallas_call(
        functools.partial(weight_kernel, shift),
        in_specs=[WHOLE] * 6,
        out_specs=WHOLE,
        out_shape=jax.ShapeDtypeStruct((D // YS, 256), F32 if shift == 0 else BF),
        compiler_params=PARAMS,
        cost_estimate=cost(2 * D * KEYS * 256 // YS, 2 * D * KEYS // YS),
        name=f"weight_grad_{shift}",
    )(tokens_t, other_t, *parts)


def input_kernel(
    dq, dq_other, dkv, dkv_other, w_query, w_key, w_value, out, left, right, sems
):
    _, core, _ = position()
    width = D // IN_CHUNKS
    copies = []
    for chunk in range(IN_CHUNKS):
        part = pl.ds(chunk * width, width)
        copies.append(
            [
                pltpu.make_async_copy(
                    source.at[part],
                    right.at[part, pl.ds(start, size)],
                    sems.at[chunk, side],
                )
                for side, (source, start, size) in enumerate(
                    ((w_query, 0, D), (w_key, D, 256), (w_value, D + 256, 256))
                )
            ]
        )
    for group in copies:
        for copy in group:
            copy.start()
    mine = pl.ds(pl.multiple_of(core * GF, 128), GF)
    theirs = pl.ds(pl.multiple_of((1 - core) * GF, 128), GF)
    left[:, mine] = dq[:TILE]
    left[:, theirs] = dq_other[...]
    for part in range(2):
        columns = slice(part * HD, (part + 1) * HD)
        base = D + part * KVH * HD
        left[:, pl.ds(pl.multiple_of(base + core * HD, 128), HD)] = dkv[:TILE, columns]
        left[:, pl.ds(pl.multiple_of(base + (1 - core) * HD, 128), HD)] = dkv_other[
            TILE:, columns
        ]
    for chunk, group in enumerate(copies):
        for copy in group:
            copy.wait()
        part = slice(chunk * width, (chunk + 1) * width)
        out[:, part] = dot_nt(left[...], right[part]).astype(BF)


def input_grad(dq, dq_other, dkv, dkv_other, w_query, w_key, w_value):
    return pl.pallas_call(
        input_kernel,
        in_specs=[WHOLE] * 4 + [STAY] * 3,
        out_specs=WHOLE,
        out_shape=jax.ShapeDtypeStruct((TILE, D), BF),
        scratch_shapes=[
            pltpu.VMEM((TILE, D + 512), BF),
            pltpu.VMEM((D, D + 512), BF),
            pltpu.SemaphoreType.DMA((IN_CHUNKS, 3)),
        ],
        compiler_params=PARAMS,
        cost_estimate=cost(2 * TILE * D * 2048, 2 * D * 2048),
        name="input_grad",
    )(dq, dq_other, dkv, dkv_other, w_query, w_key, w_value)


def final_kernel(parts, out):
    total = parts[0:48].astype(F32)
    for z in range(1, ZS):
        total += parts[z * 48 : (z + 1) * 48].astype(F32)
    out[...] = total


def final_sum(parts):
    return pl.pallas_call(
        final_kernel,
        in_specs=[WHOLE],
        out_specs=WHOLE,
        out_shape=jax.ShapeDtypeStruct((48, 256), F32),
        compiler_params=PARAMS,
        cost_estimate=cost(parts.size, 2 * parts.size),
        name="final_sum",
    )(parts)


def shards(tokens, grad_heads, tile_mask, segments, w_query, w_key, w_value):
    own, up = tokens[0], grad_heads[0]
    other = lax.ppermute(own, "ctx", CORE)
    up_other = lax.ppermute(up, "ctx", CORE)
    mask_other = lax.ppermute(tile_mask[0], "ctx", CORE)
    other, mask_other, up_other = lax.optimization_barrier((other, mask_other, up_other))

    w_query, w_key, w_value = (in_hbm(w) for w in (w_query, w_key, w_value))
    weights, kv_own = project_kv_own(in_hbm(own), w_key, w_value)
    kv = project_kv(other, weights, kv_own)
    kv2 = lax.ppermute(kv, "ctx", chip_shift(2))
    far = {d: lax.ppermute(own, "ctx", chip_shift(d)) for d in (1, 3)}
    query, limits, weights_other = project_query(
        own, other, w_query, w_key, w_value,
        in_hbm(segments), in_hbm(tile_mask[0]), mask_other,
    )
    up = stack_up(up, up_other)
    scores = {0: chip_scores(0, limits, query, up, kv)}
    far, kv2, scores[0] = lax.optimization_barrier((far, kv2, scores[0]))
    late = lax.ppermute(far[1], "ctx", chip_shift(1))
    mine, theirs = project_kv_far(far[1], far[3], weights, weights_other)
    theirs = lax.ppermute(theirs, "ctx", CORE)
    for i, d in enumerate((1, 3)):
        scores[d] = chip_scores(d, limits, query, up, mine, theirs, part=i)
    scores[2] = chip_scores(2, limits, query, up, kv2)
    factors = softmax_factors([scores[d][2] for d in range(CHIPS)])
    terms, grad_scores = {}, {}
    for d in (3, 1, 2):
        terms[d], grad_scores[d] = chip_terms(d, *scores[d][:2], factors, query, up)
    back = [lax.ppermute(terms[d], "ctx", chip_shift(CHIPS - d)) for d in (1, 3, 2)]
    terms[0], grad_scores[0] = chip_terms(0, *scores[0][:2], factors, query, up)
    dq, middle, theirs = query_grad(
        [scores[d][3] for d in range(CHIPS)], [grad_scores[d] for d in range(CHIPS)]
    )
    late, back, middle = lax.optimization_barrier((late, back, middle))
    middle_other = lax.ppermute(middle, "ctx", CORE)
    dkv = sum_four(terms[0], *back)
    dkv_other = lax.ppermute(dkv, "ctx", CORE)
    packed = pack(dq, middle_other, dkv, dkv_other)

    far, dkv = lax.optimization_barrier((far, dkv))
    tokens_t = transpose([own, late, far[1], far[3]])
    tokens_t, packed, theirs = lax.optimization_barrier((tokens_t, packed, theirs))
    dq_other = lax.ppermute(theirs, "ctx", CORE)
    other_t = lax.ppermute(tokens_t, "ctx", CORE)
    columns = {d: lax.ppermute(packed[d], "ctx", chip_shift(d)) for d in (2, 1, 3)}
    columns = [packed[0]] + [columns[d] for d in (2, 1, 3)]
    terms = [weight_grad(d, tokens_t, other_t, columns) for d in range(YS)]
    y_parts = [terms[0]] + [lax.ppermute(terms[d], "dp", y_shift(d)) for d in (1, 3, 2)]
    grad_tokens = input_grad(
        dq, dq_other, dkv, dkv_other, w_query, w_key, w_value
    )
    y_parts, grad_tokens = lax.optimization_barrier((y_parts, grad_tokens))
    y_sum = sum_four(*y_parts)
    z_parts = lax.all_to_all(y_sum, "dp", 0, 0, tiled=True, axis_index_groups=Z_GROUPS)
    grad_projection = final_sum(z_parts)
    return grad_tokens[None], grad_projection


def solution(mesh):
    return jax.shard_map(
        shards,
        mesh=mesh,
        in_specs=(
            P("dp", "ctx", None),
            P("dp", "ctx", None),
            P("dp", "ctx", None),
            P("dp", None),
            P(),
            P(),
            P(),
        ),
        out_specs=(P("dp", "ctx", None), P("dp", "ctx")),
        check_vma=False,
    )
```

```python
import functools
import math

import jax
import jax.numpy as jnp
from jax import lax
from jax.experimental import pallas as pl
from jax.experimental.pallas import tpu as pltpu
from jax.sharding import PartitionSpec as P

QH = 12
KVH = 2
HD = 128
TILE = 128
D = 1536
KEYS = 1024
CHIPS = 4
GROUP = QH // KVH
GF = GROUP * HD
STACK = GROUP * 256
YS = 4
ZS = 8
SCALE = 1.0 / math.sqrt(HD)
LOG2_SCALE = SCALE * math.log2(math.e)
BF = jnp.bfloat16
F32 = jnp.float32
VMEM_LIMIT = 24 * 1024 * 1024
W_CHUNKS = 1
Q_CHUNKS = 3
IN_CHUNKS = 3

CORE = [(i, i ^ 1) for i in range(8)]
NT = (((1,), (1,)), ((), ()))


def chip_shift(d):
    return [(i, ((i // 2 + d) % CHIPS) * 2 + i % 2) for i in range(8)]


def y_shift(d):
    return [(i, ((i // ZS + d) % YS) * ZS + i % ZS) for i in range(32)]


Z_GROUPS = [[y * ZS + z for z in range(ZS)] for y in range(YS)]


def dot(a, b):
    return jnp.dot(a, b, preferred_element_type=F32)


def dot_nt(a, b):
    return lax.dot_general(a, b, NT, preferred_element_type=F32)


def in_hbm(array):
    return pltpu.with_memory_space_constraint(array, pltpu.HBM)


def position():
    ctx, dp = lax.axis_index("ctx"), lax.axis_index("dp")
    return lax.div(ctx, 2), lax.rem(ctx, 2), lax.div(dp, ZS)


def cost(flops, bytes_accessed, transcendentals=0):
    return pl.CostEstimate(
        flops=1, bytes_accessed=1, transcendentals=0
    )


PARAMS = pltpu.CompilerParams(vmem_limit_bytes=VMEM_LIMIT)
WHOLE = pl.BlockSpec(memory_space=pltpu.VMEM)
SCALARS = pl.BlockSpec(memory_space=pltpu.SMEM)
STAY = pl.BlockSpec(memory_space=pltpu.HBM)


def kv_own_kernel(own, w_key, w_value, weights, out, rows, sems):
    _, core, _ = position()
    columns = pl.ds(pl.multiple_of(core * HD, HD), HD)
    copies = []
    for chunk in range(W_CHUNKS):
        part = pl.ds(chunk * (TILE // W_CHUNKS), TILE // W_CHUNKS)
        copies.append(pltpu.make_async_copy(own.at[part], rows.at[part], sems.at[chunk, 2]))
        part = pl.ds(chunk * (D // W_CHUNKS), D // W_CHUNKS)
        for side, source in enumerate((w_key, w_value)):
            copies.append(
                pltpu.make_async_copy(
                    source.at[part, columns],
                    weights.at[part, pl.ds(side * HD, HD)],
                    sems.at[chunk, side],
                )
            )
    for copy in copies:
        copy.start()
    for copy in copies:
        copy.wait()
    out[...] = dot(rows[...], weights[...]).astype(BF)


def project_kv_own(own, w_key, w_value):
    return pl.pallas_call(
        kv_own_kernel,
        in_specs=[STAY, STAY, STAY],
        out_specs=[WHOLE, WHOLE],
        out_shape=[
            jax.ShapeDtypeStruct((D, 2 * HD), BF),
            jax.ShapeDtypeStruct((TILE, 2 * HD), BF),
        ],
        scratch_shapes=[pltpu.VMEM((TILE, D), BF), pltpu.SemaphoreType.DMA((W_CHUNKS, 3))],
        compiler_params=PARAMS,
        cost_estimate=cost(2 * TILE * D * 256, 2 * (TILE * D + D * 256)),
        name="project_kv_own",
    )(own, w_key, w_value)


def kv_far_kernel(far1, far3, weights, weights_other, mine, theirs):
    for i, rows in enumerate((far1, far3)):
        part = slice(i * TILE, (i + 1) * TILE)
        theirs[part] = dot(rows[...], weights_other[...]).astype(BF)
        mine[part] = dot(rows[...], weights[...]).astype(BF)


def project_kv_far(far1, far3, weights, weights_other):
    return pl.pallas_call(
        kv_far_kernel,
        in_specs=[WHOLE] * 4,
        out_specs=[WHOLE] * 2,
        out_shape=[jax.ShapeDtypeStruct((2 * TILE, 2 * HD), BF)] * 2,
        compiler_params=PARAMS,
        cost_estimate=cost(8 * TILE * D * 256, 4 * (TILE * D + D * 256)),
        name="project_kv_far",
    )(far1, far3, weights, weights_other)


def kv_kernel(other, weights, kv_own, out):
    out[:TILE] = kv_own[...]
    out[TILE:] = dot(other[...], weights[...]).astype(BF)


def project_kv(other, weights, kv_own):
    return pl.pallas_call(
        kv_kernel,
        in_specs=[WHOLE] * 3,
        out_specs=WHOLE,
        out_shape=jax.ShapeDtypeStruct((2 * TILE, 2 * HD), BF),
        compiler_params=PARAMS,
        cost_estimate=cost(2 * TILE * D * 256, 2 * (TILE * D + D * 256)),
        name="project_kv",
    )(other, weights, kv_own)


def query_kernel(
    own, other, w_query, w_key, w_value, segments_far, mask_far, mask_other,
    out, limits, weights_other, weights, segments, mask_own, sems, small_sems,
):
    chip, core, _ = position()
    theirs = pl.ds(pl.multiple_of((1 - core) * HD, HD), HD)
    small = [
        pltpu.make_async_copy(segments_far, segments, small_sems.at[0]),
        pltpu.make_async_copy(mask_far, mask_own, small_sems.at[1]),
    ]
    for copy in small:
        copy.start()
    columns = pl.ds(pl.multiple_of(core * GF, HD), GF)
    copies = []
    for chunk in range(Q_CHUNKS):
        part = pl.ds(chunk * (D // Q_CHUNKS), D // Q_CHUNKS)
        copies.append(
            pltpu.make_async_copy(w_query.at[part, columns], weights.at[part], sems.at[chunk])
        )
    for side, source in enumerate((w_key, w_value)):
        copies.append(
            pltpu.make_async_copy(
                source.at[:, theirs],
                weights_other.at[:, pl.ds(side * HD, HD)],
                small_sems.at[2 + side],
            )
        )
    for copy in copies:
        copy.start()
    for copy in small:
        copy.wait()

    passages = segments[...]
    ends = [jnp.sum((passages <= s).astype(jnp.int32)) for s in range(3)]
    for slot in range(2):
        masks = mask_own if slot == 0 else mask_other
        tile = 2 * chip + (core if slot == 0 else 1 - core)
        mine = segments[:, pl.ds(pl.multiple_of(tile * TILE, TILE), TILE)]
        low = jnp.where(
            mine == 0, 0, jnp.where(mine == 1, ends[0], jnp.where(mine == 2, ends[1], ends[2]))
        )
        high = jnp.where(
            mine == 0, ends[0], jnp.where(mine == 1, ends[1], jnp.where(mine == 2, ends[2], KEYS))
        )
        for d in range(CHIPS):
            for key_slot in range(2):
                key_tile = 2 * lax.rem(chip + CHIPS - d, CHIPS) + (
                    core if key_slot == 0 else 1 - core
                )
                seen = masks[0, key_tile] == 1
                row = 4 * d + 2 * key_slot
                place_of = slice(slot * TILE, (slot + 1) * TILE)
                limits[row : row + 1, place_of] = jnp.where(seen, 0, low) - key_tile * TILE
                limits[row + 1 : row + 2, place_of] = (
                    jnp.where(seen, KEYS, high) - key_tile * TILE
                )

    for copy in copies:
        copy.wait()
    for slot, rows in enumerate((own, other)):
        queries = dot(rows[...], weights[...]).astype(BF)
        for head in range(GROUP):
            out[head * 256 + slot * TILE : head * 256 + (slot + 1) * TILE] = queries[
                :, head * HD : (head + 1) * HD
            ]


def project_query(
    own, other, w_query, w_key, w_value, segments, mask_own, mask_other
):
    return pl.pallas_call(
        query_kernel,
        in_specs=[WHOLE, WHOLE] + [STAY] * 5 + [SCALARS],
        out_specs=[WHOLE] * 3,
        out_shape=[
            jax.ShapeDtypeStruct((STACK, HD), BF),
            jax.ShapeDtypeStruct((4 * CHIPS, 2 * TILE), jnp.int32),
            jax.ShapeDtypeStruct((D, 2 * HD), BF),
        ],
        scratch_shapes=[
            pltpu.VMEM((D, GF), BF),
            pltpu.VMEM((1, KEYS), jnp.int32),
            pltpu.SMEM((1, KEYS // TILE), jnp.int32),
            pltpu.SemaphoreType.DMA((Q_CHUNKS,)),
            pltpu.SemaphoreType.DMA((4,)),
        ],
        compiler_params=PARAMS,
        cost_estimate=cost(2 * 256 * D * GF, 2 * (256 * D + D * GF + 256 * GF)),
        name="project_query",
    )(own, other, w_query, w_key, w_value, segments, mask_own, mask_other)


def stack_kernel(up_own, up_other, out):
    _, core, _ = position()
    for slot, rows in enumerate((up_own, up_other)):
        for head in range(GROUP):
            columns = pl.ds(pl.multiple_of(core * GF + head * HD, HD), HD)
            out[head * 256 + slot * TILE : head * 256 + (slot + 1) * TILE] = rows[:, columns]


def stack_up(up_own, up_other):
    return pl.pallas_call(
        stack_kernel,
        in_specs=[WHOLE, WHOLE],
        out_specs=WHOLE,
        out_shape=jax.ShapeDtypeStruct((STACK, HD), BF),
        compiler_params=PARAMS,
        cost_estimate=cost(0, 4 * STACK * HD),
        name="stack_up",
    )(up_own, up_other)


def scores_kernel(d, part, limits, query, up, *refs):
    powers, grads, stats, keys_t = refs[-4:]
    rows = slice(None) if part is None else slice(part * TILE, (part + 1) * TILE)
    kv = jnp.concatenate([ref[rows] for ref in refs[:-4]], axis=0)
    keys, values = kv[:, :HD], kv[:, HD:]
    keys_t[...] = keys.T
    position = lax.broadcasted_iota(jnp.int32, (TILE, 2 * TILE), 0)
    bias = []
    for key_slot in range(2):
        row = 4 * d + 2 * key_slot
        allowed = (position >= limits[row : row + 1]) & (position < limits[row + 1 : row + 2])
        bias.append(jnp.where(allowed, 0.0, -jnp.inf))
    bias = jnp.concatenate(bias, axis=0)
    for head in range(GROUP):
        part = slice(head * 256, (head + 1) * 256)
        scores = dot_nt(keys, query[part]) * LOG2_SCALE + bias
        top = jnp.max(scores, axis=0, keepdims=True)
        power = jnp.exp2(scores - jnp.where(top == -jnp.inf, 0.0, top))
        grad = dot_nt(values, up[part])
        powers[:, part] = power
        grads[:, part] = grad
        stats[0:1, part] = top
        stats[1:2, part] = jnp.sum(power, axis=0, keepdims=True)
        stats[2:3, part] = jnp.sum(power * grad, axis=0, keepdims=True)


def chip_scores(d, limits, query, up, *kv, part=None):
    return pl.pallas_call(
        functools.partial(scores_kernel, d, part),
        in_specs=[WHOLE] * (3 + len(kv)),
        out_specs=[WHOLE] * 4,
        out_shape=[
            jax.ShapeDtypeStruct((256, STACK), F32),
            jax.ShapeDtypeStruct((256, STACK), F32),
            jax.ShapeDtypeStruct((8, STACK), F32),
            jax.ShapeDtypeStruct((HD, 256), BF),
        ],
        compiler_params=PARAMS,
        cost_estimate=cost(4 * STACK * 256 * HD, 10 * 256 * STACK, 256 * STACK),
        name=f"chip_scores_{d}",
    )(limits, query, up, *kv)


def factors_kernel(a, b, c, d, out):
    parts = (a, b, c, d)
    top = jnp.maximum(jnp.maximum(a[0:1], b[0:1]), jnp.maximum(c[0:1], d[0:1]))
    factors = [jnp.exp2(part[0:1] - top) for part in parts]
    total = sum(factor * part[1:2] for factor, part in zip(factors, parts))
    factors = [factor / total for factor in factors]
    for chip, factor in enumerate(factors):
        out[chip : chip + 1] = factor
    out[4:5] = sum(factor * part[2:3] for factor, part in zip(factors, parts))


def softmax_factors(stats):
    return pl.pallas_call(
        factors_kernel,
        in_specs=[WHOLE] * 4,
        out_specs=WHOLE,
        out_shape=jax.ShapeDtypeStruct((8, STACK), F32),
        compiler_params=PARAMS,
        cost_estimate=cost(20 * STACK, 128 * STACK),
        name="softmax_factors",
    )(*stats)


def terms_kernel(d, powers, grads, factors, query, up, out, grad_scores, probs_low):
    for head in range(GROUP):
        part = slice(head * 256, (head + 1) * 256)
        probs = powers[:, part] * factors[d : d + 1, part]
        probs_low[:, part] = probs.astype(BF)
        grad_scores[:, part] = (probs * (grads[:, part] - factors[4:5, part])).astype(BF)
    out[:, :HD] = (dot(grad_scores[...], query[...]) * SCALE).astype(out.dtype)
    out[:, HD:] = dot(probs_low[...], up[...]).astype(out.dtype)


def chip_terms(d, powers, grads, factors, query, up):
    return pl.pallas_call(
        functools.partial(terms_kernel, d),
        in_specs=[WHOLE] * 5,
        out_specs=[WHOLE] * 2,
        out_shape=[
            jax.ShapeDtypeStruct((256, 256), F32 if d == 0 else BF),
            jax.ShapeDtypeStruct((256, STACK), BF),
        ],
        scratch_shapes=[pltpu.VMEM((256, STACK), BF)],
        compiler_params=PARAMS,
        cost_estimate=cost(4 * STACK * 256 * HD, 10 * 256 * STACK),
        name=f"chip_terms_{d}",
    )(powers, grads, factors, query, up)


def query_grad_kernel(k0, k1, k2, k3, g0, g1, g2, g3, out, middle, theirs):
    for head in range(GROUP):
        part = slice(head * 256, (head + 1) * 256)
        total = dot(k0[...], g0[:, part]) + dot(k1[...], g1[:, part])
        total += dot(k2[...], g2[:, part]) + dot(k3[...], g3[:, part])
        columns = slice(head * HD, (head + 1) * HD)
        result = (total * SCALE).T.astype(BF)
        out[:, columns] = result
        theirs[:, columns] = result[TILE:]
        if 2 <= head < 4:
            middle[:, (head - 2) * HD : (head - 1) * HD] = result


def query_grad(keys_t, grad_scores):
    return pl.pallas_call(
        query_grad_kernel,
        in_specs=[WHOLE] * 8,
        out_specs=[WHOLE] * 3,
        out_shape=[
            jax.ShapeDtypeStruct((256, GF), BF),
            jax.ShapeDtypeStruct((256, 256), BF),
            jax.ShapeDtypeStruct((TILE, GF), BF),
        ],
        compiler_params=PARAMS,
        cost_estimate=cost(2 * STACK * KEYS * HD, 2 * STACK * KEYS),
        name="query_grad",
    )(*keys_t, *grad_scores)


def sum_kernel(a, b, c, d, out):
    total = (a[...] + b[...].astype(F32)) + (c[...].astype(F32) + d[...].astype(F32))
    out[...] = total.astype(out.dtype)


def join_kernel(a, b, c, d, beside, out):
    total = (a[...] + b[...].astype(F32)) + (c[...].astype(F32) + d[...].astype(F32))
    out[:, :256] = total.astype(out.dtype)
    out[:, 256:] = beside[...]


def sum_join(a, b, c, d, beside):
    return pl.pallas_call(
        join_kernel,
        in_specs=[WHOLE] * 5,
        out_specs=WHOLE,
        out_shape=jax.ShapeDtypeStruct((256, 512), BF),
        compiler_params=PARAMS,
        cost_estimate=cost(4 * a.size, 12 * a.size),
        name="sum_join",
    )(a, b, c, d, beside)


def sum_four(a, b, c, d):
    return pl.pallas_call(
        sum_kernel,
        in_specs=[WHOLE] * 4,
        out_specs=WHOLE,
        out_shape=jax.ShapeDtypeStruct(a.shape, BF),
        compiler_params=PARAMS,
        cost_estimate=cost(4 * a.size, 12 * a.size),
        name="sum_four",
    )(a, b, c, d)


def pack_kernel(dq, joined, joined_other, *outs):
    my_chip, my_core, _ = position()
    for core in range(2):
        own_part = slice(core * HD, (core + 1) * HD)
        for chip in range(CHIPS):

            @pl.when((my_core == core) & (my_chip == chip))
            def _(core=core, own_part=own_part, chip=chip):
                for d, out in enumerate(outs):
                    target = (chip + d) % CHIPS
                    if target == 3:
                        out[:, own_part] = joined[:, own_part]
                        theirs = slice((1 - core) * HD, (2 - core) * HD)
                        out[:TILE, theirs] = joined_other[TILE:, own_part]
                        out[TILE:, theirs] = joined_other[:TILE, own_part]
                    elif target == 2 - 2 * core:
                        out[:TILE] = joined_other[TILE:, 256:]
                        out[TILE:] = joined_other[:TILE, 256:]
                    else:
                        first = target == core
                        out[...] = dq[:, 0:256] if first else dq[:, 512:768]


def pack(dq, joined, joined_other):
    return pl.pallas_call(
        pack_kernel,
        in_specs=[WHOLE] * 3,
        out_specs=[WHOLE] * 4,
        out_shape=[jax.ShapeDtypeStruct((256, 256), BF)] * 4,
        compiler_params=PARAMS,
        cost_estimate=cost(0, 4 << 19),
        name="pack",
    )(dq, joined, joined_other)


def transpose_kernel(own, far2, far1, far3, out):
    for i, rows in enumerate((own, far2, far1, far3)):
        out[:, i * TILE : (i + 1) * TILE] = rows[...].T


def transpose(parts):
    return pl.pallas_call(
        transpose_kernel,
        in_specs=[WHOLE] * 4,
        out_specs=WHOLE,
        out_shape=jax.ShapeDtypeStruct((D, KEYS // 2), BF),
        compiler_params=PARAMS,
        cost_estimate=cost(0, 2 * D * KEYS),
        name="transpose_tokens",
    )(*parts)


def weight_kernel(shift, tokens_t, other_t, a, b, c, d, out):
    parts = (a, b, c, d)
    right = jnp.concatenate([part[:TILE] for part in parts], axis=0)
    right_other = jnp.concatenate([part[TILE:] for part in parts], axis=0)
    _, _, chip = position()
    row = pl.multiple_of(lax.rem(chip + shift, YS) * (D // YS), 128)
    rows = pl.ds(row, D // YS)
    total = dot(tokens_t[rows], right) + dot(other_t[rows], right_other)
    out[...] = total.astype(out.dtype)


def weight_grad(shift, tokens_t, other_t, parts):
    return pl.pallas_call(
        functools.partial(weight_kernel, shift),
        in_specs=[WHOLE] * 6,
        out_specs=WHOLE,
        out_shape=jax.ShapeDtypeStruct((D // YS, 256), F32 if shift == 0 else BF),
        compiler_params=PARAMS,
        cost_estimate=cost(2 * D * KEYS * 256 // YS, 2 * D * KEYS // YS),
        name=f"weight_grad_{shift}",
    )(tokens_t, other_t, *parts)


def input_kernel(
    dq, dq_other, dkv, dkv_other, w_query, w_key, w_value, out, left, right, sems
):
    _, core, _ = position()
    width = D // IN_CHUNKS
    copies = []
    for chunk in range(IN_CHUNKS):
        part = pl.ds(chunk * width, width)
        copies.append(
            [
                pltpu.make_async_copy(
                    source.at[part],
                    right.at[part, pl.ds(start, size)],
                    sems.at[chunk, side],
                )
                for side, (source, start, size) in enumerate(
                    ((w_query, 0, D), (w_key, D, 256), (w_value, D + 256, 256))
                )
            ]
        )
    for group in copies:
        for copy in group:
            copy.start()
    mine = pl.ds(pl.multiple_of(core * GF, 128), GF)
    theirs = pl.ds(pl.multiple_of((1 - core) * GF, 128), GF)
    left[:, mine] = dq[:TILE]
    left[:, theirs] = dq_other[...]
    for part in range(2):
        columns = slice(part * HD, (part + 1) * HD)
        base = D + part * KVH * HD
        left[:, pl.ds(pl.multiple_of(base + core * HD, 128), HD)] = dkv[:TILE, columns]
        left[:, pl.ds(pl.multiple_of(base + (1 - core) * HD, 128), HD)] = dkv_other[
            TILE:, columns
        ]
    for chunk, group in enumerate(copies):
        for copy in group:
            copy.wait()
        part = slice(chunk * width, (chunk + 1) * width)
        out[:, part] = dot_nt(left[...], right[part]).astype(BF)


def input_grad(dq, dq_other, dkv, dkv_other, w_query, w_key, w_value):
    return pl.pallas_call(
        input_kernel,
        in_specs=[WHOLE] * 4 + [STAY] * 3,
        out_specs=WHOLE,
        out_shape=jax.ShapeDtypeStruct((TILE, D), BF),
        scratch_shapes=[
            pltpu.VMEM((TILE, D + 512), BF),
            pltpu.VMEM((D, D + 512), BF),
            pltpu.SemaphoreType.DMA((IN_CHUNKS, 3)),
        ],
        compiler_params=PARAMS,
        cost_estimate=cost(2 * TILE * D * 2048, 2 * D * 2048),
        name="input_grad",
    )(dq, dq_other, dkv, dkv_other, w_query, w_key, w_value)


def shards(tokens, grad_heads, tile_mask, segments, w_query, w_key, w_value):
    own, up = tokens[0], grad_heads[0]
    other = lax.ppermute(own, "ctx", CORE)
    up_other = lax.ppermute(up, "ctx", CORE)
    mask_other = lax.ppermute(tile_mask[0], "ctx", CORE)
    other, mask_other, up_other = lax.optimization_barrier((other, mask_other, up_other))

    w_query, w_key, w_value = (in_hbm(w) for w in (w_query, w_key, w_value))
    weights, kv_own = project_kv_own(in_hbm(own), w_key, w_value)
    kv = project_kv(other, weights, kv_own)
    kv2 = lax.ppermute(kv, "ctx", chip_shift(2))
    far = {d: lax.ppermute(own, "ctx", chip_shift(d)) for d in (1, 3)}
    query, limits, weights_other = project_query(
        own, other, w_query, w_key, w_value,
        in_hbm(segments), in_hbm(tile_mask[0]), mask_other,
    )
    up = stack_up(up, up_other)
    scores = {0: chip_scores(0, limits, query, up, kv)}
    far, kv2, scores[0] = lax.optimization_barrier((far, kv2, scores[0]))
    late = lax.ppermute(far[1], "ctx", chip_shift(1))
    mine, theirs = project_kv_far(far[1], far[3], weights, weights_other)
    theirs = lax.ppermute(theirs, "ctx", CORE)
    for i, d in enumerate((1, 3)):
        scores[d] = chip_scores(d, limits, query, up, mine, theirs, part=i)
    scores[2] = chip_scores(2, limits, query, up, kv2)
    factors = softmax_factors([scores[d][2] for d in range(CHIPS)])
    terms, grad_scores = {}, {}
    for d in (3, 1, 2):
        terms[d], grad_scores[d] = chip_terms(d, *scores[d][:2], factors, query, up)
    back = [lax.ppermute(terms[d], "ctx", chip_shift(CHIPS - d)) for d in (1, 3, 2)]
    terms[0], grad_scores[0] = chip_terms(0, *scores[0][:2], factors, query, up)
    dq, middle, theirs = query_grad(
        [scores[d][3] for d in range(CHIPS)], [grad_scores[d] for d in range(CHIPS)]
    )
    late, back, middle = lax.optimization_barrier((late, back, middle))
    dkv = sum_join(terms[0], *back, middle)
    dkv_other = lax.ppermute(dkv, "ctx", CORE)
    packed = pack(dq, dkv, dkv_other)

    far, dkv = lax.optimization_barrier((far, dkv))
    tokens_t = transpose([own, late, far[1], far[3]])
    tokens_t, packed, theirs = lax.optimization_barrier((tokens_t, packed, theirs))
    dq_other = lax.ppermute(theirs, "ctx", CORE)
    other_t = lax.ppermute(tokens_t, "ctx", CORE)
    columns = {d: lax.ppermute(packed[d], "ctx", chip_shift(d)) for d in (2, 1, 3)}
    columns = [packed[0]] + [columns[d] for d in (2, 1, 3)]
    terms = [weight_grad(d, tokens_t, other_t, columns) for d in range(YS)]
    y_parts = [terms[0]] + [lax.ppermute(terms[d], "dp", y_shift(d)) for d in (1, 3, 2)]
    grad_tokens = input_grad(
        dq, dq_other, dkv, dkv_other, w_query, w_key, w_value
    )
    y_parts, grad_tokens = lax.optimization_barrier((y_parts, grad_tokens))
    y_sum = sum_four(*y_parts)
    z_parts = lax.all_to_all(y_sum, "dp", 0, 0, tiled=True, axis_index_groups=Z_GROUPS)
    grad_projection = jnp.sum(z_parts.reshape(ZS, 48, 256).astype(F32), axis=0)
    return grad_tokens[None], grad_projection


def solution(mesh):
    return jax.shard_map(
        shards,
        mesh=mesh,
        in_specs=(
            P("dp", "ctx", None),
            P("dp", "ctx", None),
            P("dp", "ctx", None),
            P("dp", None),
            P(),
            P(),
            P(),
        ),
        out_specs=(P("dp", "ctx", None), P("dp", "ctx")),
        check_vma=False,
    )
```

```python
import functools
import math

import jax
import jax.numpy as jnp
from jax import lax
from jax.experimental import pallas as pl
from jax.experimental.pallas import tpu as pltpu
from jax.sharding import PartitionSpec as P

QH = 12
KVH = 2
HD = 128
TILE = 128
D = 1536
KEYS = 1024
CHIPS = 4
GROUP = QH // KVH
GF = GROUP * HD
STACK = GROUP * 256
YS = 4
ZS = 8
SCALE = 1.0 / math.sqrt(HD)
LOG2_SCALE = SCALE * math.log2(math.e)
BF = jnp.bfloat16
F32 = jnp.float32
VMEM_LIMIT = 24 * 1024 * 1024
W_CHUNKS = 1
Q_CHUNKS = 3
IN_CHUNKS = 3

CORE = [(i, i ^ 1) for i in range(8)]
NT = (((1,), (1,)), ((), ()))


def chip_pair(d):
    return [(i, ((i // 2) ^ d) * 2 + i % 2) for i in range(8)]


def y_pair(d):
    return [(i, ((i // ZS) ^ d) * ZS + i % ZS) for i in range(32)]


Z_GROUPS = [[y * ZS + z for z in range(ZS)] for y in range(YS)]


def dot(a, b):
    return jnp.dot(a, b, preferred_element_type=F32)


def dot_nt(a, b):
    return lax.dot_general(a, b, NT, preferred_element_type=F32)


def in_hbm(array):
    return pltpu.with_memory_space_constraint(array, pltpu.HBM)


def position():
    ctx, dp = lax.axis_index("ctx"), lax.axis_index("dp")
    return lax.div(ctx, 2), lax.rem(ctx, 2), lax.div(dp, ZS)


def cost(flops, bytes_accessed, transcendentals=0):
    return pl.CostEstimate(
        flops=1, bytes_accessed=1, transcendentals=0
    )


PARAMS = pltpu.CompilerParams(vmem_limit_bytes=VMEM_LIMIT)
WHOLE = pl.BlockSpec(memory_space=pltpu.VMEM)
SCALARS = pl.BlockSpec(memory_space=pltpu.SMEM)
STAY = pl.BlockSpec(memory_space=pltpu.HBM)


def kv_own_kernel(own, w_key, w_value, weights, out, rows, sems):
    _, core, _ = position()
    columns = pl.ds(pl.multiple_of(core * HD, HD), HD)
    copies = []
    for chunk in range(W_CHUNKS):
        part = pl.ds(chunk * (TILE // W_CHUNKS), TILE // W_CHUNKS)
        copies.append(pltpu.make_async_copy(own.at[part], rows.at[part], sems.at[chunk, 2]))
        part = pl.ds(chunk * (D // W_CHUNKS), D // W_CHUNKS)
        for side, source in enumerate((w_key, w_value)):
            copies.append(
                pltpu.make_async_copy(
                    source.at[part, columns],
                    weights.at[part, pl.ds(side * HD, HD)],
                    sems.at[chunk, side],
                )
            )
    for copy in copies:
        copy.start()
    for copy in copies:
        copy.wait()
    out[...] = dot(rows[...], weights[...]).astype(BF)


def project_kv_own(own, w_key, w_value):
    return pl.pallas_call(
        kv_own_kernel,
        in_specs=[STAY, STAY, STAY],
        out_specs=[WHOLE, WHOLE],
        out_shape=[
            jax.ShapeDtypeStruct((D, 2 * HD), BF),
            jax.ShapeDtypeStruct((TILE, 2 * HD), BF),
        ],
        scratch_shapes=[pltpu.VMEM((TILE, D), BF), pltpu.SemaphoreType.DMA((W_CHUNKS, 3))],
        compiler_params=PARAMS,
        cost_estimate=cost(2 * TILE * D * 256, 2 * (TILE * D + D * 256)),
        name="project_kv_own",
    )(own, w_key, w_value)


def kv_far_kernel(far1, far3, weights, weights_other, mine, theirs):
    for i, rows in enumerate((far1, far3)):
        part = slice(i * TILE, (i + 1) * TILE)
        theirs[part] = dot(rows[...], weights_other[...]).astype(BF)
        mine[part] = dot(rows[...], weights[...]).astype(BF)


def project_kv_far(far1, far3, weights, weights_other):
    return pl.pallas_call(
        kv_far_kernel,
        in_specs=[WHOLE] * 4,
        out_specs=[WHOLE] * 2,
        out_shape=[jax.ShapeDtypeStruct((2 * TILE, 2 * HD), BF)] * 2,
        compiler_params=PARAMS,
        cost_estimate=cost(8 * TILE * D * 256, 4 * (TILE * D + D * 256)),
        name="project_kv_far",
    )(far1, far3, weights, weights_other)


def kv_kernel(other, weights, kv_own, out):
    out[:TILE] = kv_own[...]
    out[TILE:] = dot(other[...], weights[...]).astype(BF)


def project_kv(other, weights, kv_own):
    return pl.pallas_call(
        kv_kernel,
        in_specs=[WHOLE] * 3,
        out_specs=WHOLE,
        out_shape=jax.ShapeDtypeStruct((2 * TILE, 2 * HD), BF),
        compiler_params=PARAMS,
        cost_estimate=cost(2 * TILE * D * 256, 2 * (TILE * D + D * 256)),
        name="project_kv",
    )(other, weights, kv_own)


def query_kernel(
    own, other, w_query, w_key, w_value, segments_far, mask_far, mask_other,
    out, limits, weights_other, weights, segments, mask_own, sems, small_sems,
):
    chip, core, _ = position()
    theirs = pl.ds(pl.multiple_of((1 - core) * HD, HD), HD)
    small = [
        pltpu.make_async_copy(segments_far, segments, small_sems.at[0]),
        pltpu.make_async_copy(mask_far, mask_own, small_sems.at[1]),
    ]
    for copy in small:
        copy.start()
    columns = pl.ds(pl.multiple_of(core * GF, HD), GF)
    copies = []
    for chunk in range(Q_CHUNKS):
        part = pl.ds(chunk * (D // Q_CHUNKS), D // Q_CHUNKS)
        copies.append(
            pltpu.make_async_copy(w_query.at[part, columns], weights.at[part], sems.at[chunk])
        )
    for side, source in enumerate((w_key, w_value)):
        copies.append(
            pltpu.make_async_copy(
                source.at[:, theirs],
                weights_other.at[:, pl.ds(side * HD, HD)],
                small_sems.at[2 + side],
            )
        )
    for copy in copies:
        copy.start()
    for copy in small:
        copy.wait()

    passages = segments[...]
    ends = [jnp.sum((passages <= s).astype(jnp.int32)) for s in range(3)]
    for slot in range(2):
        masks = mask_own if slot == 0 else mask_other
        tile = 2 * chip + (core if slot == 0 else 1 - core)
        mine = segments[:, pl.ds(pl.multiple_of(tile * TILE, TILE), TILE)]
        low = jnp.where(
            mine == 0, 0, jnp.where(mine == 1, ends[0], jnp.where(mine == 2, ends[1], ends[2]))
        )
        high = jnp.where(
            mine == 0, ends[0], jnp.where(mine == 1, ends[1], jnp.where(mine == 2, ends[2], KEYS))
        )
        for d in range(CHIPS):
            for key_slot in range(2):
                key_tile = 2 * lax.bitwise_xor(chip, jnp.int32(d)) + (
                    core if key_slot == 0 else 1 - core
                )
                seen = masks[0, key_tile] == 1
                row = 4 * d + 2 * key_slot
                place_of = slice(slot * TILE, (slot + 1) * TILE)
                limits[row : row + 1, place_of] = jnp.where(seen, 0, low) - key_tile * TILE
                limits[row + 1 : row + 2, place_of] = (
                    jnp.where(seen, KEYS, high) - key_tile * TILE
                )

    for copy in copies:
        copy.wait()
    for slot, rows in enumerate((own, other)):
        queries = dot(rows[...], weights[...]).astype(BF)
        for head in range(GROUP):
            out[head * 256 + slot * TILE : head * 256 + (slot + 1) * TILE] = queries[
                :, head * HD : (head + 1) * HD
            ]


def project_query(
    own, other, w_query, w_key, w_value, segments, mask_own, mask_other
):
    return pl.pallas_call(
        query_kernel,
        in_specs=[WHOLE, WHOLE] + [STAY] * 5 + [SCALARS],
        out_specs=[WHOLE] * 3,
        out_shape=[
            jax.ShapeDtypeStruct((STACK, HD), BF),
            jax.ShapeDtypeStruct((4 * CHIPS, 2 * TILE), jnp.int32),
            jax.ShapeDtypeStruct((D, 2 * HD), BF),
        ],
        scratch_shapes=[
            pltpu.VMEM((D, GF), BF),
            pltpu.VMEM((1, KEYS), jnp.int32),
            pltpu.SMEM((1, KEYS // TILE), jnp.int32),
            pltpu.SemaphoreType.DMA((Q_CHUNKS,)),
            pltpu.SemaphoreType.DMA((4,)),
        ],
        compiler_params=PARAMS,
        cost_estimate=cost(2 * 256 * D * GF, 2 * (256 * D + D * GF + 256 * GF)),
        name="project_query",
    )(own, other, w_query, w_key, w_value, segments, mask_own, mask_other)


def stack_kernel(up_own, up_other, out):
    _, core, _ = position()
    for slot, rows in enumerate((up_own, up_other)):
        for head in range(GROUP):
            columns = pl.ds(pl.multiple_of(core * GF + head * HD, HD), HD)
            out[head * 256 + slot * TILE : head * 256 + (slot + 1) * TILE] = rows[:, columns]


def stack_up(up_own, up_other):
    return pl.pallas_call(
        stack_kernel,
        in_specs=[WHOLE, WHOLE],
        out_specs=WHOLE,
        out_shape=jax.ShapeDtypeStruct((STACK, HD), BF),
        compiler_params=PARAMS,
        cost_estimate=cost(0, 4 * STACK * HD),
        name="stack_up",
    )(up_own, up_other)


def scores_kernel(d, part, limits, query, up, *refs):
    powers, grads, stats, keys_t = refs[-4:]
    rows = slice(None) if part is None else slice(part * TILE, (part + 1) * TILE)
    kv = jnp.concatenate([ref[rows] for ref in refs[:-4]], axis=0)
    keys, values = kv[:, :HD], kv[:, HD:]
    keys_t[...] = keys.T
    position = lax.broadcasted_iota(jnp.int32, (TILE, 2 * TILE), 0)
    bias = []
    for key_slot in range(2):
        row = 4 * d + 2 * key_slot
        allowed = (position >= limits[row : row + 1]) & (position < limits[row + 1 : row + 2])
        bias.append(jnp.where(allowed, 0.0, -jnp.inf))
    bias = jnp.concatenate(bias, axis=0)
    for head in range(GROUP):
        part = slice(head * 256, (head + 1) * 256)
        scores = dot_nt(keys, query[part]) * LOG2_SCALE + bias
        top = jnp.max(scores, axis=0, keepdims=True)
        power = jnp.exp2(scores - jnp.where(top == -jnp.inf, 0.0, top))
        grad = dot_nt(values, up[part])
        powers[:, part] = power
        grads[:, part] = grad
        stats[0:1, part] = top
        stats[1:2, part] = jnp.sum(power, axis=0, keepdims=True)
        stats[2:3, part] = jnp.sum(power * grad, axis=0, keepdims=True)


def chip_scores(d, limits, query, up, *kv, part=None):
    return pl.pallas_call(
        functools.partial(scores_kernel, d, part),
        in_specs=[WHOLE] * (3 + len(kv)),
        out_specs=[WHOLE] * 4,
        out_shape=[
            jax.ShapeDtypeStruct((256, STACK), F32),
            jax.ShapeDtypeStruct((256, STACK), F32),
            jax.ShapeDtypeStruct((8, STACK), F32),
            jax.ShapeDtypeStruct((HD, 256), BF),
        ],
        compiler_params=PARAMS,
        cost_estimate=cost(4 * STACK * 256 * HD, 10 * 256 * STACK, 256 * STACK),
        name=f"chip_scores_{d}",
    )(limits, query, up, *kv)


def factors_kernel(a, b, c, d, out):
    parts = (a, b, c, d)
    top = jnp.maximum(jnp.maximum(a[0:1], b[0:1]), jnp.maximum(c[0:1], d[0:1]))
    factors = [jnp.exp2(part[0:1] - top) for part in parts]
    total = sum(factor * part[1:2] for factor, part in zip(factors, parts))
    factors = [factor / total for factor in factors]
    for chip, factor in enumerate(factors):
        out[chip : chip + 1] = factor
    out[4:5] = sum(factor * part[2:3] for factor, part in zip(factors, parts))


def softmax_factors(stats):
    return pl.pallas_call(
        factors_kernel,
        in_specs=[WHOLE] * 4,
        out_specs=WHOLE,
        out_shape=jax.ShapeDtypeStruct((8, STACK), F32),
        compiler_params=PARAMS,
        cost_estimate=cost(20 * STACK, 128 * STACK),
        name="softmax_factors",
    )(*stats)


def terms_kernel(d, powers, grads, factors, query, up, out, grad_scores, probs_low):
    for head in range(GROUP):
        part = slice(head * 256, (head + 1) * 256)
        probs = powers[:, part] * factors[d : d + 1, part]
        probs_low[:, part] = probs.astype(BF)
        grad_scores[:, part] = (probs * (grads[:, part] - factors[4:5, part])).astype(BF)
    out[:, :HD] = (dot(grad_scores[...], query[...]) * SCALE).astype(out.dtype)
    out[:, HD:] = dot(probs_low[...], up[...]).astype(out.dtype)


def chip_terms(d, powers, grads, factors, query, up):
    return pl.pallas_call(
        functools.partial(terms_kernel, d),
        in_specs=[WHOLE] * 5,
        out_specs=[WHOLE] * 2,
        out_shape=[
            jax.ShapeDtypeStruct((256, 256), F32 if d == 0 else BF),
            jax.ShapeDtypeStruct((256, STACK), BF),
        ],
        scratch_shapes=[pltpu.VMEM((256, STACK), BF)],
        compiler_params=PARAMS,
        cost_estimate=cost(4 * STACK * 256 * HD, 10 * 256 * STACK),
        name=f"chip_terms_{d}",
    )(powers, grads, factors, query, up)


def query_grad_kernel(k0, k1, k2, k3, g0, g1, g2, g3, out, middle, theirs):
    for head in range(GROUP):
        part = slice(head * 256, (head + 1) * 256)
        total = dot(k0[...], g0[:, part]) + dot(k1[...], g1[:, part])
        total += dot(k2[...], g2[:, part]) + dot(k3[...], g3[:, part])
        columns = slice(head * HD, (head + 1) * HD)
        result = (total * SCALE).T.astype(BF)
        out[:, columns] = result
        theirs[:, columns] = result[TILE:]
        if 2 <= head < 4:
            middle[:, (head - 2) * HD : (head - 1) * HD] = result


def query_grad(keys_t, grad_scores):
    return pl.pallas_call(
        query_grad_kernel,
        in_specs=[WHOLE] * 8,
        out_specs=[WHOLE] * 3,
        out_shape=[
            jax.ShapeDtypeStruct((256, GF), BF),
            jax.ShapeDtypeStruct((256, 256), BF),
            jax.ShapeDtypeStruct((TILE, GF), BF),
        ],
        compiler_params=PARAMS,
        cost_estimate=cost(2 * STACK * KEYS * HD, 2 * STACK * KEYS),
        name="query_grad",
    )(*keys_t, *grad_scores)


def sum_kernel(a, b, c, d, out):
    total = (a[...] + b[...].astype(F32)) + (c[...].astype(F32) + d[...].astype(F32))
    out[...] = total.astype(out.dtype)


def join_kernel(a, b, c, d, beside, out):
    total = (a[...] + b[...].astype(F32)) + (c[...].astype(F32) + d[...].astype(F32))
    out[:, :256] = total.astype(out.dtype)
    out[:, 256:] = beside[...]


def sum_join(a, b, c, d, beside):
    return pl.pallas_call(
        join_kernel,
        in_specs=[WHOLE] * 5,
        out_specs=WHOLE,
        out_shape=jax.ShapeDtypeStruct((256, 512), BF),
        compiler_params=PARAMS,
        cost_estimate=cost(4 * a.size, 12 * a.size),
        name="sum_join",
    )(a, b, c, d, beside)


def sum_four(a, b, c, d):
    return pl.pallas_call(
        sum_kernel,
        in_specs=[WHOLE] * 4,
        out_specs=WHOLE,
        out_shape=jax.ShapeDtypeStruct(a.shape, BF),
        compiler_params=PARAMS,
        cost_estimate=cost(4 * a.size, 12 * a.size),
        name="sum_four",
    )(a, b, c, d)


def pack_kernel(dq, joined, joined_other, *outs):
    my_chip, my_core, _ = position()
    for core in range(2):
        own_part = slice(core * HD, (core + 1) * HD)
        for chip in range(CHIPS):

            @pl.when((my_core == core) & (my_chip == chip))
            def _(core=core, own_part=own_part, chip=chip):
                for d, out in enumerate(outs):
                    target = chip ^ d
                    if target == 3:
                        out[:, own_part] = joined[:, own_part]
                        theirs = slice((1 - core) * HD, (2 - core) * HD)
                        out[:TILE, theirs] = joined_other[TILE:, own_part]
                        out[TILE:, theirs] = joined_other[:TILE, own_part]
                    elif target == 2 - 2 * core:
                        out[:TILE] = joined_other[TILE:, 256:]
                        out[TILE:] = joined_other[:TILE, 256:]
                    else:
                        first = target == core
                        out[...] = dq[:, 0:256] if first else dq[:, 512:768]


def pack(dq, joined, joined_other):
    return pl.pallas_call(
        pack_kernel,
        in_specs=[WHOLE] * 3,
        out_specs=[WHOLE] * 4,
        out_shape=[jax.ShapeDtypeStruct((256, 256), BF)] * 4,
        compiler_params=PARAMS,
        cost_estimate=cost(0, 4 << 19),
        name="pack",
    )(dq, joined, joined_other)


def transpose_kernel(own, far2, far1, far3, out):
    for i, rows in enumerate((own, far2, far1, far3)):
        out[:, i * TILE : (i + 1) * TILE] = rows[...].T


def transpose(parts):
    return pl.pallas_call(
        transpose_kernel,
        in_specs=[WHOLE] * 4,
        out_specs=WHOLE,
        out_shape=jax.ShapeDtypeStruct((D, KEYS // 2), BF),
        compiler_params=PARAMS,
        cost_estimate=cost(0, 2 * D * KEYS),
        name="transpose_tokens",
    )(*parts)


def weight_kernel(shift, tokens_t, other_t, a, b, c, d, out):
    parts = (a, b, c, d)
    right = jnp.concatenate([part[:TILE] for part in parts], axis=0)
    right_other = jnp.concatenate([part[TILE:] for part in parts], axis=0)
    _, _, chip = position()
    row = pl.multiple_of(lax.bitwise_xor(chip, jnp.int32(shift)) * (D // YS), 128)
    rows = pl.ds(row, D // YS)
    total = dot(tokens_t[rows], right) + dot(other_t[rows], right_other)
    out[...] = total.astype(out.dtype)


def weight_grad(shift, tokens_t, other_t, parts):
    return pl.pallas_call(
        functools.partial(weight_kernel, shift),
        in_specs=[WHOLE] * 6,
        out_specs=WHOLE,
        out_shape=jax.ShapeDtypeStruct((D // YS, 256), F32 if shift == 0 else BF),
        compiler_params=PARAMS,
        cost_estimate=cost(2 * D * KEYS * 256 // YS, 2 * D * KEYS // YS),
        name=f"weight_grad_{shift}",
    )(tokens_t, other_t, *parts)


def input_kernel(
    dq, dq_other, dkv, dkv_other, w_query, w_key, w_value, out, left, right, sems
):
    _, core, _ = position()
    width = D // IN_CHUNKS
    copies = []
    for chunk in range(IN_CHUNKS):
        part = pl.ds(chunk * width, width)
        copies.append(
            [
                pltpu.make_async_copy(
                    source.at[part],
                    right.at[part, pl.ds(start, size)],
                    sems.at[chunk, side],
                )
                for side, (source, start, size) in enumerate(
                    ((w_query, 0, D), (w_key, D, 256), (w_value, D + 256, 256))
                )
            ]
        )
    for group in copies:
        for copy in group:
            copy.start()
    mine = pl.ds(pl.multiple_of(core * GF, 128), GF)
    theirs = pl.ds(pl.multiple_of((1 - core) * GF, 128), GF)
    left[:, mine] = dq[:TILE]
    left[:, theirs] = dq_other[...]
    for part in range(2):
        columns = slice(part * HD, (part + 1) * HD)
        base = D + part * KVH * HD
        left[:, pl.ds(pl.multiple_of(base + core * HD, 128), HD)] = dkv[:TILE, columns]
        left[:, pl.ds(pl.multiple_of(base + (1 - core) * HD, 128), HD)] = dkv_other[
            TILE:, columns
        ]
    for chunk, group in enumerate(copies):
        for copy in group:
            copy.wait()
        part = slice(chunk * width, (chunk + 1) * width)
        out[:, part] = dot_nt(left[...], right[part]).astype(BF)


def input_grad(dq, dq_other, dkv, dkv_other, w_query, w_key, w_value):
    return pl.pallas_call(
        input_kernel,
        in_specs=[WHOLE] * 4 + [STAY] * 3,
        out_specs=WHOLE,
        out_shape=jax.ShapeDtypeStruct((TILE, D), BF),
        scratch_shapes=[
            pltpu.VMEM((TILE, D + 512), BF),
            pltpu.VMEM((D, D + 512), BF),
            pltpu.SemaphoreType.DMA((IN_CHUNKS, 3)),
        ],
        compiler_params=PARAMS,
        cost_estimate=cost(2 * TILE * D * 2048, 2 * D * 2048),
        name="input_grad",
    )(dq, dq_other, dkv, dkv_other, w_query, w_key, w_value)


def shards(tokens, grad_heads, tile_mask, segments, w_query, w_key, w_value):
    own, up = tokens[0], grad_heads[0]
    other = lax.ppermute(own, "ctx", CORE)
    up_other = lax.ppermute(up, "ctx", CORE)
    mask_other = lax.ppermute(tile_mask[0], "ctx", CORE)
    other, mask_other, up_other = lax.optimization_barrier((other, mask_other, up_other))

    w_query, w_key, w_value = (in_hbm(w) for w in (w_query, w_key, w_value))
    weights, kv_own = project_kv_own(in_hbm(own), w_key, w_value)
    kv = project_kv(other, weights, kv_own)
    kv2 = lax.ppermute(kv, "ctx", chip_pair(2))
    far = {d: lax.ppermute(own, "ctx", chip_pair(d)) for d in (1, 3)}
    query, limits, weights_other = project_query(
        own, other, w_query, w_key, w_value,
        in_hbm(segments), in_hbm(tile_mask[0]), mask_other,
    )
    up = stack_up(up, up_other)
    scores = {0: chip_scores(0, limits, query, up, kv)}
    far, kv2, scores[0] = lax.optimization_barrier((far, kv2, scores[0]))
    late = lax.ppermute(far[3], "ctx", chip_pair(1))
    mine, theirs = project_kv_far(far[1], far[3], weights, weights_other)
    theirs = lax.ppermute(theirs, "ctx", CORE)
    for i, d in enumerate((1, 3)):
        scores[d] = chip_scores(d, limits, query, up, mine, theirs, part=i)
    scores[2] = chip_scores(2, limits, query, up, kv2)
    factors = softmax_factors([scores[d][2] for d in range(CHIPS)])
    terms, grad_scores = {}, {}
    for d in (3, 1, 2):
        terms[d], grad_scores[d] = chip_terms(d, *scores[d][:2], factors, query, up)
    back = [lax.ppermute(terms[d], "ctx", chip_pair(d)) for d in (1, 3, 2)]
    terms[0], grad_scores[0] = chip_terms(0, *scores[0][:2], factors, query, up)
    dq, middle, theirs = query_grad(
        [scores[d][3] for d in range(CHIPS)], [grad_scores[d] for d in range(CHIPS)]
    )
    late, back, middle = lax.optimization_barrier((late, back, middle))
    dkv = sum_join(terms[0], *back, middle)
    dkv_other = lax.ppermute(dkv, "ctx", CORE)
    packed = pack(dq, dkv, dkv_other)

    far, dkv = lax.optimization_barrier((far, dkv))
    tokens_t = transpose([own, late, far[1], far[3]])
    tokens_t, packed, theirs = lax.optimization_barrier((tokens_t, packed, theirs))
    dq_other = lax.ppermute(theirs, "ctx", CORE)
    other_t = lax.ppermute(tokens_t, "ctx", CORE)
    columns = {d: lax.ppermute(packed[d], "ctx", chip_pair(d)) for d in (2, 1, 3)}
    columns = [packed[0]] + [columns[d] for d in (2, 1, 3)]
    terms = [weight_grad(d, tokens_t, other_t, columns) for d in range(YS)]
    y_parts = [terms[0]] + [lax.ppermute(terms[d], "dp", y_pair(d)) for d in (1, 3, 2)]
    grad_tokens = input_grad(
        dq, dq_other, dkv, dkv_other, w_query, w_key, w_value
    )
    y_parts, grad_tokens = lax.optimization_barrier((y_parts, grad_tokens))
    y_sum = sum_four(*y_parts)
    z_parts = lax.all_to_all(y_sum, "dp", 0, 0, tiled=True, axis_index_groups=Z_GROUPS)
    grad_projection = jnp.sum(z_parts.reshape(ZS, 48, 256).astype(F32), axis=0)
    return grad_tokens[None], grad_projection


def solution(mesh):
    return jax.shard_map(
        shards,
        mesh=mesh,
        in_specs=(
            P("dp", "ctx", None),
            P("dp", "ctx", None),
            P("dp", "ctx", None),
            P("dp", None),
            P(),
            P(),
            P(),
        ),
        out_specs=(P("dp", "ctx", None), P("dp", "ctx")),
        check_vma=False,
    )
```

```python
import functools
import math

import jax
import jax.numpy as jnp
from jax import lax
from jax.experimental import pallas as pl
from jax.experimental.pallas import tpu as pltpu
from jax.sharding import PartitionSpec as P

QH = 12
KVH = 2
HD = 128
TILE = 128
D = 1536
KEYS = 1024
CHIPS = 4
GROUP = QH // KVH
GF = GROUP * HD
STACK = GROUP * 256
YS = 4
ZS = 8
SCALE = 1.0 / math.sqrt(HD)
LOG2_SCALE = SCALE * math.log2(math.e)
BF = jnp.bfloat16
F32 = jnp.float32
VMEM_LIMIT = 24 * 1024 * 1024
W_CHUNKS = 1
Q_CHUNKS = 3
IN_CHUNKS = 3

CORE = [(i, i ^ 1) for i in range(8)]
NT = (((1,), (1,)), ((), ()))


def chip_pair(d):
    return [(i, ((i // 2) ^ d) * 2 + i % 2) for i in range(8)]


def y_pair(d):
    return [(i, ((i // ZS) ^ d) * ZS + i % ZS) for i in range(32)]


Z_GROUPS = [[y * ZS + z for z in range(ZS)] for y in range(YS)]


def dot(a, b):
    return jnp.dot(a, b, preferred_element_type=F32)


def dot_nt(a, b):
    return lax.dot_general(a, b, NT, preferred_element_type=F32)


def in_hbm(array):
    return pltpu.with_memory_space_constraint(array, pltpu.HBM)


def position():
    ctx, dp = lax.axis_index("ctx"), lax.axis_index("dp")
    return lax.div(ctx, 2), lax.rem(ctx, 2), lax.div(dp, ZS)


def cost(flops, bytes_accessed, transcendentals=0):
    return pl.CostEstimate(
        flops=1, bytes_accessed=1, transcendentals=0
    )


PARAMS = pltpu.CompilerParams(vmem_limit_bytes=VMEM_LIMIT)
WHOLE = pl.BlockSpec(memory_space=pltpu.VMEM)
SCALARS = pl.BlockSpec(memory_space=pltpu.SMEM)
STAY = pl.BlockSpec(memory_space=pltpu.HBM)


def kv_own_kernel(own, w_key, w_value, weights, out, rows, sems):
    _, core, _ = position()
    columns = pl.ds(pl.multiple_of(core * HD, HD), HD)
    copies = []
    for chunk in range(W_CHUNKS):
        part = pl.ds(chunk * (TILE // W_CHUNKS), TILE // W_CHUNKS)
        copies.append(pltpu.make_async_copy(own.at[part], rows.at[part], sems.at[chunk, 2]))
        part = pl.ds(chunk * (D // W_CHUNKS), D // W_CHUNKS)
        for side, source in enumerate((w_key, w_value)):
            copies.append(
                pltpu.make_async_copy(
                    source.at[part, columns],
                    weights.at[part, pl.ds(side * HD, HD)],
                    sems.at[chunk, side],
                )
            )
    for copy in copies:
        copy.start()
    for copy in copies:
        copy.wait()
    out[...] = dot(rows[...], weights[...]).astype(BF)


def project_kv_own(own, w_key, w_value):
    return pl.pallas_call(
        kv_own_kernel,
        in_specs=[STAY, STAY, STAY],
        out_specs=[WHOLE, WHOLE],
        out_shape=[
            jax.ShapeDtypeStruct((D, 2 * HD), BF),
            jax.ShapeDtypeStruct((TILE, 2 * HD), BF),
        ],
        scratch_shapes=[pltpu.VMEM((TILE, D), BF), pltpu.SemaphoreType.DMA((W_CHUNKS, 3))],
        compiler_params=PARAMS,
        cost_estimate=cost(2 * TILE * D * 256, 2 * (TILE * D + D * 256)),
        name="project_kv_own",
    )(own, w_key, w_value)


def kv_far_kernel(far1, far3, weights, weights_other, mine, theirs):
    for i, rows in enumerate((far1, far3)):
        part = slice(i * TILE, (i + 1) * TILE)
        theirs[part] = dot(rows[...], weights_other[...]).astype(BF)
        mine[part] = dot(rows[...], weights[...]).astype(BF)


def project_kv_far(far1, far3, weights, weights_other):
    return pl.pallas_call(
        kv_far_kernel,
        in_specs=[WHOLE] * 4,
        out_specs=[WHOLE] * 2,
        out_shape=[jax.ShapeDtypeStruct((2 * TILE, 2 * HD), BF)] * 2,
        compiler_params=PARAMS,
        cost_estimate=cost(8 * TILE * D * 256, 4 * (TILE * D + D * 256)),
        name="project_kv_far",
    )(far1, far3, weights, weights_other)


def kv_kernel(other, weights, kv_own, out):
    out[:TILE] = kv_own[...]
    out[TILE:] = dot(other[...], weights[...]).astype(BF)


def project_kv(other, weights, kv_own):
    return pl.pallas_call(
        kv_kernel,
        in_specs=[WHOLE] * 3,
        out_specs=WHOLE,
        out_shape=jax.ShapeDtypeStruct((2 * TILE, 2 * HD), BF),
        compiler_params=PARAMS,
        cost_estimate=cost(2 * TILE * D * 256, 2 * (TILE * D + D * 256)),
        name="project_kv",
    )(other, weights, kv_own)


def query_kernel(
    own, other, w_query, w_key, w_value, segments_far, mask_far, mask_other,
    out, limits, weights_other, weights, segments, mask_own, sems, small_sems,
):
    chip, core, _ = position()
    theirs = pl.ds(pl.multiple_of((1 - core) * HD, HD), HD)
    small = [
        pltpu.make_async_copy(segments_far, segments, small_sems.at[0]),
        pltpu.make_async_copy(mask_far, mask_own, small_sems.at[1]),
    ]
    for copy in small:
        copy.start()
    columns = pl.ds(pl.multiple_of(core * GF, HD), GF)
    copies = []
    for chunk in range(Q_CHUNKS):
        part = pl.ds(chunk * (D // Q_CHUNKS), D // Q_CHUNKS)
        copies.append(
            pltpu.make_async_copy(w_query.at[part, columns], weights.at[part], sems.at[chunk])
        )
    for side, source in enumerate((w_key, w_value)):
        copies.append(
            pltpu.make_async_copy(
                source.at[:, theirs],
                weights_other.at[:, pl.ds(side * HD, HD)],
                small_sems.at[2 + side],
            )
        )
    for copy in copies:
        copy.start()
    for copy in small:
        copy.wait()

    passages = segments[...]
    ends = [jnp.sum((passages <= s).astype(jnp.int32)) for s in range(3)]
    for slot in range(2):
        masks = mask_own if slot == 0 else mask_other
        tile = 2 * chip + (core if slot == 0 else 1 - core)
        mine = segments[:, pl.ds(pl.multiple_of(tile * TILE, TILE), TILE)]
        low = jnp.where(
            mine == 0, 0, jnp.where(mine == 1, ends[0], jnp.where(mine == 2, ends[1], ends[2]))
        )
        high = jnp.where(
            mine == 0, ends[0], jnp.where(mine == 1, ends[1], jnp.where(mine == 2, ends[2], KEYS))
        )
        for d in range(CHIPS):
            for key_slot in range(2):
                key_tile = 2 * lax.bitwise_xor(chip, jnp.int32(d)) + (
                    core if key_slot == 0 else 1 - core
                )
                seen = masks[0, key_tile] == 1
                row = 4 * d + 2 * key_slot
                place_of = slice(slot * TILE, (slot + 1) * TILE)
                limits[row : row + 1, place_of] = jnp.where(seen, 0, low) - key_tile * TILE
                limits[row + 1 : row + 2, place_of] = (
                    jnp.where(seen, KEYS, high) - key_tile * TILE
                )

    for copy in copies:
        copy.wait()
    for slot, rows in enumerate((own, other)):
        queries = dot(rows[...], weights[...]).astype(BF)
        for head in range(GROUP):
            out[head * 256 + slot * TILE : head * 256 + (slot + 1) * TILE] = queries[
                :, head * HD : (head + 1) * HD
            ]


def project_query(
    own, other, w_query, w_key, w_value, segments, mask_own, mask_other
):
    return pl.pallas_call(
        query_kernel,
        in_specs=[WHOLE, WHOLE] + [STAY] * 5 + [SCALARS],
        out_specs=[WHOLE] * 3,
        out_shape=[
            jax.ShapeDtypeStruct((STACK, HD), BF),
            jax.ShapeDtypeStruct((4 * CHIPS, 2 * TILE), jnp.int32),
            jax.ShapeDtypeStruct((D, 2 * HD), BF),
        ],
        scratch_shapes=[
            pltpu.VMEM((D, GF), BF),
            pltpu.VMEM((1, KEYS), jnp.int32),
            pltpu.SMEM((1, KEYS // TILE), jnp.int32),
            pltpu.SemaphoreType.DMA((Q_CHUNKS,)),
            pltpu.SemaphoreType.DMA((4,)),
        ],
        compiler_params=PARAMS,
        cost_estimate=cost(2 * 256 * D * GF, 2 * (256 * D + D * GF + 256 * GF)),
        name="project_query",
    )(own, other, w_query, w_key, w_value, segments, mask_own, mask_other)


def stack_kernel(up_own, up_other, out):
    _, core, _ = position()
    for slot, rows in enumerate((up_own, up_other)):
        for head in range(GROUP):
            columns = pl.ds(pl.multiple_of(core * GF + head * HD, HD), HD)
            out[head * 256 + slot * TILE : head * 256 + (slot + 1) * TILE] = rows[:, columns]


def stack_up(up_own, up_other):
    return pl.pallas_call(
        stack_kernel,
        in_specs=[WHOLE, WHOLE],
        out_specs=WHOLE,
        out_shape=jax.ShapeDtypeStruct((STACK, HD), BF),
        compiler_params=PARAMS,
        cost_estimate=cost(0, 4 * STACK * HD),
        name="stack_up",
    )(up_own, up_other)


def scores_kernel(d, part, limits, query, up, *refs):
    powers, grads, stats, keys_t = refs[-4:]
    rows = slice(None) if part is None else slice(part * TILE, (part + 1) * TILE)
    kv = jnp.concatenate([ref[rows] for ref in refs[:-4]], axis=0)
    keys, values = kv[:, :HD], kv[:, HD:]
    keys_t[...] = keys.T
    position = lax.broadcasted_iota(jnp.int32, (TILE, 2 * TILE), 0)
    bias = []
    for key_slot in range(2):
        row = 4 * d + 2 * key_slot
        allowed = (position >= limits[row : row + 1]) & (position < limits[row + 1 : row + 2])
        bias.append(jnp.where(allowed, 0.0, -jnp.inf))
    bias = jnp.concatenate(bias, axis=0)
    for head in range(GROUP):
        part = slice(head * 256, (head + 1) * 256)
        scores = dot_nt(keys, query[part]) * LOG2_SCALE + bias
        top = jnp.max(scores, axis=0, keepdims=True)
        power = jnp.exp2(scores - jnp.where(top == -jnp.inf, 0.0, top))
        grad = dot_nt(values, up[part])
        powers[:, part] = power
        grads[:, part] = grad
        stats[0:1, part] = top
        stats[1:2, part] = jnp.sum(power, axis=0, keepdims=True)
        stats[2:3, part] = jnp.sum(power * grad, axis=0, keepdims=True)


def chip_scores(d, limits, query, up, *kv, part=None):
    return pl.pallas_call(
        functools.partial(scores_kernel, d, part),
        in_specs=[WHOLE] * (3 + len(kv)),
        out_specs=[WHOLE] * 4,
        out_shape=[
            jax.ShapeDtypeStruct((256, STACK), F32),
            jax.ShapeDtypeStruct((256, STACK), F32),
            jax.ShapeDtypeStruct((8, STACK), F32),
            jax.ShapeDtypeStruct((HD, 256), BF),
        ],
        compiler_params=PARAMS,
        cost_estimate=cost(4 * STACK * 256 * HD, 10 * 256 * STACK, 256 * STACK),
        name=f"chip_scores_{d}",
    )(limits, query, up, *kv)


def factors_kernel(a, b, c, d, out):
    parts = (a, b, c, d)
    top = jnp.maximum(jnp.maximum(a[0:1], b[0:1]), jnp.maximum(c[0:1], d[0:1]))
    factors = [jnp.exp2(part[0:1] - top) for part in parts]
    total = sum(factor * part[1:2] for factor, part in zip(factors, parts))
    factors = [factor / total for factor in factors]
    for chip, factor in enumerate(factors):
        out[chip : chip + 1] = factor
    out[4:5] = sum(factor * part[2:3] for factor, part in zip(factors, parts))


def softmax_factors(stats):
    return pl.pallas_call(
        factors_kernel,
        in_specs=[WHOLE] * 4,
        out_specs=WHOLE,
        out_shape=jax.ShapeDtypeStruct((8, STACK), F32),
        compiler_params=PARAMS,
        cost_estimate=cost(20 * STACK, 128 * STACK),
        name="softmax_factors",
    )(*stats)


def terms_kernel(d, powers, grads, factors, query, up, out, grad_scores, probs_low):
    for head in range(GROUP):
        part = slice(head * 256, (head + 1) * 256)
        probs = powers[:, part] * factors[d : d + 1, part]
        probs_low[:, part] = probs.astype(BF)
        grad_scores[:, part] = (probs * (grads[:, part] - factors[4:5, part])).astype(BF)
    out[:, :HD] = (dot(grad_scores[...], query[...]) * SCALE).astype(out.dtype)
    out[:, HD:] = dot(probs_low[...], up[...]).astype(out.dtype)


def chip_terms(d, powers, grads, factors, query, up):
    return pl.pallas_call(
        functools.partial(terms_kernel, d),
        in_specs=[WHOLE] * 5,
        out_specs=[WHOLE] * 2,
        out_shape=[
            jax.ShapeDtypeStruct((256, 256), F32 if d == 0 else BF),
            jax.ShapeDtypeStruct((256, STACK), BF),
        ],
        scratch_shapes=[pltpu.VMEM((256, STACK), BF)],
        compiler_params=PARAMS,
        cost_estimate=cost(4 * STACK * 256 * HD, 10 * 256 * STACK),
        name=f"chip_terms_{d}",
    )(powers, grads, factors, query, up)


def query_grad_kernel(k0, k1, k2, k3, g0, g1, g2, g3, out, middle, theirs):
    for head in range(GROUP):
        part = slice(head * 256, (head + 1) * 256)
        total = dot(k0[...], g0[:, part]) + dot(k1[...], g1[:, part])
        total += dot(k2[...], g2[:, part]) + dot(k3[...], g3[:, part])
        columns = slice(head * HD, (head + 1) * HD)
        result = (total * SCALE).T.astype(BF)
        out[:, columns] = result
        theirs[:, columns] = result[TILE:]
        if 2 <= head < 4:
            middle[:, (head - 2) * HD : (head - 1) * HD] = result


def query_grad(keys_t, grad_scores):
    return pl.pallas_call(
        query_grad_kernel,
        in_specs=[WHOLE] * 8,
        out_specs=[WHOLE] * 3,
        out_shape=[
            jax.ShapeDtypeStruct((256, GF), BF),
            jax.ShapeDtypeStruct((256, 256), BF),
            jax.ShapeDtypeStruct((TILE, GF), BF),
        ],
        compiler_params=PARAMS,
        cost_estimate=cost(2 * STACK * KEYS * HD, 2 * STACK * KEYS),
        name="query_grad",
    )(*keys_t, *grad_scores)


def sum_kernel(a, b, c, d, out):
    total = (a[...] + b[...].astype(F32)) + (c[...].astype(F32) + d[...].astype(F32))
    out[...] = total.astype(out.dtype)


def join_kernel(a, b, c, d, beside, out):
    total = (a[...] + b[...].astype(F32)) + (c[...].astype(F32) + d[...].astype(F32))
    out[:, :256] = total.astype(out.dtype)
    out[:, 256:] = beside[...]


def sum_join(a, b, c, d, beside):
    return pl.pallas_call(
        join_kernel,
        in_specs=[WHOLE] * 5,
        out_specs=WHOLE,
        out_shape=jax.ShapeDtypeStruct((256, 512), BF),
        compiler_params=PARAMS,
        cost_estimate=cost(4 * a.size, 12 * a.size),
        name="sum_join",
    )(a, b, c, d, beside)


def sum_four(a, b, c, d):
    return pl.pallas_call(
        sum_kernel,
        in_specs=[WHOLE] * 4,
        out_specs=WHOLE,
        out_shape=jax.ShapeDtypeStruct(a.shape, BF),
        compiler_params=PARAMS,
        cost_estimate=cost(4 * a.size, 12 * a.size),
        name="sum_four",
    )(a, b, c, d)


def pack_kernel(dq, joined, joined_other, *outs):
    my_chip, my_core, _ = position()
    for core in range(2):
        own_part = slice(core * HD, (core + 1) * HD)
        for chip in range(CHIPS):

            @pl.when((my_core == core) & (my_chip == chip))
            def _(core=core, own_part=own_part, chip=chip):
                for d, out in enumerate(outs):
                    target = chip ^ d
                    if target == 3:
                        out[:, own_part] = joined[:, own_part]
                        theirs = slice((1 - core) * HD, (2 - core) * HD)
                        out[:TILE, theirs] = joined_other[TILE:, own_part]
                        out[TILE:, theirs] = joined_other[:TILE, own_part]
                    elif target == 2 - 2 * core:
                        out[:TILE] = joined_other[TILE:, 256:]
                        out[TILE:] = joined_other[:TILE, 256:]
                    else:
                        first = target == core
                        out[...] = dq[:, 0:256] if first else dq[:, 512:768]


def pack(dq, joined, joined_other):
    return pl.pallas_call(
        pack_kernel,
        in_specs=[WHOLE] * 3,
        out_specs=[WHOLE] * 4,
        out_shape=[jax.ShapeDtypeStruct((256, 256), BF)] * 4,
        compiler_params=PARAMS,
        cost_estimate=cost(0, 4 << 19),
        name="pack",
    )(dq, joined, joined_other)


def transpose_kernel(own, far2, far1, far3, out):
    for i, rows in enumerate((own, far2, far1, far3)):
        out[:, i * TILE : (i + 1) * TILE] = rows[...].T


def transpose(parts):
    return pl.pallas_call(
        transpose_kernel,
        in_specs=[WHOLE] * 4,
        out_specs=WHOLE,
        out_shape=jax.ShapeDtypeStruct((D, KEYS // 2), BF),
        compiler_params=PARAMS,
        cost_estimate=cost(0, 2 * D * KEYS),
        name="transpose_tokens",
    )(*parts)


def weight_kernel(shift, tokens_t, other_t, a, b, c, d, out):
    parts = (a, b, c, d)
    right = jnp.concatenate([part[:TILE] for part in parts], axis=0)
    right_other = jnp.concatenate([part[TILE:] for part in parts], axis=0)
    _, _, chip = position()
    row = pl.multiple_of(lax.bitwise_xor(chip, jnp.int32(shift)) * (D // YS), 128)
    rows = pl.ds(row, D // YS)
    total = dot(tokens_t[rows], right) + dot(other_t[rows], right_other)
    out[...] = total.astype(out.dtype)


def weight_grad(shift, tokens_t, other_t, parts):
    return pl.pallas_call(
        functools.partial(weight_kernel, shift),
        in_specs=[WHOLE] * 6,
        out_specs=WHOLE,
        out_shape=jax.ShapeDtypeStruct((D // YS, 256), F32 if shift == 0 else BF),
        compiler_params=PARAMS,
        cost_estimate=cost(2 * D * KEYS * 256 // YS, 2 * D * KEYS // YS),
        name=f"weight_grad_{shift}",
    )(tokens_t, other_t, *parts)


def input_kernel(
    dq, dq_other, dkv, dkv_other, w_query, w_key, w_value, out, left, right, sems
):
    _, core, _ = position()
    width = D // IN_CHUNKS
    copies = []
    for chunk in range(IN_CHUNKS):
        part = pl.ds(chunk * width, width)
        copies.append(
            [
                pltpu.make_async_copy(
                    source.at[part],
                    right.at[part, pl.ds(start, size)],
                    sems.at[chunk, side],
                )
                for side, (source, start, size) in enumerate(
                    ((w_query, 0, D), (w_key, D, 256), (w_value, D + 256, 256))
                )
            ]
        )
    for group in copies:
        for copy in group:
            copy.start()
    mine = pl.ds(pl.multiple_of(core * GF, 128), GF)
    theirs = pl.ds(pl.multiple_of((1 - core) * GF, 128), GF)
    left[:, mine] = dq[:TILE]
    left[:, theirs] = dq_other[...]
    for part in range(2):
        columns = slice(part * HD, (part + 1) * HD)
        base = D + part * KVH * HD
        left[:, pl.ds(pl.multiple_of(base + core * HD, 128), HD)] = dkv[:TILE, columns]
        left[:, pl.ds(pl.multiple_of(base + (1 - core) * HD, 128), HD)] = dkv_other[
            TILE:, columns
        ]
    for chunk, group in enumerate(copies):
        for copy in group:
            copy.wait()
        part = slice(chunk * width, (chunk + 1) * width)
        out[:, part] = dot_nt(left[...], right[part]).astype(BF)


def input_grad(dq, dq_other, dkv, dkv_other, w_query, w_key, w_value):
    return pl.pallas_call(
        input_kernel,
        in_specs=[WHOLE] * 4 + [STAY] * 3,
        out_specs=WHOLE,
        out_shape=jax.ShapeDtypeStruct((TILE, D), BF),
        scratch_shapes=[
            pltpu.VMEM((TILE, D + 512), BF),
            pltpu.VMEM((D, D + 512), BF),
            pltpu.SemaphoreType.DMA((IN_CHUNKS, 3)),
        ],
        compiler_params=PARAMS,
        cost_estimate=cost(2 * TILE * D * 2048, 2 * D * 2048),
        name="input_grad",
    )(dq, dq_other, dkv, dkv_other, w_query, w_key, w_value)


def shards(tokens, grad_heads, tile_mask, segments, w_query, w_key, w_value):
    own, up = tokens[0], grad_heads[0]
    other = lax.ppermute(own, "ctx", CORE)
    up_other = lax.ppermute(up, "ctx", CORE)
    mask_other = lax.ppermute(tile_mask[0], "ctx", CORE)
    other, mask_other, up_other = lax.optimization_barrier((other, mask_other, up_other))

    w_query, w_key, w_value = (in_hbm(w) for w in (w_query, w_key, w_value))
    weights, kv_own = project_kv_own(in_hbm(own), w_key, w_value)
    kv = project_kv(other, weights, kv_own)
    kv2 = lax.ppermute(kv, "ctx", chip_pair(2))
    far = {d: lax.ppermute(own, "ctx", chip_pair(d)) for d in (1, 3)}
    query, limits, weights_other = project_query(
        own, other, w_query, w_key, w_value,
        in_hbm(segments), in_hbm(tile_mask[0]), mask_other,
    )
    up = stack_up(up, up_other)
    scores = {0: chip_scores(0, limits, query, up, kv)}
    far[1], kv2, scores[0] = lax.optimization_barrier((far[1], kv2, scores[0]))
    late = lax.ppermute(far[1], "ctx", chip_pair(3))
    mine, theirs = project_kv_far(far[1], far[3], weights, weights_other)
    theirs = lax.ppermute(theirs, "ctx", CORE)
    for i, d in enumerate((1, 3)):
        scores[d] = chip_scores(d, limits, query, up, mine, theirs, part=i)
    scores[2] = chip_scores(2, limits, query, up, kv2)
    factors = softmax_factors([scores[d][2] for d in range(CHIPS)])
    terms, grad_scores = {}, {}
    for d in (3, 1, 2):
        terms[d], grad_scores[d] = chip_terms(d, *scores[d][:2], factors, query, up)
    back = [lax.ppermute(terms[d], "ctx", chip_pair(d)) for d in (3, 1, 2)]
    terms[0], grad_scores[0] = chip_terms(0, *scores[0][:2], factors, query, up)
    dq, middle, theirs = query_grad(
        [scores[d][3] for d in range(CHIPS)], [grad_scores[d] for d in range(CHIPS)]
    )
    late, back, middle = lax.optimization_barrier((late, back, middle))
    dkv = sum_join(terms[0], *back, middle)
    dkv_other = lax.ppermute(dkv, "ctx", CORE)
    packed = pack(dq, dkv, dkv_other)

    far, dkv = lax.optimization_barrier((far, dkv))
    tokens_t = transpose([own, late, far[1], far[3]])
    tokens_t, packed, theirs = lax.optimization_barrier((tokens_t, packed, theirs))
    dq_other = lax.ppermute(theirs, "ctx", CORE)
    other_t = lax.ppermute(tokens_t, "ctx", CORE)
    columns = {d: lax.ppermute(packed[d], "ctx", chip_pair(d)) for d in (2, 1, 3)}
    columns = [packed[0]] + [columns[d] for d in (2, 1, 3)]
    terms = [weight_grad(d, tokens_t, other_t, columns) for d in range(YS)]
    y_parts = [terms[0]] + [lax.ppermute(terms[d], "dp", y_pair(d)) for d in (1, 3, 2)]
    grad_tokens = input_grad(
        dq, dq_other, dkv, dkv_other, w_query, w_key, w_value
    )
    y_parts, grad_tokens = lax.optimization_barrier((y_parts, grad_tokens))
    y_sum = sum_four(*y_parts)
    z_parts = lax.all_to_all(y_sum, "dp", 0, 0, tiled=True, axis_index_groups=Z_GROUPS)
    grad_projection = jnp.sum(z_parts.reshape(ZS, 48, 256).astype(F32), axis=0)
    return grad_tokens[None], grad_projection


def solution(mesh):
    return jax.shard_map(
        shards,
        mesh=mesh,
        in_specs=(
            P("dp", "ctx", None),
            P("dp", "ctx", None),
            P("dp", "ctx", None),
            P("dp", None),
            P(),
            P(),
            P(),
        ),
        out_specs=(P("dp", "ctx", None), P("dp", "ctx")),
        check_vma=False,
    )
```

```python
import functools
import math

import jax
import jax.numpy as jnp
from jax import lax
from jax.experimental import pallas as pl
from jax.experimental.pallas import tpu as pltpu
from jax.sharding import PartitionSpec as P

QH = 12
KVH = 2
HD = 128
TILE = 128
D = 1536
KEYS = 1024
CHIPS = 4
GROUP = QH // KVH
GF = GROUP * HD
STACK = GROUP * 256
YS = 4
ZS = 8
SCALE = 1.0 / math.sqrt(HD)
LOG2_SCALE = SCALE * math.log2(math.e)
BF = jnp.bfloat16
F32 = jnp.float32
VMEM_LIMIT = 24 * 1024 * 1024
W_CHUNKS = 1
Q_CHUNKS = 3
IN_CHUNKS = 3

CORE = [(i, i ^ 1) for i in range(8)]
NT = (((1,), (1,)), ((), ()))


def chip_pair(d):
    return [(i, ((i // 2) ^ d) * 2 + i % 2) for i in range(8)]


def y_pair(d):
    return [(i, ((i // ZS) ^ d) * ZS + i % ZS) for i in range(32)]


Z_GROUPS = [[y * ZS + z for z in range(ZS)] for y in range(YS)]


def dot(a, b):
    return jnp.dot(a, b, preferred_element_type=F32)


def dot_nt(a, b):
    return lax.dot_general(a, b, NT, preferred_element_type=F32)


def in_hbm(array):
    return pltpu.with_memory_space_constraint(array, pltpu.HBM)


def position():
    ctx, dp = lax.axis_index("ctx"), lax.axis_index("dp")
    return lax.div(ctx, 2), lax.rem(ctx, 2), lax.div(dp, ZS)


def cost(flops, bytes_accessed, transcendentals=0):
    return pl.CostEstimate(
        flops=1, bytes_accessed=1, transcendentals=0
    )


PARAMS = pltpu.CompilerParams(vmem_limit_bytes=VMEM_LIMIT)
WHOLE = pl.BlockSpec(memory_space=pltpu.VMEM)
SCALARS = pl.BlockSpec(memory_space=pltpu.SMEM)
STAY = pl.BlockSpec(memory_space=pltpu.HBM)


def kv_own_kernel(own, w_key, w_value, weights, out, rows, sems):
    _, core, _ = position()
    columns = pl.ds(pl.multiple_of(core * HD, HD), HD)
    copies = []
    for chunk in range(W_CHUNKS):
        part = pl.ds(chunk * (TILE // W_CHUNKS), TILE // W_CHUNKS)
        copies.append(pltpu.make_async_copy(own.at[part], rows.at[part], sems.at[chunk, 2]))
        part = pl.ds(chunk * (D // W_CHUNKS), D // W_CHUNKS)
        for side, source in enumerate((w_key, w_value)):
            copies.append(
                pltpu.make_async_copy(
                    source.at[part, columns],
                    weights.at[part, pl.ds(side * HD, HD)],
                    sems.at[chunk, side],
                )
            )
    for copy in copies:
        copy.start()
    for copy in copies:
        copy.wait()
    out[...] = dot(rows[...], weights[...]).astype(BF)


def project_kv_own(own, w_key, w_value):
    return pl.pallas_call(
        kv_own_kernel,
        in_specs=[STAY, STAY, STAY],
        out_specs=[WHOLE, WHOLE],
        out_shape=[
            jax.ShapeDtypeStruct((D, 2 * HD), BF),
            jax.ShapeDtypeStruct((TILE, 2 * HD), BF),
        ],
        scratch_shapes=[pltpu.VMEM((TILE, D), BF), pltpu.SemaphoreType.DMA((W_CHUNKS, 3))],
        compiler_params=PARAMS,
        cost_estimate=cost(2 * TILE * D * 256, 2 * (TILE * D + D * 256)),
        name="project_kv_own",
    )(own, w_key, w_value)


def kv_far_kernel(far1, far3, weights, weights_other, mine, theirs):
    for i, rows in enumerate((far1, far3)):
        part = slice(i * TILE, (i + 1) * TILE)
        theirs[part] = dot(rows[...], weights_other[...]).astype(BF)
        mine[part] = dot(rows[...], weights[...]).astype(BF)


def project_kv_far(far1, far3, weights, weights_other):
    return pl.pallas_call(
        kv_far_kernel,
        in_specs=[WHOLE] * 4,
        out_specs=[WHOLE] * 2,
        out_shape=[jax.ShapeDtypeStruct((2 * TILE, 2 * HD), BF)] * 2,
        compiler_params=PARAMS,
        cost_estimate=cost(8 * TILE * D * 256, 4 * (TILE * D + D * 256)),
        name="project_kv_far",
    )(far1, far3, weights, weights_other)


def kv_kernel(other, weights, kv_own, out):
    out[:TILE] = kv_own[...]
    out[TILE:] = dot(other[...], weights[...]).astype(BF)


def project_kv(other, weights, kv_own):
    return pl.pallas_call(
        kv_kernel,
        in_specs=[WHOLE] * 3,
        out_specs=WHOLE,
        out_shape=jax.ShapeDtypeStruct((2 * TILE, 2 * HD), BF),
        compiler_params=PARAMS,
        cost_estimate=cost(2 * TILE * D * 256, 2 * (TILE * D + D * 256)),
        name="project_kv",
    )(other, weights, kv_own)


def query_kernel(
    own, other, w_query, w_key, w_value, segments_far, mask_far, mask_other,
    out, limits, weights_other, weights, segments, mask_own, sems, small_sems,
):
    chip, core, _ = position()
    theirs = pl.ds(pl.multiple_of((1 - core) * HD, HD), HD)
    small = [
        pltpu.make_async_copy(segments_far, segments, small_sems.at[0]),
        pltpu.make_async_copy(mask_far, mask_own, small_sems.at[1]),
    ]
    for copy in small:
        copy.start()
    columns = pl.ds(pl.multiple_of(core * GF, HD), GF)
    copies = []
    for chunk in range(Q_CHUNKS):
        part = pl.ds(chunk * (D // Q_CHUNKS), D // Q_CHUNKS)
        copies.append(
            pltpu.make_async_copy(w_query.at[part, columns], weights.at[part], sems.at[chunk])
        )
    for side, source in enumerate((w_key, w_value)):
        copies.append(
            pltpu.make_async_copy(
                source.at[:, theirs],
                weights_other.at[:, pl.ds(side * HD, HD)],
                small_sems.at[2 + side],
            )
        )
    for copy in copies:
        copy.start()
    for copy in small:
        copy.wait()

    passages = segments[...]
    ends = [jnp.sum((passages <= s).astype(jnp.int32)) for s in range(3)]
    for slot in range(2):
        masks = mask_own if slot == 0 else mask_other
        tile = 2 * chip + (core if slot == 0 else 1 - core)
        mine = segments[:, pl.ds(pl.multiple_of(tile * TILE, TILE), TILE)]
        low = jnp.where(
            mine == 0, 0, jnp.where(mine == 1, ends[0], jnp.where(mine == 2, ends[1], ends[2]))
        )
        high = jnp.where(
            mine == 0, ends[0], jnp.where(mine == 1, ends[1], jnp.where(mine == 2, ends[2], KEYS))
        )
        for d in range(CHIPS):
            for key_slot in range(2):
                key_tile = 2 * lax.bitwise_xor(chip, jnp.int32(d)) + (
                    core if key_slot == 0 else 1 - core
                )
                seen = masks[0, key_tile] == 1
                row = 4 * d + 2 * key_slot
                place_of = slice(slot * TILE, (slot + 1) * TILE)
                limits[row : row + 1, place_of] = jnp.where(seen, 0, low) - key_tile * TILE
                limits[row + 1 : row + 2, place_of] = (
                    jnp.where(seen, KEYS, high) - key_tile * TILE
                )

    for copy in copies:
        copy.wait()
    for slot, rows in enumerate((own, other)):
        queries = dot(rows[...], weights[...]).astype(BF)
        for head in range(GROUP):
            out[head * 256 + slot * TILE : head * 256 + (slot + 1) * TILE] = queries[
                :, head * HD : (head + 1) * HD
            ]


def project_query(
    own, other, w_query, w_key, w_value, segments, mask_own, mask_other
):
    return pl.pallas_call(
        query_kernel,
        in_specs=[WHOLE, WHOLE] + [STAY] * 5 + [SCALARS],
        out_specs=[WHOLE] * 3,
        out_shape=[
            jax.ShapeDtypeStruct((STACK, HD), BF),
            jax.ShapeDtypeStruct((4 * CHIPS, 2 * TILE), jnp.int32),
            jax.ShapeDtypeStruct((D, 2 * HD), BF),
        ],
        scratch_shapes=[
            pltpu.VMEM((D, GF), BF),
            pltpu.VMEM((1, KEYS), jnp.int32),
            pltpu.SMEM((1, KEYS // TILE), jnp.int32),
            pltpu.SemaphoreType.DMA((Q_CHUNKS,)),
            pltpu.SemaphoreType.DMA((4,)),
        ],
        compiler_params=PARAMS,
        cost_estimate=cost(2 * 256 * D * GF, 2 * (256 * D + D * GF + 256 * GF)),
        name="project_query",
    )(own, other, w_query, w_key, w_value, segments, mask_own, mask_other)


def stack_kernel(up_own, up_other, out):
    _, core, _ = position()
    for slot, rows in enumerate((up_own, up_other)):
        for head in range(GROUP):
            columns = pl.ds(pl.multiple_of(core * GF + head * HD, HD), HD)
            out[head * 256 + slot * TILE : head * 256 + (slot + 1) * TILE] = rows[:, columns]


def stack_up(up_own, up_other):
    return pl.pallas_call(
        stack_kernel,
        in_specs=[WHOLE, WHOLE],
        out_specs=WHOLE,
        out_shape=jax.ShapeDtypeStruct((STACK, HD), BF),
        compiler_params=PARAMS,
        cost_estimate=cost(0, 4 * STACK * HD),
        name="stack_up",
    )(up_own, up_other)


def scores_kernel(d, part, limits, query, up, *refs):
    powers, grads, stats, keys_t = refs[-4:]
    rows = slice(None) if part is None else slice(part * TILE, (part + 1) * TILE)
    kv = jnp.concatenate([ref[rows] for ref in refs[:-4]], axis=0)
    keys, values = kv[:, :HD], kv[:, HD:]
    keys_t[...] = keys.T
    position = lax.broadcasted_iota(jnp.int32, (TILE, 2 * TILE), 0)
    bias = []
    for key_slot in range(2):
        row = 4 * d + 2 * key_slot
        allowed = (position >= limits[row : row + 1]) & (position < limits[row + 1 : row + 2])
        bias.append(jnp.where(allowed, 0.0, -jnp.inf))
    bias = jnp.concatenate(bias, axis=0)
    for head in range(GROUP):
        part = slice(head * 256, (head + 1) * 256)
        scores = dot_nt(keys, query[part]) * LOG2_SCALE + bias
        top = jnp.max(scores, axis=0, keepdims=True)
        power = jnp.exp2(scores - jnp.where(top == -jnp.inf, 0.0, top))
        grad = dot_nt(values, up[part])
        powers[:, part] = power
        grads[:, part] = grad
        stats[0:1, part] = top
        stats[1:2, part] = jnp.sum(power, axis=0, keepdims=True)
        stats[2:3, part] = jnp.sum(power * grad, axis=0, keepdims=True)


def chip_scores(d, limits, query, up, *kv, part=None):
    return pl.pallas_call(
        functools.partial(scores_kernel, d, part),
        in_specs=[WHOLE] * (3 + len(kv)),
        out_specs=[WHOLE] * 4,
        out_shape=[
            jax.ShapeDtypeStruct((256, STACK), F32),
            jax.ShapeDtypeStruct((256, STACK), F32),
            jax.ShapeDtypeStruct((8, STACK), F32),
            jax.ShapeDtypeStruct((HD, 256), BF),
        ],
        compiler_params=PARAMS,
        cost_estimate=cost(4 * STACK * 256 * HD, 10 * 256 * STACK, 256 * STACK),
        name=f"chip_scores_{d}",
    )(limits, query, up, *kv)


def factors_kernel(a, b, c, d, out):
    parts = (a, b, c, d)
    top = jnp.maximum(jnp.maximum(a[0:1], b[0:1]), jnp.maximum(c[0:1], d[0:1]))
    factors = [jnp.exp2(part[0:1] - top) for part in parts]
    total = sum(factor * part[1:2] for factor, part in zip(factors, parts))
    factors = [factor / total for factor in factors]
    for chip, factor in enumerate(factors):
        out[chip : chip + 1] = factor
    out[4:5] = sum(factor * part[2:3] for factor, part in zip(factors, parts))


def softmax_factors(stats):
    return pl.pallas_call(
        factors_kernel,
        in_specs=[WHOLE] * 4,
        out_specs=WHOLE,
        out_shape=jax.ShapeDtypeStruct((8, STACK), F32),
        compiler_params=PARAMS,
        cost_estimate=cost(20 * STACK, 128 * STACK),
        name="softmax_factors",
    )(*stats)


def terms_kernel(d, powers, grads, factors, query, up, out, grad_scores, probs_low):
    for head in range(GROUP):
        part = slice(head * 256, (head + 1) * 256)
        probs = powers[:, part] * factors[d : d + 1, part]
        probs_low[:, part] = probs.astype(BF)
        grad_scores[:, part] = (probs * (grads[:, part] - factors[4:5, part])).astype(BF)
    out[:, :HD] = (dot(grad_scores[...], query[...]) * SCALE).astype(out.dtype)
    out[:, HD:] = dot(probs_low[...], up[...]).astype(out.dtype)


def chip_terms(d, powers, grads, factors, query, up):
    return pl.pallas_call(
        functools.partial(terms_kernel, d),
        in_specs=[WHOLE] * 5,
        out_specs=[WHOLE] * 2,
        out_shape=[
            jax.ShapeDtypeStruct((256, 256), F32 if d == 0 else BF),
            jax.ShapeDtypeStruct((256, STACK), BF),
        ],
        scratch_shapes=[pltpu.VMEM((256, STACK), BF)],
        compiler_params=PARAMS,
        cost_estimate=cost(4 * STACK * 256 * HD, 10 * 256 * STACK),
        name=f"chip_terms_{d}",
    )(powers, grads, factors, query, up)


def query_grad_kernel(k0, k1, k2, k3, g0, g1, g2, g3, out, middle, theirs):
    for head in range(GROUP):
        part = slice(head * 256, (head + 1) * 256)
        total = dot(k0[...], g0[:, part]) + dot(k1[...], g1[:, part])
        total += dot(k2[...], g2[:, part]) + dot(k3[...], g3[:, part])
        columns = slice(head * HD, (head + 1) * HD)
        result = (total * SCALE).T.astype(BF)
        out[:, columns] = result
        theirs[:, columns] = result[TILE:]
        if 2 <= head < 4:
            middle[:, (head - 2) * HD : (head - 1) * HD] = result


def query_grad(keys_t, grad_scores):
    return pl.pallas_call(
        query_grad_kernel,
        in_specs=[WHOLE] * 8,
        out_specs=[WHOLE] * 3,
        out_shape=[
            jax.ShapeDtypeStruct((256, GF), BF),
            jax.ShapeDtypeStruct((256, 256), BF),
            jax.ShapeDtypeStruct((TILE, GF), BF),
        ],
        compiler_params=PARAMS,
        cost_estimate=cost(2 * STACK * KEYS * HD, 2 * STACK * KEYS),
        name="query_grad",
    )(*keys_t, *grad_scores)


def sum_kernel(a, b, c, d, out):
    total = (a[...] + b[...].astype(F32)) + (c[...].astype(F32) + d[...].astype(F32))
    out[...] = total.astype(out.dtype)


def join_kernel(a, b, c, d, beside, out):
    total = (a[...] + b[...].astype(F32)) + (c[...].astype(F32) + d[...].astype(F32))
    out[:, :256] = total.astype(out.dtype)
    out[:, 256:] = beside[...]


def sum_join(a, b, c, d, beside):
    return pl.pallas_call(
        join_kernel,
        in_specs=[WHOLE] * 5,
        out_specs=WHOLE,
        out_shape=jax.ShapeDtypeStruct((256, 512), BF),
        compiler_params=PARAMS,
        cost_estimate=cost(4 * a.size, 12 * a.size),
        name="sum_join",
    )(a, b, c, d, beside)


def sum_four(a, b, c, d):
    return pl.pallas_call(
        sum_kernel,
        in_specs=[WHOLE] * 4,
        out_specs=WHOLE,
        out_shape=jax.ShapeDtypeStruct(a.shape, BF),
        compiler_params=PARAMS,
        cost_estimate=cost(4 * a.size, 12 * a.size),
        name="sum_four",
    )(a, b, c, d)


def pack_kernel(dq, joined, joined_other, *outs):
    my_chip, my_core, _ = position()
    for core in range(2):
        own_part = slice(core * HD, (core + 1) * HD)
        for chip in range(CHIPS):

            @pl.when((my_core == core) & (my_chip == chip))
            def _(core=core, own_part=own_part, chip=chip):
                for d, out in enumerate(outs):
                    target = chip ^ d
                    if target == 3:
                        out[:, own_part] = joined[:, own_part]
                        theirs = slice((1 - core) * HD, (2 - core) * HD)
                        out[:TILE, theirs] = joined_other[TILE:, own_part]
                        out[TILE:, theirs] = joined_other[:TILE, own_part]
                    elif target == 2 - 2 * core:
                        out[:TILE] = joined_other[TILE:, 256:]
                        out[TILE:] = joined_other[:TILE, 256:]
                    else:
                        first = target == core
                        out[...] = dq[:, 0:256] if first else dq[:, 512:768]


def pack(dq, joined, joined_other):
    return pl.pallas_call(
        pack_kernel,
        in_specs=[WHOLE] * 3,
        out_specs=[WHOLE] * 4,
        out_shape=[jax.ShapeDtypeStruct((256, 256), BF)] * 4,
        compiler_params=PARAMS,
        cost_estimate=cost(0, 4 << 19),
        name="pack",
    )(dq, joined, joined_other)


def transpose_kernel(own, far2, far1, far3, out):
    for i, rows in enumerate((own, far2, far1, far3)):
        out[:, i * TILE : (i + 1) * TILE] = rows[...].T


def transpose(parts):
    return pl.pallas_call(
        transpose_kernel,
        in_specs=[WHOLE] * 4,
        out_specs=WHOLE,
        out_shape=jax.ShapeDtypeStruct((D, KEYS // 2), BF),
        compiler_params=PARAMS,
        cost_estimate=cost(0, 2 * D * KEYS),
        name="transpose_tokens",
    )(*parts)


def weight_kernel(shift, tokens_t, other_t, a, b, c, d, out):
    parts = (a, b, c, d)
    right = jnp.concatenate([part[:TILE] for part in parts], axis=0)
    right_other = jnp.concatenate([part[TILE:] for part in parts], axis=0)
    _, _, chip = position()
    row = pl.multiple_of(lax.bitwise_xor(chip, jnp.int32(shift)) * (D // YS), 128)
    rows = pl.ds(row, D // YS)
    total = dot(tokens_t[rows], right) + dot(other_t[rows], right_other)
    out[...] = total.astype(out.dtype)


def weight_grad(shift, tokens_t, other_t, parts):
    return pl.pallas_call(
        functools.partial(weight_kernel, shift),
        in_specs=[WHOLE] * 6,
        out_specs=WHOLE,
        out_shape=jax.ShapeDtypeStruct((D // YS, 256), F32 if shift == 0 else BF),
        compiler_params=PARAMS,
        cost_estimate=cost(2 * D * KEYS * 256 // YS, 2 * D * KEYS // YS),
        name=f"weight_grad_{shift}",
    )(tokens_t, other_t, *parts)


def input_kernel(
    dq, dq_other, dkv, dkv_other, w_query, w_key, w_value, out, left, right, sems
):
    _, core, _ = position()
    width = D // IN_CHUNKS
    copies = []
    for chunk in range(IN_CHUNKS):
        part = pl.ds(chunk * width, width)
        copies.append(
            [
                pltpu.make_async_copy(
                    source.at[part],
                    right.at[part, pl.ds(start, size)],
                    sems.at[chunk, side],
                )
                for side, (source, start, size) in enumerate(
                    ((w_query, 0, D), (w_key, D, 256), (w_value, D + 256, 256))
                )
            ]
        )
    for group in copies:
        for copy in group:
            copy.start()
    mine = pl.ds(pl.multiple_of(core * GF, 128), GF)
    theirs = pl.ds(pl.multiple_of((1 - core) * GF, 128), GF)
    left[:, mine] = dq[:TILE]
    left[:, theirs] = dq_other[...]
    for part in range(2):
        columns = slice(part * HD, (part + 1) * HD)
        base = D + part * KVH * HD
        left[:, pl.ds(pl.multiple_of(base + core * HD, 128), HD)] = dkv[:TILE, columns]
        left[:, pl.ds(pl.multiple_of(base + (1 - core) * HD, 128), HD)] = dkv_other[
            TILE:, columns
        ]
    for chunk, group in enumerate(copies):
        for copy in group:
            copy.wait()
        part = slice(chunk * width, (chunk + 1) * width)
        out[:, part] = dot_nt(left[...], right[part]).astype(BF)


def input_grad(dq, dq_other, dkv, dkv_other, w_query, w_key, w_value):
    return pl.pallas_call(
        input_kernel,
        in_specs=[WHOLE] * 4 + [STAY] * 3,
        out_specs=WHOLE,
        out_shape=jax.ShapeDtypeStruct((TILE, D), BF),
        scratch_shapes=[
            pltpu.VMEM((TILE, D + 512), BF),
            pltpu.VMEM((D, D + 512), BF),
            pltpu.SemaphoreType.DMA((IN_CHUNKS, 3)),
        ],
        compiler_params=PARAMS,
        cost_estimate=cost(2 * TILE * D * 2048, 2 * D * 2048),
        name="input_grad",
    )(dq, dq_other, dkv, dkv_other, w_query, w_key, w_value)


def shards(tokens, grad_heads, tile_mask, segments, w_query, w_key, w_value):
    own, up = tokens[0], grad_heads[0]
    other = lax.ppermute(own, "ctx", CORE)
    up_other = lax.ppermute(up, "ctx", CORE)
    mask_other = lax.ppermute(tile_mask[0], "ctx", CORE)
    other, mask_other, up_other = lax.optimization_barrier((other, mask_other, up_other))

    w_query, w_key, w_value = (in_hbm(w) for w in (w_query, w_key, w_value))
    weights, kv_own = project_kv_own(in_hbm(own), w_key, w_value)
    kv = project_kv(other, weights, kv_own)
    kv2 = lax.ppermute(kv, "ctx", chip_pair(2))
    far = {d: lax.ppermute(own, "ctx", chip_pair(d)) for d in (1, 3)}
    query, limits, weights_other = project_query(
        own, other, w_query, w_key, w_value,
        in_hbm(segments), in_hbm(tile_mask[0]), mask_other,
    )
    up = stack_up(up, up_other)
    scores = {0: chip_scores(0, limits, query, up, kv)}
    far[1], kv2, scores[0] = lax.optimization_barrier((far[1], kv2, scores[0]))
    late = lax.ppermute(far[1], "ctx", chip_pair(3))
    mine, theirs = project_kv_far(far[1], far[3], weights, weights_other)
    theirs = lax.ppermute(theirs, "ctx", CORE)
    for i, d in enumerate((1, 3)):
        scores[d] = chip_scores(d, limits, query, up, mine, theirs, part=i)
    scores[2] = chip_scores(2, limits, query, up, kv2)
    factors = softmax_factors([scores[d][2] for d in range(CHIPS)])
    terms, grad_scores = {}, {}
    for d in (3, 1, 2):
        terms[d], grad_scores[d] = chip_terms(d, *scores[d][:2], factors, query, up)
    back = [lax.ppermute(terms[d], "ctx", chip_pair(d)) for d in (1, 3, 2)]
    terms[0], grad_scores[0] = chip_terms(0, *scores[0][:2], factors, query, up)
    dq, middle, theirs = query_grad(
        [scores[d][3] for d in range(CHIPS)], [grad_scores[d] for d in range(CHIPS)]
    )
    late, back, middle = lax.optimization_barrier((late, back, middle))
    dkv = sum_join(terms[0], *back, middle)
    dkv_other = lax.ppermute(dkv, "ctx", CORE)
    packed = pack(dq, dkv, dkv_other)

    far, dkv = lax.optimization_barrier((far, dkv))
    tokens_t = transpose([own, late, far[1], far[3]])
    tokens_t, packed, theirs = lax.optimization_barrier((tokens_t, packed, theirs))
    dq_other = lax.ppermute(theirs, "ctx", CORE)
    other_t = lax.ppermute(tokens_t, "ctx", CORE)
    columns = {d: lax.ppermute(packed[d], "ctx", chip_pair(d)) for d in (2, 1, 3)}
    columns = [packed[0]] + [columns[d] for d in (2, 1, 3)]
    terms = [weight_grad(d, tokens_t, other_t, columns) for d in range(YS)]
    y_parts = [terms[0]] + [lax.ppermute(terms[d], "dp", y_pair(d)) for d in (1, 3, 2)]
    grad_tokens = input_grad(
        dq, dq_other, dkv, dkv_other, w_query, w_key, w_value
    )
    y_parts, grad_tokens = lax.optimization_barrier((y_parts, grad_tokens))
    y_sum = sum_four(*y_parts)
    z_parts = lax.all_to_all(y_sum, "dp", 0, 0, tiled=True, axis_index_groups=Z_GROUPS)
    grad_projection = jnp.sum(z_parts.reshape(ZS, 48, 256).astype(F32), axis=0)
    return grad_tokens[None], grad_projection


def solution(mesh):
    return jax.shard_map(
        shards,
        mesh=mesh,
        in_specs=(
            P("dp", "ctx", None),
            P("dp", "ctx", None),
            P("dp", "ctx", None),
            P("dp", None),
            P(),
            P(),
            P(),
        ),
        out_specs=(P("dp", "ctx", None), P("dp", "ctx")),
        check_vma=False,
    )
```

```python
import functools
import math

import jax
import jax.numpy as jnp
from jax import lax
from jax.experimental import pallas as pl
from jax.experimental.pallas import tpu as pltpu
from jax.sharding import PartitionSpec as P

QH = 12
KVH = 2
HD = 128
TILE = 128
D = 1536
KEYS = 1024
CHIPS = 4
GROUP = QH // KVH
GF = GROUP * HD
STACK = GROUP * 256
YS = 4
ZS = 8
SCALE = 1.0 / math.sqrt(HD)
LOG2_SCALE = SCALE * math.log2(math.e)
BF = jnp.bfloat16
F32 = jnp.float32
VMEM_LIMIT = 24 * 1024 * 1024
W_CHUNKS = 1
Q_CHUNKS = 3
IN_CHUNKS = 3

CORE = [(i, i ^ 1) for i in range(8)]
NT = (((1,), (1,)), ((), ()))


def chip_pair(d):
    return [(i, ((i // 2) ^ d) * 2 + i % 2) for i in range(8)]


def y_pair(d):
    return [(i, ((i // ZS) ^ d) * ZS + i % ZS) for i in range(32)]


Z_GROUPS = [[y * ZS + z for z in range(ZS)] for y in range(YS)]


def dot(a, b):
    return jnp.dot(a, b, preferred_element_type=F32)


def dot_nt(a, b):
    return lax.dot_general(a, b, NT, preferred_element_type=F32)


def in_hbm(array):
    return pltpu.with_memory_space_constraint(array, pltpu.HBM)


def position():
    ctx, dp = lax.axis_index("ctx"), lax.axis_index("dp")
    return lax.div(ctx, 2), lax.rem(ctx, 2), lax.div(dp, ZS)


def cost(flops, bytes_accessed, transcendentals=0):
    return pl.CostEstimate(
        flops=1, bytes_accessed=1, transcendentals=0
    )


PARAMS = pltpu.CompilerParams(vmem_limit_bytes=VMEM_LIMIT)
WHOLE = pl.BlockSpec(memory_space=pltpu.VMEM)
SCALARS = pl.BlockSpec(memory_space=pltpu.SMEM)
STAY = pl.BlockSpec(memory_space=pltpu.HBM)


def kv_own_kernel(own, w_key, w_value, weights, out, rows, sems):
    _, core, _ = position()
    columns = pl.ds(pl.multiple_of(core * HD, HD), HD)
    copies = []
    for chunk in range(W_CHUNKS):
        part = pl.ds(chunk * (TILE // W_CHUNKS), TILE // W_CHUNKS)
        copies.append(pltpu.make_async_copy(own.at[part], rows.at[part], sems.at[chunk, 2]))
        part = pl.ds(chunk * (D // W_CHUNKS), D // W_CHUNKS)
        for side, source in enumerate((w_key, w_value)):
            copies.append(
                pltpu.make_async_copy(
                    source.at[part, columns],
                    weights.at[part, pl.ds(side * HD, HD)],
                    sems.at[chunk, side],
                )
            )
    for copy in copies:
        copy.start()
    for copy in copies:
        copy.wait()
    out[...] = dot(rows[...], weights[...]).astype(BF)


def project_kv_own(own, w_key, w_value):
    return pl.pallas_call(
        kv_own_kernel,
        in_specs=[STAY, STAY, STAY],
        out_specs=[WHOLE, WHOLE],
        out_shape=[
            jax.ShapeDtypeStruct((D, 2 * HD), BF),
            jax.ShapeDtypeStruct((TILE, 2 * HD), BF),
        ],
        scratch_shapes=[pltpu.VMEM((TILE, D), BF), pltpu.SemaphoreType.DMA((W_CHUNKS, 3))],
        compiler_params=PARAMS,
        cost_estimate=cost(2 * TILE * D * 256, 2 * (TILE * D + D * 256)),
        name="project_kv_own",
    )(own, w_key, w_value)


def kv_far_kernel(far1, far3, weights, out):
    out[:TILE] = dot(far1[...], weights[...]).astype(BF)
    out[TILE:] = dot(far3[...], weights[...]).astype(BF)


def project_kv_far(far1, far3, weights):
    return pl.pallas_call(
        kv_far_kernel,
        in_specs=[WHOLE] * 3,
        out_specs=WHOLE,
        out_shape=jax.ShapeDtypeStruct((2 * TILE, 2 * HD), BF),
        compiler_params=PARAMS,
        cost_estimate=cost(4 * TILE * D * 256, 2 * (2 * TILE * D + D * 256)),
        name="project_kv_far",
    )(far1, far3, weights)


def kv_kernel(other, weights, kv_own, out):
    out[:TILE] = kv_own[...]
    out[TILE:] = dot(other[...], weights[...]).astype(BF)


def project_kv(other, weights, kv_own):
    return pl.pallas_call(
        kv_kernel,
        in_specs=[WHOLE] * 3,
        out_specs=WHOLE,
        out_shape=jax.ShapeDtypeStruct((2 * TILE, 2 * HD), BF),
        compiler_params=PARAMS,
        cost_estimate=cost(2 * TILE * D * 256, 2 * (TILE * D + D * 256)),
        name="project_kv",
    )(other, weights, kv_own)


def query_kernel(
    own, other, w_query, w_key, w_value, segments_far, mask_far, mask_other,
    out, limits, weights_other, weights, segments, mask_own, sems, small_sems,
):
    chip, core, _ = position()
    theirs = pl.ds(pl.multiple_of((1 - core) * HD, HD), HD)
    small = [
        pltpu.make_async_copy(segments_far, segments, small_sems.at[0]),
        pltpu.make_async_copy(mask_far, mask_own, small_sems.at[1]),
    ]
    for copy in small:
        copy.start()
    columns = pl.ds(pl.multiple_of(core * GF, HD), GF)
    copies = []
    for chunk in range(Q_CHUNKS):
        part = pl.ds(chunk * (D // Q_CHUNKS), D // Q_CHUNKS)
        copies.append(
            pltpu.make_async_copy(w_query.at[part, columns], weights.at[part], sems.at[chunk])
        )
    for side, source in enumerate((w_key, w_value)):
        copies.append(
            pltpu.make_async_copy(
                source.at[:, theirs],
                weights_other.at[:, pl.ds(side * HD, HD)],
                small_sems.at[2 + side],
            )
        )
    for copy in copies:
        copy.start()
    for copy in small:
        copy.wait()

    passages = segments[...]
    ends = [jnp.sum((passages <= s).astype(jnp.int32)) for s in range(3)]
    for slot in range(2):
        masks = mask_own if slot == 0 else mask_other
        tile = 2 * chip + (core if slot == 0 else 1 - core)
        mine = segments[:, pl.ds(pl.multiple_of(tile * TILE, TILE), TILE)]
        low = jnp.where(
            mine == 0, 0, jnp.where(mine == 1, ends[0], jnp.where(mine == 2, ends[1], ends[2]))
        )
        high = jnp.where(
            mine == 0, ends[0], jnp.where(mine == 1, ends[1], jnp.where(mine == 2, ends[2], KEYS))
        )
        for d in range(CHIPS):
            for key_slot in range(2):
                key_tile = 2 * lax.bitwise_xor(chip, jnp.int32(d)) + (
                    core if key_slot == 0 else 1 - core
                )
                seen = masks[0, key_tile] == 1
                row = 4 * d + 2 * key_slot
                place_of = slice(slot * TILE, (slot + 1) * TILE)
                limits[row : row + 1, place_of] = jnp.where(seen, 0, low) - key_tile * TILE
                limits[row + 1 : row + 2, place_of] = (
                    jnp.where(seen, KEYS, high) - key_tile * TILE
                )

    for copy in copies:
        copy.wait()
    for slot, rows in enumerate((own, other)):
        queries = dot(rows[...], weights[...]).astype(BF)
        for head in range(GROUP):
            out[head * 256 + slot * TILE : head * 256 + (slot + 1) * TILE] = queries[
                :, head * HD : (head + 1) * HD
            ]


def project_query(
    own, other, w_query, w_key, w_value, segments, mask_own, mask_other
):
    return pl.pallas_call(
        query_kernel,
        in_specs=[WHOLE, WHOLE] + [STAY] * 5 + [SCALARS],
        out_specs=[WHOLE] * 3,
        out_shape=[
            jax.ShapeDtypeStruct((STACK, HD), BF),
            jax.ShapeDtypeStruct((4 * CHIPS, 2 * TILE), jnp.int32),
            jax.ShapeDtypeStruct((D, 2 * HD), BF),
        ],
        scratch_shapes=[
            pltpu.VMEM((D, GF), BF),
            pltpu.VMEM((1, KEYS), jnp.int32),
            pltpu.SMEM((1, KEYS // TILE), jnp.int32),
            pltpu.SemaphoreType.DMA((Q_CHUNKS,)),
            pltpu.SemaphoreType.DMA((4,)),
        ],
        compiler_params=PARAMS,
        cost_estimate=cost(2 * 256 * D * GF, 2 * (256 * D + D * GF + 256 * GF)),
        name="project_query",
    )(own, other, w_query, w_key, w_value, segments, mask_own, mask_other)


def stack_kernel(up_own, up_other, out):
    _, core, _ = position()
    for slot, rows in enumerate((up_own, up_other)):
        for head in range(GROUP):
            columns = pl.ds(pl.multiple_of(core * GF + head * HD, HD), HD)
            out[head * 256 + slot * TILE : head * 256 + (slot + 1) * TILE] = rows[:, columns]


def stack_up(up_own, up_other):
    return pl.pallas_call(
        stack_kernel,
        in_specs=[WHOLE, WHOLE],
        out_specs=WHOLE,
        out_shape=jax.ShapeDtypeStruct((STACK, HD), BF),
        compiler_params=PARAMS,
        cost_estimate=cost(0, 4 * STACK * HD),
        name="stack_up",
    )(up_own, up_other)


def scores_kernel(d, part, limits, query, up, *refs):
    powers, grads, stats, keys_t = refs[-4:]
    rows = slice(None) if part is None else slice(part * TILE, (part + 1) * TILE)
    kv = jnp.concatenate([ref[rows] for ref in refs[:-4]], axis=0)
    keys, values = kv[:, :HD], kv[:, HD:]
    keys_t[...] = keys.T
    position = lax.broadcasted_iota(jnp.int32, (TILE, 2 * TILE), 0)
    bias = []
    for key_slot in range(2):
        row = 4 * d + 2 * key_slot
        allowed = (position >= limits[row : row + 1]) & (position < limits[row + 1 : row + 2])
        bias.append(jnp.where(allowed, 0.0, -jnp.inf))
    bias = jnp.concatenate(bias, axis=0)
    for head in range(GROUP):
        part = slice(head * 256, (head + 1) * 256)
        scores = dot_nt(keys, query[part]) * LOG2_SCALE + bias
        top = jnp.max(scores, axis=0, keepdims=True)
        power = jnp.exp2(scores - jnp.where(top == -jnp.inf, 0.0, top))
        grad = dot_nt(values, up[part])
        powers[:, part] = power
        grads[:, part] = grad
        stats[0:1, part] = top
        stats[1:2, part] = jnp.sum(power, axis=0, keepdims=True)
        stats[2:3, part] = jnp.sum(power * grad, axis=0, keepdims=True)


def chip_scores(d, limits, query, up, *kv, part=None):
    return pl.pallas_call(
        functools.partial(scores_kernel, d, part),
        in_specs=[WHOLE] * (3 + len(kv)),
        out_specs=[WHOLE] * 4,
        out_shape=[
            jax.ShapeDtypeStruct((256, STACK), F32),
            jax.ShapeDtypeStruct((256, STACK), F32),
            jax.ShapeDtypeStruct((8, STACK), F32),
            jax.ShapeDtypeStruct((HD, 256), BF),
        ],
        compiler_params=PARAMS,
        cost_estimate=cost(4 * STACK * 256 * HD, 10 * 256 * STACK, 256 * STACK),
        name=f"chip_scores_{d}",
    )(limits, query, up, *kv)


def factors_kernel(a, b, c, d, out):
    parts = (a, b, c, d)
    top = jnp.maximum(jnp.maximum(a[0:1], b[0:1]), jnp.maximum(c[0:1], d[0:1]))
    factors = [jnp.exp2(part[0:1] - top) for part in parts]
    total = sum(factor * part[1:2] for factor, part in zip(factors, parts))
    factors = [factor / total for factor in factors]
    for chip, factor in enumerate(factors):
        out[chip : chip + 1] = factor
    out[4:5] = sum(factor * part[2:3] for factor, part in zip(factors, parts))


def softmax_factors(stats):
    return pl.pallas_call(
        factors_kernel,
        in_specs=[WHOLE] * 4,
        out_specs=WHOLE,
        out_shape=jax.ShapeDtypeStruct((8, STACK), F32),
        compiler_params=PARAMS,
        cost_estimate=cost(20 * STACK, 128 * STACK),
        name="softmax_factors",
    )(*stats)


def terms_kernel(d, powers, grads, factors, query, up, out, grad_scores, probs_low):
    for head in range(GROUP):
        part = slice(head * 256, (head + 1) * 256)
        probs = powers[:, part] * factors[d : d + 1, part]
        probs_low[:, part] = probs.astype(BF)
        grad_scores[:, part] = (probs * (grads[:, part] - factors[4:5, part])).astype(BF)
    out[:, :HD] = (dot(grad_scores[...], query[...]) * SCALE).astype(out.dtype)
    out[:, HD:] = dot(probs_low[...], up[...]).astype(out.dtype)


def chip_terms(d, powers, grads, factors, query, up):
    return pl.pallas_call(
        functools.partial(terms_kernel, d),
        in_specs=[WHOLE] * 5,
        out_specs=[WHOLE] * 2,
        out_shape=[
            jax.ShapeDtypeStruct((256, 256), F32 if d == 0 else BF),
            jax.ShapeDtypeStruct((256, STACK), BF),
        ],
        scratch_shapes=[pltpu.VMEM((256, STACK), BF)],
        compiler_params=PARAMS,
        cost_estimate=cost(4 * STACK * 256 * HD, 10 * 256 * STACK),
        name=f"chip_terms_{d}",
    )(powers, grads, factors, query, up)


def query_grad_kernel(k0, k1, k2, k3, g0, g1, g2, g3, out, middle, theirs):
    for head in range(GROUP):
        part = slice(head * 256, (head + 1) * 256)
        total = dot(k0[...], g0[:, part]) + dot(k1[...], g1[:, part])
        total += dot(k2[...], g2[:, part]) + dot(k3[...], g3[:, part])
        columns = slice(head * HD, (head + 1) * HD)
        result = (total * SCALE).T.astype(BF)
        out[:, columns] = result
        theirs[:, columns] = result[TILE:]
        if 2 <= head < 4:
            middle[:, (head - 2) * HD : (head - 1) * HD] = result


def query_grad(keys_t, grad_scores):
    return pl.pallas_call(
        query_grad_kernel,
        in_specs=[WHOLE] * 8,
        out_specs=[WHOLE] * 3,
        out_shape=[
            jax.ShapeDtypeStruct((256, GF), BF),
            jax.ShapeDtypeStruct((256, 256), BF),
            jax.ShapeDtypeStruct((TILE, GF), BF),
        ],
        compiler_params=PARAMS,
        cost_estimate=cost(2 * STACK * KEYS * HD, 2 * STACK * KEYS),
        name="query_grad",
    )(*keys_t, *grad_scores)


def sum_kernel(a, b, c, d, out):
    total = (a[...] + b[...].astype(F32)) + (c[...].astype(F32) + d[...].astype(F32))
    out[...] = total.astype(out.dtype)


def join_kernel(a, b, c, d, beside, out):
    total = (a[...] + b[...].astype(F32)) + (c[...].astype(F32) + d[...].astype(F32))
    out[:, :256] = total.astype(out.dtype)
    out[:, 256:] = beside[...]


def sum_join(a, b, c, d, beside):
    return pl.pallas_call(
        join_kernel,
        in_specs=[WHOLE] * 5,
        out_specs=WHOLE,
        out_shape=jax.ShapeDtypeStruct((256, 512), BF),
        compiler_params=PARAMS,
        cost_estimate=cost(4 * a.size, 12 * a.size),
        name="sum_join",
    )(a, b, c, d, beside)


def sum_four(a, b, c, d):
    return pl.pallas_call(
        sum_kernel,
        in_specs=[WHOLE] * 4,
        out_specs=WHOLE,
        out_shape=jax.ShapeDtypeStruct(a.shape, BF),
        compiler_params=PARAMS,
        cost_estimate=cost(4 * a.size, 12 * a.size),
        name="sum_four",
    )(a, b, c, d)


def pack_kernel(dq, joined, joined_other, *outs):
    my_chip, my_core, _ = position()
    for core in range(2):
        own_part = slice(core * HD, (core + 1) * HD)
        for chip in range(CHIPS):

            @pl.when((my_core == core) & (my_chip == chip))
            def _(core=core, own_part=own_part, chip=chip):
                for d, out in enumerate(outs):
                    target = chip ^ d
                    if target == 3:
                        out[:, own_part] = joined[:, own_part]
                        theirs = slice((1 - core) * HD, (2 - core) * HD)
                        out[:TILE, theirs] = joined_other[TILE:, own_part]
                        out[TILE:, theirs] = joined_other[:TILE, own_part]
                    elif target == 2 - 2 * core:
                        out[:TILE] = joined_other[TILE:, 256:]
                        out[TILE:] = joined_other[:TILE, 256:]
                    else:
                        first = target == core
                        out[...] = dq[:, 0:256] if first else dq[:, 512:768]


def pack(dq, joined, joined_other):
    return pl.pallas_call(
        pack_kernel,
        in_specs=[WHOLE] * 3,
        out_specs=[WHOLE] * 4,
        out_shape=[jax.ShapeDtypeStruct((256, 256), BF)] * 4,
        compiler_params=PARAMS,
        cost_estimate=cost(0, 4 << 19),
        name="pack",
    )(dq, joined, joined_other)


def transpose_kernel(own, far2, far1, far3, out):
    for i, rows in enumerate((own, far2, far1, far3)):
        out[:, i * TILE : (i + 1) * TILE] = rows[...].T


def transpose(parts):
    return pl.pallas_call(
        transpose_kernel,
        in_specs=[WHOLE] * 4,
        out_specs=WHOLE,
        out_shape=jax.ShapeDtypeStruct((D, KEYS // 2), BF),
        compiler_params=PARAMS,
        cost_estimate=cost(0, 2 * D * KEYS),
        name="transpose_tokens",
    )(*parts)


def weight_kernel(shift, tokens_t, other_t, a, b, c, d, out):
    parts = (a, b, c, d)
    right = jnp.concatenate([part[:TILE] for part in parts], axis=0)
    right_other = jnp.concatenate([part[TILE:] for part in parts], axis=0)
    _, _, chip = position()
    row = pl.multiple_of(lax.bitwise_xor(chip, jnp.int32(shift)) * (D // YS), 128)
    rows = pl.ds(row, D // YS)
    total = dot(tokens_t[rows], right) + dot(other_t[rows], right_other)
    out[...] = total.astype(out.dtype)


def weight_grad(shift, tokens_t, other_t, parts):
    return pl.pallas_call(
        functools.partial(weight_kernel, shift),
        in_specs=[WHOLE] * 6,
        out_specs=WHOLE,
        out_shape=jax.ShapeDtypeStruct((D // YS, 256), F32 if shift == 0 else BF),
        compiler_params=PARAMS,
        cost_estimate=cost(2 * D * KEYS * 256 // YS, 2 * D * KEYS // YS),
        name=f"weight_grad_{shift}",
    )(tokens_t, other_t, *parts)


def input_kernel(
    dq, dq_other, dkv, dkv_other, w_query, w_key, w_value, out, left, right, sems
):
    _, core, _ = position()
    width = D // IN_CHUNKS
    copies = []
    for chunk in range(IN_CHUNKS):
        part = pl.ds(chunk * width, width)
        copies.append(
            [
                pltpu.make_async_copy(
                    source.at[part],
                    right.at[part, pl.ds(start, size)],
                    sems.at[chunk, side],
                )
                for side, (source, start, size) in enumerate(
                    ((w_query, 0, D), (w_key, D, 256), (w_value, D + 256, 256))
                )
            ]
        )
    for group in copies:
        for copy in group:
            copy.start()
    mine = pl.ds(pl.multiple_of(core * GF, 128), GF)
    theirs = pl.ds(pl.multiple_of((1 - core) * GF, 128), GF)
    left[:, mine] = dq[:TILE]
    left[:, theirs] = dq_other[...]
    for part in range(2):
        columns = slice(part * HD, (part + 1) * HD)
        base = D + part * KVH * HD
        left[:, pl.ds(pl.multiple_of(base + core * HD, 128), HD)] = dkv[:TILE, columns]
        left[:, pl.ds(pl.multiple_of(base + (1 - core) * HD, 128), HD)] = dkv_other[
            TILE:, columns
        ]
    for chunk, group in enumerate(copies):
        for copy in group:
            copy.wait()
        part = slice(chunk * width, (chunk + 1) * width)
        out[:, part] = dot_nt(left[...], right[part]).astype(BF)


def input_grad(dq, dq_other, dkv, dkv_other, w_query, w_key, w_value):
    return pl.pallas_call(
        input_kernel,
        in_specs=[WHOLE] * 4 + [STAY] * 3,
        out_specs=WHOLE,
        out_shape=jax.ShapeDtypeStruct((TILE, D), BF),
        scratch_shapes=[
            pltpu.VMEM((TILE, D + 512), BF),
            pltpu.VMEM((D, D + 512), BF),
            pltpu.SemaphoreType.DMA((IN_CHUNKS, 3)),
        ],
        compiler_params=PARAMS,
        cost_estimate=cost(2 * TILE * D * 2048, 2 * D * 2048),
        name="input_grad",
    )(dq, dq_other, dkv, dkv_other, w_query, w_key, w_value)


def shards(tokens, grad_heads, tile_mask, segments, w_query, w_key, w_value):
    own, up = tokens[0], grad_heads[0]
    other = lax.ppermute(own, "ctx", CORE)
    up_other = lax.ppermute(up, "ctx", CORE)
    mask_other = lax.ppermute(tile_mask[0], "ctx", CORE)
    other, mask_other, up_other = lax.optimization_barrier((other, mask_other, up_other))

    w_query, w_key, w_value = (in_hbm(w) for w in (w_query, w_key, w_value))
    weights, kv_own = project_kv_own(in_hbm(own), w_key, w_value)
    kv = project_kv(other, weights, kv_own)
    kv2 = lax.ppermute(kv, "ctx", chip_pair(2))
    far = {d: lax.ppermute(own, "ctx", chip_pair(d)) for d in (1, 3)}
    query, limits, weights_other = project_query(
        own, other, w_query, w_key, w_value,
        in_hbm(segments), in_hbm(tile_mask[0]), mask_other,
    )
    up = stack_up(up, up_other)
    scores = {0: chip_scores(0, limits, query, up, kv)}
    far, kv2, scores[0] = lax.optimization_barrier((far, kv2, scores[0]))
    late = lax.ppermute(far[3], "ctx", chip_pair(1))
    theirs = project_kv_far(far[1], far[3], weights_other)
    theirs = lax.ppermute(theirs, "ctx", CORE)
    mine = project_kv_far(far[1], far[3], weights)
    for i, d in enumerate((1, 3)):
        scores[d] = chip_scores(d, limits, query, up, mine, theirs, part=i)
    scores[2] = chip_scores(2, limits, query, up, kv2)
    factors = softmax_factors([scores[d][2] for d in range(CHIPS)])
    terms, grad_scores = {}, {}
    for d in (3, 1, 2):
        terms[d], grad_scores[d] = chip_terms(d, *scores[d][:2], factors, query, up)
    back = [lax.ppermute(terms[d], "ctx", chip_pair(d)) for d in (1, 3, 2)]
    terms[0], grad_scores[0] = chip_terms(0, *scores[0][:2], factors, query, up)
    dq, middle, theirs = query_grad(
        [scores[d][3] for d in range(CHIPS)], [grad_scores[d] for d in range(CHIPS)]
    )
    late, back, middle = lax.optimization_barrier((late, back, middle))
    dkv = sum_join(terms[0], *back, middle)
    dkv_other = lax.ppermute(dkv, "ctx", CORE)
    packed = pack(dq, dkv, dkv_other)

    far, dkv = lax.optimization_barrier((far, dkv))
    tokens_t = transpose([own, late, far[1], far[3]])
    tokens_t, packed, theirs = lax.optimization_barrier((tokens_t, packed, theirs))
    dq_other = lax.ppermute(theirs, "ctx", CORE)
    other_t = lax.ppermute(tokens_t, "ctx", CORE)
    columns = {d: lax.ppermute(packed[d], "ctx", chip_pair(d)) for d in (2, 1, 3)}
    columns = [packed[0]] + [columns[d] for d in (2, 1, 3)]
    terms = [weight_grad(d, tokens_t, other_t, columns) for d in range(YS)]
    y_parts = [terms[0]] + [lax.ppermute(terms[d], "dp", y_pair(d)) for d in (1, 3, 2)]
    grad_tokens = input_grad(
        dq, dq_other, dkv, dkv_other, w_query, w_key, w_value
    )
    y_parts, grad_tokens = lax.optimization_barrier((y_parts, grad_tokens))
    y_sum = sum_four(*y_parts)
    z_parts = lax.all_to_all(y_sum, "dp", 0, 0, tiled=True, axis_index_groups=Z_GROUPS)
    grad_projection = jnp.sum(z_parts.reshape(ZS, 48, 256).astype(F32), axis=0)
    return grad_tokens[None], grad_projection


def solution(mesh):
    return jax.shard_map(
        shards,
        mesh=mesh,
        in_specs=(
            P("dp", "ctx", None),
            P("dp", "ctx", None),
            P("dp", "ctx", None),
            P("dp", None),
            P(),
            P(),
            P(),
        ),
        out_specs=(P("dp", "ctx", None), P("dp", "ctx")),
        check_vma=False,
    )
```
